32 devices in a mesh: wide: 16 (over z, y, core), narrow: 2 (over x).
Axes of the slice: x: 2, y: 2, z: 4, core: 2. Of those that a mesh axis runs over, the one named last changes fastest.
Arguments:
- hidden_in: bfloat16 [8192, 768], P('wide'), may hold values from -6 to 6
- gainfirst: float32 [768], replicated, may hold values from 0.5 to 1.5
- shiftfirst: float32 [768], replicated, may hold values from -2 to 2
- valueright: bfloat16 [192, 768], replicated, may hold values from -0.4375 to 0.4375
- valueleft: bfloat16 [192, 768], replicated, may hold values from -0.4375 to 0.4375
- shaperight: bfloat16 [192, 768], replicated, may hold values from -0.4375 to 0.4375
- shapeleft: bfloat16 [192, 768], replicated, may hold values from -0.4375 to 0.4375
- convtaps: float32 [3, 768], replicated, may hold values from -3 to 3
- posweight: float32 [5, 128], replicated, may hold values from -14 to 14
- posbias: float32 [128], replicated, may hold values from -3 to 3
- sinefreq: float32 [128], replicated, may hold values from 1.5 to 2
- midweight: float32 [128, 128], replicated, may hold values from -2.2 to 2.2
- midbias: float32 [128], replicated, may hold values from -3 to 3
- filterout: float32 [128, 768], replicated, may hold values from -0.5 to 0.5
- outright: bfloat16 [192, 768], replicated, may hold values from -0.4375 to 0.4375
- outleft: bfloat16 [192, 768], replicated, may hold values from -0.4375 to 0.4375
- gainsecond: float32 [768], replicated, may hold values from 0.5 to 1.5
- shiftsecond: float32 [768], replicated, may hold values from -2 to 2
- gateright: bfloat16 [192, 768], P(None, 'narrow'), may hold values from -0.4375 to 0.4375
- gateleft: bfloat16 [192, 3072], P(None, 'narrow'), may hold values from -0.4375 to 0.4375
- liftright: bfloat16 [192, 768], P(None, 'narrow'), may hold values from -0.4375 to 0.4375
- liftleft: bfloat16 [192, 3072], P(None, 'narrow'), may hold values from -0.4375 to 0.4375
- lowerright: bfloat16 [768, 768], P(None, 'narrow'), may hold values from -0.21875 to 0.21875
- lowerleft: bfloat16 [192, 768], P('narrow'), may hold values from -0.4375 to 0.4375
- grad_out: bfloat16 [8192, 768], P('wide', 'narrow'), may hold values from -6 to 6
Outputs:
- hidden_out: bfloat16 [8192, 768], P('wide', 'narrow')
- hidden_grad: bfloat16 [8192, 768], P('wide', 'narrow')
- grad_gainfirst: float32 [768], replicated
- grad_shiftfirst: float32 [768], replicated
- grad_valueright: float32 [192, 768], replicated
- grad_valueleft: float32 [192, 768], replicated
- grad_shaperight: float32 [192, 768], replicated
- grad_shapeleft: float32 [192, 768], replicated
- grad_convtaps: float32 [3, 768], replicated
- grad_posweight: float32 [5, 128], replicated
- grad_posbias: float32 [128], replicated
- grad_sinefreq: float32 [128], replicated
- grad_midweight: float32 [128, 128], replicated
- grad_midbias: float32 [128], replicated
- grad_filterout: float32 [128, 768], P(None, ('wide', 'narrow'))
- grad_outright: float32 [192, 768], replicated
- grad_outleft: float32 [192, 768], replicated
- grad_gainsecond: float32 [768], replicated
- grad_shiftsecond: float32 [768], replicated
- grad_gateright: float32 [192, 768], P(None, 'narrow')
- grad_gateleft: float32 [192, 3072], P(None, 'narrow')
- grad_liftright: float32 [192, 768], P(None, 'narrow')
- grad_liftleft: float32 [192, 3072], P(None, 'narrow')
- grad_lowerright: float32 [768, 768], P(None, 'narrow')
- grad_lowerleft: float32 [192, 768], P('narrow')
The draws below stay inside these ranges and needn't reach their ends.
All inputs are finite; a program needn't handle non-finite values.
Results may differ from the reference program's by a relative error of at most 0.02.
Values may be sent and summed in bfloat16 or wider, within the bound.
A program may use at most 192 MiB of HBM per device.

```python
import math
import jax
import jax.numpy as jnp
from jax import lax

D = 768
FF = 3072
BLOCKS = 4
ORDER = 128
EMB = 5
SEQS = 8
TOKENS = 8192
SEQ_LEN = 1024


def steps_of(stream_key, extent, shards, least, high):
    loudness = 1.0
    for axis_at, parts in shards:
        heights = jax.random.uniform(jax.random.fold_in(jax.random.fold_in(stream_key, 6), axis_at), (parts,), jnp.float32, least / len(shards), high / len(shards))
        loudness = loudness * jnp.repeat(jnp.exp(heights), extent[axis_at] // parts).reshape((-1,) + (1,) * (len(extent) - 1 - axis_at))
    return loudness


def bell_draw(rng, extent, scale, bound, shards=(), kind=jnp.bfloat16):
    values = jax.random.normal(rng, extent, jnp.float32) * scale
    if len(shards) > 0:
        values = steps_of(rng, extent, shards, -0.22, 0.18) * values
    return jnp.clip(values, min=-bound, max=bound).astype(kind)


def setup_inputs(seed: int = 0) -> dict:
    splits = jax.random.split(jax.random.key(seed), 26)
    return {
        "hidden_in": bell_draw(splits[0], (TOKENS, D), 1.0, 6.0, ((0, 16),)),
        "gainfirst": jnp.clip(1.0 + 0.1 * jax.random.normal(splits[1], (D,), jnp.float32), 0.5, 1.5),
        "shiftfirst": bell_draw(splits[2], (D,), 0.3, 2.0, (), jnp.float32),
        "valueright": bell_draw(splits[3], (D // BLOCKS, D), (D // BLOCKS) ** -0.5, 0.4375),
        "valueleft": bell_draw(splits[4], (D // BLOCKS, D), (D // BLOCKS) ** -0.5, 0.4375),
        "shaperight": bell_draw(splits[5], (D // BLOCKS, D), (D // BLOCKS) ** -0.5, 0.4375),
        "shapeleft": bell_draw(splits[6], (D // BLOCKS, D), (D // BLOCKS) ** -0.5, 0.4375),
        "convtaps": bell_draw(splits[7], (3, D), 0.6, 3.0, (), jnp.float32),
        "posweight": jnp.clip(jax.random.uniform(splits[8], (EMB, ORDER), jnp.float32, -14.0, 14.0), -14.0, 14.0),
        "posbias": bell_draw(splits[9], (ORDER,), 0.5, 3.0, (), jnp.float32),
        "sinefreq": jnp.clip(jax.random.uniform(splits[10], (ORDER,), jnp.float32, 1.5, 2.0), 1.5, 2.0),
        "midweight": jnp.clip(jax.random.uniform(splits[11], (ORDER, ORDER), jnp.float32, -2.2, 2.2), -2.2, 2.2),
        "midbias": bell_draw(splits[12], (ORDER,), 0.5, 3.0, (), jnp.float32),
        "filterout": bell_draw(splits[13], (ORDER, D), ORDER ** -0.5, 0.5, (), jnp.float32),
        "outright": bell_draw(splits[14], (D // BLOCKS, D), (D // BLOCKS) ** -0.5, 0.4375),
        "outleft": bell_draw(splits[15], (D // BLOCKS, D), (D // BLOCKS) ** -0.5, 0.4375),
        "gainsecond": jnp.clip(1.0 + 0.1 * jax.random.normal(splits[16], (D,), jnp.float32), 0.5, 1.5),
        "shiftsecond": bell_draw(splits[17], (D,), 0.3, 2.0, (), jnp.float32),
        "gateright": bell_draw(splits[18], (D // BLOCKS, D), (D // BLOCKS) ** -0.5, 0.4375, ((1, 2),)),
        "gateleft": bell_draw(splits[19], (D // BLOCKS, FF), (D // BLOCKS) ** -0.5, 0.4375, ((1, 2),)),
        "liftright": bell_draw(splits[20], (D // BLOCKS, D), (D // BLOCKS) ** -0.5, 0.4375, ((1, 2),)),
        "liftleft": bell_draw(splits[21], (D // BLOCKS, FF), (D // BLOCKS) ** -0.5, 0.4375, ((1, 2),)),
        "lowerright": bell_draw(splits[22], (FF // BLOCKS, D), (FF // BLOCKS) ** -0.5, 0.21875, ((1, 2),)),
        "lowerleft": bell_draw(splits[23], (D // BLOCKS, D), (D // BLOCKS) ** -0.5, 0.4375, ((0, 2),)),
        "grad_out": bell_draw(splits[24], (TOKENS, D), 1.0, 6.0, ((0, 16), (1, 2))),
    }


HIGHEST = lax.Precision.HIGHEST

@jax.custom_vjp
def low(v):
    return lax.optimization_barrier(v.astype(jnp.bfloat16)).astype(jnp.float32)

@jax.custom_vjp
def low_back(v):
    return v

def low_keep(v):
    return (low(v), None)

def low_pass(kept, grad):
    return (grad,)

def back_keep(v):
    return (v, None)

def back_low(kept, grad):
    return (low(grad),)
low.defvjp(low_keep, low_pass)
low_back.defvjp(back_keep, back_low)

def layer_norm(values, gain, shift):
    center = values - lax.optimization_barrier(jnp.mean(values, axis=-1, keepdims=True))
    spread = lax.optimization_barrier(jnp.mean(center * center, axis=-1, keepdims=True))
    return center * lax.rsqrt(spread + 1e-05) * gain + shift

def monarch(inputs, right, left, group_first):
    rowcount = inputs.shape[0]
    width_in = right.shape[0]
    nblocks = inputs.shape[1] // width_in
    groups = BLOCKS
    piece = left.shape[0] // nblocks
    blocked = inputs.reshape(rowcount, nblocks, width_in)
    if group_first:
        first = jnp.einsum('tbi,ikbc->tkbc', blocked, right.reshape(width_in, groups, nblocks, piece), precision=HIGHEST)
    else:
        first = jnp.einsum('tbi,ibkc->tkbc', blocked, right.reshape(width_in, nblocks, groups, piece), precision=HIGHEST)
    first = first.reshape(rowcount, groups, nblocks * piece)
    first = low_back(low(first))
    result = jnp.einsum('tkj,jke->tke', first, left.reshape(left.shape[0], groups, -1), precision=HIGHEST)
    return result.reshape(rowcount, -1)

def position_features(length):
    places = jnp.arange(length, dtype=jnp.float32)
    angle = places * (2.0 * math.pi / length)
    return jnp.stack([places / length, jnp.cos(angle), jnp.sin(angle), jnp.cos(2.0 * angle), jnp.sin(2.0 * angle)], axis=1)

def decay_factors(channel_ids, length):
    rank = (channel_ids * 5 % D).astype(jnp.float32) / D
    lowest = math.log(0.25 / length)
    highest = math.log(1.0 / 30.0)
    rate = jnp.exp(lowest + rank * (highest - lowest))
    places = jnp.arange(length, dtype=jnp.float32)
    return jnp.exp(-rate[:, None] * places[None, :]) * jnp.sqrt(2.0 * rate)[:, None]

def filter_taps(posweight, posbias, sinefreq, midweight, midbias, filterout):
    feats = position_features(SEQ_LEN)
    act_one = jnp.sin(sinefreq * (jnp.dot(feats, posweight, precision=HIGHEST) + posbias))
    act_two = jnp.sin(sinefreq * (jnp.dot(act_one, midweight, precision=HIGHEST) + midbias))
    raw = jnp.dot(act_two, filterout, precision=HIGHEST)
    return raw.T * decay_factors(jnp.arange(D, dtype=jnp.int32), SEQ_LEN)

def long_conv(signal, weights):
    length = signal.shape[0]
    spectrum = jnp.fft.rfft(signal, n=2 * length, axis=0) * jnp.fft.rfft(weights.T, n=2 * length, axis=0)
    return jnp.fft.irfft(spectrum, n=2 * length, axis=0)[:length]

def layer_pass(inputs, params):
    gainfirst, shiftfirst, valueright, valueleft, shaperight, shapeleft, convtaps, posweight, posbias, sinefreq, midweight, midbias, filterout, outright, outleft, gainsecond, shiftsecond, gateright, gateleft, liftright, liftleft, lowerright, lowerleft = params
    taps = filter_taps(posweight, posbias, sinefreq, midweight, midbias, filterout)
    normone = low(layer_norm(inputs, gainfirst, shiftfirst))
    signal = low_back(low(monarch(normone, valueright, valueleft, False)))
    shaping = low_back(monarch(normone, shaperight, shapeleft, False))
    padded = jnp.concatenate([jnp.zeros((2, inputs.shape[1]), jnp.float32), signal], axis=0)
    shortconv = convtaps[0] * padded[2:] + convtaps[1] * padded[1:-1] + convtaps[2] * padded[:-2]
    shortconv = low_back(low(shortconv))
    longconv = low_back(low(long_conv(shortconv, taps)))
    mixed = low(shaping * longconv)
    middle = inputs + low_back(monarch(mixed, outright, outleft, False))
    normtwo = low(layer_norm(middle, gainsecond, shiftsecond))
    pregate = low_back(monarch(normtwo, gateright, gateleft, True))
    prelift = low_back(monarch(normtwo, liftright, liftleft, True))
    hidden = low(jax.nn.gelu(pregate, approximate=False) * prelift)
    return middle + monarch(hidden, lowerright, lowerleft, False)

def reference(hidden_in, gainfirst, shiftfirst, valueright, valueleft, shaperight, shapeleft, convtaps, posweight, posbias, sinefreq, midweight, midbias, filterout, outright, outleft, gainsecond, shiftsecond, gateright, gateleft, liftright, liftleft, lowerright, lowerleft, grad_out):
    params = tuple((item_array.astype(jnp.float32) for item_array in (gainfirst, shiftfirst, valueright, valueleft, shaperight, shapeleft, convtaps, posweight, posbias, sinefreq, midweight, midbias, filterout, outright, outleft, gainsecond, shiftsecond, gateright, gateleft, liftright, liftleft, lowerright, lowerleft)))
    sequences = hidden_in.astype(jnp.float32).reshape(SEQS, SEQ_LEN, D)
    cotangent = grad_out.astype(jnp.float32).reshape(SEQS, SEQ_LEN, D)

    def one_sequence(summed, pair_item):
        inputs, upstream = pair_item
        outputs, pullback = jax.vjp(layer_pass, inputs, params)
        grad_inputs, grad_params = pullback(upstream)
        return (jax.tree.map(jnp.add, summed, grad_params), (outputs, grad_inputs))
    zeros_init = jax.tree.map(jnp.zeros_like, params)
    summed, (outputs, grad_inputs) = lax.scan(one_sequence, zeros_init, (sequences, cotangent))
    return (outputs.reshape(TOKENS, D).astype(jnp.bfloat16), grad_inputs.reshape(TOKENS, D).astype(jnp.bfloat16), summed[0], summed[1], summed[2], summed[3], summed[4], summed[5], summed[6], summed[7], summed[8], summed[9], summed[10], summed[11], summed[12], summed[13], summed[14], summed[15], summed[16], summed[17], summed[18], summed[19], summed[20], summed[21], summed[22])
```

```python
import math

import jax
import jax.numpy as jnp
import numpy as np
from jax import lax
from jax.experimental import pallas as pl
from jax.experimental.pallas import tpu as pltpu
from jax.sharding import PartitionSpec as P

D = 768
BLOCKS = 4
SEQS = 8


EPSILON = 1e-05
HIGHEST = lax.Precision.HIGHEST


def from_behind(x, axis, by):
    length = lax.axis_size(axis)
    pairs = [(i, i + by) for i in range(length) if 0 <= i + by < length]
    return lax.ppermute(x, axis, pairs)


def norm_forward(values, gain, shift):
    center = values - jnp.mean(values, axis=-1, keepdims=True)
    inverse = lax.rsqrt(jnp.mean(center * center, axis=-1, keepdims=True) + EPSILON)
    normed = center * inverse
    return (normed * gain + shift, normed, inverse)


def norm_backward(upstream, normed, inverse, gain):
    scaled = upstream * gain
    result = inverse * (
        scaled
        - jnp.mean(scaled, axis=-1, keepdims=True)
        - normed * jnp.mean(scaled * normed, axis=-1, keepdims=True)
    )
    return (result, jnp.sum(upstream * normed, axis=0), jnp.sum(upstream, axis=0))


def right_view(right, nblocks, groups, group_first):
    width_in = right.shape[0]
    piece = right.shape[1] // (nblocks * groups)
    if group_first:
        return (right.reshape(width_in, groups, nblocks, piece), "ikbc")
    return (right.reshape(width_in, nblocks, groups, piece), "ibkc")


def section_one(inputs, right, groups, group_first):
    rowcount = inputs.shape[0]
    width_in = right.shape[0]
    nblocks = inputs.shape[1] // width_in
    factor, letters = right_view(right, nblocks, groups, group_first)
    first = jnp.einsum(
        "tbi," + letters + "->tkbc",
        inputs.reshape(rowcount, nblocks, width_in),
        factor,
        preferred_element_type=jnp.float32,
    )
    return first.reshape(rowcount, groups, -1).astype(jnp.bfloat16)


def section_two(middle_part, left):
    groups = middle_part.shape[1]
    result = jnp.einsum(
        "tkj,jke->tke",
        middle_part,
        left.reshape(left.shape[0], groups, -1),
        preferred_element_type=jnp.float32,
    )
    return result.reshape(result.shape[0], -1)


def back_two(middle_part, left, upstream):
    groups = middle_part.shape[1]
    left_view = left.reshape(left.shape[0], groups, -1)
    grad_left = jnp.einsum(
        "tkj,tke->jke", middle_part, upstream, preferred_element_type=jnp.float32
    )
    grad_middle = jnp.einsum(
        "tke,jke->tkj", upstream, left_view, preferred_element_type=jnp.float32
    )
    return (grad_left.reshape(left.shape[0], -1), grad_middle.astype(jnp.bfloat16))


def back_one(inputs, right, grad_middle, group_first):
    rowcount = inputs.shape[0]
    width_in = right.shape[0]
    nblocks = inputs.shape[1] // width_in
    groups = grad_middle.shape[1]
    factor, letters = right_view(right, nblocks, groups, group_first)
    spread_back = grad_middle.reshape(rowcount, groups, nblocks, -1)
    blocked = inputs.reshape(rowcount, nblocks, width_in)
    grad_right = jnp.einsum(
        "tbi,tkbc->" + letters, blocked, spread_back, preferred_element_type=jnp.float32
    )
    grad_inputs = jnp.einsum(
        "tkbc," + letters + "->tbi", spread_back, factor, preferred_element_type=jnp.float32
    )
    return (grad_right.reshape(width_in, -1), grad_inputs.reshape(rowcount, -1))


def fourier_tables(length):
    span = length // 128
    slow_index = jnp.arange(span, dtype=jnp.int32)
    fast_index = jnp.arange(128, dtype=jnp.int32)
    small = (slow_index[:, None] * slow_index[None, :] % span).astype(jnp.float32) * (
        2.0 * math.pi / span
    )
    twist = (slow_index[:, None] * fast_index[None, :] % length).astype(jnp.float32) * (
        2.0 * math.pi / length
    )
    large = (fast_index[:, None] * fast_index[None, :] % 128).astype(jnp.float32) * (
        2.0 * math.pi / 128
    )
    return (
        jnp.cos(small),
        jnp.sin(small),
        jnp.cos(twist),
        jnp.sin(twist),
        jnp.cos(large),
        jnp.sin(large),
    )


def to_spectrum(signal, tables):
    cos_small, sin_small, cos_twist, sin_twist, cos_large, sin_large = tables
    span = cos_small.shape[0]
    padded = jnp.concatenate([signal, jnp.zeros_like(signal)], axis=-1)
    padded = padded.reshape(signal.shape[:-1] + (span, 128))
    first_re = jnp.einsum("...qp,qk->...kp", padded, cos_small, precision=HIGHEST)
    first_im = -jnp.einsum("...qp,qk->...kp", padded, sin_small, precision=HIGHEST)
    turned_re = first_re * cos_twist + first_im * sin_twist
    turned_im = first_im * cos_twist - first_re * sin_twist
    out_re = jnp.einsum("...kp,pj->...kj", turned_re, cos_large, precision=HIGHEST) + jnp.einsum(
        "...kp,pj->...kj", turned_im, sin_large, precision=HIGHEST
    )
    out_im = jnp.einsum("...kp,pj->...kj", turned_im, cos_large, precision=HIGHEST) - jnp.einsum(
        "...kp,pj->...kj", turned_re, sin_large, precision=HIGHEST
    )
    return (out_re, out_im)


def from_spectrum(real_part, imag_part, tables):
    cos_small, sin_small, cos_twist, sin_twist, cos_large, sin_large = tables
    span = cos_small.shape[0]
    back_re = jnp.einsum("...kj,pj->...kp", real_part, cos_large, precision=HIGHEST) - jnp.einsum(
        "...kj,pj->...kp", imag_part, sin_large, precision=HIGHEST
    )
    back_im = jnp.einsum("...kj,pj->...kp", imag_part, cos_large, precision=HIGHEST) + jnp.einsum(
        "...kj,pj->...kp", real_part, sin_large, precision=HIGHEST
    )
    turned_re = back_re * cos_twist - back_im * sin_twist
    turned_im = back_im * cos_twist + back_re * sin_twist
    signal = (
        jnp.einsum("...kp,qk->...qp", turned_re, cos_small, precision=HIGHEST)
        - jnp.einsum("...kp,qk->...qp", turned_im, sin_small, precision=HIGHEST)
    ) / (span * 128)
    signal = signal.reshape(signal.shape[:-2] + (span * 128,))
    return signal[..., : span * 64]


def position_features(length):
    places = jnp.arange(length, dtype=jnp.float32)
    angle = places * (2.0 * math.pi / length)
    return jnp.stack(
        [
            places / length,
            jnp.cos(angle),
            jnp.sin(angle),
            jnp.cos(2.0 * angle),
            jnp.sin(2.0 * angle),
        ],
        axis=1,
    )


def decay_factors(channel_ids, length):
    rank = (channel_ids * 5 % D).astype(jnp.float32) / D
    lowest = math.log(0.25 / length)
    highest = math.log(1.0 / 30.0)
    rate = jnp.exp(lowest + rank * (highest - lowest))
    places = jnp.arange(length, dtype=jnp.float32)
    return jnp.exp(-rate[:, None] * places[None, :]) * jnp.sqrt(2.0 * rate)[:, None]


def channel_order(data, nwide, nnarrow, rows_half):
    count = data.shape[0]
    return data.reshape(count, nnarrow, nwide, rows_half).transpose(0, 2, 1, 3).reshape(count, -1)


def row_order(data, nwide, nnarrow):
    total = data.shape[0]
    rows_half = data.shape[1]
    count = total // (nwide * nnarrow)
    return (
        data.reshape(nnarrow, nwide, count, rows_half)
        .transpose(1, 0, 2, 3)
        .reshape(total, rows_half)
        .T
    )


def body(
    hidden_in,
    gainfirst,
    shiftfirst,
    valueright,
    valueleft,
    shaperight,
    shapeleft,
    convtaps,
    posweight,
    posbias,
    sinefreq,
    midweight,
    midbias,
    filterout,
    outright,
    outleft,
    gainsecond,
    shiftsecond,
    gateright,
    gateleft,
    liftright,
    liftleft,
    lowerright,
    lowerleft,
    grad_out,
):
    rowcount = hidden_in.shape[0]
    local_groups = gateright.shape[1] // gateleft.shape[0]
    nwide = lax.axis_size("wide")
    nnarrow = lax.axis_size("narrow")
    narrow_index = lax.axis_index("narrow")
    rows_half = rowcount // nnarrow
    row_start = narrow_index * rows_half
    combined = lax.axis_index("wide") * nnarrow + narrow_index
    resid = lax.dynamic_slice_in_dim(hidden_in, row_start, rows_half, 0).astype(jnp.float32)
    normone, hat_one, inv_one = norm_forward(resid, gainfirst, shiftfirst)
    normone = normone.astype(jnp.bfloat16)
    mid_value = section_one(normone, valueright, BLOCKS, False)
    signal = section_two(mid_value, valueleft).astype(jnp.bfloat16)
    mid_shape = section_one(normone, shaperight, BLOCKS, False)
    shaping = section_two(mid_shape, shapeleft)
    group = nwide // SEQS * nnarrow
    place = combined % group
    before = from_behind(signal[-2:], ("wide", "narrow"), 1)
    before = jnp.where(place == 0, jnp.zeros_like(before), before)
    extended = jnp.concatenate([before, signal], axis=0).astype(jnp.float32)
    shortconv = (
        convtaps[0] * extended[2:] + convtaps[1] * extended[1:-1] + convtaps[2] * extended[:-2]
    ).astype(jnp.bfloat16)
    channels = lax.all_to_all(
        lax.all_to_all(shortconv.T, "wide", split_axis=0, concat_axis=1, tiled=True),
        "narrow",
        split_axis=0,
        concat_axis=1,
        tiled=True,
    )
    channels = channel_order(channels, nwide, nnarrow, rows_half)
    count = channels.shape[0]
    length = channels.shape[1] // SEQS
    feats = position_features(length)
    lin_one = jnp.dot(feats, posweight, precision=HIGHEST) + posbias
    act_one = jnp.sin(sinefreq * lin_one)
    lin_two = jnp.dot(act_one, midweight, precision=HIGHEST) + midbias
    act_two = jnp.sin(sinefreq * lin_two)
    own_cols = lax.dynamic_slice_in_dim(filterout, combined * count, count, 1)
    channel_ids = combined * count + jnp.arange(count, dtype=jnp.int32)
    modulation = decay_factors(channel_ids, length)
    taps = jnp.dot(act_two, own_cols, precision=HIGHEST).T * modulation
    tables = fourier_tables(2 * length)
    sig_re, sig_im = to_spectrum(channels.astype(jnp.float32).reshape(count, SEQS, length), tables)
    fil_re, fil_im = to_spectrum(taps.reshape(count, 1, length), tables)
    conv_chan = from_spectrum(
        sig_re * fil_re - sig_im * fil_im, sig_re * fil_im + sig_im * fil_re, tables
    )
    conv_chan = conv_chan.reshape(count, SEQS * length).astype(jnp.bfloat16)
    longconv = lax.all_to_all(
        lax.all_to_all(conv_chan, "wide", split_axis=1, concat_axis=0, tiled=True),
        "narrow",
        split_axis=1,
        concat_axis=0,
        tiled=True,
    )
    longconv = row_order(longconv, nwide, nnarrow)
    mixed = (shaping * longconv.astype(jnp.float32)).astype(jnp.bfloat16)
    mid_out = section_one(mixed, outright, BLOCKS, False)
    middle = resid + section_two(mid_out, outleft)
    normtwo, hat_two, inv_two = norm_forward(middle, gainsecond, shiftsecond)
    normtwo = normtwo.astype(jnp.bfloat16)
    norm_all = lax.all_gather(normtwo, "narrow", axis=0, tiled=True)
    mid_gate = section_one(norm_all, gateright, local_groups, True)
    pregate = section_two(mid_gate, gateleft)
    mid_lift = section_one(norm_all, liftright, local_groups, True)
    prelift = section_two(mid_lift, liftleft)
    cumulative = 0.5 * (1.0 + lax.erf(pregate * (1.0 / math.sqrt(2.0))))
    activated = pregate * cumulative
    hidden = (activated * prelift).astype(jnp.bfloat16)
    mid_lower = section_one(hidden, lowerright, BLOCKS, False)
    partial_sum = section_two(mid_lower, lowerleft)
    partial_sum = partial_sum + lax.dynamic_update_slice_in_dim(
        jnp.zeros_like(partial_sum), middle, row_start, 0
    )
    hidden_out = lax.psum_scatter(
        partial_sum.astype(jnp.bfloat16), "narrow", scatter_dimension=1, tiled=True
    )
    upstream = lax.all_gather(grad_out, "narrow", axis=1, tiled=True)
    grad_lowerleft, grad_mid_lower = back_two(
        mid_lower, lowerleft, upstream.reshape(rowcount, BLOCKS, -1)
    )
    grad_lowerright, grad_hidden = back_one(hidden, lowerright, grad_mid_lower, False)
    density = jnp.exp(-0.5 * pregate * pregate) * (1.0 / math.sqrt(2.0 * math.pi))
    grad_pregate = (grad_hidden * prelift * (cumulative + pregate * density)).astype(jnp.bfloat16)
    grad_prelift = (grad_hidden * activated).astype(jnp.bfloat16)
    grad_gateleft, grad_mid_gate = back_two(
        mid_gate, gateleft, grad_pregate.reshape(rowcount, local_groups, -1)
    )
    grad_gateright, into_gate = back_one(norm_all, gateright, grad_mid_gate, True)
    grad_liftleft, grad_mid_lift = back_two(
        mid_lift, liftleft, grad_prelift.reshape(rowcount, local_groups, -1)
    )
    grad_liftright, into_lift = back_one(norm_all, liftright, grad_mid_lift, True)
    ffn_local = (
        grad_gateright,
        grad_gateleft,
        grad_liftright,
        grad_liftleft,
        grad_lowerright,
        grad_lowerleft,
    )
    dnormtwo = lax.psum_scatter(
        (into_gate + into_lift).astype(jnp.bfloat16), "narrow", scatter_dimension=0, tiled=True
    ).astype(jnp.float32)
    back_two_norm, grad_gainsecond, grad_shiftsecond = norm_backward(
        dnormtwo, hat_two, inv_two, gainsecond
    )
    up_rows = lax.dynamic_slice_in_dim(upstream, row_start, rows_half, 0)
    dmiddle = up_rows.astype(jnp.float32) + back_two_norm
    dbranch = dmiddle.astype(jnp.bfloat16)
    grad_outleft, grad_mid_out = back_two(mid_out, outleft, dbranch.reshape(rows_half, BLOCKS, -1))
    grad_outright, dmixed = back_one(mixed, outright, grad_mid_out, False)
    dshaping = (dmixed * longconv.astype(jnp.float32)).astype(jnp.bfloat16)
    dlong = (dmixed * shaping).astype(jnp.bfloat16)
    grad_chan = lax.all_to_all(
        lax.all_to_all(dlong.T, "wide", split_axis=0, concat_axis=1, tiled=True),
        "narrow",
        split_axis=0,
        concat_axis=1,
        tiled=True,
    )
    grad_chan = channel_order(grad_chan, nwide, nnarrow, rows_half)
    dlong_re, dlong_im = to_spectrum(
        grad_chan.astype(jnp.float32).reshape(count, SEQS, length), tables
    )
    dshort_chan = from_spectrum(
        dlong_re * fil_re + dlong_im * fil_im, dlong_im * fil_re - dlong_re * fil_im, tables
    )
    dshort_chan = dshort_chan.reshape(count, SEQS * length).astype(jnp.bfloat16)
    filt_re = jnp.sum(dlong_re * sig_re + dlong_im * sig_im, axis=1, keepdims=True)
    filt_im = jnp.sum(dlong_im * sig_re - dlong_re * sig_im, axis=1, keepdims=True)
    grad_taps = from_spectrum(filt_re, filt_im, tables).reshape(count, length)
    dshort = lax.all_to_all(
        lax.all_to_all(dshort_chan, "wide", split_axis=1, concat_axis=0, tiled=True),
        "narrow",
        split_axis=1,
        concat_axis=0,
        tiled=True,
    )
    dshort = row_order(dshort, nwide, nnarrow)
    grad_modded = grad_taps * modulation
    grad_filterout = jnp.dot(act_two.T, grad_modded.T, precision=HIGHEST)
    dact_two = jnp.dot(grad_modded.T, own_cols.T, precision=HIGHEST)
    dlin_two = dact_two * jnp.cos(sinefreq * lin_two)
    scaled_two = dlin_two * sinefreq
    grad_midweight = jnp.dot(act_one.T, scaled_two, precision=HIGHEST)
    grad_midbias = jnp.sum(scaled_two, axis=0)
    dact_one = jnp.dot(scaled_two, midweight.T, precision=HIGHEST)
    dlin_one = dact_one * jnp.cos(sinefreq * lin_one)
    scaled_one = dlin_one * sinefreq
    grad_posweight = jnp.dot(feats.T, scaled_one, precision=HIGHEST)
    grad_posbias = jnp.sum(scaled_one, axis=0)
    grad_sinefreq = jnp.sum(dlin_one * lin_one, axis=0) + jnp.sum(dlin_two * lin_two, axis=0)
    after = from_behind(dshort[:2], ("wide", "narrow"), -1)
    after = jnp.where(place == group - 1, jnp.zeros_like(after), after)
    ext_grad = jnp.concatenate([dshort, after], axis=0).astype(jnp.float32)
    dsignal = (
        convtaps[0] * ext_grad[:-2] + convtaps[1] * ext_grad[1:-1] + convtaps[2] * ext_grad[2:]
    ).astype(jnp.bfloat16)
    short_grad = dshort.astype(jnp.float32)
    grad_convtaps = jnp.stack(
        [
            jnp.sum(extended[2:] * short_grad, axis=0),
            jnp.sum(extended[1:-1] * short_grad, axis=0),
            jnp.sum(extended[:-2] * short_grad, axis=0),
        ]
    )
    grad_valueleft, grad_mid_value = back_two(
        mid_value, valueleft, dsignal.reshape(rows_half, BLOCKS, -1)
    )
    grad_valueright, into_value = back_one(normone, valueright, grad_mid_value, False)
    grad_shapeleft, grad_mid_shape = back_two(
        mid_shape, shapeleft, dshaping.reshape(rows_half, BLOCKS, -1)
    )
    grad_shaperight, into_shape = back_one(normone, shaperight, grad_mid_shape, False)
    back_one_norm, grad_gainfirst, grad_shiftfirst = norm_backward(
        into_value + into_shape, hat_one, inv_one, gainfirst
    )
    full_grad = (dmiddle + back_one_norm).astype(jnp.bfloat16)
    hidden_grad = lax.all_to_all(full_grad, "narrow", split_axis=1, concat_axis=0, tiled=True)
    mixer_grads = lax.psum(
        (
            grad_gainfirst,
            grad_shiftfirst,
            grad_valueright,
            grad_valueleft,
            grad_shaperight,
            grad_shapeleft,
            grad_convtaps,
            grad_posweight,
            grad_posbias,
            grad_sinefreq,
            grad_midweight,
            grad_midbias,
            grad_outright,
            grad_outleft,
            grad_gainsecond,
            grad_shiftsecond,
        ),
        ("wide", "narrow"),
    )
    ffn_grads = lax.psum(
        (ffn_local[0], ffn_local[1], ffn_local[2], ffn_local[3], ffn_local[4], ffn_local[5]), "wide"
    )
    return (
        hidden_out,
        hidden_grad,
        mixer_grads[0],
        mixer_grads[1],
        mixer_grads[2],
        mixer_grads[3],
        mixer_grads[4],
        mixer_grads[5],
        mixer_grads[6],
        mixer_grads[7],
        mixer_grads[8],
        mixer_grads[9],
        mixer_grads[10],
        mixer_grads[11],
        grad_filterout,
        mixer_grads[12],
        mixer_grads[13],
        mixer_grads[14],
        mixer_grads[15],
        ffn_grads[0],
        ffn_grads[1],
        ffn_grads[2],
        ffn_grads[3],
        ffn_grads[4],
        ffn_grads[5],
    )


F32 = jnp.float32
BF16 = jnp.bfloat16
MESH = pl.DeviceIdType.MESH
TILE = 256
PAD = 256


def mm(a, b, precision=None):
    return lax.dot_general(
        a, b, (((1,), (0,)), ((), ())), precision=precision, preferred_element_type=F32
    )


def mm_nt(a, b, precision=None):
    return lax.dot_general(
        a, b, (((1,), (1,)), ((), ())), precision=precision, preferred_element_type=F32
    )


def mm_tn(a, b, precision=None):
    return lax.dot_general(
        a, b, (((0,), (0,)), ((), ())), precision=precision, preferred_element_type=F32
    )


def lanes(width):
    return lax.broadcasted_iota(jnp.int32, (1, width), 1)


def mask(condition, dtype=BF16):
    return jnp.where(condition, 1.0, 0.0).astype(dtype)


def between(width, low, high, dtype=BF16):
    lane = lanes(width)
    return mask((lane >= low) & (lane < high), dtype)


def join(first, second):
    return jnp.concatenate(
        [first[:, :128], first[:, 128:] + second[:, :128], second[:, 128:]], axis=1
    )


def sine_cosine(angle):
    turns = jnp.floor(angle * (1.0 / math.pi) + 0.5)
    rest = angle - turns * 3.140625
    rest = rest - turns * 9.67502593994140625e-4
    rest = rest - turns * 1.509957990978376e-7
    flip = 1.0 - 2.0 * (turns - 2.0 * jnp.floor(turns * 0.5))
    square = rest * rest
    sine = 1.0
    for divisor in (110.0, 72.0, 42.0, 20.0, 6.0):
        sine = 1.0 - square * (1.0 / divisor) * sine
    cosine = 1.0
    for divisor in (132.0, 90.0, 56.0, 30.0, 12.0, 2.0):
        cosine = 1.0 - square * (1.0 / divisor) * cosine
    return (sine * rest * flip, cosine * flip)


def fold(whole, side):
    return [
        whole[192 * b + 96 * side : 192 * b + 96 * side + 48, :] * between(384, 0, 192, F32)
        + whole[192 * b + 96 * side + 48 : 192 * b + 96 * side + 96, :] * between(384, 192, 384, F32)
        for b in range(2)
    ]


def tile_rows(index, size=TILE):
    return pl.ds(pl.multiple_of(index * size, size), size)


def whole_kernel(
    inputs,
    upstream,
    table_cos,
    table_sin,
    place,
    vectors,
    filter_vectors,
    midweight,
    filterout,
    valueright,
    valueleft,
    shaperight,
    shapeleft,
    outright,
    outleft,
    gateright,
    gateleft,
    liftright,
    liftleft,
    lowerright,
    lowerleft,
    hidden_out,
    hidden_grad,
    grad_valueright,
    grad_valueleft,
    grad_shaperight,
    grad_shapeleft,
    grad_outright,
    grad_outleft,
    grad_gateright,
    grad_gateleft,
    grad_liftright,
    grad_liftleft,
    grad_lowerright,
    grad_lowerleft,
    grad_filterout,
    grad_vectors,
    grad_filter,
    w_first,
    w_value,
    w_shape,
    w_out_first,
    w_out_second,
    w_glu,
    w_gate,
    w_lift,
    w_lower,
    w_lower_second,
    up_halves,
    stats,
    norm_one,
    inner_one,
    sig_halves,
    sig_rows,
    shaping,
    sig_pad,
    short,
    lin_one,
    act_one,
    cos_one,
    lin_two,
    act_two,
    cos_two,
    fil_spec,
    sig_spec,
    prod_spec,
    long_rows,
    long_halves,
    inner_out,
    hat_two,
    norm_two,
    inner_glu,
    factor_gate,
    factor_lift,
    hid,
    inner_lower,
    out_own,
    part_send,
    part_recv,
    d_inner_lower,
    d_gate,
    d_lift,
    d_inner_glu,
    dn_own,
    dn_send,
    dn_recv,
    d_inner_out,
    d_shaping,
    dl_rows,
    ds_pad,
    ds_halves,
    d_inner_one,
    tail_own,
    do_send,
    do_recv,
    d_lin,
    own_out,
    send_sem,
    recv_sem,
    load_sem,
):
    rows = inputs.shape[0]
    half = rows // 2
    tiles = rows // TILE
    length = 2 * rows
    spans = length // TILE
    wide = lax.axis_index("wide")
    narrow = lax.axis_index("narrow")
    core = lax.rem(wide, 2)
    sibling = (wide + 1 - 2 * core, narrow)
    partner = (wide, 1 - narrow)
    quarter = 2 * narrow + core
    own_half = pl.ds(pl.multiple_of(narrow * 384, 384), 384)
    other_half = pl.ds(pl.multiple_of((1 - narrow) * 384, 384), 384)

    barrier = pltpu.get_barrier_semaphore()
    for device in (sibling, partner):
        pl.semaphore_signal(barrier, inc=1, device_id=device, device_id_type=MESH)
    pl.semaphore_wait(barrier, 2)

    def send(source, target, device, index):
        return pltpu.make_async_remote_copy(
            src_ref=source,
            dst_ref=target,
            send_sem=send_sem.at[index],
            recv_sem=recv_sem.at[index],
            device_id=device,
            device_id_type=MESH,
        )

    load_copies = []
    for source, target in ((gateleft, w_gate), (liftleft, w_lift)):
        for k in range(2):
            copy = pltpu.make_async_copy(
                source.at[:, pl.ds(D * k, D)],
                target.at[k, pl.ds(64 * k, 192)],
                load_sem.at[len(load_copies)],
            )
            copy.start()
            load_copies.append(copy)

    up_copy = send(upstream, up_halves.at[narrow], partner, 0)
    up_copy.start()
    up_halves[narrow] = upstream[...]

    row = lax.broadcasted_iota(jnp.int32, (D, 384), 0)
    lane = lax.broadcasted_iota(jnp.int32, (D, 384), 1)
    step = jnp.where(lane >= 96, 96, 0) + jnp.where(lane >= 192, 96, 0) + jnp.where(lane >= 288, 96, 0)
    select = mask(row == lane + step + narrow * 96)
    right_half = mm(valueright[...], select).astype(BF16)
    shape_half = mm(shaperight[...], select).astype(BF16)
    for b in range(4):
        kept = between(384, 96 * b, 96 * b + 96)
        w_first[192 * b : 192 * b + 192, 0:384] = right_half * kept
        w_first[192 * b : 192 * b + 192, 384:768] = shape_half * kept
    row = lax.broadcasted_iota(jnp.int32, (D, 2 * PAD), 0)
    lane = lax.broadcasted_iota(jnp.int32, (D, 2 * PAD), 1)
    group = jnp.where(lane >= PAD, 1, 0)
    entry = lane - PAD * group
    spread = mask((row == (2 * narrow + group) * 192 + entry) & (entry < 192))
    for source, target in ((valueleft, w_value), (shapeleft, w_shape)):
        wider = mm(source[...], spread).astype(BF16)
        for b in range(4):
            for k in range(2):
                target[96 * b + 48 * k : 96 * b + 48 * k + 48, :] = wider[
                    48 * b : 48 * b + 48, :
                ] * between(2 * PAD, PAD * k, PAD * k + PAD)
    first = vectors[0:1, :]
    shift_first = vectors[1:2, :]

    @pl.loop(0, tiles)
    def _(index):
        at = tile_rows(index)
        values = inputs[at, :].astype(F32)
        average = jnp.mean(values, axis=-1, keepdims=True)
        center = values - average
        inverse = lax.rsqrt(jnp.mean(center * center, axis=-1, keepdims=True) + EPSILON)
        hat = center * inverse
        stats[at, 0:1] = average
        stats[at, 1:2] = inverse
        normed = (hat * first + shift_first).astype(BF16)
        norm_one[at, :] = normed
        inner = mm(normed, w_first[...]).astype(BF16)
        inner_one[at, :] = inner
        signal = mm(inner[:, :384], w_value[...]).astype(BF16)
        sig_halves[0, at, :] = signal[:, :PAD]
        sig_halves[1, at, :] = signal[:, PAD:]
        shaped = mm(inner[:, 384:], w_shape[...])
        shaping[0, at, :] = shaped[:, :PAD]
        shaping[1, at, :] = shaped[:, PAD:]

    sig_copy = send(sig_halves.at[1 - core], sig_rows.at[core], sibling, 1)
    sig_copy.start()
    sig_rows[core] = sig_halves[core]

    row = lax.broadcasted_iota(jnp.int32, (D, PAD), 0)
    lane = lax.broadcasted_iota(jnp.int32, (D, PAD), 1)
    pick = mask((row == quarter * 192 + lane) & (lane < 192), F32)
    conv = mm(vectors[...], pick, HIGHEST)
    own_out[...] = mm(filterout[...], pick, HIGHEST)
    pos_bias = filter_vectors[8:9, :]
    mid_bias = filter_vectors[9:10, :]
    frequency = filter_vectors[10:11, :]
    ranks = 5 * (quarter * 192 + lanes(PAD))
    for bound in range(5):
        ranks = jnp.where(ranks >= D, ranks - D, ranks)
    lowest = math.log(0.25 / length)
    highest = math.log(1.0 / 30.0)
    rate = jnp.exp(lowest + ranks.astype(F32) * (1.0 / D) * (highest - lowest))
    loud = jnp.sqrt(2.0 * rate)

    def decay(index):
        places = (lax.broadcasted_iota(jnp.int32, (TILE, PAD), 0) + index * TILE).astype(F32)
        return jnp.exp(-rate * places) * loud

    @pl.loop(0, spans)
    def _(index):
        at = tile_rows(index)
        one = mm(place[at, :], filter_vectors[0:8, :], HIGHEST) + pos_bias
        sine, cosine = sine_cosine(frequency * one)
        lin_one[at, :] = one
        act_one[at, :] = sine
        cos_one[at, :] = cosine
        two = mm(sine, midweight[...], HIGHEST) + mid_bias
        sine, cosine = sine_cosine(frequency * two)
        lin_two[at, :] = two
        act_two[at, :] = sine
        cos_two[at, :] = cosine
        short[at, :] = (mm(sine, own_out[...], HIGHEST) * decay(index)).astype(BF16)

    @pl.loop(0, spans)
    def _(index):
        at = tile_rows(index)
        real = mm(table_cos[at, :], short[...])
        imag = mm(table_sin[at, :], short[...])
        turn_cos = place[at, 5:6] * (1.0 / length)
        turn_sin = place[at, 6:7] * (1.0 / length)
        fil_spec[0, at, :] = real * turn_cos + imag * turn_sin
        fil_spec[1, at, :] = imag * turn_cos - real * turn_sin

    out_half = outright[:, own_half]
    w_out_first[0:192, :] = out_half * between(384, 0, 192)
    w_out_first[192:256, :] = jnp.zeros((64, 384), BF16)
    w_out_first[256:448, :] = out_half * between(384, 192, 384)
    w_out_first[448:512, :] = jnp.zeros((64, 384), BF16)
    for b in range(4):
        for k in range(4):
            w_out_second[b // 2, 192 * (b % 2) + 48 * k : 192 * (b % 2) + 48 * k + 48, :] = outleft[
                48 * b : 48 * b + 48, :
            ] * between(D, 192 * k, 192 * k + 192)
    lane = lanes(384)
    inside = lane - jnp.where(lane >= 192, 192, 0)
    for b in range(4):
        kept = mask((inside >= 48 * b) & (inside < 48 * b + 48))
        w_glu[192 * b : 192 * b + 192, 0:384] = gateright[...] * kept
        w_glu[192 * b : 192 * b + 192, 384:768] = liftright[...] * kept
    for target in (w_gate, w_lift):
        target[0, 192:256, :] = jnp.zeros((64, D), BF16)
        target[1, 0:64, :] = jnp.zeros((64, D), BF16)
    w_lower[0] = lowerright[:, 0:256] * between(256, 0, 192)
    w_lower[1] = lowerright[:, 128:384] * between(256, 64, 256)
    for b in range(2):
        for k in range(4):
            w_lower_second[192 * b + 48 * k : 192 * b + 48 * k + 48, :] = lowerleft[
                48 * b : 48 * b + 48, :
            ] * between(D, 192 * k, 192 * k + 192)

    sig_copy.wait_recv()
    sig_pad[0:8, :] = jnp.zeros((8, PAD), F32)
    for part in range(2):
        sig_pad[8 + part * rows : 8 + part * rows + rows, :] = sig_rows[part].astype(F32)
    for index in range(spans):
        start = 8 + index * TILE
        total = conv[4:5, :] * sig_pad[start : start + TILE, :]
        total += conv[5:6, :] * sig_pad[start - 1 : start - 1 + TILE, :]
        total += conv[6:7, :] * sig_pad[start - 2 : start - 2 + TILE, :]
        short[index * TILE : index * TILE + TILE, :] = total.astype(BF16)

    @pl.loop(0, spans)
    def _(index):
        at = tile_rows(index)
        real = mm(table_cos[at, :], short[...])
        imag = mm(table_sin[at, :], short[...])
        sig_spec[0, at, :] = real
        sig_spec[1, at, :] = imag
        fil_re = fil_spec[0, at, :]
        fil_im = fil_spec[1, at, :]
        prod_spec[0, at, :] = (real * fil_re - imag * fil_im).astype(BF16)
        prod_spec[1, at, :] = (real * fil_im + imag * fil_re).astype(BF16)

    per_half = rows // TILE

    @pl.loop(0, spans)
    def _(index):
        at = tile_rows(index)
        result = mm(table_cos[at, :], prod_spec[0]) + mm(table_sin[at, :], prod_spec[1])
        long_rows[index // per_half, tile_rows(lax.rem(index, per_half)), :] = result.astype(BF16)

    long_copy = send(long_rows.at[1 - core], long_halves.at[core], sibling, 2)
    long_copy.start()
    long_halves[core] = long_rows[core]
    long_copy.wait_recv()
    sig_copy.wait_send()
    long_copy.wait_send()

    def inner_copy(index):
        at = tile_rows(index)
        return send(inner_out.at[narrow, at], inner_out.at[narrow, at], partner, 3 + index)

    def dn_copy(index):
        at = tile_rows(index)
        return send(dn_send.at[at], dn_recv.at[at], partner, 5 + index)

    def part_copy(index):
        at = tile_rows(index)
        return send(part_send.at[at], part_recv.at[at], partner, 7 + index)

    def do_copy(index):
        at = tile_rows(index)
        return send(do_send.at[at], do_recv.at[at], partner, 11 + index)

    @pl.loop(0, tiles)
    def _(index):
        at = tile_rows(index)
        inner = None
        for k in range(2):
            product = (shaping[k, at, :] * long_halves[k, at, :].astype(F32)).astype(BF16)
            term = mm(product, w_out_first[k * PAD : k * PAD + PAD, :])
            inner = term if inner is None else inner + term
        inner_out[narrow, at, :] = inner.astype(BF16)
        inner_copy(index).start()

    up_copy.wait_recv()
    for copy in load_copies:
        copy.wait()

    gain_second = vectors[2:3, :]
    shift_second = vectors[3:4, :]

    @pl.loop(0, tiles)
    def _(index):
        at = tile_rows(index)
        inner_copy(index).wait_recv()
        mid = inputs[at, :].astype(F32)
        mid += mm(inner_out[0, at, :], w_out_second[0])
        mid += mm(inner_out[1, at, :], w_out_second[1])
        dn_own[at, :] = mid
        center = mid - jnp.mean(mid, axis=-1, keepdims=True)
        inverse = lax.rsqrt(jnp.mean(center * center, axis=-1, keepdims=True) + EPSILON)
        hat = center * inverse
        hat_two[at, :] = hat
        stats[at, 2:3] = inverse
        normed = (hat * gain_second + shift_second).astype(BF16)
        norm_two[at, :] = normed
        inner = mm(normed, w_glu[...]).astype(BF16)
        inner_glu[at, :] = inner
        lower = [None, None]
        for k in range(2):
            for columns in (slice(0, 256), slice(256, 512), slice(512, 768)):
                gate = mm(inner[:, 128 * k : 128 * k + 256], w_gate[k, :, columns])
                lift = mm(inner[:, 384 + 128 * k : 384 + 128 * k + 256], w_lift[k, :, columns])
                cumulative = 0.5 * (1.0 + lax.erf(gate * (1.0 / math.sqrt(2.0))))
                density = jnp.exp(-0.5 * gate * gate) * (1.0 / math.sqrt(2.0 * math.pi))
                activated = gate * cumulative
                unit = (activated * lift).astype(BF16)
                hid[k, at, columns] = unit
                factor_lift[k, :, columns] = activated
                factor_gate[k, :, columns] = lift * (cumulative + gate * density)
                term = mm(unit, w_lower[k, columns, :])
                lower[k] = term if lower[k] is None else lower[k] + term
        inner_low = join(*lower).astype(BF16)
        inner_lower[at, :] = inner_low
        out_own[at, :] = dn_own[at, own_half] + mm(inner_low, w_lower_second[:, own_half])
        part_send[at, :] = mm(inner_low, w_lower_second[:, other_half]).astype(BF16)

        above = jnp.concatenate([up_halves[0, at, :], up_halves[1, at, :]], axis=1)
        d_low = mm_nt(above, w_lower_second[...]).astype(BF16)
        d_inner_lower[at, :] = d_low
        gates = [None, None]
        lifts = [None, None]
        for k in range(2):
            for columns in (slice(0, 256), slice(256, 512), slice(512, 768)):
                d_hidden = mm_nt(d_low[:, 128 * k : 128 * k + 256], w_lower[k, columns, :])
                to_gate = (d_hidden * factor_gate[k, :, columns]).astype(BF16)
                to_lift = (d_hidden * factor_lift[k, :, columns]).astype(BF16)
                d_gate[k, at, columns] = to_gate
                d_lift[k, at, columns] = to_lift
                term = mm_nt(to_gate, w_gate[k, :, columns])
                gates[k] = term if gates[k] is None else gates[k] + term
                term = mm_nt(to_lift, w_lift[k, :, columns])
                lifts[k] = term if lifts[k] is None else lifts[k] + term
        d_glu = jnp.concatenate([join(*gates), join(*lifts)], axis=1).astype(BF16)
        d_inner_glu[at, :] = d_glu
        into = mm_nt(d_glu, w_glu[...])
        dn_own[at, :] = into
        dn_send[at, :] = into.astype(BF16)
        dn_copy(index).start()

    @pl.loop(0, tiles)
    def _(index):
        part_copy(index).start()

    for side in range(2):
        columns = slice(384 * side, 384 * side + 384)
        folded = fold(mm_tn(inner_lower[...], up_halves[side]), side)
        for b in range(2):
            grad_lowerleft[48 * b : 48 * b + 48, columns] = folded[b].astype(BF16)
    low_lanes = lanes(128) < 64
    for columns in (slice(0, 384), slice(384, 768)):
        parts = [
            mm_tn(hid[k, :, columns], d_inner_lower[:, 128 * k : 128 * k + 256]) for k in range(2)
        ]
        grad_lowerright[columns, 0:128] = parts[0][:, 0:128].astype(BF16)
        grad_lowerright[columns, 128:256] = jnp.where(
            low_lanes, parts[0][:, 128:256], parts[1][:, 0:128]
        ).astype(BF16)
        grad_lowerright[columns, 256:384] = parts[1][:, 128:256].astype(BF16)
    for offset, upper, target in ((0, d_gate, grad_gateleft), (384, d_lift, grad_liftleft)):
        for k in range(2):
            for start in (0, 384):
                whole = mm_tn(
                    inner_glu[:, offset + 128 * k : offset + 128 * k + 256],
                    upper[k, :, start : start + 384],
                )
                target[:, D * k + start : D * k + start + 384] = whole[
                    64 * k : 64 * k + 192, :
                ].astype(BF16)
    for offset, target in ((0, grad_gateright), (384, grad_liftright)):
        whole = mm_tn(norm_two[...], d_inner_glu[:, offset : offset + 384])
        total = None
        for b in range(4):
            term = whole[192 * b : 192 * b + 192, :] * mask(
                (inside >= 48 * b) & (inside < 48 * b + 48), F32
            )
            total = term if total is None else total + term
        target[...] = total.astype(BF16)

    half_mask = mask((lanes(D) >= narrow * 384) & (lanes(D) < narrow * 384 + 384), F32)
    grad_vectors[...] = jnp.zeros(grad_vectors.shape, F32)

    @pl.loop(0, tiles)
    def _(index):
        at = tile_rows(index)
        dn_copy(index).wait_recv()
        into = dn_own[at, :] + dn_recv[at, :].astype(F32)
        hat = hat_two[at, :]
        grad_vectors[2:3, :] += jnp.sum(into * hat, axis=0, keepdims=True) * half_mask
        grad_vectors[3:4, :] += jnp.sum(into, axis=0, keepdims=True) * half_mask
        scaled = into * gain_second
        above = jnp.concatenate([up_halves[0, at, :], up_halves[1, at, :]], axis=1)
        d_mid = above.astype(F32) + stats[at, 2:3] * (
            scaled
            - jnp.mean(scaled, axis=-1, keepdims=True)
            - hat * jnp.mean(scaled * hat, axis=-1, keepdims=True)
        )
        hat_two[at, :] = d_mid
        branch = d_mid.astype(BF16)
        d_inner = mm_nt(branch, w_out_second[narrow]).astype(BF16)
        d_inner_out[at, :] = d_inner
        for k in range(2):
            d_mixed = mm_nt(d_inner, w_out_first[k * PAD : k * PAD + PAD, :])
            d_shaping[k, at, :] = (d_mixed * long_halves[k, at, :].astype(F32)).astype(BF16)
            sig_halves[k, at, :] = (d_mixed * shaping[k, at, :]).astype(BF16)

    dl_copy = send(sig_halves.at[1 - core], dl_rows.at[core], sibling, 9)
    dl_copy.start()
    dl_rows[core] = sig_halves[core]

    for side in range(2):
        columns = slice(384 * side, 384 * side + 384)
        folded = fold(mm_tn(inner_out[narrow], hat_two[:, columns].astype(BF16)), side)
        for b in range(2):
            at = pl.ds(pl.multiple_of(narrow * 96 + 48 * b, 16), 48)
            grad_outleft[at, columns] = folded[b].astype(BF16)
            at = pl.ds(pl.multiple_of((1 - narrow) * 96 + 48 * b, 16), 48)
            grad_outleft[at, columns] = jnp.zeros((48, 384), BF16)
    parts = []
    for k in range(2):
        product = (shaping[k] * long_halves[k].astype(F32)).astype(BF16)
        parts.append(mm_tn(product, d_inner_out[...]))
    grad_outright[:, own_half] = jnp.where(
        lanes(384) < 192, parts[0][0:192, :], parts[1][0:192, :]
    ).astype(BF16)
    grad_outright[:, other_half] = jnp.zeros((192, 384), BF16)

    dl_copy.wait_recv()

    @pl.loop(0, spans)
    def _(index):
        at = tile_rows(index)
        upper = dl_rows[...].reshape(length, PAD)
        real = mm(table_cos[at, :], upper)
        imag = mm(table_sin[at, :], upper)
        fil_re = fil_spec[0, at, :]
        fil_im = fil_spec[1, at, :]
        prod_spec[0, at, :] = (real * fil_re + imag * fil_im).astype(BF16)
        prod_spec[1, at, :] = (imag * fil_re - real * fil_im).astype(BF16)
        sig_re = sig_spec[0, at, :]
        sig_im = sig_spec[1, at, :]
        sig_spec[0, at, :] = real * sig_re + imag * sig_im
        sig_spec[1, at, :] = imag * sig_re - real * sig_im

    ds_pad[length : length + 8, :] = jnp.zeros((8, PAD), F32)

    @pl.loop(0, spans)
    def _(index):
        at = tile_rows(index)
        result = mm(table_cos[at, :], prod_spec[0]) + mm(table_sin[at, :], prod_spec[1])
        ds_pad[at, :] = result.astype(BF16).astype(F32)

    for index in range(spans):
        start = index * TILE
        total = conv[4:5, :] * ds_pad[start : start + TILE, :]
        total += conv[5:6, :] * ds_pad[start + 1 : start + 1 + TILE, :]
        total += conv[6:7, :] * ds_pad[start + 2 : start + 2 + TILE, :]
        part, inner_start = divmod(start, rows)
        long_rows[part, inner_start : inner_start + TILE, :] = total.astype(BF16)
    ds_copy = send(long_rows.at[1 - core], ds_halves.at[core], sibling, 10)
    ds_copy.start()
    ds_halves[core] = long_rows[core]

    sums = [jnp.zeros((1, PAD), F32) for _ in range(3)]
    for index in range(spans):
        start = index * TILE
        upper = ds_pad[start : start + TILE, :]
        for j in range(3):
            sums[j] += jnp.sum(
                upper * sig_pad[8 + start - j : 8 + start - j + TILE, :], axis=0, keepdims=True
            )
    sums = jnp.concatenate(sums + [jnp.zeros((5, PAD), F32)], axis=0)
    lane = lax.broadcasted_iota(jnp.int32, (PAD, D), 1)
    row = lax.broadcasted_iota(jnp.int32, (PAD, D), 0)
    unpick = mask((lane == quarter * 192 + row) & (row < 192), F32)
    conv_sums = mm(sums, unpick, HIGHEST)
    grad_vectors[4:7, :] = conv_sums[0:3, :]

    @pl.loop(0, spans)
    def _(index):
        at = tile_rows(index)
        turn_cos = place[at, 5:6] * (1.0 / length)
        turn_sin = place[at, 6:7] * (1.0 / length)
        real = sig_spec[0, at, :]
        imag = sig_spec[1, at, :]
        prod_spec[0, at, :] = (real * turn_cos - imag * turn_sin).astype(BF16)
        prod_spec[1, at, :] = (imag * turn_cos + real * turn_sin).astype(BF16)

    d_lin[...] = jnp.zeros(d_lin.shape, F32)
    grad_filter[...] = jnp.zeros(grad_filter.shape, F32)

    @pl.loop(0, spans)
    def _(index):
        at = tile_rows(index)
        d_taps = mm(table_cos[at, :], prod_spec[0]) + mm(table_sin[at, :], prod_spec[1])
        d_mod = d_taps * decay(index)
        d_lin[...] += mm_tn(act_two[at, :], d_mod, HIGHEST)
        two = mm_nt(d_mod, own_out[...], HIGHEST) * cos_two[at, :]
        scaled_two = two * frequency
        grad_filter[0:128, :] += mm_tn(act_one[at, :], scaled_two, HIGHEST)
        one = mm_nt(scaled_two, midweight[...], HIGHEST) * cos_one[at, :]
        scaled_one = one * frequency
        grad_filter[128:136, :] += mm_tn(place[at, :], scaled_one, HIGHEST)
        grad_filter[136:137, :] += jnp.sum(scaled_one, axis=0, keepdims=True)
        grad_filter[137:138, :] += jnp.sum(scaled_two, axis=0, keepdims=True)
        grad_filter[138:139, :] += jnp.sum(one * lin_one[at, :] + two * lin_two[at, :], axis=0, keepdims=True)

    grad_filterout[...] = mm(d_lin[...], unpick, HIGHEST)

    ds_copy.wait_recv()
    first_half = vectors[0:1, own_half]
    tail_lane = lax.broadcasted_iota(jnp.int32, (TILE, 128), 1)

    @pl.loop(0, tiles)
    def _(index):
        at = tile_rows(index)
        to_value = jnp.concatenate([ds_halves[0, at, :], ds_halves[1, at, :]], axis=1)
        to_shape = jnp.concatenate([d_shaping[0, at, :], d_shaping[1, at, :]], axis=1)
        d_inner = jnp.concatenate(
            [mm_nt(to_value, w_value[...]), mm_nt(to_shape, w_shape[...])], axis=1
        ).astype(BF16)
        d_inner_one[at, :] = d_inner
        into = mm_nt(d_inner, w_first[...])
        dn_own[at, :] = into
        scaled = into * first
        plain = jnp.sum(scaled, axis=-1, keepdims=True)
        hat = (inputs[at, :].astype(F32) - stats[at, 0:1]) * stats[at, 1:2]
        along = jnp.sum(scaled * hat, axis=-1, keepdims=True)
        tail = jnp.where(tail_lane == 0, plain, jnp.where(tail_lane == 1, along, 0.0))
        tail_own[at, :] = tail
        do_send[at, 0:384] = dn_own[at, other_half].astype(BF16)
        do_send[at, 384:512] = tail.astype(BF16)
        do_copy(index).start()

    lane = lax.broadcasted_iota(jnp.int32, (384, D), 1)
    row = lax.broadcasted_iota(jnp.int32, (384, D), 0)
    step = jnp.where(row >= 96, 96, 0) + jnp.where(row >= 192, 96, 0) + jnp.where(row >= 288, 96, 0)
    unselect = mask(lane == row + step + narrow * 96)
    for offset, target in ((0, grad_valueright), (384, grad_shaperight)):
        whole = mm_tn(norm_one[...], d_inner_one[:, offset : offset + 384])
        total = None
        for b in range(4):
            term = whole[192 * b : 192 * b + 192, :] * between(
                384, 96 * b, 96 * b + 96, F32
            )
            total = term if total is None else total + term
        target[...] = mm(total.astype(BF16), unselect).astype(BF16)
    lane = lax.broadcasted_iota(jnp.int32, (2 * PAD, D), 1)
    row = lax.broadcasted_iota(jnp.int32, (2 * PAD, D), 0)
    group = jnp.where(row >= PAD, 1, 0)
    entry = row - PAD * group
    unspread = mask((lane == (2 * narrow + group) * 192 + entry) & (entry < 192))
    for offset, upper, target in ((0, ds_halves, grad_valueleft), (384, d_shaping, grad_shapeleft)):
        above = jnp.concatenate([upper[0], upper[1]], axis=1)
        whole = mm_tn(inner_one[:, offset : offset + 384], above)
        pieces = []
        for b in range(4):
            total = None
            for k in range(2):
                term = whole[96 * b + 48 * k : 96 * b + 48 * k + 48, :] * between(
                    2 * PAD, PAD * k, PAD * k + PAD, F32
                )
                total = term if total is None else total + term
            pieces.append(total)
        total = jnp.concatenate(pieces, axis=0).astype(BF16)
        target[...] = mm(total, unspread).astype(BF16)

    @pl.loop(0, tiles)
    def _(index):
        at = tile_rows(index)
        part_copy(index).wait_recv()
        hidden_out[at, :] = (out_own[at, :] + part_recv[at, :].astype(F32)).astype(BF16)
        do_copy(index).wait_recv()
        came = do_recv[at, :].astype(F32)
        into = dn_own[at, own_half] + came[:, 0:384]
        tail = (tail_own[at, :] + came[:, 384:512]) * (1.0 / D)
        hat = (inputs[at, own_half].astype(F32) - stats[at, 0:1]) * stats[at, 1:2]
        grad_vectors[0:1, own_half] += jnp.sum(into * hat, axis=0, keepdims=True)
        grad_vectors[1:2, own_half] += jnp.sum(into, axis=0, keepdims=True)
        hidden_grad[at, :] = (
            hat_two[at, own_half]
            + stats[at, 1:2] * (into * first_half - tail[:, 0:1] - hat * tail[:, 1:2])
        ).astype(BF16)

    for copy in (up_copy, dl_copy, ds_copy):
        copy.wait_send()

    @pl.loop(0, tiles)
    def _(index):
        for copy in (inner_copy, dn_copy, part_copy, do_copy):
            copy(index).wait_send()


def transform_tables(length):
    index = np.arange(length, dtype=np.float64) + 0.5
    angle = np.outer(index, index) * (math.pi / length)
    return (np.cos(angle).astype(jnp.bfloat16), np.sin(angle).astype(jnp.bfloat16))


def place_table(length):
    places = np.arange(length, dtype=np.float64)
    angle = places * (2.0 * math.pi / length)
    turn = (places + 0.5) * (math.pi / (2.0 * length))
    columns = [
        places / length,
        np.cos(angle),
        np.sin(angle),
        np.cos(2.0 * angle),
        np.sin(2.0 * angle),
        np.cos(turn),
        np.sin(turn),
        np.zeros(length),
    ]
    return np.stack(columns, axis=1).astype(np.float32)


def pair_body(
    hidden_in,
    gainfirst,
    shiftfirst,
    valueright,
    valueleft,
    shaperight,
    shapeleft,
    convtaps,
    posweight,
    posbias,
    sinefreq,
    midweight,
    midbias,
    filterout,
    outright,
    outleft,
    gainsecond,
    shiftsecond,
    gateright,
    gateleft,
    liftright,
    liftleft,
    lowerright,
    lowerleft,
    grad_out,
):
    rows = hidden_in.shape[0]
    length = 2 * rows
    table_cos, table_sin = transform_tables(length)
    vectors = jnp.concatenate(
        [jnp.stack([gainfirst, shiftfirst, gainsecond, shiftsecond]), convtaps, jnp.zeros((1, D), F32)]
    )
    filter_vectors = jnp.concatenate(
        [posweight, jnp.zeros((3, 128), F32), jnp.stack([posbias, midbias, sinefreq]), jnp.zeros((5, 128), F32)]
    )

    def out(extent, dtype=BF16):
        return jax.ShapeDtypeStruct(extent, dtype)

    def buf(*extent, dtype=BF16):
        return pltpu.VMEM(extent, dtype)

    vmem = pl.BlockSpec(memory_space=pltpu.VMEM)
    hbm = pl.BlockSpec(memory_space=pl.ANY)
    results = pl.pallas_call(
        whole_kernel,
        out_shape=(
            out((rows, 384)),
            out((rows, 384)),
            out((192, D)),
            out((192, D)),
            out((192, D)),
            out((192, D)),
            out((192, D)),
            out((192, D)),
            out(gateright.shape),
            out(gateleft.shape),
            out(liftright.shape),
            out(liftleft.shape),
            out(lowerright.shape),
            out(lowerleft.shape),
            out((128, D), F32),
            out((8, D), F32),
            out((144, 128), F32),
        ),
        in_specs=[vmem] * 16 + [hbm, vmem, hbm, vmem, vmem],
        out_specs=[vmem] * 17,
        scratch_shapes=[
            buf(D, D),
            buf(384, 512),
            buf(384, 512),
            buf(512, 384),
            buf(2, 384, D),
            buf(D, D),
            buf(2, 256, D),
            buf(2, 256, D),
            buf(2, D, 256),
            buf(384, D),
            buf(2, rows, 384),
            buf(rows, 128, dtype=F32),
            buf(rows, D),
            buf(rows, D),
            buf(2, rows, PAD),
            buf(2, rows, PAD),
            buf(2, rows, PAD, dtype=F32),
            buf(length + 8, PAD, dtype=F32),
            buf(length, PAD),
            buf(length, 128, dtype=F32),
            buf(length, 128, dtype=F32),
            buf(length, 128, dtype=F32),
            buf(length, 128, dtype=F32),
            buf(length, 128, dtype=F32),
            buf(length, 128, dtype=F32),
            buf(2, length, PAD, dtype=F32),
            buf(2, length, PAD, dtype=F32),
            buf(2, length, PAD),
            buf(2, rows, PAD),
            buf(2, rows, PAD),
            buf(2, rows, 384),
            buf(rows, D, dtype=F32),
            buf(rows, D),
            buf(rows, D),
            buf(2, TILE, D, dtype=F32),
            buf(2, TILE, D, dtype=F32),
            buf(2, rows, D),
            buf(rows, 384),
            buf(rows, 384, dtype=F32),
            buf(rows, 384),
            buf(rows, 384),
            buf(rows, 384),
            buf(2, rows, D),
            buf(2, rows, D),
            buf(rows, D),
            buf(rows, D, dtype=F32),
            buf(rows, D),
            buf(rows, D),
            buf(rows, 384),
            buf(2, rows, PAD),
            buf(2, rows, PAD),
            buf(length + 8, PAD, dtype=F32),
            buf(2, rows, PAD),
            buf(rows, D),
            buf(rows, 128, dtype=F32),
            buf(rows, 512),
            buf(rows, 512),
            buf(128, PAD, dtype=F32),
            buf(128, PAD, dtype=F32),
            pltpu.SemaphoreType.DMA((13,)),
            pltpu.SemaphoreType.DMA((13,)),
            pltpu.SemaphoreType.DMA((4,)),
        ],
        compiler_params=pltpu.CompilerParams(
            collective_id=0, has_side_effects=True, vmem_limit_bytes=63 * 1024 * 1024
        ),
    )(
        hidden_in,
        grad_out,
        table_cos,
        table_sin,
        place_table(length),
        vectors,
        filter_vectors,
        midweight,
        filterout,
        valueright,
        valueleft,
        shaperight,
        shapeleft,
        outright,
        outleft,
        gateright,
        gateleft,
        liftright,
        liftleft,
        lowerright,
        lowerleft,
    )
    hidden_out, hidden_grad = results[:2]
    mixer = lax.psum([grad.astype(F32) for grad in results[2:8]], ("wide", "narrow"))
    channel = lax.psum([grad.astype(F32) for grad in results[8:14]], "wide")
    grad_filterout, grad_vectors, grad_filter = lax.psum(results[14:17], ("wide", "narrow"))
    count = D // (lax.axis_size("wide") * lax.axis_size("narrow"))
    combined = lax.axis_index("wide") * lax.axis_size("narrow") + lax.axis_index("narrow")
    grad_filterout = lax.dynamic_slice_in_dim(grad_filterout, combined * count, count, 1)
    return (
        hidden_out,
        hidden_grad,
        grad_vectors[0],
        grad_vectors[1],
        mixer[0],
        mixer[1],
        mixer[2],
        mixer[3],
        grad_vectors[4:7],
        grad_filter[128:133],
        grad_filter[136],
        grad_filter[138],
        grad_filter[:128],
        grad_filter[137],
        grad_filterout,
        mixer[4],
        mixer[5],
        grad_vectors[2],
        grad_vectors[3],
        *channel,
    )


def solution(mesh):
    pairs = mesh.shape["wide"] == 2 * SEQS and mesh.shape["narrow"] == 2
    return jax.shard_map(
        pair_body if pairs else body,
        mesh=mesh,
        in_specs=(
            P("wide", None),
            P(),
            P(),
            P(),
            P(),
            P(),
            P(),
            P(),
            P(),
            P(),
            P(),
            P(),
            P(),
            P(),
            P(),
            P(),
            P(),
            P(),
            P(None, "narrow"),
            P(None, "narrow"),
            P(None, "narrow"),
            P(None, "narrow"),
            P(None, "narrow"),
            P("narrow", None),
            P("wide", "narrow"),
        ),
        out_specs=(
            P("wide", "narrow"),
            P("wide", "narrow"),
            P(),
            P(),
            P(),
            P(),
            P(),
            P(),
            P(),
            P(),
            P(),
            P(),
            P(),
            P(),
            P(None, ("wide", "narrow")),
            P(),
            P(),
            P(),
            P(),
            P(None, "narrow"),
            P(None, "narrow"),
            P(None, "narrow"),
            P(None, "narrow"),
            P(None, "narrow"),
            P("narrow", None),
        ),
        check_vma=False,
    )
```

```python
import math

import jax
import jax.numpy as jnp
import numpy as np
from jax import lax
from jax.experimental import pallas as pl
from jax.experimental.pallas import tpu as pltpu
from jax.sharding import PartitionSpec as P

D = 768
BLOCKS = 4
SEQS = 8


EPSILON = 1e-05
HIGHEST = lax.Precision.HIGHEST


def from_behind(x, axis, by):
    length = lax.axis_size(axis)
    pairs = [(i, i + by) for i in range(length) if 0 <= i + by < length]
    return lax.ppermute(x, axis, pairs)


def norm_forward(values, gain, shift):
    center = values - jnp.mean(values, axis=-1, keepdims=True)
    inverse = lax.rsqrt(jnp.mean(center * center, axis=-1, keepdims=True) + EPSILON)
    normed = center * inverse
    return (normed * gain + shift, normed, inverse)


def norm_backward(upstream, normed, inverse, gain):
    scaled = upstream * gain
    result = inverse * (
        scaled
        - jnp.mean(scaled, axis=-1, keepdims=True)
        - normed * jnp.mean(scaled * normed, axis=-1, keepdims=True)
    )
    return (result, jnp.sum(upstream * normed, axis=0), jnp.sum(upstream, axis=0))


def right_view(right, nblocks, groups, group_first):
    width_in = right.shape[0]
    piece = right.shape[1] // (nblocks * groups)
    if group_first:
        return (right.reshape(width_in, groups, nblocks, piece), "ikbc")
    return (right.reshape(width_in, nblocks, groups, piece), "ibkc")


def section_one(inputs, right, groups, group_first):
    rowcount = inputs.shape[0]
    width_in = right.shape[0]
    nblocks = inputs.shape[1] // width_in
    factor, letters = right_view(right, nblocks, groups, group_first)
    first = jnp.einsum(
        "tbi," + letters + "->tkbc",
        inputs.reshape(rowcount, nblocks, width_in),
        factor,
        preferred_element_type=jnp.float32,
    )
    return first.reshape(rowcount, groups, -1).astype(jnp.bfloat16)


def section_two(middle_part, left):
    groups = middle_part.shape[1]
    result = jnp.einsum(
        "tkj,jke->tke",
        middle_part,
        left.reshape(left.shape[0], groups, -1),
        preferred_element_type=jnp.float32,
    )
    return result.reshape(result.shape[0], -1)


def back_two(middle_part, left, upstream):
    groups = middle_part.shape[1]
    left_view = left.reshape(left.shape[0], groups, -1)
    grad_left = jnp.einsum(
        "tkj,tke->jke", middle_part, upstream, preferred_element_type=jnp.float32
    )
    grad_middle = jnp.einsum(
        "tke,jke->tkj", upstream, left_view, preferred_element_type=jnp.float32
    )
    return (grad_left.reshape(left.shape[0], -1), grad_middle.astype(jnp.bfloat16))


def back_one(inputs, right, grad_middle, group_first):
    rowcount = inputs.shape[0]
    width_in = right.shape[0]
    nblocks = inputs.shape[1] // width_in
    groups = grad_middle.shape[1]
    factor, letters = right_view(right, nblocks, groups, group_first)
    spread_back = grad_middle.reshape(rowcount, groups, nblocks, -1)
    blocked = inputs.reshape(rowcount, nblocks, width_in)
    grad_right = jnp.einsum(
        "tbi,tkbc->" + letters, blocked, spread_back, preferred_element_type=jnp.float32
    )
    grad_inputs = jnp.einsum(
        "tkbc," + letters + "->tbi", spread_back, factor, preferred_element_type=jnp.float32
    )
    return (grad_right.reshape(width_in, -1), grad_inputs.reshape(rowcount, -1))


def fourier_tables(length):
    span = length // 128
    slow_index = jnp.arange(span, dtype=jnp.int32)
    fast_index = jnp.arange(128, dtype=jnp.int32)
    small = (slow_index[:, None] * slow_index[None, :] % span).astype(jnp.float32) * (
        2.0 * math.pi / span
    )
    twist = (slow_index[:, None] * fast_index[None, :] % length).astype(jnp.float32) * (
        2.0 * math.pi / length
    )
    large = (fast_index[:, None] * fast_index[None, :] % 128).astype(jnp.float32) * (
        2.0 * math.pi / 128
    )
    return (
        jnp.cos(small),
        jnp.sin(small),
        jnp.cos(twist),
        jnp.sin(twist),
        jnp.cos(large),
        jnp.sin(large),
    )


def to_spectrum(signal, tables):
    cos_small, sin_small, cos_twist, sin_twist, cos_large, sin_large = tables
    span = cos_small.shape[0]
    padded = jnp.concatenate([signal, jnp.zeros_like(signal)], axis=-1)
    padded = padded.reshape(signal.shape[:-1] + (span, 128))
    first_re = jnp.einsum("...qp,qk->...kp", padded, cos_small, precision=HIGHEST)
    first_im = -jnp.einsum("...qp,qk->...kp", padded, sin_small, precision=HIGHEST)
    turned_re = first_re * cos_twist + first_im * sin_twist
    turned_im = first_im * cos_twist - first_re * sin_twist
    out_re = jnp.einsum("...kp,pj->...kj", turned_re, cos_large, precision=HIGHEST) + jnp.einsum(
        "...kp,pj->...kj", turned_im, sin_large, precision=HIGHEST
    )
    out_im = jnp.einsum("...kp,pj->...kj", turned_im, cos_large, precision=HIGHEST) - jnp.einsum(
        "...kp,pj->...kj", turned_re, sin_large, precision=HIGHEST
    )
    return (out_re, out_im)


def from_spectrum(real_part, imag_part, tables):
    cos_small, sin_small, cos_twist, sin_twist, cos_large, sin_large = tables
    span = cos_small.shape[0]
    back_re = jnp.einsum("...kj,pj->...kp", real_part, cos_large, precision=HIGHEST) - jnp.einsum(
        "...kj,pj->...kp", imag_part, sin_large, precision=HIGHEST
    )
    back_im = jnp.einsum("...kj,pj->...kp", imag_part, cos_large, precision=HIGHEST) + jnp.einsum(
        "...kj,pj->...kp", real_part, sin_large, precision=HIGHEST
    )
    turned_re = back_re * cos_twist - back_im * sin_twist
    turned_im = back_im * cos_twist + back_re * sin_twist
    signal = (
        jnp.einsum("...kp,qk->...qp", turned_re, cos_small, precision=HIGHEST)
        - jnp.einsum("...kp,qk->...qp", turned_im, sin_small, precision=HIGHEST)
    ) / (span * 128)
    signal = signal.reshape(signal.shape[:-2] + (span * 128,))
    return signal[..., : span * 64]


def position_features(length):
    places = jnp.arange(length, dtype=jnp.float32)
    angle = places * (2.0 * math.pi / length)
    return jnp.stack(
        [
            places / length,
            jnp.cos(angle),
            jnp.sin(angle),
            jnp.cos(2.0 * angle),
            jnp.sin(2.0 * angle),
        ],
        axis=1,
    )


def decay_factors(channel_ids, length):
    rank = (channel_ids * 5 % D).astype(jnp.float32) / D
    lowest = math.log(0.25 / length)
    highest = math.log(1.0 / 30.0)
    rate = jnp.exp(lowest + rank * (highest - lowest))
    places = jnp.arange(length, dtype=jnp.float32)
    return jnp.exp(-rate[:, None] * places[None, :]) * jnp.sqrt(2.0 * rate)[:, None]


def channel_order(data, nwide, nnarrow, rows_half):
    count = data.shape[0]
    return data.reshape(count, nnarrow, nwide, rows_half).transpose(0, 2, 1, 3).reshape(count, -1)


def row_order(data, nwide, nnarrow):
    total = data.shape[0]
    rows_half = data.shape[1]
    count = total // (nwide * nnarrow)
    return (
        data.reshape(nnarrow, nwide, count, rows_half)
        .transpose(1, 0, 2, 3)
        .reshape(total, rows_half)
        .T
    )


def body(
    hidden_in,
    gainfirst,
    shiftfirst,
    valueright,
    valueleft,
    shaperight,
    shapeleft,
    convtaps,
    posweight,
    posbias,
    sinefreq,
    midweight,
    midbias,
    filterout,
    outright,
    outleft,
    gainsecond,
    shiftsecond,
    gateright,
    gateleft,
    liftright,
    liftleft,
    lowerright,
    lowerleft,
    grad_out,
):
    rowcount = hidden_in.shape[0]
    local_groups = gateright.shape[1] // gateleft.shape[0]
    nwide = lax.axis_size("wide")
    nnarrow = lax.axis_size("narrow")
    narrow_index = lax.axis_index("narrow")
    rows_half = rowcount // nnarrow
    row_start = narrow_index * rows_half
    combined = lax.axis_index("wide") * nnarrow + narrow_index
    resid = lax.dynamic_slice_in_dim(hidden_in, row_start, rows_half, 0).astype(jnp.float32)
    normone, hat_one, inv_one = norm_forward(resid, gainfirst, shiftfirst)
    normone = normone.astype(jnp.bfloat16)
    mid_value = section_one(normone, valueright, BLOCKS, False)
    signal = section_two(mid_value, valueleft).astype(jnp.bfloat16)
    mid_shape = section_one(normone, shaperight, BLOCKS, False)
    shaping = section_two(mid_shape, shapeleft)
    group = nwide // SEQS * nnarrow
    place = combined % group
    before = from_behind(signal[-2:], ("wide", "narrow"), 1)
    before = jnp.where(place == 0, jnp.zeros_like(before), before)
    extended = jnp.concatenate([before, signal], axis=0).astype(jnp.float32)
    shortconv = (
        convtaps[0] * extended[2:] + convtaps[1] * extended[1:-1] + convtaps[2] * extended[:-2]
    ).astype(jnp.bfloat16)
    channels = lax.all_to_all(
        lax.all_to_all(shortconv.T, "wide", split_axis=0, concat_axis=1, tiled=True),
        "narrow",
        split_axis=0,
        concat_axis=1,
        tiled=True,
    )
    channels = channel_order(channels, nwide, nnarrow, rows_half)
    count = channels.shape[0]
    length = channels.shape[1] // SEQS
    feats = position_features(length)
    lin_one = jnp.dot(feats, posweight, precision=HIGHEST) + posbias
    act_one = jnp.sin(sinefreq * lin_one)
    lin_two = jnp.dot(act_one, midweight, precision=HIGHEST) + midbias
    act_two = jnp.sin(sinefreq * lin_two)
    own_cols = lax.dynamic_slice_in_dim(filterout, combined * count, count, 1)
    channel_ids = combined * count + jnp.arange(count, dtype=jnp.int32)
    modulation = decay_factors(channel_ids, length)
    taps = jnp.dot(act_two, own_cols, precision=HIGHEST).T * modulation
    tables = fourier_tables(2 * length)
    sig_re, sig_im = to_spectrum(channels.astype(jnp.float32).reshape(count, SEQS, length), tables)
    fil_re, fil_im = to_spectrum(taps.reshape(count, 1, length), tables)
    conv_chan = from_spectrum(
        sig_re * fil_re - sig_im * fil_im, sig_re * fil_im + sig_im * fil_re, tables
    )
    conv_chan = conv_chan.reshape(count, SEQS * length).astype(jnp.bfloat16)
    longconv = lax.all_to_all(
        lax.all_to_all(conv_chan, "wide", split_axis=1, concat_axis=0, tiled=True),
        "narrow",
        split_axis=1,
        concat_axis=0,
        tiled=True,
    )
    longconv = row_order(longconv, nwide, nnarrow)
    mixed = (shaping * longconv.astype(jnp.float32)).astype(jnp.bfloat16)
    mid_out = section_one(mixed, outright, BLOCKS, False)
    middle = resid + section_two(mid_out, outleft)
    normtwo, hat_two, inv_two = norm_forward(middle, gainsecond, shiftsecond)
    normtwo = normtwo.astype(jnp.bfloat16)
    norm_all = lax.all_gather(normtwo, "narrow", axis=0, tiled=True)
    mid_gate = section_one(norm_all, gateright, local_groups, True)
    pregate = section_two(mid_gate, gateleft)
    mid_lift = section_one(norm_all, liftright, local_groups, True)
    prelift = section_two(mid_lift, liftleft)
    cumulative = 0.5 * (1.0 + lax.erf(pregate * (1.0 / math.sqrt(2.0))))
    activated = pregate * cumulative
    hidden = (activated * prelift).astype(jnp.bfloat16)
    mid_lower = section_one(hidden, lowerright, BLOCKS, False)
    partial_sum = section_two(mid_lower, lowerleft)
    partial_sum = partial_sum + lax.dynamic_update_slice_in_dim(
        jnp.zeros_like(partial_sum), middle, row_start, 0
    )
    hidden_out = lax.psum_scatter(
        partial_sum.astype(jnp.bfloat16), "narrow", scatter_dimension=1, tiled=True
    )
    upstream = lax.all_gather(grad_out, "narrow", axis=1, tiled=True)
    grad_lowerleft, grad_mid_lower = back_two(
        mid_lower, lowerleft, upstream.reshape(rowcount, BLOCKS, -1)
    )
    grad_lowerright, grad_hidden = back_one(hidden, lowerright, grad_mid_lower, False)
    density = jnp.exp(-0.5 * pregate * pregate) * (1.0 / math.sqrt(2.0 * math.pi))
    grad_pregate = (grad_hidden * prelift * (cumulative + pregate * density)).astype(jnp.bfloat16)
    grad_prelift = (grad_hidden * activated).astype(jnp.bfloat16)
    grad_gateleft, grad_mid_gate = back_two(
        mid_gate, gateleft, grad_pregate.reshape(rowcount, local_groups, -1)
    )
    grad_gateright, into_gate = back_one(norm_all, gateright, grad_mid_gate, True)
    grad_liftleft, grad_mid_lift = back_two(
        mid_lift, liftleft, grad_prelift.reshape(rowcount, local_groups, -1)
    )
    grad_liftright, into_lift = back_one(norm_all, liftright, grad_mid_lift, True)
    ffn_local = (
        grad_gateright,
        grad_gateleft,
        grad_liftright,
        grad_liftleft,
        grad_lowerright,
        grad_lowerleft,
    )
    dnormtwo = lax.psum_scatter(
        (into_gate + into_lift).astype(jnp.bfloat16), "narrow", scatter_dimension=0, tiled=True
    ).astype(jnp.float32)
    back_two_norm, grad_gainsecond, grad_shiftsecond = norm_backward(
        dnormtwo, hat_two, inv_two, gainsecond
    )
    up_rows = lax.dynamic_slice_in_dim(upstream, row_start, rows_half, 0)
    dmiddle = up_rows.astype(jnp.float32) + back_two_norm
    dbranch = dmiddle.astype(jnp.bfloat16)
    grad_outleft, grad_mid_out = back_two(mid_out, outleft, dbranch.reshape(rows_half, BLOCKS, -1))
    grad_outright, dmixed = back_one(mixed, outright, grad_mid_out, False)
    dshaping = (dmixed * longconv.astype(jnp.float32)).astype(jnp.bfloat16)
    dlong = (dmixed * shaping).astype(jnp.bfloat16)
    grad_chan = lax.all_to_all(
        lax.all_to_all(dlong.T, "wide", split_axis=0, concat_axis=1, tiled=True),
        "narrow",
        split_axis=0,
        concat_axis=1,
        tiled=True,
    )
    grad_chan = channel_order(grad_chan, nwide, nnarrow, rows_half)
    dlong_re, dlong_im = to_spectrum(
        grad_chan.astype(jnp.float32).reshape(count, SEQS, length), tables
    )
    dshort_chan = from_spectrum(
        dlong_re * fil_re + dlong_im * fil_im, dlong_im * fil_re - dlong_re * fil_im, tables
    )
    dshort_chan = dshort_chan.reshape(count, SEQS * length).astype(jnp.bfloat16)
    filt_re = jnp.sum(dlong_re * sig_re + dlong_im * sig_im, axis=1, keepdims=True)
    filt_im = jnp.sum(dlong_im * sig_re - dlong_re * sig_im, axis=1, keepdims=True)
    grad_taps = from_spectrum(filt_re, filt_im, tables).reshape(count, length)
    dshort = lax.all_to_all(
        lax.all_to_all(dshort_chan, "wide", split_axis=1, concat_axis=0, tiled=True),
        "narrow",
        split_axis=1,
        concat_axis=0,
        tiled=True,
    )
    dshort = row_order(dshort, nwide, nnarrow)
    grad_modded = grad_taps * modulation
    grad_filterout = jnp.dot(act_two.T, grad_modded.T, precision=HIGHEST)
    dact_two = jnp.dot(grad_modded.T, own_cols.T, precision=HIGHEST)
    dlin_two = dact_two * jnp.cos(sinefreq * lin_two)
    scaled_two = dlin_two * sinefreq
    grad_midweight = jnp.dot(act_one.T, scaled_two, precision=HIGHEST)
    grad_midbias = jnp.sum(scaled_two, axis=0)
    dact_one = jnp.dot(scaled_two, midweight.T, precision=HIGHEST)
    dlin_one = dact_one * jnp.cos(sinefreq * lin_one)
    scaled_one = dlin_one * sinefreq
    grad_posweight = jnp.dot(feats.T, scaled_one, precision=HIGHEST)
    grad_posbias = jnp.sum(scaled_one, axis=0)
    grad_sinefreq = jnp.sum(dlin_one * lin_one, axis=0) + jnp.sum(dlin_two * lin_two, axis=0)
    after = from_behind(dshort[:2], ("wide", "narrow"), -1)
    after = jnp.where(place == group - 1, jnp.zeros_like(after), after)
    ext_grad = jnp.concatenate([dshort, after], axis=0).astype(jnp.float32)
    dsignal = (
        convtaps[0] * ext_grad[:-2] + convtaps[1] * ext_grad[1:-1] + convtaps[2] * ext_grad[2:]
    ).astype(jnp.bfloat16)
    short_grad = dshort.astype(jnp.float32)
    grad_convtaps = jnp.stack(
        [
            jnp.sum(extended[2:] * short_grad, axis=0),
            jnp.sum(extended[1:-1] * short_grad, axis=0),
            jnp.sum(extended[:-2] * short_grad, axis=0),
        ]
    )
    grad_valueleft, grad_mid_value = back_two(
        mid_value, valueleft, dsignal.reshape(rows_half, BLOCKS, -1)
    )
    grad_valueright, into_value = back_one(normone, valueright, grad_mid_value, False)
    grad_shapeleft, grad_mid_shape = back_two(
        mid_shape, shapeleft, dshaping.reshape(rows_half, BLOCKS, -1)
    )
    grad_shaperight, into_shape = back_one(normone, shaperight, grad_mid_shape, False)
    back_one_norm, grad_gainfirst, grad_shiftfirst = norm_backward(
        into_value + into_shape, hat_one, inv_one, gainfirst
    )
    full_grad = (dmiddle + back_one_norm).astype(jnp.bfloat16)
    hidden_grad = lax.all_to_all(full_grad, "narrow", split_axis=1, concat_axis=0, tiled=True)
    mixer_grads = lax.psum(
        (
            grad_gainfirst,
            grad_shiftfirst,
            grad_valueright,
            grad_valueleft,
            grad_shaperight,
            grad_shapeleft,
            grad_convtaps,
            grad_posweight,
            grad_posbias,
            grad_sinefreq,
            grad_midweight,
            grad_midbias,
            grad_outright,
            grad_outleft,
            grad_gainsecond,
            grad_shiftsecond,
        ),
        ("wide", "narrow"),
    )
    ffn_grads = lax.psum(
        (ffn_local[0], ffn_local[1], ffn_local[2], ffn_local[3], ffn_local[4], ffn_local[5]), "wide"
    )
    return (
        hidden_out,
        hidden_grad,
        mixer_grads[0],
        mixer_grads[1],
        mixer_grads[2],
        mixer_grads[3],
        mixer_grads[4],
        mixer_grads[5],
        mixer_grads[6],
        mixer_grads[7],
        mixer_grads[8],
        mixer_grads[9],
        mixer_grads[10],
        mixer_grads[11],
        grad_filterout,
        mixer_grads[12],
        mixer_grads[13],
        mixer_grads[14],
        mixer_grads[15],
        ffn_grads[0],
        ffn_grads[1],
        ffn_grads[2],
        ffn_grads[3],
        ffn_grads[4],
        ffn_grads[5],
    )


F32 = jnp.float32
BF16 = jnp.bfloat16
MESH = pl.DeviceIdType.MESH
TILE = 256
PAD = 256


def mm(a, b, precision=None):
    return lax.dot_general(
        a, b, (((1,), (0,)), ((), ())), precision=precision, preferred_element_type=F32
    )


def mm_nt(a, b, precision=None):
    return lax.dot_general(
        a, b, (((1,), (1,)), ((), ())), precision=precision, preferred_element_type=F32
    )


def mm_tn(a, b, precision=None):
    return lax.dot_general(
        a, b, (((0,), (0,)), ((), ())), precision=precision, preferred_element_type=F32
    )


def lanes(width):
    return lax.broadcasted_iota(jnp.int32, (1, width), 1)


def mask(condition, dtype=BF16):
    return jnp.where(condition, 1.0, 0.0).astype(dtype)


def between(width, low, high, dtype=BF16):
    lane = lanes(width)
    return mask((lane >= low) & (lane < high), dtype)


def join(first, second):
    return jnp.concatenate(
        [first[:, :128], first[:, 128:] + second[:, :128], second[:, 128:]], axis=1
    )


def sine_cosine(angle):
    turns = jnp.floor(angle * (1.0 / math.pi) + 0.5)
    rest = angle - turns * 3.140625
    rest = rest - turns * 9.67502593994140625e-4
    rest = rest - turns * 1.509957990978376e-7
    flip = 1.0 - 2.0 * (turns - 2.0 * jnp.floor(turns * 0.5))
    square = rest * rest
    sine = 1.0
    for divisor in (110.0, 72.0, 42.0, 20.0, 6.0):
        sine = 1.0 - square * (1.0 / divisor) * sine
    cosine = 1.0
    for divisor in (132.0, 90.0, 56.0, 30.0, 12.0, 2.0):
        cosine = 1.0 - square * (1.0 / divisor) * cosine
    return (sine * rest * flip, cosine * flip)


def fold(whole, side):
    return [
        whole[192 * b + 96 * side : 192 * b + 96 * side + 48, :] * between(384, 0, 192, F32)
        + whole[192 * b + 96 * side + 48 : 192 * b + 96 * side + 96, :] * between(384, 192, 384, F32)
        for b in range(2)
    ]


STRIDES = (1, 2, 4, 8)
ORDERS = ((0, 1, 2, 3), (0, 2, 3, 1))
LOWER_RIGHT, LOWER_LEFT, GATE_RIGHT, LIFT_RIGHT, GATE_LEFT, LIFT_LEFT, CHANNEL_ROWS = (
    0,
    768,
    960,
    1152,
    1344,
    2112,
    3072,
)
(
    OUT_RIGHT,
    OUT_LEFT,
    SHAPE_RIGHT,
    SHAPE_LEFT,
    VALUE_RIGHT,
    VALUE_LEFT,
    FILTER_OUT,
    VECTORS,
    FILTER,
    MIXER_ROWS,
) = (0, 192, 576, 768, 960, 1152, 1344, 1472, 1488, 1536)


def tile_rows(index, size=TILE):
    return pl.ds(pl.multiple_of(index * size, size), size)


def whole_kernel(
    inputs,
    upstream,
    table_cos,
    table_sin,
    place,
    vectors,
    filter_vectors,
    midweight,
    filterout,
    valueright,
    valueleft,
    shaperight,
    shapeleft,
    outright,
    outleft,
    gateright,
    gateleft,
    liftright,
    liftleft,
    lowerright,
    lowerleft,
    hidden_out,
    hidden_grad,
    sums_channel,
    sums_mixer,
    w_first,
    w_value,
    w_shape,
    w_out_first,
    w_out_second,
    w_glu,
    w_gate,
    w_lift,
    w_lower,
    w_lower_second,
    up_halves,
    stats,
    norm_one,
    inner_one,
    sig_halves,
    sig_rows,
    shaping,
    sig_pad,
    short,
    act_one,
    cos_one,
    act_two,
    cos_two,
    fil_spec,
    sig_spec,
    prod_spec,
    long_rows,
    long_halves,
    inner_out,
    hat_two,
    norm_two,
    inner_glu,
    factor_gate,
    factor_lift,
    hid,
    inner_lower,
    out_own,
    part_send,
    part_recv,
    d_inner_lower,
    d_gate,
    d_lift,
    d_inner_glu,
    dn_own,
    dn_send,
    dn_recv,
    d_inner_out,
    d_shaping,
    dl_rows,
    ds_pad,
    ds_halves,
    d_inner_one,
    cross_send,
    mid_send,
    mid_recv,
    d_middle,
    branch,
    shape_send,
    shape_recv,
    value_send,
    value_recv,
    w_cross,
    through,
    d_lin,
    own_out,
    grad_vectors,
    grad_filter,
    gain_sums,
    send_sem,
    recv_sem,
    load_sem,
    got_core,
    got_one,
    got_two,
    got_three,
    sum_send,
    sum_recv,
    sum_free,
):
    rows = inputs.shape[0]
    half = rows // 2
    tiles = rows // TILE
    length = 2 * rows
    spans = length // TILE
    wide = lax.axis_index("wide")
    narrow = lax.axis_index("narrow")
    bits = [lax.rem(wide // stride, 2) for stride in STRIDES]
    core = bits[0]
    sibling = (wide + 1 - 2 * core, narrow)
    partner = (wide, 1 - narrow)
    quarter = 2 * narrow + core
    own_half = pl.ds(pl.multiple_of(narrow * 384, 384), 384)
    other_half = pl.ds(pl.multiple_of((1 - narrow) * 384, 384), 384)

    barrier = pltpu.get_barrier_semaphore()
    others = [(wide + stride * (1 - 2 * bit), narrow) for stride, bit in zip(STRIDES, bits)]
    for device in others + [partner]:
        pl.semaphore_signal(barrier, inc=1, device_id=device, device_id_type=MESH)
    pl.semaphore_wait(barrier, len(others) + 1)

    def send(source, target, device, index):
        return pltpu.make_async_remote_copy(
            src_ref=source,
            dst_ref=target,
            send_sem=send_sem.at[index],
            recv_sem=recv_sem.at[index],
            device_id=device,
            device_id_type=MESH,
        )

    received = (got_core, got_one, got_two, got_three)

    def summing(slab, first_sem):
        part = slab.shape[0] // 2
        offsets = [[0], [part]]
        for i in range(2):
            for step in range(4):
                move = bits[ORDERS[i][step]] * (part >> (step + 1))
                offsets[i].append(pl.multiple_of(offsets[i][step] + move, 16))

        def copy(source, target, i, step, back):
            index = first_sem + 8 * back + 2 * step + i
            return pltpu.make_async_remote_copy(
                src_ref=source,
                dst_ref=target,
                send_sem=sum_send.at[index],
                recv_sem=sum_recv.at[index],
                device_id=others[ORDERS[i][step]],
                device_id_type=MESH,
            )

        def scatter(i, step):
            size = part >> (step + 1)
            away = (1 - bits[ORDERS[i][step]]) * size
            away = pl.multiple_of(offsets[i][step] + away, 16)
            return copy(
                slab.at[pl.ds(away, size)], received[step].at[pl.ds(i * size, size)], i, step, 0
            )

        def gather(i, step):
            at = pl.ds(offsets[i][step + 1], part >> (step + 1))
            return copy(slab.at[at], slab.at[at], i, step, 1)

        def start(step):
            for i in range(2):
                scatter(i, step).start()

        def add(step):
            size = part >> (step + 1)
            for i in range(2):
                scatter(i, step).wait()

                @pl.loop(0, size // 48)
                def _(index):
                    own = pl.ds(pl.multiple_of(offsets[i][step + 1] + index * 48, 16), 48)
                    came = received[step][pl.ds(pl.multiple_of(i * size + index * 48, 16), 48), :]
                    slab[own, :] = (slab[own, :].astype(F32) + came.astype(F32)).astype(BF16)

            for i in range(2):
                pl.semaphore_signal(
                    sum_free.at[first_sem // 2 + 2 * step + i],
                    inc=1,
                    device_id=others[ORDERS[i][step]],
                    device_id_type=MESH,
                )

        def clear(step):
            for i in range(2):
                pl.semaphore_wait(sum_free.at[first_sem // 2 + 2 * step + i], 1)

        def back(step):
            for i in range(2):
                gather(i, step).start()

        def take(step):
            for i in range(2):
                gather(i, step).wait()

        return (start, add, clear, back, take, offsets)

    mixer_slab = sums_mixer.at[narrow]
    channel_start, channel_add, channel_clear, channel_back, channel_take, _ = summing(sums_channel, 0)
    mixer_start, mixer_add, mixer_clear, mixer_back, mixer_take, mixer_offsets = summing(mixer_slab, 16)

    load_copies = []
    for source, target in ((gateleft, w_gate), (liftleft, w_lift)):
        for k in range(2):
            copy = pltpu.make_async_copy(
                source.at[:, pl.ds(D * k, D)],
                target.at[k, pl.ds(64 * k, 192)],
                load_sem.at[len(load_copies)],
            )
            copy.start()
            load_copies.append(copy)

    up_copy = send(upstream, up_halves.at[narrow], partner, 0)
    up_copy.start()
    up_halves[narrow] = upstream[...]

    row = lax.broadcasted_iota(jnp.int32, (D, 384), 0)
    lane = lax.broadcasted_iota(jnp.int32, (D, 384), 1)
    step = jnp.where(lane >= 96, 96, 0) + jnp.where(lane >= 192, 96, 0) + jnp.where(lane >= 288, 96, 0)
    select = mask(row == lane + step + narrow * 96)
    right_half = mm(valueright[...], select).astype(BF16)
    shape_half = mm(shaperight[...], select).astype(BF16)
    for b in range(4):
        kept = between(384, 96 * b, 96 * b + 96)
        w_first[192 * b : 192 * b + 192, 0:384] = right_half * kept
        w_first[192 * b : 192 * b + 192, 384:768] = shape_half * kept
    row = lax.broadcasted_iota(jnp.int32, (D, 2 * PAD), 0)
    lane = lax.broadcasted_iota(jnp.int32, (D, 2 * PAD), 1)
    group = jnp.where(lane >= PAD, 1, 0)
    entry = lane - PAD * group
    spread = mask((row == (2 * narrow + group) * 192 + entry) & (entry < 192))
    for source, target in ((valueleft, w_value), (shapeleft, w_shape)):
        wider = mm(source[...], spread).astype(BF16)
        for b in range(4):
            for k in range(2):
                target[96 * b + 48 * k : 96 * b + 48 * k + 48, :] = wider[
                    48 * b : 48 * b + 48, :
                ] * between(2 * PAD, PAD * k, PAD * k + PAD)
    row = lax.broadcasted_iota(jnp.int32, (D, 192), 0)
    lane = lax.broadcasted_iota(jnp.int32, (D, 192), 1)
    start = (2 * narrow) * 192 + (1 - narrow) * 96
    cross = mask(row == start + lane + jnp.where(lane >= 96, 96, 0))
    for i, source in enumerate((valueright, shaperight)):
        part = mm(source[...], cross).astype(BF16)
        for b in range(2):
            w_cross[i, 192 * b : 192 * b + 192, :] = part * between(192, 96 * b, 96 * b + 96)
    first = vectors[0:1, :]
    shift_first = vectors[1:2, :]

    coarse = vectors[...].astype(BF16)
    fine = (vectors[...] - coarse.astype(F32)).astype(BF16)
    through[...] = mm(coarse, w_first[...]) + mm(fine, w_first[...])

    @pl.loop(0, tiles)
    def _(index):
        at = tile_rows(index)
        values = inputs[at, :].astype(F32)
        average = jnp.mean(values, axis=-1, keepdims=True)
        center = values - average
        inverse = lax.rsqrt(jnp.mean(center * center, axis=-1, keepdims=True) + EPSILON)
        hat = center * inverse
        stats[at, 0:1] = average
        stats[at, 1:2] = inverse
        normed = (hat * first + shift_first).astype(BF16)
        norm_one[at, :] = normed
        inner = mm(normed, w_first[...]).astype(BF16)
        inner_one[at, :] = inner
        signal = mm(inner[:, :384], w_value[...]).astype(BF16)
        sig_halves[0, at, :] = signal[:, :PAD]
        sig_halves[1, at, :] = signal[:, PAD:]
        shaped = mm(inner[:, 384:], w_shape[...])
        shaping[0, at, :] = shaped[:, :PAD]
        shaping[1, at, :] = shaped[:, PAD:]

    sig_copy = send(sig_halves.at[1 - core], sig_rows.at[core], sibling, 1)
    sig_copy.start()
    sig_rows[core] = sig_halves[core]

    row = lax.broadcasted_iota(jnp.int32, (D, PAD), 0)
    lane = lax.broadcasted_iota(jnp.int32, (D, PAD), 1)
    pick = mask((row == quarter * 192 + lane) & (lane < 192), F32)
    conv = mm(vectors[...], pick, HIGHEST)
    own_out[...] = mm(filterout[...], pick, HIGHEST)
    pos_bias = filter_vectors[8:9, :]
    mid_bias = filter_vectors[9:10, :]
    frequency = filter_vectors[10:11, :]
    ranks = 5 * (quarter * 192 + lanes(PAD))
    for bound in range(5):
        ranks = jnp.where(ranks >= D, ranks - D, ranks)
    lowest = math.log(0.25 / length)
    highest = math.log(1.0 / 30.0)
    rate = jnp.exp(lowest + ranks.astype(F32) * (1.0 / D) * (highest - lowest))
    loud = jnp.sqrt(2.0 * rate)

    def decay(index):
        places = (lax.broadcasted_iota(jnp.int32, (TILE, PAD), 0) + index * TILE).astype(F32)
        return jnp.exp(-rate * places) * loud

    @pl.loop(0, spans)
    def _(index):
        at = tile_rows(index)
        one = mm(place[at, :], filter_vectors[0:8, :], HIGHEST) + pos_bias
        sine, cosine = sine_cosine(frequency * one)
        act_one[at, :] = sine
        cos_one[at, :] = cosine
        two = mm(sine, midweight[...], HIGHEST) + mid_bias
        sine, cosine = sine_cosine(frequency * two)
        act_two[at, :] = sine
        cos_two[at, :] = cosine
        short[at, :] = (mm(sine, own_out[...], HIGHEST) * decay(index)).astype(BF16)

    @pl.loop(0, spans)
    def _(index):
        at = tile_rows(index)
        real = mm(table_cos[at, :], short[...])
        imag = mm(table_sin[at, :], short[...])
        turn_cos = place[at, 5:6] * (1.0 / length)
        turn_sin = place[at, 6:7] * (1.0 / length)
        fil_spec[0, at, :] = real * turn_cos + imag * turn_sin
        fil_spec[1, at, :] = imag * turn_cos - real * turn_sin

    out_half = outright[:, own_half]
    w_out_first[0:192, :] = out_half * between(384, 0, 192)
    w_out_first[192:256, :] = jnp.zeros((64, 384), BF16)
    w_out_first[256:448, :] = out_half * between(384, 192, 384)
    w_out_first[448:512, :] = jnp.zeros((64, 384), BF16)
    for b in range(4):
        for k in range(4):
            w_out_second[b // 2, 192 * (b % 2) + 48 * k : 192 * (b % 2) + 48 * k + 48, :] = outleft[
                48 * b : 48 * b + 48, :
            ] * between(D, 192 * k, 192 * k + 192)
    lane = lanes(384)
    inside = lane - jnp.where(lane >= 192, 192, 0)
    for b in range(4):
        kept = mask((inside >= 48 * b) & (inside < 48 * b + 48))
        w_glu[192 * b : 192 * b + 192, 0:384] = gateright[...] * kept
        w_glu[192 * b : 192 * b + 192, 384:768] = liftright[...] * kept
    for target in (w_gate, w_lift):
        target[0, 192:256, :] = jnp.zeros((64, D), BF16)
        target[1, 0:64, :] = jnp.zeros((64, D), BF16)
    w_lower[0] = lowerright[:, 0:256] * between(256, 0, 192)
    w_lower[1] = lowerright[:, 128:384] * between(256, 64, 256)
    for b in range(2):
        for k in range(4):
            w_lower_second[192 * b + 48 * k : 192 * b + 48 * k + 48, :] = lowerleft[
                48 * b : 48 * b + 48, :
            ] * between(D, 192 * k, 192 * k + 192)

    sig_copy.wait_recv()
    sig_pad[0:8, :] = jnp.zeros((8, PAD), F32)
    for part in range(2):
        sig_pad[8 + part * rows : 8 + part * rows + rows, :] = sig_rows[part].astype(F32)
    for index in range(spans):
        start = 8 + index * TILE
        total = conv[4:5, :] * sig_pad[start : start + TILE, :]
        total += conv[5:6, :] * sig_pad[start - 1 : start - 1 + TILE, :]
        total += conv[6:7, :] * sig_pad[start - 2 : start - 2 + TILE, :]
        short[index * TILE : index * TILE + TILE, :] = total.astype(BF16)

    @pl.loop(0, spans)
    def _(index):
        at = tile_rows(index)
        real = mm(table_cos[at, :], short[...])
        imag = mm(table_sin[at, :], short[...])
        sig_spec[0, at, :] = real.astype(BF16)
        sig_spec[1, at, :] = imag.astype(BF16)
        fil_re = fil_spec[0, at, :]
        fil_im = fil_spec[1, at, :]
        prod_spec[0, at, :] = (real * fil_re - imag * fil_im).astype(BF16)
        prod_spec[1, at, :] = (real * fil_im + imag * fil_re).astype(BF16)

    per_half = rows // TILE

    @pl.loop(0, spans)
    def _(index):
        at = tile_rows(index)
        result = mm(table_cos[at, :], prod_spec[0]) + mm(table_sin[at, :], prod_spec[1])
        long_rows[index // per_half, tile_rows(lax.rem(index, per_half)), :] = result.astype(BF16)

    long_copy = send(long_rows.at[1 - core], long_halves.at[core], sibling, 2)
    long_copy.start()
    long_halves[core] = long_rows[core]
    long_copy.wait_recv()
    sig_copy.wait_send()
    long_copy.wait_send()

    def inner_copy(index):
        at = tile_rows(index)
        return send(inner_out.at[narrow, at], inner_out.at[narrow, at], partner, 3 + index)

    dn_copy = send(dn_send, dn_recv, partner, 5)
    own_rows = tile_rows(narrow)
    cross_copy = send(cross_send, d_inner_out.at[own_rows], partner, 6)
    middle_copy = send(mid_send, mid_recv, partner, 11)

    def part_copy(index):
        at = tile_rows(index)
        return send(part_send.at[at], part_recv.at[at], partner, 7 + index)

    def shape_copy(index):
        at = tile_rows(index)
        return send(shape_send.at[at], shape_recv.at[at], partner, 12 + index)

    def value_copy(index):
        at = tile_rows(index)
        return send(value_send.at[at], value_recv.at[at], partner, 14 + index)

    def first_other(index):
        return 1 - narrow + index * (2 * narrow - 1)

    @pl.loop(0, tiles)
    def _(order):
        index = narrow + order * (1 - 2 * narrow)
        at = tile_rows(index)
        inner = None
        for k in range(2):
            product = (shaping[k, at, :] * long_halves[k, at, :].astype(F32)).astype(BF16)
            term = mm(product, w_out_first[k * PAD : k * PAD + PAD, :])
            inner = term if inner is None else inner + term
        inner_out[narrow, at, :] = inner.astype(BF16)
        inner_copy(index).start()

    up_copy.wait_recv()
    for copy in load_copies:
        copy.wait()

    gain_second = vectors[2:3, :]
    shift_second = vectors[3:4, :]

    @pl.loop(0, tiles)
    def _(order):
        index = first_other(order)
        at = tile_rows(index)
        inner_copy(index).wait_recv()
        mid = inputs[at, :].astype(F32)
        mid += mm(inner_out[0, at, :], w_out_second[0])
        mid += mm(inner_out[1, at, :], w_out_second[1])
        dn_own[...] = mid
        center = mid - jnp.mean(mid, axis=-1, keepdims=True)
        inverse = lax.rsqrt(jnp.mean(center * center, axis=-1, keepdims=True) + EPSILON)
        hat = center * inverse
        hat_two[...] = hat
        stats[0:TILE, 2:3] = inverse
        normed = (hat * gain_second + shift_second).astype(BF16)
        norm_two[at, :] = normed
        inner = mm(normed, w_glu[...]).astype(BF16)
        inner_glu[at, :] = inner
        lower = [None, None]
        for k in range(2):
            for columns in (slice(0, 256), slice(256, 512), slice(512, 768)):
                gate = mm(inner[:, 128 * k : 128 * k + 256], w_gate[k, :, columns])
                lift = mm(inner[:, 384 + 128 * k : 384 + 128 * k + 256], w_lift[k, :, columns])
                cumulative = 0.5 * (1.0 + lax.erf(gate * (1.0 / math.sqrt(2.0))))
                density = jnp.exp(-0.5 * gate * gate) * (1.0 / math.sqrt(2.0 * math.pi))
                activated = gate * cumulative
                unit = (activated * lift).astype(BF16)
                hid[k, at, columns] = unit
                factor_lift[k, :, columns] = activated
                factor_gate[k, :, columns] = lift * (cumulative + gate * density)
                term = mm(unit, w_lower[k, columns, :])
                lower[k] = term if lower[k] is None else lower[k] + term
        inner_low = join(*lower).astype(BF16)
        inner_lower[at, :] = inner_low
        out_own[at, :] = dn_own[:, own_half] + mm(inner_low, w_lower_second[:, own_half])
        part_send[at, :] = mm(inner_low, w_lower_second[:, other_half]).astype(BF16)

        above = jnp.concatenate([up_halves[0, at, :], up_halves[1, at, :]], axis=1)
        d_low = mm_nt(above, w_lower_second[...]).astype(BF16)
        d_inner_lower[at, :] = d_low
        gates = [None, None]
        lifts = [None, None]
        for k in range(2):
            for columns in (slice(0, 256), slice(256, 512), slice(512, 768)):
                d_hidden = mm_nt(d_low[:, 128 * k : 128 * k + 256], w_lower[k, columns, :])
                to_gate = (d_hidden * factor_gate[k, :, columns]).astype(BF16)
                to_lift = (d_hidden * factor_lift[k, :, columns]).astype(BF16)
                d_gate[k, at, columns] = to_gate
                d_lift[k, at, columns] = to_lift
                term = mm_nt(to_gate, w_gate[k, :, columns])
                gates[k] = term if gates[k] is None else gates[k] + term
                term = mm_nt(to_lift, w_lift[k, :, columns])
                lifts[k] = term if lifts[k] is None else lifts[k] + term
        d_glu = jnp.concatenate([join(*gates), join(*lifts)], axis=1).astype(BF16)
        d_inner_glu[at, :] = d_glu
        into = mm_nt(d_glu, w_glu[...])
        dn_own[...] = into

        @pl.when(order == 0)
        def _():
            dn_send[...] = dn_own[...].astype(BF16)
            dn_copy.start()

    @pl.loop(0, tiles)
    def _(index):
        part_copy(index).start()

    for side in range(2):
        columns = slice(384 * side, 384 * side + 384)
        folded = fold(mm_tn(inner_lower[...], up_halves[side]), side)
        for b in range(2):
            first_row = LOWER_LEFT + 96 * side + 48 * b
            sums_channel[first_row : first_row + 48, :] = folded[b].astype(BF16)
    low_lanes = lanes(128) < 64
    for columns in (slice(0, 384), slice(384, 768)):
        columns_at = slice(LOWER_RIGHT + columns.start, LOWER_RIGHT + columns.stop)
        parts = [
            mm_tn(hid[k, :, columns], d_inner_lower[:, 128 * k : 128 * k + 256]) for k in range(2)
        ]
        sums_channel[columns_at, 0:128] = parts[0][:, 0:128].astype(BF16)
        sums_channel[columns_at, 128:256] = jnp.where(
            low_lanes, parts[0][:, 128:256], parts[1][:, 0:128]
        ).astype(BF16)
        sums_channel[columns_at, 256:384] = parts[1][:, 128:256].astype(BF16)
    for offset, upper, target in ((0, d_gate, GATE_LEFT), (384, d_lift, LIFT_LEFT)):
        for k in range(2):
            for start in (0, 384):
                whole = mm_tn(
                    inner_glu[:, offset + 128 * k : offset + 128 * k + 256],
                    upper[k, :, start : start + 384],
                )
                first_row = target + 384 * k + start // 2
                sums_channel[first_row : first_row + 192, :] = whole[
                    64 * k : 64 * k + 192, :
                ].astype(BF16)
    for offset, target in ((0, GATE_RIGHT), (384, LIFT_RIGHT)):
        whole = mm_tn(norm_two[...], d_inner_glu[:, offset : offset + 384])
        total = None
        for b in range(4):
            term = whole[192 * b : 192 * b + 192, :] * mask(
                (inside >= 48 * b) & (inside < 48 * b + 48), F32
            )
            total = term if total is None else total + term
        sums_channel[target : target + 192, :] = total.astype(BF16)

    sums_channel[2880:3072, :] = jnp.zeros((192, 384), BF16)
    channel_start(0)

    dn_copy.wait_recv()
    into = dn_own[...] + dn_recv[...].astype(F32)
    hat = hat_two[...]
    gain_sums[0:1, :] = jnp.sum(into * hat, axis=0, keepdims=True)
    gain_sums[1:2, :] = jnp.sum(into, axis=0, keepdims=True)
    scaled = into * gain_second
    above = jnp.concatenate([up_halves[0, own_rows, :], up_halves[1, own_rows, :]], axis=1)
    d_mid = above.astype(F32) + stats[0:TILE, 2:3] * (
        scaled
        - jnp.mean(scaled, axis=-1, keepdims=True)
        - hat * jnp.mean(scaled * hat, axis=-1, keepdims=True)
    )
    hat_two[...] = d_mid
    branch[...] = d_mid.astype(BF16)
    cross_send[...] = mm_nt(branch[...], w_out_second[1 - narrow]).astype(BF16)
    cross_copy.start()
    mid_send[...] = hat_two[:, other_half].astype(BF16)
    middle_copy.start()
    d_inner_out[own_rows, :] = mm_nt(branch[...], w_out_second[narrow]).astype(BF16)

    @pl.loop(0, tiles)
    def _(order):
        index = narrow + order * (1 - 2 * narrow)
        at = tile_rows(index)

        @pl.when(order == 1)
        def _():
            cross_copy.wait_recv()

        d_inner = d_inner_out[at, :]
        for k in range(2):
            d_mixed = mm_nt(d_inner, w_out_first[k * PAD : k * PAD + PAD, :])
            d_shaping[k, at, :] = (d_mixed * long_halves[k, at, :].astype(F32)).astype(BF16)
            sig_halves[k, at, :] = (d_mixed * shaping[k, at, :]).astype(BF16)

    dl_copy = send(sig_halves.at[1 - core], dl_rows.at[core], sibling, 9)
    dl_copy.start()
    dl_rows[core] = sig_halves[core]

    @pl.loop(0, tiles)
    def _(index):
        at = tile_rows(index)
        to_shape = jnp.concatenate([d_shaping[0, at, :], d_shaping[1, at, :]], axis=1)
        d_inner_one[at, 384:768] = mm_nt(to_shape, w_shape[...]).astype(BF16)
        shape_send[at, :] = mm_nt(
            to_shape, w_shape[pl.ds(pl.multiple_of((1 - narrow) * 192, 192), 192), :]
        ).astype(BF16)
        shape_copy(index).start()


    channel_add(0)
    channel_start(1)
    for h in range(2):
        for side in range(2):
            columns = slice(384 * side, 384 * side + 384)
            folded = fold(mm_tn(inner_out[h, own_rows, :], branch[:, columns]), side)
            for b in range(2):
                first_row = OUT_LEFT + 192 * h + 96 * side + 48 * b
                mixer_slab[first_row : first_row + 48, :] = folded[b].astype(BF16)
    parts = []
    for k in range(2):
        product = (shaping[k] * long_halves[k].astype(F32)).astype(BF16)
        parts.append(mm_tn(product, d_inner_out[...]))
    mixer_slab[OUT_RIGHT : OUT_RIGHT + 192, :] = jnp.where(
        lanes(384) < 192, parts[0][0:192, :], parts[1][0:192, :]
    ).astype(BF16)

    dl_copy.wait_recv()

    @pl.loop(0, spans)
    def _(index):
        at = tile_rows(index)
        upper = dl_rows[...].reshape(length, PAD)
        real = mm(table_cos[at, :], upper)
        imag = mm(table_sin[at, :], upper)
        fil_re = fil_spec[0, at, :]
        fil_im = fil_spec[1, at, :]
        prod_spec[0, at, :] = (real * fil_re + imag * fil_im).astype(BF16)
        prod_spec[1, at, :] = (imag * fil_re - real * fil_im).astype(BF16)
        sig_re = sig_spec[0, at, :].astype(F32)
        sig_im = sig_spec[1, at, :].astype(F32)
        turn_cos = place[at, 5:6] * (1.0 / length)
        turn_sin = place[at, 6:7] * (1.0 / length)
        both_re = real * sig_re + imag * sig_im
        both_im = imag * sig_re - real * sig_im
        sig_spec[0, at, :] = (both_re * turn_cos - both_im * turn_sin).astype(BF16)
        sig_spec[1, at, :] = (both_im * turn_cos + both_re * turn_sin).astype(BF16)

    ds_pad[length : length + 8, :] = jnp.zeros((8, PAD), F32)

    @pl.loop(0, spans)
    def _(index):
        at = tile_rows(index)
        result = mm(table_cos[at, :], prod_spec[0]) + mm(table_sin[at, :], prod_spec[1])
        ds_pad[at, :] = result.astype(BF16).astype(F32)

    for index in range(spans):
        start = index * TILE
        total = conv[4:5, :] * ds_pad[start : start + TILE, :]
        total += conv[5:6, :] * ds_pad[start + 1 : start + 1 + TILE, :]
        total += conv[6:7, :] * ds_pad[start + 2 : start + 2 + TILE, :]
        part, inner_start = divmod(start, rows)
        long_rows[part, inner_start : inner_start + TILE, :] = total.astype(BF16)
    ds_copy = send(long_rows.at[1 - core], ds_halves.at[core], sibling, 10)
    ds_copy.start()
    ds_halves[core] = long_rows[core]

    channel_add(1)
    channel_start(2)
    grad_vectors[...] = jnp.zeros(grad_vectors.shape, F32)
    sums = [jnp.zeros((1, PAD), F32) for _ in range(3)]
    for index in range(spans):
        start = index * TILE
        upper = ds_pad[start : start + TILE, :]
        for j in range(3):
            sums[j] += jnp.sum(
                upper * sig_pad[8 + start - j : 8 + start - j + TILE, :], axis=0, keepdims=True
            )
    sums = jnp.concatenate(sums + [jnp.zeros((5, PAD), F32)], axis=0)
    lane = lax.broadcasted_iota(jnp.int32, (PAD, 384), 1)
    row = lax.broadcasted_iota(jnp.int32, (PAD, 384), 0)
    place_core = mask((lane == core * 192 + row) & (row < 192))
    conv_sums = mm(sums.astype(BF16), place_core)
    grad_vectors[4:7, :] = conv_sums[0:3, :]

    d_lin[...] = jnp.zeros(d_lin.shape, F32)
    grad_filter[...] = jnp.zeros(grad_filter.shape, F32)

    @pl.loop(0, spans)
    def _(index):
        at = tile_rows(index)
        d_taps = mm(table_cos[at, :], sig_spec[0]) + mm(table_sin[at, :], sig_spec[1])
        d_mod = d_taps * decay(index)
        d_lin[...] += mm_tn(act_two[at, :], d_mod, HIGHEST)
        two = mm_nt(d_mod, own_out[...], HIGHEST) * cos_two[at, :]
        scaled_two = two * frequency
        grad_filter[0:128, :] += mm_tn(act_one[at, :], scaled_two, HIGHEST)
        one = mm_nt(scaled_two, midweight[...], HIGHEST) * cos_one[at, :]
        scaled_one = one * frequency
        grad_filter[128:136, :] += mm_tn(place[at, :], scaled_one, HIGHEST)
        grad_filter[136:137, :] += jnp.sum(scaled_one, axis=0, keepdims=True)
        grad_filter[137:138, :] += jnp.sum(scaled_two, axis=0, keepdims=True)
        lin_one = mm(place[at, :], filter_vectors[0:8, :], HIGHEST) + pos_bias
        lin_two = mm(act_one[at, :], midweight[...], HIGHEST) + mid_bias
        grad_filter[138:139, :] += jnp.sum(one * lin_one + two * lin_two, axis=0, keepdims=True)

    mixer_slab[FILTER_OUT : FILTER_OUT + 128, :] = mm(d_lin[...].astype(BF16), place_core).astype(BF16)
    for i in range(3):
        mixer_slab[FILTER : FILTER + 48, 128 * i : 128 * i + 128] = grad_filter[48 * i : 48 * i + 48, :].astype(BF16)

    channel_add(2)
    channel_start(3)

    ds_copy.wait_recv()
    other_blocks = pl.ds(pl.multiple_of((1 - narrow) * 192, 192), 192)

    @pl.loop(0, tiles)
    def _(index):
        at = tile_rows(index)
        to_value = jnp.concatenate([ds_halves[0, at, :], ds_halves[1, at, :]], axis=1)
        d_inner = mm_nt(to_value, w_value[...]).astype(BF16)
        d_inner_one[at, 0:384] = d_inner
        against = inner_one[at, :].astype(F32) - through[1:2, :]
        d_inner = d_inner_one[at, :].astype(F32)
        plain = jnp.sum(d_inner * through[0:1, :], axis=-1, keepdims=True)
        along = jnp.sum(d_inner * against, axis=-1, keepdims=True)
        stats[at, 2:3] = plain
        stats[at, 3:4] = along
        lane = lanes(128)
        tail = jnp.where(lane == 64, plain, jnp.where(lane == 65, along, 0.0))
        away = mm_nt(to_value, w_value[other_blocks, :])
        value_send[at, 0:128] = away[:, 0:128].astype(BF16)
        value_send[at, 128:192] = away[:, 128:192].astype(BF16)
        value_send[at, 192:256] = tail[:, 64:128].astype(BF16)
        value_copy(index).start()

    channel_add(3)
    for step in range(4):
        channel_clear(step)
    channel_back(3)
    for offset, target in ((0, VALUE_RIGHT), (384, SHAPE_RIGHT)):
        whole = mm_tn(norm_one[...], d_inner_one[:, offset : offset + 384])
        total = None
        for b in range(4):
            term = whole[192 * b : 192 * b + 192, :] * between(
                384, 96 * b, 96 * b + 96, F32
            )
            total = term if total is None else total + term
        mixer_slab[target : target + 192, :] = total.astype(BF16)
    lane = lax.broadcasted_iota(jnp.int32, (2 * PAD, 384), 1)
    row = lax.broadcasted_iota(jnp.int32, (2 * PAD, 384), 0)
    squeeze = mask(row == lane + jnp.where(lane >= 192, 64, 0))
    for offset, upper, target in ((0, ds_halves, VALUE_LEFT), (384, d_shaping, SHAPE_LEFT)):
        above = jnp.concatenate([upper[0], upper[1]], axis=1)
        whole = mm_tn(inner_one[:, offset : offset + 384], above)
        pieces = []
        for b in range(4):
            total = None
            for k in range(2):
                term = whole[96 * b + 48 * k : 96 * b + 48 * k + 48, :] * between(
                    2 * PAD, PAD * k, PAD * k + PAD, F32
                )
                total = term if total is None else total + term
            pieces.append(total)
        total = jnp.concatenate(pieces, axis=0).astype(BF16)
        mixer_slab[target : target + 192, :] = mm(total, squeeze).astype(BF16)

    channel_take(3)
    channel_back(2)

    first_half = vectors[0:1, own_half]
    middle_copy.wait_recv()
    d_middle[own_rows, :] = hat_two[:, own_half]
    d_middle[tile_rows(1 - narrow), :] = mid_recv[...].astype(F32)
    @pl.loop(0, tiles)
    def _(index):
        at = tile_rows(index)
        part_copy(index).wait_recv()
        hidden_out[at, :] = (out_own[at, :] + part_recv[at, :].astype(F32)).astype(BF16)
        shape_copy(index).wait_recv()
        value_copy(index).wait_recv()
        into = mm_nt(d_inner_one[at, :], w_first[own_half, :])
        into += mm_nt(value_recv[at, 0:192], w_cross[0])
        into += mm_nt(shape_recv[at, :], w_cross[1])
        plain = (stats[at, 2:3] + value_recv[at, 192:193].astype(F32)) * (1.0 / D)
        along = (stats[at, 3:4] + value_recv[at, 193:194].astype(F32)) * (1.0 / D)
        hat = (inputs[at, own_half].astype(F32) - stats[at, 0:1]) * stats[at, 1:2]
        grad_vectors[0:1, :] += jnp.sum(into * hat, axis=0, keepdims=True)
        grad_vectors[1:2, :] += jnp.sum(into, axis=0, keepdims=True)
        hidden_grad[at, :] = (
            d_middle[at, :] + stats[at, 1:2] * (into * first_half - plain - hat * along)
        ).astype(BF16)

    grad_vectors[2:4, :] = gain_sums[0:2, 0:384]
    grad_vectors[8:10, :] = gain_sums[0:2, 384:768]
    mixer_slab[VECTORS : VECTORS + 16, :] = grad_vectors[...].astype(BF16)
    mixer_start(0)
    channel_take(2)
    channel_back(1)
    mixer_add(0)
    for step in range(1, 4):
        mixer_start(step)
        mixer_add(step)
    for step in range(4):
        mixer_clear(step)
    mixer_back(3)
    channel_take(1)
    channel_back(0)
    for step in (3, 2, 1):
        mixer_take(step)
        if step > 1:
            mixer_back(step - 1)
    size = MIXER_ROWS // 4
    across = []
    for i in range(2):
        at = pl.ds(mixer_offsets[i][1], size)
        across.append(
            pltpu.make_async_remote_copy(
                src_ref=mixer_slab.at[at],
                dst_ref=mixer_slab.at[at],
                send_sem=sum_send.at[32 + i],
                recv_sem=sum_recv.at[32 + i],
                device_id=partner,
                device_id_type=MESH,
            )
        )
        across[i].start()
    mixer_back(0)
    for i in range(2):
        across[i].wait()
        at = pl.ds(mixer_offsets[i][1], size)
        across.append(
            pltpu.make_async_remote_copy(
                src_ref=sums_mixer.at[1 - narrow, at],
                dst_ref=sums_mixer.at[1 - narrow, at],
                send_sem=sum_send.at[34 + i],
                recv_sem=sum_recv.at[34 + i],
                device_id=sibling,
                device_id_type=MESH,
            )
        )
        across[2 + i].start()
    for i in range(2):
        across[2 + i].wait()
    mixer_take(0)
    channel_take(0)

    for copy in (up_copy, dl_copy, ds_copy, dn_copy, cross_copy, middle_copy):
        copy.wait_send()

    @pl.loop(0, tiles)
    def _(index):
        for copy in (inner_copy, part_copy, shape_copy, value_copy):
            copy(index).wait_send()


def finish_kernel(
    sums_channel,
    sums_mixer,
    grad_vectors,
    grad_valueright,
    grad_valueleft,
    grad_shaperight,
    grad_shapeleft,
    grad_filter,
    grad_filterout,
    grad_outright,
    grad_outleft,
    grad_gateright,
    grad_gateleft,
    grad_liftright,
    grad_liftleft,
    grad_lowerright,
    grad_lowerleft,
):
    grad_lowerright[...] = sums_channel[LOWER_RIGHT : LOWER_RIGHT + D, :].astype(F32)
    grad_gateright[...] = sums_channel[GATE_RIGHT : GATE_RIGHT + 192, :].astype(F32)
    grad_liftright[...] = sums_channel[LIFT_RIGHT : LIFT_RIGHT + 192, :].astype(F32)
    for i in range(4):
        columns = slice(384 * i, 384 * i + 384)
        first_row = GATE_LEFT + 192 * i
        grad_gateleft[:, columns] = sums_channel[first_row : first_row + 192, :].astype(F32)
        first_row = LIFT_LEFT + 192 * i
        grad_liftleft[:, columns] = sums_channel[first_row : first_row + 192, :].astype(F32)
    lane = lax.broadcasted_iota(jnp.int32, (384, D), 1)
    row = lax.broadcasted_iota(jnp.int32, (384, D), 0)
    step = jnp.where(row >= 96, 96, 0) + jnp.where(row >= 192, 96, 0) + jnp.where(row >= 288, 96, 0)
    unselect = [mask(lane == row + step + 96 * h) for h in range(2)]
    for first_row, target in ((VALUE_RIGHT, grad_valueright), (SHAPE_RIGHT, grad_shaperight)):
        target[...] = mm(sums_mixer[0, first_row : first_row + 192, :], unselect[0]) + mm(
            sums_mixer[1, first_row : first_row + 192, :], unselect[1]
        )
    for h in range(2):
        columns = slice(384 * h, 384 * h + 384)
        grad_lowerleft[:, columns] = sums_channel[
            LOWER_LEFT + 96 * h : LOWER_LEFT + 96 * h + 96, :
        ].astype(F32)
        for first_row, target in (
            (OUT_RIGHT, grad_outright),
            (SHAPE_LEFT, grad_shapeleft),
            (VALUE_LEFT, grad_valueleft),
        ):
            target[:, columns] = sums_mixer[h, first_row : first_row + 192, :].astype(F32)
        for side in range(2):
            at = slice(OUT_LEFT + 192 * h + 96 * side, OUT_LEFT + 192 * h + 96 * side + 96)
            grad_outleft[96 * h : 96 * h + 96, 384 * side : 384 * side + 384] = sums_mixer[
                0, at, :
            ].astype(F32) + sums_mixer[1, at, :].astype(F32)
        own = sums_mixer[h, VECTORS : VECTORS + 16, :].astype(F32)
        both = own + sums_mixer[1 - h, VECTORS : VECTORS + 16, :].astype(F32)
        grad_vectors[0:2, columns] = own[0:2, :]
        grad_vectors[2:4, columns] = both[2 + 6 * h : 4 + 6 * h, :]
        grad_vectors[4:7, columns] = own[4:7, :]
    for i in range(3):
        columns = slice(128 * i, 128 * i + 128)
        grad_filter[48 * i : 48 * i + 48, :] = sums_mixer[
            0, FILTER : FILTER + 48, columns
        ].astype(F32) + sums_mixer[1, FILTER : FILTER + 48, columns].astype(F32)
    count = grad_filterout.shape[1]
    first = (lax.axis_index("wide") * 2 + lax.axis_index("narrow")) * count
    total = jnp.zeros(grad_filterout.shape, F32)
    row = lax.broadcasted_iota(jnp.int32, (384, count), 0)
    lane = lax.broadcasted_iota(jnp.int32, (384, count), 1)
    for h in range(2):
        total += mm(
            sums_mixer[h, FILTER_OUT : FILTER_OUT + 128, :], mask(row + 384 * h == first + lane)
        )
    grad_filterout[...] = total


def transform_tables(length):
    index = np.arange(length, dtype=np.float64) + 0.5
    angle = np.outer(index, index) * (math.pi / length)
    return (np.cos(angle).astype(jnp.bfloat16), np.sin(angle).astype(jnp.bfloat16))


def place_table(length):
    places = np.arange(length, dtype=np.float64)
    angle = places * (2.0 * math.pi / length)
    turn = (places + 0.5) * (math.pi / (2.0 * length))
    columns = [
        places / length,
        np.cos(angle),
        np.sin(angle),
        np.cos(2.0 * angle),
        np.sin(2.0 * angle),
        np.cos(turn),
        np.sin(turn),
        np.zeros(length),
    ]
    return np.stack(columns, axis=1).astype(np.float32)


def pair_body(
    hidden_in,
    gainfirst,
    shiftfirst,
    valueright,
    valueleft,
    shaperight,
    shapeleft,
    convtaps,
    posweight,
    posbias,
    sinefreq,
    midweight,
    midbias,
    filterout,
    outright,
    outleft,
    gainsecond,
    shiftsecond,
    gateright,
    gateleft,
    liftright,
    liftleft,
    lowerright,
    lowerleft,
    grad_out,
):
    rows = hidden_in.shape[0]
    length = 2 * rows
    table_cos, table_sin = transform_tables(length)
    vectors = jnp.concatenate(
        [jnp.stack([gainfirst, shiftfirst, gainsecond, shiftsecond]), convtaps, jnp.zeros((1, D), F32)]
    )
    filter_vectors = jnp.concatenate(
        [posweight, jnp.zeros((3, 128), F32), jnp.stack([posbias, midbias, sinefreq]), jnp.zeros((5, 128), F32)]
    )

    def out(extent, dtype=BF16):
        return jax.ShapeDtypeStruct(extent, dtype)

    def buf(*extent, dtype=BF16):
        return pltpu.VMEM(extent, dtype)

    vmem = pl.BlockSpec(memory_space=pltpu.VMEM)
    hbm = pl.BlockSpec(memory_space=pl.ANY)
    results = pl.pallas_call(
        whole_kernel,
        out_shape=(
            out((rows, 384)),
            out((rows, 384)),
            out((CHANNEL_ROWS, 384)),
            out((2, MIXER_ROWS, 384)),
        ),
        in_specs=[vmem] * 16 + [hbm, vmem, hbm, vmem, vmem],
        out_specs=[vmem] * 4,
        scratch_shapes=[
            buf(D, D),
            buf(384, 512),
            buf(384, 512),
            buf(512, 384),
            buf(2, 384, D),
            buf(D, D),
            buf(2, 256, D),
            buf(2, 256, D),
            buf(2, D, 256),
            buf(384, D),
            buf(2, rows, 384),
            buf(rows, 128, dtype=F32),
            buf(rows, D),
            buf(rows, D),
            buf(2, rows, PAD),
            buf(2, rows, PAD),
            buf(2, rows, PAD, dtype=F32),
            buf(length + 8, PAD, dtype=F32),
            buf(length, PAD),
            buf(length, 128, dtype=F32),
            buf(length, 128, dtype=F32),
            buf(length, 128, dtype=F32),
            buf(length, 128, dtype=F32),
            buf(2, length, PAD, dtype=F32),
            buf(2, length, PAD),
            buf(2, length, PAD),
            buf(2, rows, PAD),
            buf(2, rows, PAD),
            buf(2, rows, 384),
            buf(TILE, D, dtype=F32),
            buf(rows, D),
            buf(rows, D),
            buf(2, TILE, D, dtype=F32),
            buf(2, TILE, D, dtype=F32),
            buf(2, rows, D),
            buf(rows, 384),
            buf(rows, 384, dtype=F32),
            buf(rows, 384),
            buf(rows, 384),
            buf(rows, 384),
            buf(2, rows, D),
            buf(2, rows, D),
            buf(rows, D),
            buf(TILE, D, dtype=F32),
            buf(TILE, D),
            buf(TILE, D),
            buf(rows, 384),
            buf(2, rows, PAD),
            buf(2, rows, PAD),
            buf(length + 8, PAD, dtype=F32),
            buf(2, rows, PAD),
            buf(rows, D),
            buf(TILE, 384),
            buf(TILE, 384),
            buf(TILE, 384),
            buf(rows, 384, dtype=F32),
            buf(TILE, D),
            buf(rows, 192),
            buf(rows, 192),
            buf(rows, 256),
            buf(rows, 256),
            buf(2, 384, 192),
            buf(8, D, dtype=F32),
            buf(128, PAD, dtype=F32),
            buf(128, PAD, dtype=F32),
            buf(16, 384, dtype=F32),
            buf(144, 128, dtype=F32),
            buf(8, D, dtype=F32),
            pltpu.SemaphoreType.DMA((16,)),
            pltpu.SemaphoreType.DMA((16,)),
            pltpu.SemaphoreType.DMA((4,)),
            buf(CHANNEL_ROWS // 2, 384),
            buf(CHANNEL_ROWS // 4, 384),
            buf(CHANNEL_ROWS // 8, 384),
            buf(CHANNEL_ROWS // 16, 384),
            pltpu.SemaphoreType.DMA((36,)),
            pltpu.SemaphoreType.DMA((36,)),
            pltpu.SemaphoreType.REGULAR((16,)),
        ],
        compiler_params=pltpu.CompilerParams(
            collective_id=0, has_side_effects=True, vmem_limit_bytes=63 * 1024 * 1024
        ),
    )(
        hidden_in,
        grad_out,
        table_cos,
        table_sin,
        place_table(length),
        vectors,
        filter_vectors,
        midweight,
        filterout,
        valueright,
        valueleft,
        shaperight,
        shapeleft,
        outright,
        outleft,
        gateright,
        gateleft,
        liftright,
        liftleft,
        lowerright,
        lowerleft,
    )
    hidden_out, hidden_grad, sums_channel, sums_mixer = results
    count = D // (lax.axis_size("wide") * lax.axis_size("narrow"))
    grads = pl.pallas_call(
        finish_kernel,
        out_shape=(
            out((8, D), F32),
            out((192, D), F32),
            out((192, D), F32),
            out((192, D), F32),
            out((192, D), F32),
            out((144, 128), F32),
            out((128, count), F32),
            out((192, D), F32),
            out((192, D), F32),
            out(gateright.shape, F32),
            out(gateleft.shape, F32),
            out(liftright.shape, F32),
            out(liftleft.shape, F32),
            out(lowerright.shape, F32),
            out(lowerleft.shape, F32),
        ),
        in_specs=[vmem] * 2,
        out_specs=[vmem] * 15,
        compiler_params=pltpu.CompilerParams(vmem_limit_bytes=32 * 1024 * 1024),
    )(sums_channel, sums_mixer)
    grad_vectors, grad_filter = grads[0], grads[5]
    return (
        hidden_out,
        hidden_grad,
        grad_vectors[0],
        grad_vectors[1],
        *grads[1:5],
        grad_vectors[4:7],
        grad_filter[128:133],
        grad_filter[136],
        grad_filter[138],
        grad_filter[:128],
        grad_filter[137],
        grads[6],
        *grads[7:9],
        grad_vectors[2],
        grad_vectors[3],
        *grads[9:],
    )


def solution(mesh):
    pairs = mesh.shape["wide"] == 2 * SEQS and mesh.shape["narrow"] == 2
    return jax.shard_map(
        pair_body if pairs else body,
        mesh=mesh,
        in_specs=(
            P("wide", None),
            P(),
            P(),
            P(),
            P(),
            P(),
            P(),
            P(),
            P(),
            P(),
            P(),
            P(),
            P(),
            P(),
            P(),
            P(),
            P(),
            P(),
            P(None, "narrow"),
            P(None, "narrow"),
            P(None, "narrow"),
            P(None, "narrow"),
            P(None, "narrow"),
            P("narrow", None),
            P("wide", "narrow"),
        ),
        out_specs=(
            P("wide", "narrow"),
            P("wide", "narrow"),
            P(),
            P(),
            P(),
            P(),
            P(),
            P(),
            P(),
            P(),
            P(),
            P(),
            P(),
            P(),
            P(None, ("wide", "narrow")),
            P(),
            P(),
            P(),
            P(),
            P(None, "narrow"),
            P(None, "narrow"),
            P(None, "narrow"),
            P(None, "narrow"),
            P(None, "narrow"),
            P("narrow", None),
        ),
        check_vma=False,
    )
```

```python
import math

import jax
import jax.numpy as jnp
import numpy as np
from jax import lax
from jax.experimental import pallas as pl
from jax.experimental.pallas import tpu as pltpu
from jax.sharding import PartitionSpec as P

D = 768
BLOCKS = 4
SEQS = 8


EPSILON = 1e-05
HIGHEST = lax.Precision.HIGHEST


def from_behind(x, axis, by):
    length = lax.axis_size(axis)
    pairs = [(i, i + by) for i in range(length) if 0 <= i + by < length]
    return lax.ppermute(x, axis, pairs)


def norm_forward(values, gain, shift):
    center = values - jnp.mean(values, axis=-1, keepdims=True)
    inverse = lax.rsqrt(jnp.mean(center * center, axis=-1, keepdims=True) + EPSILON)
    normed = center * inverse
    return (normed * gain + shift, normed, inverse)


def norm_backward(upstream, normed, inverse, gain):
    scaled = upstream * gain
    result = inverse * (
        scaled
        - jnp.mean(scaled, axis=-1, keepdims=True)
        - normed * jnp.mean(scaled * normed, axis=-1, keepdims=True)
    )
    return (result, jnp.sum(upstream * normed, axis=0), jnp.sum(upstream, axis=0))


def right_view(right, nblocks, groups, group_first):
    width_in = right.shape[0]
    piece = right.shape[1] // (nblocks * groups)
    if group_first:
        return (right.reshape(width_in, groups, nblocks, piece), "ikbc")
    return (right.reshape(width_in, nblocks, groups, piece), "ibkc")


def section_one(inputs, right, groups, group_first):
    rowcount = inputs.shape[0]
    width_in = right.shape[0]
    nblocks = inputs.shape[1] // width_in
    factor, letters = right_view(right, nblocks, groups, group_first)
    first = jnp.einsum(
        "tbi," + letters + "->tkbc",
        inputs.reshape(rowcount, nblocks, width_in),
        factor,
        preferred_element_type=jnp.float32,
    )
    return first.reshape(rowcount, groups, -1).astype(jnp.bfloat16)


def section_two(middle_part, left):
    groups = middle_part.shape[1]
    result = jnp.einsum(
        "tkj,jke->tke",
        middle_part,
        left.reshape(left.shape[0], groups, -1),
        preferred_element_type=jnp.float32,
    )
    return result.reshape(result.shape[0], -1)


def back_two(middle_part, left, upstream):
    groups = middle_part.shape[1]
    left_view = left.reshape(left.shape[0], groups, -1)
    grad_left = jnp.einsum(
        "tkj,tke->jke", middle_part, upstream, preferred_element_type=jnp.float32
    )
    grad_middle = jnp.einsum(
        "tke,jke->tkj", upstream, left_view, preferred_element_type=jnp.float32
    )
    return (grad_left.reshape(left.shape[0], -1), grad_middle.astype(jnp.bfloat16))


def back_one(inputs, right, grad_middle, group_first):
    rowcount = inputs.shape[0]
    width_in = right.shape[0]
    nblocks = inputs.shape[1] // width_in
    groups = grad_middle.shape[1]
    factor, letters = right_view(right, nblocks, groups, group_first)
    spread_back = grad_middle.reshape(rowcount, groups, nblocks, -1)
    blocked = inputs.reshape(rowcount, nblocks, width_in)
    grad_right = jnp.einsum(
        "tbi,tkbc->" + letters, blocked, spread_back, preferred_element_type=jnp.float32
    )
    grad_inputs = jnp.einsum(
        "tkbc," + letters + "->tbi", spread_back, factor, preferred_element_type=jnp.float32
    )
    return (grad_right.reshape(width_in, -1), grad_inputs.reshape(rowcount, -1))


def fourier_tables(length):
    span = length // 128
    slow_index = jnp.arange(span, dtype=jnp.int32)
    fast_index = jnp.arange(128, dtype=jnp.int32)
    small = (slow_index[:, None] * slow_index[None, :] % span).astype(jnp.float32) * (
        2.0 * math.pi / span
    )
    twist = (slow_index[:, None] * fast_index[None, :] % length).astype(jnp.float32) * (
        2.0 * math.pi / length
    )
    large = (fast_index[:, None] * fast_index[None, :] % 128).astype(jnp.float32) * (
        2.0 * math.pi / 128
    )
    return (
        jnp.cos(small),
        jnp.sin(small),
        jnp.cos(twist),
        jnp.sin(twist),
        jnp.cos(large),
        jnp.sin(large),
    )


def to_spectrum(signal, tables):
    cos_small, sin_small, cos_twist, sin_twist, cos_large, sin_large = tables
    span = cos_small.shape[0]
    padded = jnp.concatenate([signal, jnp.zeros_like(signal)], axis=-1)
    padded = padded.reshape(signal.shape[:-1] + (span, 128))
    first_re = jnp.einsum("...qp,qk->...kp", padded, cos_small, precision=HIGHEST)
    first_im = -jnp.einsum("...qp,qk->...kp", padded, sin_small, precision=HIGHEST)
    turned_re = first_re * cos_twist + first_im * sin_twist
    turned_im = first_im * cos_twist - first_re * sin_twist
    out_re = jnp.einsum("...kp,pj->...kj", turned_re, cos_large, precision=HIGHEST) + jnp.einsum(
        "...kp,pj->...kj", turned_im, sin_large, precision=HIGHEST
    )
    out_im = jnp.einsum("...kp,pj->...kj", turned_im, cos_large, precision=HIGHEST) - jnp.einsum(
        "...kp,pj->...kj", turned_re, sin_large, precision=HIGHEST
    )
    return (out_re, out_im)


def from_spectrum(real_part, imag_part, tables):
    cos_small, sin_small, cos_twist, sin_twist, cos_large, sin_large = tables
    span = cos_small.shape[0]
    back_re = jnp.einsum("...kj,pj->...kp", real_part, cos_large, precision=HIGHEST) - jnp.einsum(
        "...kj,pj->...kp", imag_part, sin_large, precision=HIGHEST
    )
    back_im = jnp.einsum("...kj,pj->...kp", imag_part, cos_large, precision=HIGHEST) + jnp.einsum(
        "...kj,pj->...kp", real_part, sin_large, precision=HIGHEST
    )
    turned_re = back_re * cos_twist - back_im * sin_twist
    turned_im = back_im * cos_twist + back_re * sin_twist
    signal = (
        jnp.einsum("...kp,qk->...qp", turned_re, cos_small, precision=HIGHEST)
        - jnp.einsum("...kp,qk->...qp", turned_im, sin_small, precision=HIGHEST)
    ) / (span * 128)
    signal = signal.reshape(signal.shape[:-2] + (span * 128,))
    return signal[..., : span * 64]


def position_features(length):
    places = jnp.arange(length, dtype=jnp.float32)
    angle = places * (2.0 * math.pi / length)
    return jnp.stack(
        [
            places / length,
            jnp.cos(angle),
            jnp.sin(angle),
            jnp.cos(2.0 * angle),
            jnp.sin(2.0 * angle),
        ],
        axis=1,
    )


def decay_factors(channel_ids, length):
    rank = (channel_ids * 5 % D).astype(jnp.float32) / D
    lowest = math.log(0.25 / length)
    highest = math.log(1.0 / 30.0)
    rate = jnp.exp(lowest + rank * (highest - lowest))
    places = jnp.arange(length, dtype=jnp.float32)
    return jnp.exp(-rate[:, None] * places[None, :]) * jnp.sqrt(2.0 * rate)[:, None]


def channel_order(data, nwide, nnarrow, rows_half):
    count = data.shape[0]
    return data.reshape(count, nnarrow, nwide, rows_half).transpose(0, 2, 1, 3).reshape(count, -1)


def row_order(data, nwide, nnarrow):
    total = data.shape[0]
    rows_half = data.shape[1]
    count = total // (nwide * nnarrow)
    return (
        data.reshape(nnarrow, nwide, count, rows_half)
        .transpose(1, 0, 2, 3)
        .reshape(total, rows_half)
        .T
    )


def body(
    hidden_in,
    gainfirst,
    shiftfirst,
    valueright,
    valueleft,
    shaperight,
    shapeleft,
    convtaps,
    posweight,
    posbias,
    sinefreq,
    midweight,
    midbias,
    filterout,
    outright,
    outleft,
    gainsecond,
    shiftsecond,
    gateright,
    gateleft,
    liftright,
    liftleft,
    lowerright,
    lowerleft,
    grad_out,
):
    rowcount = hidden_in.shape[0]
    local_groups = gateright.shape[1] // gateleft.shape[0]
    nwide = lax.axis_size("wide")
    nnarrow = lax.axis_size("narrow")
    narrow_index = lax.axis_index("narrow")
    rows_half = rowcount // nnarrow
    row_start = narrow_index * rows_half
    combined = lax.axis_index("wide") * nnarrow + narrow_index
    resid = lax.dynamic_slice_in_dim(hidden_in, row_start, rows_half, 0).astype(jnp.float32)
    normone, hat_one, inv_one = norm_forward(resid, gainfirst, shiftfirst)
    normone = normone.astype(jnp.bfloat16)
    mid_value = section_one(normone, valueright, BLOCKS, False)
    signal = section_two(mid_value, valueleft).astype(jnp.bfloat16)
    mid_shape = section_one(normone, shaperight, BLOCKS, False)
    shaping = section_two(mid_shape, shapeleft)
    group = nwide // SEQS * nnarrow
    place = combined % group
    before = from_behind(signal[-2:], ("wide", "narrow"), 1)
    before = jnp.where(place == 0, jnp.zeros_like(before), before)
    extended = jnp.concatenate([before, signal], axis=0).astype(jnp.float32)
    shortconv = (
        convtaps[0] * extended[2:] + convtaps[1] * extended[1:-1] + convtaps[2] * extended[:-2]
    ).astype(jnp.bfloat16)
    channels = lax.all_to_all(
        lax.all_to_all(shortconv.T, "wide", split_axis=0, concat_axis=1, tiled=True),
        "narrow",
        split_axis=0,
        concat_axis=1,
        tiled=True,
    )
    channels = channel_order(channels, nwide, nnarrow, rows_half)
    count = channels.shape[0]
    length = channels.shape[1] // SEQS
    feats = position_features(length)
    lin_one = jnp.dot(feats, posweight, precision=HIGHEST) + posbias
    act_one = jnp.sin(sinefreq * lin_one)
    lin_two = jnp.dot(act_one, midweight, precision=HIGHEST) + midbias
    act_two = jnp.sin(sinefreq * lin_two)
    own_cols = lax.dynamic_slice_in_dim(filterout, combined * count, count, 1)
    channel_ids = combined * count + jnp.arange(count, dtype=jnp.int32)
    modulation = decay_factors(channel_ids, length)
    taps = jnp.dot(act_two, own_cols, precision=HIGHEST).T * modulation
    tables = fourier_tables(2 * length)
    sig_re, sig_im = to_spectrum(channels.astype(jnp.float32).reshape(count, SEQS, length), tables)
    fil_re, fil_im = to_spectrum(taps.reshape(count, 1, length), tables)
    conv_chan = from_spectrum(
        sig_re * fil_re - sig_im * fil_im, sig_re * fil_im + sig_im * fil_re, tables
    )
    conv_chan = conv_chan.reshape(count, SEQS * length).astype(jnp.bfloat16)
    longconv = lax.all_to_all(
        lax.all_to_all(conv_chan, "wide", split_axis=1, concat_axis=0, tiled=True),
        "narrow",
        split_axis=1,
        concat_axis=0,
        tiled=True,
    )
    longconv = row_order(longconv, nwide, nnarrow)
    mixed = (shaping * longconv.astype(jnp.float32)).astype(jnp.bfloat16)
    mid_out = section_one(mixed, outright, BLOCKS, False)
    middle = resid + section_two(mid_out, outleft)
    normtwo, hat_two, inv_two = norm_forward(middle, gainsecond, shiftsecond)
    normtwo = normtwo.astype(jnp.bfloat16)
    norm_all = lax.all_gather(normtwo, "narrow", axis=0, tiled=True)
    mid_gate = section_one(norm_all, gateright, local_groups, True)
    pregate = section_two(mid_gate, gateleft)
    mid_lift = section_one(norm_all, liftright, local_groups, True)
    prelift = section_two(mid_lift, liftleft)
    cumulative = 0.5 * (1.0 + lax.erf(pregate * (1.0 / math.sqrt(2.0))))
    activated = pregate * cumulative
    hidden = (activated * prelift).astype(jnp.bfloat16)
    mid_lower = section_one(hidden, lowerright, BLOCKS, False)
    partial_sum = section_two(mid_lower, lowerleft)
    partial_sum = partial_sum + lax.dynamic_update_slice_in_dim(
        jnp.zeros_like(partial_sum), middle, row_start, 0
    )
    hidden_out = lax.psum_scatter(
        partial_sum.astype(jnp.bfloat16), "narrow", scatter_dimension=1, tiled=True
    )
    upstream = lax.all_gather(grad_out, "narrow", axis=1, tiled=True)
    grad_lowerleft, grad_mid_lower = back_two(
        mid_lower, lowerleft, upstream.reshape(rowcount, BLOCKS, -1)
    )
    grad_lowerright, grad_hidden = back_one(hidden, lowerright, grad_mid_lower, False)
    density = jnp.exp(-0.5 * pregate * pregate) * (1.0 / math.sqrt(2.0 * math.pi))
    grad_pregate = (grad_hidden * prelift * (cumulative + pregate * density)).astype(jnp.bfloat16)
    grad_prelift = (grad_hidden * activated).astype(jnp.bfloat16)
    grad_gateleft, grad_mid_gate = back_two(
        mid_gate, gateleft, grad_pregate.reshape(rowcount, local_groups, -1)
    )
    grad_gateright, into_gate = back_one(norm_all, gateright, grad_mid_gate, True)
    grad_liftleft, grad_mid_lift = back_two(
        mid_lift, liftleft, grad_prelift.reshape(rowcount, local_groups, -1)
    )
    grad_liftright, into_lift = back_one(norm_all, liftright, grad_mid_lift, True)
    ffn_local = (
        grad_gateright,
        grad_gateleft,
        grad_liftright,
        grad_liftleft,
        grad_lowerright,
        grad_lowerleft,
    )
    dnormtwo = lax.psum_scatter(
        (into_gate + into_lift).astype(jnp.bfloat16), "narrow", scatter_dimension=0, tiled=True
    ).astype(jnp.float32)
    back_two_norm, grad_gainsecond, grad_shiftsecond = norm_backward(
        dnormtwo, hat_two, inv_two, gainsecond
    )
    up_rows = lax.dynamic_slice_in_dim(upstream, row_start, rows_half, 0)
    dmiddle = up_rows.astype(jnp.float32) + back_two_norm
    dbranch = dmiddle.astype(jnp.bfloat16)
    grad_outleft, grad_mid_out = back_two(mid_out, outleft, dbranch.reshape(rows_half, BLOCKS, -1))
    grad_outright, dmixed = back_one(mixed, outright, grad_mid_out, False)
    dshaping = (dmixed * longconv.astype(jnp.float32)).astype(jnp.bfloat16)
    dlong = (dmixed * shaping).astype(jnp.bfloat16)
    grad_chan = lax.all_to_all(
        lax.all_to_all(dlong.T, "wide", split_axis=0, concat_axis=1, tiled=True),
        "narrow",
        split_axis=0,
        concat_axis=1,
        tiled=True,
    )
    grad_chan = channel_order(grad_chan, nwide, nnarrow, rows_half)
    dlong_re, dlong_im = to_spectrum(
        grad_chan.astype(jnp.float32).reshape(count, SEQS, length), tables
    )
    dshort_chan = from_spectrum(
        dlong_re * fil_re + dlong_im * fil_im, dlong_im * fil_re - dlong_re * fil_im, tables
    )
    dshort_chan = dshort_chan.reshape(count, SEQS * length).astype(jnp.bfloat16)
    filt_re = jnp.sum(dlong_re * sig_re + dlong_im * sig_im, axis=1, keepdims=True)
    filt_im = jnp.sum(dlong_im * sig_re - dlong_re * sig_im, axis=1, keepdims=True)
    grad_taps = from_spectrum(filt_re, filt_im, tables).reshape(count, length)
    dshort = lax.all_to_all(
        lax.all_to_all(dshort_chan, "wide", split_axis=1, concat_axis=0, tiled=True),
        "narrow",
        split_axis=1,
        concat_axis=0,
        tiled=True,
    )
    dshort = row_order(dshort, nwide, nnarrow)
    grad_modded = grad_taps * modulation
    grad_filterout = jnp.dot(act_two.T, grad_modded.T, precision=HIGHEST)
    dact_two = jnp.dot(grad_modded.T, own_cols.T, precision=HIGHEST)
    dlin_two = dact_two * jnp.cos(sinefreq * lin_two)
    scaled_two = dlin_two * sinefreq
    grad_midweight = jnp.dot(act_one.T, scaled_two, precision=HIGHEST)
    grad_midbias = jnp.sum(scaled_two, axis=0)
    dact_one = jnp.dot(scaled_two, midweight.T, precision=HIGHEST)
    dlin_one = dact_one * jnp.cos(sinefreq * lin_one)
    scaled_one = dlin_one * sinefreq
    grad_posweight = jnp.dot(feats.T, scaled_one, precision=HIGHEST)
    grad_posbias = jnp.sum(scaled_one, axis=0)
    grad_sinefreq = jnp.sum(dlin_one * lin_one, axis=0) + jnp.sum(dlin_two * lin_two, axis=0)
    after = from_behind(dshort[:2], ("wide", "narrow"), -1)
    after = jnp.where(place == group - 1, jnp.zeros_like(after), after)
    ext_grad = jnp.concatenate([dshort, after], axis=0).astype(jnp.float32)
    dsignal = (
        convtaps[0] * ext_grad[:-2] + convtaps[1] * ext_grad[1:-1] + convtaps[2] * ext_grad[2:]
    ).astype(jnp.bfloat16)
    short_grad = dshort.astype(jnp.float32)
    grad_convtaps = jnp.stack(
        [
            jnp.sum(extended[2:] * short_grad, axis=0),
            jnp.sum(extended[1:-1] * short_grad, axis=0),
            jnp.sum(extended[:-2] * short_grad, axis=0),
        ]
    )
    grad_valueleft, grad_mid_value = back_two(
        mid_value, valueleft, dsignal.reshape(rows_half, BLOCKS, -1)
    )
    grad_valueright, into_value = back_one(normone, valueright, grad_mid_value, False)
    grad_shapeleft, grad_mid_shape = back_two(
        mid_shape, shapeleft, dshaping.reshape(rows_half, BLOCKS, -1)
    )
    grad_shaperight, into_shape = back_one(normone, shaperight, grad_mid_shape, False)
    back_one_norm, grad_gainfirst, grad_shiftfirst = norm_backward(
        into_value + into_shape, hat_one, inv_one, gainfirst
    )
    full_grad = (dmiddle + back_one_norm).astype(jnp.bfloat16)
    hidden_grad = lax.all_to_all(full_grad, "narrow", split_axis=1, concat_axis=0, tiled=True)
    mixer_grads = lax.psum(
        (
            grad_gainfirst,
            grad_shiftfirst,
            grad_valueright,
            grad_valueleft,
            grad_shaperight,
            grad_shapeleft,
            grad_convtaps,
            grad_posweight,
            grad_posbias,
            grad_sinefreq,
            grad_midweight,
            grad_midbias,
            grad_outright,
            grad_outleft,
            grad_gainsecond,
            grad_shiftsecond,
        ),
        ("wide", "narrow"),
    )
    ffn_grads = lax.psum(
        (ffn_local[0], ffn_local[1], ffn_local[2], ffn_local[3], ffn_local[4], ffn_local[5]), "wide"
    )
    return (
        hidden_out,
        hidden_grad,
        mixer_grads[0],
        mixer_grads[1],
        mixer_grads[2],
        mixer_grads[3],
        mixer_grads[4],
        mixer_grads[5],
        mixer_grads[6],
        mixer_grads[7],
        mixer_grads[8],
        mixer_grads[9],
        mixer_grads[10],
        mixer_grads[11],
        grad_filterout,
        mixer_grads[12],
        mixer_grads[13],
        mixer_grads[14],
        mixer_grads[15],
        ffn_grads[0],
        ffn_grads[1],
        ffn_grads[2],
        ffn_grads[3],
        ffn_grads[4],
        ffn_grads[5],
    )


F32 = jnp.float32
BF16 = jnp.bfloat16
MESH = pl.DeviceIdType.MESH
TILE = 256
PAD = 256


def mm(a, b, precision=None):
    return lax.dot_general(
        a, b, (((1,), (0,)), ((), ())), precision=precision, preferred_element_type=F32
    )


def mm_nt(a, b, precision=None):
    return lax.dot_general(
        a, b, (((1,), (1,)), ((), ())), precision=precision, preferred_element_type=F32
    )


def mm_tn(a, b, precision=None):
    return lax.dot_general(
        a, b, (((0,), (0,)), ((), ())), precision=precision, preferred_element_type=F32
    )


def lanes(width):
    return lax.broadcasted_iota(jnp.int32, (1, width), 1)


def mask(condition, dtype=BF16):
    return jnp.where(condition, 1.0, 0.0).astype(dtype)


def between(width, low, high, dtype=BF16):
    lane = lanes(width)
    return mask((lane >= low) & (lane < high), dtype)


def join(first, second):
    return jnp.concatenate(
        [first[:, :128], first[:, 128:] + second[:, :128], second[:, 128:]], axis=1
    )


def sine_cosine(angle):
    turns = jnp.floor(angle * (1.0 / math.pi) + 0.5)
    rest = angle - turns * 3.140625
    rest = rest - turns * 9.67502593994140625e-4
    rest = rest - turns * 1.509957990978376e-7
    flip = 1.0 - 2.0 * (turns - 2.0 * jnp.floor(turns * 0.5))
    square = rest * rest
    sine = 1.0
    for divisor in (110.0, 72.0, 42.0, 20.0, 6.0):
        sine = 1.0 - square * (1.0 / divisor) * sine
    cosine = 1.0
    for divisor in (132.0, 90.0, 56.0, 30.0, 12.0, 2.0):
        cosine = 1.0 - square * (1.0 / divisor) * cosine
    return (sine * rest * flip, cosine * flip)


def fold(whole, side):
    return [
        whole[192 * b + 96 * side : 192 * b + 96 * side + 48, :] * between(384, 0, 192, F32)
        + whole[192 * b + 96 * side + 48 : 192 * b + 96 * side + 96, :] * between(384, 192, 384, F32)
        for b in range(2)
    ]


STRIDES = (1, 2, 4, 8)
PART = 768
STEP_ROWS = (0, 384, 576, 672, 720)
ORDERS = ((0, 1, 2, 3), (0, 2, 3, 1), (0, 1, 2, 3), (0, 1, 2, 3), (0, 1, 2, 3))
CHUNK = 48
LOWER_RIGHT, LOWER_LEFT, GATE_RIGHT, LIFT_RIGHT, GATE_LEFT, LIFT_LEFT, CHANNEL_ROWS = (
    0,
    768,
    960,
    1152,
    1344,
    2112,
    4 * PART,
)
OUT_LEFT, SHAPE_RIGHT, SHAPE_LEFT = (0, 384, 576)
VALUE_RIGHT, VALUE_LEFT, FILTER_OUT, VECTORS, FILTER, OUT_RIGHT = (0, 192, 384, 512, 528, 576)


def tile_rows(index, size=TILE):
    return pl.ds(pl.multiple_of(index * size, size), size)


def whole_kernel(
    hidden_in,
    upstream,
    hbm_cos,
    hbm_sin,
    place,
    place_parts,
    gainfirst,
    shiftfirst,
    gainsecond,
    shiftsecond,
    convtaps,
    posweight,
    posbias,
    midbias,
    sinefreq,
    midweight,
    filterout,
    valueright,
    valueleft,
    shaperight,
    shapeleft,
    outright,
    outleft,
    gateright,
    gateleft,
    liftright,
    liftleft,
    lowerright,
    lowerleft,
    hidden_out,
    hidden_grad,
    sums_channel,
    sums_mixer,
    inputs,
    table_cos,
    table_sin,
    vectors,
    filter_vectors,
    w_first,
    w_value,
    w_shape,
    w_out_first,
    w_out_second,
    w_glu,
    w_gate,
    w_lift,
    w_lower,
    w_lower_second,
    up_halves,
    stats,
    norm_one,
    inner_one,
    sig_halves,
    sig_rows,
    shaping,
    sig_pad,
    short,
    act_one,
    cos_one,
    lin_one,
    act_two,
    cos_two,
    lin_two,
    fil_spec,
    sig_spec,
    prod_spec,
    long_rows,
    long_halves,
    inner_out,
    hat_two,
    norm_two,
    inner_glu,
    factor_gate,
    factor_lift,
    hid,
    inner_lower,
    out_own,
    part_send,
    part_recv,
    d_inner_lower,
    d_gate,
    d_lift,
    d_inner_glu,
    dn_own,
    dn_send,
    dn_recv,
    d_inner_out,
    d_shaping,
    dl_rows,
    ds_pad,
    ds_halves,
    d_inner_one,
    cross_send,
    mid_send,
    mid_recv,
    d_middle,
    branch,
    shape_send,
    shape_recv,
    value_send,
    value_recv,
    w_cross,
    through,
    d_lin,
    own_out,
    grad_vectors,
    grad_filter,
    gain_sums,
    send_sem,
    recv_sem,
    load_sem,
    got,
    sum_send,
    sum_recv,
    sum_free,
    late,
    late_core,
    late_slots,
    late_send,
    late_recv,
):
    rows = inputs.shape[0]
    tiles = rows // TILE
    length = 2 * rows
    spans = length // TILE
    wide = lax.axis_index("wide")
    narrow = lax.axis_index("narrow")
    bits = [lax.rem(wide // stride, 2) for stride in STRIDES]
    core = bits[0]
    sibling = (wide + 1 - 2 * core, narrow)
    partner = (wide, 1 - narrow)
    quarter = 2 * narrow + core
    own_half = pl.ds(pl.multiple_of(narrow * 384, 384), 384)
    other_half = pl.ds(pl.multiple_of((1 - narrow) * 384, 384), 384)

    loads = {}

    def load(name, source, target):
        loads[name] = pltpu.make_async_copy(source, target, load_sem.at[len(loads)])
        loads[name].start()

    load("inputs", hidden_in, inputs)
    load("valueright", valueright, hid.at[0, pl.ds(0, 192)])
    load("shaperight", shaperight, hid.at[0, pl.ds(192, 192)])
    load("valueleft", valueleft, hid.at[1, pl.ds(0, 192)])
    load("shapeleft", shapeleft, hid.at[1, pl.ds(192, 192)])
    load("filterout", filterout, factor_gate.at[0, pl.ds(0, 128)])
    load("cos", hbm_cos, table_cos)
    load("sin", hbm_sin, table_sin)
    load("outright", outright, d_gate.at[0, pl.ds(0, 192)])
    load("outleft", outleft, d_gate.at[0, pl.ds(192, 192)])
    load("gateright", gateright, d_lift.at[1, pl.ds(96, 192), pl.ds(0, 384)])
    load("liftright", liftright, d_lift.at[1, pl.ds(96, 192), pl.ds(384, 384)])
    load("lowerleft", lowerleft, d_lift.at[1, pl.ds(0, 96)])
    load("lower_top", lowerright.at[pl.ds(0, 512)], d_lift.at[0, :, pl.ds(0, 384)])
    load("lower_end", lowerright.at[pl.ds(512, 256)], d_lift.at[0, pl.ds(0, 256), pl.ds(384, 384)])
    for k in range(2):
        at = pl.ds(64 * k, 192)
        load(("gate", k), gateleft.at[:, pl.ds(D * k, D)], w_gate.at[k, at])
        load(("lift", k), liftleft.at[:, pl.ds(D * k, D)], w_lift.at[k, at])
    load("upstream", upstream, up_halves.at[narrow])

    barrier = pltpu.get_barrier_semaphore()
    others = [(wide + stride * (1 - 2 * bit), narrow) for stride, bit in zip(STRIDES, bits)]
    chip = wide // 2
    fellows = [(2 * lax.rem(chip + t, 8) + core, narrow) for t in range(8)]
    for device in [sibling, partner] + fellows[1:]:
        pl.semaphore_signal(barrier, inc=1, device_id=device, device_id_type=MESH)

    for i, source in enumerate((gainfirst, shiftfirst, gainsecond, shiftsecond)):
        vectors[i : i + 1, :] = source[...].reshape(1, D)
    vectors[4:7, :] = convtaps[...]
    vectors[7:8, :] = jnp.zeros((1, D), F32)
    filter_vectors[...] = jnp.zeros(filter_vectors.shape, F32)
    filter_vectors[0:5, :] = posweight[...]
    for i, source in enumerate((posbias, midbias, sinefreq)):
        filter_vectors[8 + i : 9 + i, :] = source[...].reshape(1, 128)

    pl.semaphore_wait(barrier, 9)

    def send(source, target, device, index):
        return pltpu.make_async_remote_copy(
            src_ref=source,
            dst_ref=target,
            send_sem=send_sem.at[index],
            recv_sem=recv_sem.at[index],
            device_id=device,
            device_id_type=MESH,
        )

    mixer_slab = sums_mixer.at[narrow]
    parts_of = [sums_channel.at[pl.ds(PART * i, PART)] for i in range(4)] + [mixer_slab.at[pl.ds(0, PART)]]
    offsets = []
    for order in ORDERS:
        found = [0]
        for step in range(4):
            found.append(pl.multiple_of(found[step] + bits[order[step]] * (PART >> (step + 1)), 16))
        offsets.append(found)

    def sum_copy(source, target, i, step, back):
        index = 8 * i + 4 * back + step
        return pltpu.make_async_remote_copy(
            src_ref=source,
            dst_ref=target,
            send_sem=sum_send.at[index],
            recv_sem=sum_recv.at[index],
            device_id=others[ORDERS[i][step]],
            device_id_type=MESH,
        )

    def scatter(i, step):
        size = PART >> (step + 1)
        away = pl.multiple_of(offsets[i][step] + (1 - bits[ORDERS[i][step]]) * size, 16)
        return sum_copy(
            parts_of[i].at[pl.ds(away, size)], got.at[i, pl.ds(STEP_ROWS[step], size)], i, step, 0
        )

    def gather(i, step):
        at = pl.ds(offsets[i][step + 1], PART >> (step + 1))
        return sum_copy(parts_of[i].at[at], parts_of[i].at[at], i, step, 1)

    def hand_back(i, step):
        pl.semaphore_wait(sum_free.at[4 * i + step], 1)
        gather(i, step).start()

    def advance(i, step):
        scatter(i, step).wait()

        @pl.loop(0, (PART >> (step + 1)) // CHUNK)
        def _(index):
            own = pl.ds(pl.multiple_of(offsets[i][step + 1] + index * CHUNK, 16), CHUNK)
            came = got[i, pl.ds(pl.multiple_of(STEP_ROWS[step] + index * CHUNK, 16), CHUNK), :]
            parts_of[i][own, :] = (parts_of[i][own, :].astype(F32) + came.astype(F32)).astype(BF16)

        pl.semaphore_signal(
            sum_free.at[4 * i + step],
            inc=1,
            device_id=others[ORDERS[i][step]],
            device_id_type=MESH,
        )
        if step < 3:
            scatter(i, step + 1).start()
        else:
            hand_back(i, 3)

    def retreat(i, step):
        gather(i, step).wait()
        if step > 0:
            hand_back(i, step - 1)

    def late_copy(source, target, device, index):
        return pltpu.make_async_remote_copy(
            src_ref=source,
            dst_ref=target,
            send_sem=late_send.at[index],
            recv_sem=late_recv.at[index],
            device_id=device,
            device_id_type=MESH,
        )

    up_copy = send(upstream, up_halves.at[narrow], partner, 0)
    up_copy.start()

    row = lax.broadcasted_iota(jnp.int32, (D, 384), 0)
    lane = lax.broadcasted_iota(jnp.int32, (D, 384), 1)
    step = jnp.where(lane >= 96, 96, 0) + jnp.where(lane >= 192, 96, 0) + jnp.where(lane >= 288, 96, 0)
    select = mask(row == lane + step + narrow * 96)
    for name in ("valueright", "shaperight", "valueleft", "shapeleft"):
        loads[name].wait()
    right_half = mm(hid[0, 0:192, :], select).astype(BF16)
    shape_half = mm(hid[0, 192:384, :], select).astype(BF16)
    for b in range(4):
        kept = between(384, 96 * b, 96 * b + 96)
        w_first[192 * b : 192 * b + 192, 0:384] = right_half * kept
        w_first[192 * b : 192 * b + 192, 384:768] = shape_half * kept
    row = lax.broadcasted_iota(jnp.int32, (D, 2 * PAD), 0)
    lane = lax.broadcasted_iota(jnp.int32, (D, 2 * PAD), 1)
    group = jnp.where(lane >= PAD, 1, 0)
    entry = lane - PAD * group
    spread = mask((row == (2 * narrow + group) * 192 + entry) & (entry < 192))
    for source, target in ((0, w_value), (192, w_shape)):
        wider = mm(hid[1, source : source + 192, :], spread).astype(BF16)
        for b in range(4):
            for k in range(2):
                target[96 * b + 48 * k : 96 * b + 48 * k + 48, :] = wider[
                    48 * b : 48 * b + 48, :
                ] * between(2 * PAD, PAD * k, PAD * k + PAD)
    row = lax.broadcasted_iota(jnp.int32, (D, 192), 0)
    lane = lax.broadcasted_iota(jnp.int32, (D, 192), 1)
    start = (2 * narrow) * 192 + (1 - narrow) * 96
    cross = mask(row == start + lane + jnp.where(lane >= 96, 96, 0))
    for i in range(2):
        part = mm(hid[0, 192 * i : 192 * i + 192, :], cross).astype(BF16)
        for b in range(2):
            w_cross[i, 192 * b : 192 * b + 192, :] = part * between(192, 96 * b, 96 * b + 96)
    first = vectors[0:1, :]
    shift_first = vectors[1:2, :]

    coarse = vectors[...].astype(BF16)
    fine = (vectors[...] - coarse.astype(F32)).astype(BF16)
    through[...] = mm(coarse, w_first[...]) + mm(fine, w_first[...])
    loads["inputs"].wait()

    @pl.loop(0, tiles)
    def _(index):
        at = tile_rows(index)
        values = inputs[at, :].astype(F32)
        average = jnp.mean(values, axis=-1, keepdims=True)
        center = values - average
        inverse = lax.rsqrt(jnp.mean(center * center, axis=-1, keepdims=True) + EPSILON)
        hat = center * inverse
        stats[at, 0:1] = average
        stats[at, 1:2] = inverse
        normed = (hat * first + shift_first).astype(BF16)
        norm_one[at, :] = normed
        inner = mm(normed, w_first[...]).astype(BF16)
        inner_one[at, :] = inner
        signal = mm(inner[:, :384], w_value[...]).astype(BF16)
        sig_halves[0, at, :] = signal[:, :PAD]
        sig_halves[1, at, :] = signal[:, PAD:]
        shaped = mm(inner[:, 384:], w_shape[...])
        shaping[0, at, :] = shaped[:, :PAD]
        shaping[1, at, :] = shaped[:, PAD:]

    sig_copy = send(sig_halves.at[1 - core], sig_rows.at[core], sibling, 1)
    sig_copy.start()
    sig_rows[core] = sig_halves[core]

    row = lax.broadcasted_iota(jnp.int32, (D, PAD), 0)
    lane = lax.broadcasted_iota(jnp.int32, (D, PAD), 1)
    pick = mask((row == quarter * 192 + lane) & (lane < 192))
    conv = mm(coarse, pick) + mm(fine, pick)
    loads["filterout"].wait()
    own_out[...] = mm(factor_gate[0, 0:128, :].astype(BF16), pick).astype(BF16)
    pos_bias = filter_vectors[8:9, :]
    mid_bias = filter_vectors[9:10, :]
    frequency = filter_vectors[10:11, :]
    mid_high = midweight[...].astype(BF16)
    mid_low = (midweight[...] - mid_high.astype(F32)).astype(BF16)
    pos_high = filter_vectors[0:8, :].astype(BF16).astype(F32)
    pos_parts = jnp.concatenate(
        [pos_high, pos_high, filter_vectors[0:8, :] - pos_high, jnp.zeros((8, 128), F32)], axis=0
    ).astype(BF16)
    ranks = 5 * (quarter * 192 + lanes(PAD))
    for bound in range(5):
        ranks = jnp.where(ranks >= D, ranks - D, ranks)
    lowest = math.log(0.25 / length)
    highest = math.log(1.0 / 30.0)
    rate = jnp.exp(lowest + ranks.astype(F32) * (1.0 / D) * (highest - lowest))
    loud = jnp.sqrt(2.0 * rate)

    def decay(index):
        places = (lax.broadcasted_iota(jnp.int32, (TILE, PAD), 0) + index * TILE).astype(F32)
        return jnp.exp(-rate * places) * loud

    @pl.loop(0, spans)
    def _(index):
        at = tile_rows(index)
        one = mm(place_parts[at, :], pos_parts) + pos_bias
        sine, cosine = sine_cosine(frequency * one)
        high = sine.astype(BF16)
        low = (sine - high.astype(F32)).astype(BF16)
        lin_one[at, :] = one.astype(BF16)
        act_one[at, :] = high
        cos_one[at, :] = cosine.astype(BF16)
        two = mm(high, mid_high) + mm(low, mid_high) + mm(high, mid_low) + mid_bias
        sine, cosine = sine_cosine(frequency * two)
        high = sine.astype(BF16)
        lin_two[at, :] = two.astype(BF16)
        act_two[at, :] = high
        cos_two[at, :] = cosine.astype(BF16)
        short[at, :] = (mm(high, own_out[...]) * decay(index)).astype(BF16)

    loads["cos"].wait()
    loads["sin"].wait()

    @pl.loop(0, spans)
    def _(index):
        at = tile_rows(index)
        real = mm(table_cos[at, :], short[...])
        imag = mm(table_sin[at, :], short[...])
        turn_cos = place[at, 5:6] * (1.0 / length)
        turn_sin = place[at, 6:7] * (1.0 / length)
        fil_spec[0, at, :] = real * turn_cos + imag * turn_sin
        fil_spec[1, at, :] = imag * turn_cos - real * turn_sin

    for name in ("outright", "outleft", "gateright", "liftright", "lowerleft", "lower_top", "lower_end"):
        loads[name].wait()
    out_half = d_gate[0, 0:192, own_half]
    w_out_first[0:192, :] = out_half * between(384, 0, 192)
    w_out_first[192:256, :] = jnp.zeros((64, 384), BF16)
    w_out_first[256:448, :] = out_half * between(384, 192, 384)
    w_out_first[448:512, :] = jnp.zeros((64, 384), BF16)
    for b in range(4):
        for k in range(4):
            w_out_second[b // 2, 192 * (b % 2) + 48 * k : 192 * (b % 2) + 48 * k + 48, :] = d_gate[
                0, 192 + 48 * b : 240 + 48 * b, :
            ] * between(D, 192 * k, 192 * k + 192)
    lane = lanes(384)
    inside = lane - jnp.where(lane >= 192, 192, 0)
    for b in range(4):
        kept = mask((inside >= 48 * b) & (inside < 48 * b + 48))
        w_glu[192 * b : 192 * b + 192, 0:384] = d_lift[1, 96:288, 0:384] * kept
        w_glu[192 * b : 192 * b + 192, 384:768] = d_lift[1, 96:288, 384:768] * kept
    for target in (w_gate, w_lift):
        target[0, 192:256, :] = jnp.zeros((64, D), BF16)
        target[1, 0:64, :] = jnp.zeros((64, D), BF16)
    w_lower[0, 0:512, :] = d_lift[0, :, 0:256] * between(256, 0, 192)
    w_lower[0, 512:768, :] = d_lift[0, 0:256, 384:640] * between(256, 0, 192)
    w_lower[1, 0:512, :] = d_lift[0, :, 128:384] * between(256, 64, 256)
    w_lower[1, 512:768, :] = d_lift[0, 0:256, 512:768] * between(256, 64, 256)
    for b in range(2):
        for k in range(4):
            w_lower_second[192 * b + 48 * k : 192 * b + 48 * k + 48, :] = d_lift[
                1, 48 * b : 48 * b + 48, :
            ] * between(D, 192 * k, 192 * k + 192)

    sig_copy.wait_recv()
    sig_pad[0:8, :] = jnp.zeros((8, PAD), F32)
    for part in range(2):
        sig_pad[8 + part * rows : 8 + part * rows + rows, :] = sig_rows[part].astype(F32)
    for index in range(spans):
        start = 8 + index * TILE
        total = conv[4:5, :] * sig_pad[start : start + TILE, :]
        total += conv[5:6, :] * sig_pad[start - 1 : start - 1 + TILE, :]
        total += conv[6:7, :] * sig_pad[start - 2 : start - 2 + TILE, :]
        short[index * TILE : index * TILE + TILE, :] = total.astype(BF16)

    @pl.loop(0, spans)
    def _(index):
        at = tile_rows(index)
        real = mm(table_cos[at, :], short[...])
        imag = mm(table_sin[at, :], short[...])
        sig_spec[0, at, :] = real.astype(BF16)
        sig_spec[1, at, :] = imag.astype(BF16)
        fil_re = fil_spec[0, at, :]
        fil_im = fil_spec[1, at, :]
        prod_spec[0, at, :] = (real * fil_re - imag * fil_im).astype(BF16)
        prod_spec[1, at, :] = (real * fil_im + imag * fil_re).astype(BF16)

    per_half = rows // TILE

    @pl.loop(0, spans)
    def _(index):
        at = tile_rows(index)
        result = mm(table_cos[at, :], prod_spec[0]) + mm(table_sin[at, :], prod_spec[1])
        long_rows[index // per_half, tile_rows(lax.rem(index, per_half)), :] = result.astype(BF16)

    long_copy = send(long_rows.at[1 - core], long_halves.at[core], sibling, 2)
    long_copy.start()
    long_halves[core] = long_rows[core]
    long_copy.wait_recv()
    sig_copy.wait_send()
    long_copy.wait_send()

    def inner_copy(index):
        at = tile_rows(index)
        return send(inner_out.at[narrow, at], inner_out.at[narrow, at], partner, 3 + index)

    dn_copy = send(dn_send, dn_recv, partner, 5)
    own_rows = tile_rows(narrow)
    cross_copy = send(cross_send, d_inner_out.at[own_rows], partner, 6)
    middle_copy = send(mid_send, mid_recv, partner, 11)

    def part_copy(index):
        at = tile_rows(index)
        return send(part_send.at[at], part_recv.at[at], partner, 7 + index)

    def shape_copy(index):
        at = tile_rows(index)
        return send(shape_send.at[at], shape_recv.at[at], partner, 12 + index)

    def value_copy(index):
        at = tile_rows(index)
        return send(value_send.at[at], value_recv.at[at], partner, 14 + index)

    def first_other(index):
        return 1 - narrow + index * (2 * narrow - 1)

    @pl.loop(0, tiles)
    def _(order):
        index = narrow + order * (1 - 2 * narrow)
        at = tile_rows(index)
        inner = None
        for k in range(2):
            product = (shaping[k, at, :] * long_halves[k, at, :].astype(F32)).astype(BF16)
            term = mm(product, w_out_first[k * PAD : k * PAD + PAD, :])
            inner = term if inner is None else inner + term
        inner_out[narrow, at, :] = inner.astype(BF16)
        inner_copy(index).start()

    up_copy.wait_recv()
    for k in range(2):
        loads["gate", k].wait()
        loads["lift", k].wait()
    loads["upstream"].wait()

    gain_second = vectors[2:3, :]
    shift_second = vectors[3:4, :]

    @pl.loop(0, tiles)
    def _(order):
        index = first_other(order)
        at = tile_rows(index)
        inner_copy(index).wait_recv()
        mid = inputs[at, :].astype(F32)
        mid += mm(inner_out[0, at, :], w_out_second[0])
        mid += mm(inner_out[1, at, :], w_out_second[1])
        dn_own[...] = mid
        center = mid - jnp.mean(mid, axis=-1, keepdims=True)
        inverse = lax.rsqrt(jnp.mean(center * center, axis=-1, keepdims=True) + EPSILON)
        hat = center * inverse
        hat_two[...] = hat
        stats[0:TILE, 2:3] = inverse
        normed = (hat * gain_second + shift_second).astype(BF16)
        norm_two[at, :] = normed
        inner = mm(normed, w_glu[...]).astype(BF16)
        inner_glu[at, :] = inner
        lower = [None, None]
        for k in range(2):
            for columns in (slice(0, 256), slice(256, 512), slice(512, 768)):
                gate = mm(inner[:, 128 * k : 128 * k + 256], w_gate[k, :, columns])
                lift = mm(inner[:, 384 + 128 * k : 384 + 128 * k + 256], w_lift[k, :, columns])
                cumulative = 0.5 * (1.0 + lax.erf(gate * (1.0 / math.sqrt(2.0))))
                density = jnp.exp(-0.5 * gate * gate) * (1.0 / math.sqrt(2.0 * math.pi))
                activated = gate * cumulative
                unit = (activated * lift).astype(BF16)
                hid[k, at, columns] = unit
                factor_lift[k, :, columns] = activated
                factor_gate[k, :, columns] = lift * (cumulative + gate * density)
                term = mm(unit, w_lower[k, columns, :])
                lower[k] = term if lower[k] is None else lower[k] + term
        inner_low = join(*lower).astype(BF16)
        inner_lower[at, :] = inner_low
        out_own[at, :] = dn_own[:, own_half] + mm(inner_low, w_lower_second[:, own_half])
        part_send[at, :] = mm(inner_low, w_lower_second[:, other_half]).astype(BF16)

        above = jnp.concatenate([up_halves[0, at, :], up_halves[1, at, :]], axis=1)
        d_low = mm_nt(above, w_lower_second[...]).astype(BF16)
        d_inner_lower[at, :] = d_low
        gates = [None, None]
        lifts = [None, None]
        for k in range(2):
            for columns in (slice(0, 256), slice(256, 512), slice(512, 768)):
                d_hidden = mm_nt(d_low[:, 128 * k : 128 * k + 256], w_lower[k, columns, :])
                to_gate = (d_hidden * factor_gate[k, :, columns]).astype(BF16)
                to_lift = (d_hidden * factor_lift[k, :, columns]).astype(BF16)
                d_gate[k, at, columns] = to_gate
                d_lift[k, at, columns] = to_lift
                term = mm_nt(to_gate, w_gate[k, :, columns])
                gates[k] = term if gates[k] is None else gates[k] + term
                term = mm_nt(to_lift, w_lift[k, :, columns])
                lifts[k] = term if lifts[k] is None else lifts[k] + term
        d_glu = jnp.concatenate([join(*gates), join(*lifts)], axis=1).astype(BF16)
        d_inner_glu[at, :] = d_glu
        into = mm_nt(d_glu, w_glu[...])
        dn_own[...] = into

        @pl.when(order == 0)
        def _():
            dn_send[...] = dn_own[...].astype(BF16)
            dn_copy.start()

    @pl.loop(0, tiles)
    def _(index):
        part_copy(index).start()

    for side in range(2):
        columns = slice(384 * side, 384 * side + 384)
        folded = fold(mm_tn(inner_lower[...], up_halves[side]), side)
        for b in range(2):
            first_row = LOWER_LEFT + 96 * side + 48 * b
            sums_channel[first_row : first_row + 48, :] = folded[b].astype(BF16)
    low_lanes = lanes(128) < 64
    for columns in (slice(0, 384), slice(384, 768)):
        columns_at = slice(LOWER_RIGHT + columns.start, LOWER_RIGHT + columns.stop)
        parts = [
            mm_tn(hid[k, :, columns], d_inner_lower[:, 128 * k : 128 * k + 256]) for k in range(2)
        ]
        sums_channel[columns_at, 0:128] = parts[0][:, 0:128].astype(BF16)
        sums_channel[columns_at, 128:256] = jnp.where(
            low_lanes, parts[0][:, 128:256], parts[1][:, 0:128]
        ).astype(BF16)
        sums_channel[columns_at, 256:384] = parts[1][:, 128:256].astype(BF16)
    for offset, upper, target in ((0, d_gate, GATE_LEFT), (384, d_lift, LIFT_LEFT)):
        for k in range(2):
            for start in (0, 384):
                whole = mm_tn(
                    inner_glu[:, offset + 128 * k : offset + 128 * k + 256],
                    upper[k, :, start : start + 384],
                )
                first_row = target + 384 * k + start // 2
                sums_channel[first_row : first_row + 192, :] = whole[
                    64 * k : 64 * k + 192, :
                ].astype(BF16)
    for offset, target in ((0, GATE_RIGHT), (384, LIFT_RIGHT)):
        whole = mm_tn(norm_two[...], d_inner_glu[:, offset : offset + 384])
        total = None
        for b in range(4):
            term = whole[192 * b : 192 * b + 192, :] * mask(
                (inside >= 48 * b) & (inside < 48 * b + 48), F32
            )
            total = term if total is None else total + term
        sums_channel[target : target + 192, :] = total.astype(BF16)

    sums_channel[2880:3072, :] = jnp.zeros((192, 384), BF16)
    for i in range(4):
        scatter(i, 0).start()

    dn_copy.wait_recv()
    into = dn_own[...] + dn_recv[...].astype(F32)
    hat = hat_two[...]
    gain_sums[0:1, :] = jnp.sum(into * hat, axis=0, keepdims=True)
    gain_sums[1:2, :] = jnp.sum(into, axis=0, keepdims=True)
    scaled = into * gain_second
    above = jnp.concatenate([up_halves[0, own_rows, :], up_halves[1, own_rows, :]], axis=1)
    d_mid = above.astype(F32) + stats[0:TILE, 2:3] * (
        scaled
        - jnp.mean(scaled, axis=-1, keepdims=True)
        - hat * jnp.mean(scaled * hat, axis=-1, keepdims=True)
    )
    hat_two[...] = d_mid
    branch[...] = d_mid.astype(BF16)
    cross_send[...] = mm_nt(branch[...], w_out_second[1 - narrow]).astype(BF16)
    cross_copy.start()
    mid_send[...] = hat_two[:, other_half].astype(BF16)
    middle_copy.start()
    d_inner_out[own_rows, :] = mm_nt(branch[...], w_out_second[narrow]).astype(BF16)
    for i in range(4):
        advance(i, 0)

    @pl.loop(0, tiles)
    def _(order):
        index = narrow + order * (1 - 2 * narrow)
        at = tile_rows(index)

        @pl.when(order == 1)
        def _():
            cross_copy.wait_recv()

        d_inner = d_inner_out[at, :]
        for k in range(2):
            d_mixed = mm_nt(d_inner, w_out_first[k * PAD : k * PAD + PAD, :])
            d_shaping[k, at, :] = (d_mixed * long_halves[k, at, :].astype(F32)).astype(BF16)
            sig_halves[k, at, :] = (d_mixed * shaping[k, at, :]).astype(BF16)

    dl_copy = send(sig_halves.at[1 - core], dl_rows.at[core], sibling, 9)
    dl_copy.start()
    dl_rows[core] = sig_halves[core]

    @pl.loop(0, tiles)
    def _(index):
        at = tile_rows(index)
        to_shape = jnp.concatenate([d_shaping[0, at, :], d_shaping[1, at, :]], axis=1)
        d_inner_one[at, 384:768] = mm_nt(to_shape, w_shape[...]).astype(BF16)
        shape_send[at, :] = mm_nt(
            to_shape, w_shape[pl.ds(pl.multiple_of((1 - narrow) * 192, 192), 192), :]
        ).astype(BF16)
        shape_copy(index).start()

    for h in range(2):
        for side in range(2):
            columns = slice(384 * side, 384 * side + 384)
            folded = fold(mm_tn(inner_out[h, own_rows, :], branch[:, columns]), side)
            for b in range(2):
                first_row = OUT_LEFT + 192 * h + 96 * side + 48 * b
                mixer_slab[first_row : first_row + 48, :] = folded[b].astype(BF16)
    lane = lax.broadcasted_iota(jnp.int32, (2 * PAD, 384), 1)
    row = lax.broadcasted_iota(jnp.int32, (2 * PAD, 384), 0)
    squeeze = mask(row == lane + jnp.where(lane >= 192, 64, 0))

    def first_gradient(offset):
        whole = mm_tn(norm_one[...], d_inner_one[:, offset : offset + 384])
        total = None
        for b in range(4):
            term = whole[192 * b : 192 * b + 192, :] * between(384, 96 * b, 96 * b + 96, F32)
            total = term if total is None else total + term
        return total.astype(BF16)

    def second_gradient(offset, upper):
        above = jnp.concatenate([upper[0], upper[1]], axis=1)
        whole = mm_tn(inner_one[:, offset : offset + 384], above)
        pieces = []
        for b in range(4):
            total = None
            for k in range(2):
                term = whole[96 * b + 48 * k : 96 * b + 48 * k + 48, :] * between(
                    2 * PAD, PAD * k, PAD * k + PAD, F32
                )
                total = term if total is None else total + term
            pieces.append(total)
        return mm(jnp.concatenate(pieces, axis=0).astype(BF16), squeeze).astype(BF16)

    mixer_slab[SHAPE_RIGHT : SHAPE_RIGHT + 192, :] = first_gradient(384)
    mixer_slab[SHAPE_LEFT : SHAPE_LEFT + 192, :] = second_gradient(384, d_shaping)
    scatter(4, 0).start()
    parts = []
    for k in range(2):
        product = (shaping[k] * long_halves[k].astype(F32)).astype(BF16)
        parts.append(mm_tn(product, d_inner_out[...]))
    late[OUT_RIGHT : OUT_RIGHT + 192, :] = jnp.where(
        lanes(384) < 192, parts[0][0:192, :], parts[1][0:192, :]
    ).astype(BF16)

    dl_copy.wait_recv()

    @pl.loop(0, spans)
    def _(index):
        at = tile_rows(index)
        upper = dl_rows[...].reshape(length, PAD)
        real = mm(table_cos[at, :], upper)
        imag = mm(table_sin[at, :], upper)
        fil_re = fil_spec[0, at, :]
        fil_im = fil_spec[1, at, :]
        prod_spec[0, at, :] = (real * fil_re + imag * fil_im).astype(BF16)
        prod_spec[1, at, :] = (imag * fil_re - real * fil_im).astype(BF16)
        sig_re = sig_spec[0, at, :].astype(F32)
        sig_im = sig_spec[1, at, :].astype(F32)
        turn_cos = place[at, 5:6] * (1.0 / length)
        turn_sin = place[at, 6:7] * (1.0 / length)
        both_re = real * sig_re + imag * sig_im
        both_im = imag * sig_re - real * sig_im
        sig_spec[0, at, :] = (both_re * turn_cos - both_im * turn_sin).astype(BF16)
        sig_spec[1, at, :] = (both_im * turn_cos + both_re * turn_sin).astype(BF16)

    ds_pad[length : length + 8, :] = jnp.zeros((8, PAD), F32)

    @pl.loop(0, spans)
    def _(index):
        at = tile_rows(index)
        result = mm(table_cos[at, :], prod_spec[0]) + mm(table_sin[at, :], prod_spec[1])
        ds_pad[at, :] = result.astype(BF16).astype(F32)

    for index in range(spans):
        start = index * TILE
        total = conv[4:5, :] * ds_pad[start : start + TILE, :]
        total += conv[5:6, :] * ds_pad[start + 1 : start + 1 + TILE, :]
        total += conv[6:7, :] * ds_pad[start + 2 : start + 2 + TILE, :]
        part, inner_start = divmod(start, rows)
        long_rows[part, inner_start : inner_start + TILE, :] = total.astype(BF16)
    ds_copy = send(long_rows.at[1 - core], ds_halves.at[core], sibling, 10)
    ds_copy.start()
    ds_halves[core] = long_rows[core]

    advance(4, 0)
    advance(1, 1)
    advance(0, 1)
    grad_vectors[...] = jnp.zeros(grad_vectors.shape, F32)
    sums = [jnp.zeros((1, PAD), F32) for _ in range(3)]
    for index in range(spans):
        start = index * TILE
        upper = ds_pad[start : start + TILE, :]
        for j in range(3):
            sums[j] += jnp.sum(
                upper * sig_pad[8 + start - j : 8 + start - j + TILE, :], axis=0, keepdims=True
            )
    sums = jnp.concatenate(sums + [jnp.zeros((5, PAD), F32)], axis=0)
    lane = lax.broadcasted_iota(jnp.int32, (PAD, 384), 1)
    row = lax.broadcasted_iota(jnp.int32, (PAD, 384), 0)
    place_core = mask((lane == core * 192 + row) & (row < 192))
    conv_sums = mm(sums.astype(BF16), place_core)
    grad_vectors[4:7, :] = conv_sums[0:3, :]

    d_lin[...] = jnp.zeros(d_lin.shape, F32)
    grad_filter[...] = jnp.zeros(grad_filter.shape, F32)

    @pl.loop(0, spans)
    def _(index):
        at = tile_rows(index)
        d_taps = mm(table_cos[at, :], sig_spec[0]) + mm(table_sin[at, :], sig_spec[1])
        d_mod = d_taps * decay(index)
        d_mod = d_mod.astype(BF16)
        d_lin[...] += mm_tn(act_two[at, :], d_mod)
        two = mm_nt(d_mod, own_out[...]) * cos_two[at, :].astype(F32)
        scaled_two = two * frequency
        coarse_two = scaled_two.astype(BF16)
        grad_filter[0:128, :] += mm_tn(act_one[at, :], coarse_two)
        one = mm_nt(coarse_two, mid_high) * cos_one[at, :].astype(F32)
        scaled_one = one * frequency
        grad_filter[128:136, :] += mm_tn(place_parts[at, :], scaled_one.astype(BF16))[0:8, :]
        grad_filter[136:137, :] += jnp.sum(scaled_one, axis=0, keepdims=True)
        grad_filter[137:138, :] += jnp.sum(scaled_two, axis=0, keepdims=True)
        grad_filter[138:139, :] += jnp.sum(
            one * lin_one[at, :].astype(F32) + two * lin_two[at, :].astype(F32), axis=0, keepdims=True
        )

    late[FILTER_OUT : FILTER_OUT + 128, :] = mm(d_lin[...].astype(BF16), place_core).astype(BF16)
    for i in range(3):
        late[FILTER : FILTER + 48, 128 * i : 128 * i + 128] = grad_filter[
            48 * i : 48 * i + 48, :
        ].astype(BF16)

    advance(2, 1)
    advance(1, 2)

    ds_copy.wait_recv()
    other_blocks = pl.ds(pl.multiple_of((1 - narrow) * 192, 192), 192)

    @pl.loop(0, tiles)
    def _(index):
        at = tile_rows(index)
        to_value = jnp.concatenate([ds_halves[0, at, :], ds_halves[1, at, :]], axis=1)
        d_inner = mm_nt(to_value, w_value[...]).astype(BF16)
        d_inner_one[at, 0:384] = d_inner
        against = inner_one[at, :].astype(F32) - through[1:2, :]
        d_inner = d_inner_one[at, :].astype(F32)
        plain = jnp.sum(d_inner * through[0:1, :], axis=-1, keepdims=True)
        along = jnp.sum(d_inner * against, axis=-1, keepdims=True)
        stats[at, 2:3] = plain
        stats[at, 3:4] = along
        lane = lanes(128)
        tail = jnp.where(lane == 64, plain, jnp.where(lane == 65, along, 0.0))
        away = mm_nt(to_value, w_value[other_blocks, :])
        value_send[at, 0:128] = away[:, 0:128].astype(BF16)
        value_send[at, 128:192] = away[:, 128:192].astype(BF16)
        value_send[at, 192:256] = tail[:, 64:128].astype(BF16)
        value_copy(index).start()

    advance(3, 1)
    advance(0, 2)
    late[VALUE_RIGHT : VALUE_RIGHT + 192, :] = first_gradient(0)
    late[VALUE_LEFT : VALUE_LEFT + 192, :] = second_gradient(0, ds_halves)
    advance(4, 1)
    advance(1, 3)
    advance(2, 2)
    advance(0, 3)

    first_half = vectors[0:1, own_half]
    middle_copy.wait_recv()
    d_middle[own_rows, :] = hat_two[:, own_half]
    d_middle[tile_rows(1 - narrow), :] = mid_recv[...].astype(F32)
    @pl.loop(0, tiles)
    def _(index):
        at = tile_rows(index)
        part_copy(index).wait_recv()
        hidden_out[at, :] = (out_own[at, :] + part_recv[at, :].astype(F32)).astype(BF16)
        shape_copy(index).wait_recv()
        value_copy(index).wait_recv()
        into = mm_nt(d_inner_one[at, :], w_first[own_half, :])
        into += mm_nt(value_recv[at, 0:192], w_cross[0])
        into += mm_nt(shape_recv[at, :], w_cross[1])
        plain = (stats[at, 2:3] + value_recv[at, 192:193].astype(F32)) * (1.0 / D)
        along = (stats[at, 3:4] + value_recv[at, 193:194].astype(F32)) * (1.0 / D)
        hat = (inputs[at, own_half].astype(F32) - stats[at, 0:1]) * stats[at, 1:2]
        grad_vectors[0:1, :] += jnp.sum(into * hat, axis=0, keepdims=True)
        grad_vectors[1:2, :] += jnp.sum(into, axis=0, keepdims=True)
        hidden_grad[at, :] = (
            d_middle[at, :] + stats[at, 1:2] * (into * first_half - plain - hat * along)
        ).astype(BF16)

    grad_vectors[2:4, :] = gain_sums[0:2, 0:384]
    grad_vectors[8:10, :] = gain_sums[0:2, 384:768]
    late[VECTORS : VECTORS + 16, :] = grad_vectors[...].astype(BF16)

    core_rows = pl.ds(pl.multiple_of(core * 384, 16), 384)
    to_core = late_copy(
        late.at[pl.ds(pl.multiple_of((1 - core) * 384, 16), 384)], late_core, sibling, 0
    )
    to_core.start()
    advance(3, 2)
    advance(4, 2)
    to_core.wait()

    @pl.loop(0, 384 // CHUNK)
    def _(index):
        at = pl.ds(pl.multiple_of(core * 384 + index * CHUNK, 16), CHUNK)
        came = late_core[pl.ds(pl.multiple_of(index * CHUNK, 16), CHUNK), :]
        late[at, :] = (late[at, :].astype(F32) + came.astype(F32)).astype(BF16)

    def share(t):
        return pl.multiple_of(core * 384 + lax.rem(chip + 8 - t, 8) * CHUNK, 16)

    direct = [
        late_copy(late.at[pl.ds(share(8 - t), CHUNK)], late_slots.at[t - 1], fellows[t], t)
        for t in range(1, 8)
    ]
    for copy in direct:
        copy.start()
    advance(2, 3)
    retreat(1, 3)
    advance(3, 3)
    advance(4, 3)
    retreat(0, 3)
    total = late[pl.ds(share(0), CHUNK), :].astype(F32)
    for t in range(1, 8):
        direct[t - 1].wait()
        total += late_slots[t - 1].astype(F32)
    own_share = pl.ds(pl.multiple_of(PART + share(0), 16), CHUNK)
    mixer_slab[own_share, :] = total.astype(BF16)
    spread_out = [
        late_copy(mixer_slab.at[own_share], mixer_slab.at[own_share], fellows[t], 8 + t)
        for t in range(1, 8)
    ]
    for copy in spread_out:
        copy.start()
    retreat(2, 3)
    retreat(1, 2)
    retreat(0, 2)
    retreat(3, 3)
    retreat(4, 3)
    across = []
    along_own = []
    for t in range(8):
        if t > 0:
            spread_out[t - 1].wait()
        at = pl.ds(pl.multiple_of(PART + share(t), 16), CHUNK)
        across.append(late_copy(mixer_slab.at[at], mixer_slab.at[at], partner, 16 + t))
        across[t].start()
        along_own.append(late_copy(mixer_slab.at[at], mixer_slab.at[at], sibling, 24 + t))
        along_own[t].start()
    retreat(1, 1)
    retreat(2, 2)
    retreat(0, 1)
    retreat(3, 2)
    retreat(4, 2)
    retreat(2, 1)
    retreat(3, 1)
    retreat(4, 1)
    early_rows = pl.ds(offsets[4][1], PART // 2)
    across_early = late_copy(mixer_slab.at[early_rows], mixer_slab.at[early_rows], partner, 40)
    across_early.start()
    along_other = []
    for t in range(8):
        across[t].wait()
        at = pl.ds(pl.multiple_of(PART + share(t), 16), CHUNK)
        other = sums_mixer.at[1 - narrow, at]
        along_other.append(late_copy(other, other, sibling, 32 + t))
        along_other[t].start()
    for i in range(4):
        retreat(i, 0)
    across_early.wait()
    other = sums_mixer.at[1 - narrow, early_rows]
    along_early = late_copy(other, other, sibling, 41)
    along_early.start()
    retreat(4, 0)
    for copy in along_own + along_other + [along_early]:
        copy.wait()

    for copy in (up_copy, dl_copy, ds_copy, dn_copy, cross_copy, middle_copy):
        copy.wait_send()

    @pl.loop(0, tiles)
    def _(index):
        for copy in (inner_copy, part_copy, shape_copy, value_copy):
            copy(index).wait_send()


def finish_kernel(
    hidden_in,
    hidden_grad_in,
    hbm_channel,
    hbm_mixer,
    hidden_out,
    hidden_grad,
    grad_gainfirst,
    grad_shiftfirst,
    grad_valueright,
    grad_valueleft,
    grad_shaperight,
    grad_shapeleft,
    grad_convtaps,
    grad_posweight,
    grad_posbias,
    grad_sinefreq,
    grad_midweight,
    grad_midbias,
    grad_filterout,
    grad_outright,
    grad_outleft,
    grad_gainsecond,
    grad_shiftsecond,
    grad_gateright,
    grad_gateleft,
    grad_liftright,
    grad_liftleft,
    grad_lowerright,
    grad_lowerleft,
    channel,
    mixer,
    gateright,
    gateleft,
    liftright,
    liftleft,
    lowerright,
    lowerleft,
    both_filter,
    in_sem,
    out_sem,
):
    ins = []
    outs = []

    def fetch(source, target):
        ins.append(pltpu.make_async_copy(source, target, in_sem.at[len(ins)]))
        ins[-1].start()

    def store(source, target):
        outs.append(pltpu.make_async_copy(source, target, out_sem.at[len(outs)]))
        outs[-1].start()

    for i in range(4):
        at = pl.ds(PART * i, PART)
        fetch(hbm_channel.at[at], channel.at[at])
    fetch(hbm_mixer, mixer)
    hidden_out[...] = hidden_in[...]
    hidden_grad[...] = hidden_grad_in[...]

    ins[0].wait()
    lowerright[...] = channel[LOWER_RIGHT : LOWER_RIGHT + D, :].astype(F32)
    store(lowerright, grad_lowerright)
    ins[1].wait()
    for h in range(2):
        columns = slice(384 * h, 384 * h + 384)
        lowerleft[:, columns] = channel[LOWER_LEFT + 96 * h : LOWER_LEFT + 96 * h + 96, :].astype(F32)
    gateright[...] = channel[GATE_RIGHT : GATE_RIGHT + 192, :].astype(F32)
    liftright[...] = channel[LIFT_RIGHT : LIFT_RIGHT + 192, :].astype(F32)
    store(lowerleft, grad_lowerleft)
    store(gateright, grad_gateright)
    store(liftright, grad_liftright)
    ins[2].wait()
    for i in range(4):
        first_row = GATE_LEFT + 192 * i
        gateleft[:, 384 * i : 384 * i + 384] = channel[first_row : first_row + 192, :].astype(F32)
    store(gateleft, grad_gateleft)
    ins[3].wait()
    for i in range(4):
        first_row = LIFT_LEFT + 192 * i
        liftleft[:, 384 * i : 384 * i + 384] = channel[first_row : first_row + 192, :].astype(F32)
    store(liftleft, grad_liftleft)
    ins[4].wait()

    lane = lax.broadcasted_iota(jnp.int32, (384, D), 1)
    row = lax.broadcasted_iota(jnp.int32, (384, D), 0)
    step = jnp.where(row >= 96, 96, 0) + jnp.where(row >= 192, 96, 0) + jnp.where(row >= 288, 96, 0)
    unselect = [mask(lane == row + step + 96 * h) for h in range(2)]
    for first_row, target in ((PART + VALUE_RIGHT, grad_valueright), (SHAPE_RIGHT, grad_shaperight)):
        target[...] = mm(mixer[0, first_row : first_row + 192, :], unselect[0]) + mm(
            mixer[1, first_row : first_row + 192, :], unselect[1]
        )
    for h in range(2):
        columns = slice(384 * h, 384 * h + 384)
        for first_row, target in (
            (PART + OUT_RIGHT, grad_outright),
            (SHAPE_LEFT, grad_shapeleft),
            (PART + VALUE_LEFT, grad_valueleft),
        ):
            target[:, columns] = mixer[h, first_row : first_row + 192, :].astype(F32)
        for side in range(2):
            at = slice(OUT_LEFT + 192 * h + 96 * side, OUT_LEFT + 192 * h + 96 * side + 96)
            grad_outleft[96 * h : 96 * h + 96, 384 * side : 384 * side + 384] = mixer[
                0, at, :
            ].astype(F32) + mixer[1, at, :].astype(F32)
    vectors = [mixer[h, PART + VECTORS : PART + VECTORS + 16, :].astype(F32) for h in range(2)]
    whole = jnp.concatenate(vectors, axis=1)
    both = vectors[0] + vectors[1]
    grad_gainfirst[...] = whole[0:1, :].reshape(D)
    grad_shiftfirst[...] = whole[1:2, :].reshape(D)
    grad_convtaps[...] = whole[4:7, :]
    grad_gainsecond[...] = jnp.concatenate([both[2:3, :], both[8:9, :]], axis=1).reshape(D)
    grad_shiftsecond[...] = jnp.concatenate([both[3:4, :], both[9:10, :]], axis=1).reshape(D)
    for i in range(3):
        columns = slice(128 * i, 128 * i + 128)
        at = slice(PART + FILTER, PART + FILTER + 48)
        both_filter[48 * i : 48 * i + 48, :] = mixer[0, at, columns].astype(F32) + mixer[
            1, at, columns
        ].astype(F32)
    grad_midweight[...] = both_filter[0:128, :]
    grad_posweight[...] = both_filter[128:133, :]
    grad_posbias[...] = both_filter[136:137, :].reshape(128)
    grad_midbias[...] = both_filter[137:138, :].reshape(128)
    grad_sinefreq[...] = both_filter[138:139, :].reshape(128)
    count = grad_filterout.shape[1]
    first = (lax.axis_index("wide") * 2 + lax.axis_index("narrow")) * count
    total = jnp.zeros(grad_filterout.shape, F32)
    row = lax.broadcasted_iota(jnp.int32, (384, count), 0)
    lane = lax.broadcasted_iota(jnp.int32, (384, count), 1)
    for h in range(2):
        total += mm(
            mixer[h, PART + FILTER_OUT : PART + FILTER_OUT + 128, :],
            mask(row + 384 * h == first + lane),
        )
    grad_filterout[...] = total
    for copy in outs:
        copy.wait()


def transform_tables(length):
    index = np.arange(length, dtype=np.float64) + 0.5
    angle = np.outer(index, index) * (math.pi / length)
    return (np.cos(angle).astype(jnp.bfloat16), np.sin(angle).astype(jnp.bfloat16))


def place_table(length):
    places = np.arange(length, dtype=np.float64)
    angle = places * (2.0 * math.pi / length)
    turn = (places + 0.5) * (math.pi / (2.0 * length))
    columns = [
        places / length,
        np.cos(angle),
        np.sin(angle),
        np.cos(2.0 * angle),
        np.sin(2.0 * angle),
        np.cos(turn),
        np.sin(turn),
        np.zeros(length),
    ]
    table = np.stack(columns, axis=1).astype(np.float32)
    feats = np.concatenate([table[:, :5], np.zeros((length, 3), np.float32)], axis=1)
    high = feats.astype(jnp.bfloat16)
    low = (feats - high.astype(np.float32)).astype(jnp.bfloat16)
    return (table, np.concatenate([high, low, high, np.zeros_like(high)], axis=1))


def pair_body(
    hidden_in,
    gainfirst,
    shiftfirst,
    valueright,
    valueleft,
    shaperight,
    shapeleft,
    convtaps,
    posweight,
    posbias,
    sinefreq,
    midweight,
    midbias,
    filterout,
    outright,
    outleft,
    gainsecond,
    shiftsecond,
    gateright,
    gateleft,
    liftright,
    liftleft,
    lowerright,
    lowerleft,
    grad_out,
):
    rows = hidden_in.shape[0]
    length = 2 * rows
    table_cos, table_sin = transform_tables(length)
    def out(extent, dtype=BF16):
        return jax.ShapeDtypeStruct(extent, dtype)

    def buf(*extent, dtype=BF16):
        return pltpu.VMEM(extent, dtype)

    vmem = pl.BlockSpec(memory_space=pltpu.VMEM)
    hbm = pl.BlockSpec(memory_space=pl.ANY)
    results = pl.pallas_call(
        whole_kernel,
        out_shape=(
            out((rows, 384)),
            out((rows, 384)),
            out((CHANNEL_ROWS, 384)),
            out((2, 2 * PART, 384)),
        ),
        in_specs=[hbm] * 4 + [vmem] * 12 + [hbm] * 13,
        out_specs=[vmem] * 4,
        scratch_shapes=[
            buf(rows, D),
            buf(length, length),
            buf(length, length),
            buf(8, D, dtype=F32),
            buf(16, 128, dtype=F32),
            buf(D, D),
            buf(384, 512),
            buf(384, 512),
            buf(512, 384),
            buf(2, 384, D),
            buf(D, D),
            buf(2, 256, D),
            buf(2, 256, D),
            buf(2, D, 256),
            buf(384, D),
            buf(2, rows, 384),
            buf(rows, 128, dtype=F32),
            buf(rows, D),
            buf(rows, D),
            buf(2, rows, PAD),
            buf(2, rows, PAD),
            buf(2, rows, PAD, dtype=F32),
            buf(length + 8, PAD, dtype=F32),
            buf(length, PAD),
            buf(length, 128),
            buf(length, 128),
            buf(length, 128),
            buf(length, 128),
            buf(length, 128),
            buf(length, 128),
            buf(2, length, PAD, dtype=F32),
            buf(2, length, PAD),
            buf(2, length, PAD),
            buf(2, rows, PAD),
            buf(2, rows, PAD),
            buf(2, rows, 384),
            buf(TILE, D, dtype=F32),
            buf(rows, D),
            buf(rows, D),
            buf(2, TILE, D, dtype=F32),
            buf(2, TILE, D, dtype=F32),
            buf(2, rows, D),
            buf(rows, 384),
            buf(rows, 384, dtype=F32),
            buf(rows, 384),
            buf(rows, 384),
            buf(rows, 384),
            buf(2, rows, D),
            buf(2, rows, D),
            buf(rows, D),
            buf(TILE, D, dtype=F32),
            buf(TILE, D),
            buf(TILE, D),
            buf(rows, 384),
            buf(2, rows, PAD),
            buf(2, rows, PAD),
            buf(length + 8, PAD, dtype=F32),
            buf(2, rows, PAD),
            buf(rows, D),
            buf(TILE, 384),
            buf(TILE, 384),
            buf(TILE, 384),
            buf(rows, 384, dtype=F32),
            buf(TILE, D),
            buf(rows, 192),
            buf(rows, 192),
            buf(rows, 256),
            buf(rows, 256),
            buf(2, 384, 192),
            buf(8, D, dtype=F32),
            buf(128, PAD, dtype=F32),
            buf(128, PAD),
            buf(16, 384, dtype=F32),
            buf(144, 128, dtype=F32),
            buf(8, D, dtype=F32),
            pltpu.SemaphoreType.DMA((16,)),
            pltpu.SemaphoreType.DMA((16,)),
            pltpu.SemaphoreType.DMA((20,)),
            buf(5, STEP_ROWS[4], 384),
            pltpu.SemaphoreType.DMA((40,)),
            pltpu.SemaphoreType.DMA((40,)),
            pltpu.SemaphoreType.REGULAR((20,)),
            buf(PART, 384),
            buf(PART // 2, 384),
            buf(7, CHUNK, 384),
            pltpu.SemaphoreType.DMA((42,)),
            pltpu.SemaphoreType.DMA((42,)),
        ],
        compiler_params=pltpu.CompilerParams(
            collective_id=0, has_side_effects=True, vmem_limit_bytes=63 * 1024 * 1024
        ),
    )(
        hidden_in,
        grad_out,
        table_cos,
        table_sin,
        *place_table(length),
        gainfirst,
        shiftfirst,
        gainsecond,
        shiftsecond,
        convtaps,
        posweight,
        posbias,
        midbias,
        sinefreq,
        midweight,
        filterout,
        valueright,
        valueleft,
        shaperight,
        shapeleft,
        outright,
        outleft,
        gateright,
        gateleft,
        liftright,
        liftleft,
        lowerright,
        lowerleft,
    )
    count = D // (lax.axis_size("wide") * lax.axis_size("narrow"))
    square = out((192, D), F32)
    return pl.pallas_call(
        finish_kernel,
        out_shape=(
            out((rows, 384)),
            out((rows, 384)),
            out((D,), F32),
            out((D,), F32),
            square,
            square,
            square,
            square,
            out((3, D), F32),
            out((5, 128), F32),
            out((128,), F32),
            out((128,), F32),
            out((128, 128), F32),
            out((128,), F32),
            out((128, count), F32),
            square,
            square,
            out((D,), F32),
            out((D,), F32),
            out(gateright.shape, F32),
            out(gateleft.shape, F32),
            out(liftright.shape, F32),
            out(liftleft.shape, F32),
            out(lowerright.shape, F32),
            out(lowerleft.shape, F32),
        ),
        in_specs=[vmem] * 2 + [hbm] * 2,
        out_specs=[vmem] * 19 + [hbm] * 6,
        scratch_shapes=[
            buf(CHANNEL_ROWS, 384),
            buf(2, 2 * PART, 384),
            buf(*gateright.shape, dtype=F32),
            buf(*gateleft.shape, dtype=F32),
            buf(*liftright.shape, dtype=F32),
            buf(*liftleft.shape, dtype=F32),
            buf(*lowerright.shape, dtype=F32),
            buf(*lowerleft.shape, dtype=F32),
            buf(144, 128, dtype=F32),
            pltpu.SemaphoreType.DMA((5,)),
            pltpu.SemaphoreType.DMA((6,)),
        ],
        compiler_params=pltpu.CompilerParams(vmem_limit_bytes=60 * 1024 * 1024),
    )(*results)


def solution(mesh):
    pairs = mesh.shape["wide"] == 2 * SEQS and mesh.shape["narrow"] == 2
    return jax.shard_map(
        pair_body if pairs else body,
        mesh=mesh,
        in_specs=(
            P("wide", None),
            P(),
            P(),
            P(),
            P(),
            P(),
            P(),
            P(),
            P(),
            P(),
            P(),
            P(),
            P(),
            P(),
            P(),
            P(),
            P(),
            P(),
            P(None, "narrow"),
            P(None, "narrow"),
            P(None, "narrow"),
            P(None, "narrow"),
            P(None, "narrow"),
            P("narrow", None),
            P("wide", "narrow"),
        ),
        out_specs=(
            P("wide", "narrow"),
            P("wide", "narrow"),
            P(),
            P(),
            P(),
            P(),
            P(),
            P(),
            P(),
            P(),
            P(),
            P(),
            P(),
            P(),
            P(None, ("wide", "narrow")),
            P(),
            P(),
            P(),
            P(),
            P(None, "narrow"),
            P(None, "narrow"),
            P(None, "narrow"),
            P(None, "narrow"),
            P(None, "narrow"),
            P("narrow", None),
        ),
        check_vma=False,
    )
```

```python
import math

import jax
import jax.numpy as jnp
import numpy as np
from jax import lax
from jax.experimental import pallas as pl
from jax.experimental.pallas import tpu as pltpu
from jax.sharding import PartitionSpec as P

D = 768
BLOCKS = 4
SEQS = 8


EPSILON = 1e-05
HIGHEST = lax.Precision.HIGHEST


def from_behind(x, axis, by):
    length = lax.axis_size(axis)
    pairs = [(i, i + by) for i in range(length) if 0 <= i + by < length]
    return lax.ppermute(x, axis, pairs)


def norm_forward(values, gain, shift):
    center = values - jnp.mean(values, axis=-1, keepdims=True)
    inverse = lax.rsqrt(jnp.mean(center * center, axis=-1, keepdims=True) + EPSILON)
    normed = center * inverse
    return (normed * gain + shift, normed, inverse)


def norm_backward(upstream, normed, inverse, gain):
    scaled = upstream * gain
    result = inverse * (
        scaled
        - jnp.mean(scaled, axis=-1, keepdims=True)
        - normed * jnp.mean(scaled * normed, axis=-1, keepdims=True)
    )
    return (result, jnp.sum(upstream * normed, axis=0), jnp.sum(upstream, axis=0))


def right_view(right, nblocks, groups, group_first):
    width_in = right.shape[0]
    piece = right.shape[1] // (nblocks * groups)
    if group_first:
        return (right.reshape(width_in, groups, nblocks, piece), "ikbc")
    return (right.reshape(width_in, nblocks, groups, piece), "ibkc")


def section_one(inputs, right, groups, group_first):
    rowcount = inputs.shape[0]
    width_in = right.shape[0]
    nblocks = inputs.shape[1] // width_in
    factor, letters = right_view(right, nblocks, groups, group_first)
    first = jnp.einsum(
        "tbi," + letters + "->tkbc",
        inputs.reshape(rowcount, nblocks, width_in),
        factor,
        preferred_element_type=jnp.float32,
    )
    return first.reshape(rowcount, groups, -1).astype(jnp.bfloat16)


def section_two(middle_part, left):
    groups = middle_part.shape[1]
    result = jnp.einsum(
        "tkj,jke->tke",
        middle_part,
        left.reshape(left.shape[0], groups, -1),
        preferred_element_type=jnp.float32,
    )
    return result.reshape(result.shape[0], -1)


def back_two(middle_part, left, upstream):
    groups = middle_part.shape[1]
    left_view = left.reshape(left.shape[0], groups, -1)
    grad_left = jnp.einsum(
        "tkj,tke->jke", middle_part, upstream, preferred_element_type=jnp.float32
    )
    grad_middle = jnp.einsum(
        "tke,jke->tkj", upstream, left_view, preferred_element_type=jnp.float32
    )
    return (grad_left.reshape(left.shape[0], -1), grad_middle.astype(jnp.bfloat16))


def back_one(inputs, right, grad_middle, group_first):
    rowcount = inputs.shape[0]
    width_in = right.shape[0]
    nblocks = inputs.shape[1] // width_in
    groups = grad_middle.shape[1]
    factor, letters = right_view(right, nblocks, groups, group_first)
    spread_back = grad_middle.reshape(rowcount, groups, nblocks, -1)
    blocked = inputs.reshape(rowcount, nblocks, width_in)
    grad_right = jnp.einsum(
        "tbi,tkbc->" + letters, blocked, spread_back, preferred_element_type=jnp.float32
    )
    grad_inputs = jnp.einsum(
        "tkbc," + letters + "->tbi", spread_back, factor, preferred_element_type=jnp.float32
    )
    return (grad_right.reshape(width_in, -1), grad_inputs.reshape(rowcount, -1))


def fourier_tables(length):
    span = length // 128
    slow_index = jnp.arange(span, dtype=jnp.int32)
    fast_index = jnp.arange(128, dtype=jnp.int32)
    small = (slow_index[:, None] * slow_index[None, :] % span).astype(jnp.float32) * (
        2.0 * math.pi / span
    )
    twist = (slow_index[:, None] * fast_index[None, :] % length).astype(jnp.float32) * (
        2.0 * math.pi / length
    )
    large = (fast_index[:, None] * fast_index[None, :] % 128).astype(jnp.float32) * (
        2.0 * math.pi / 128
    )
    return (
        jnp.cos(small),
        jnp.sin(small),
        jnp.cos(twist),
        jnp.sin(twist),
        jnp.cos(large),
        jnp.sin(large),
    )


def to_spectrum(signal, tables):
    cos_small, sin_small, cos_twist, sin_twist, cos_large, sin_large = tables
    span = cos_small.shape[0]
    padded = jnp.concatenate([signal, jnp.zeros_like(signal)], axis=-1)
    padded = padded.reshape(signal.shape[:-1] + (span, 128))
    first_re = jnp.einsum("...qp,qk->...kp", padded, cos_small, precision=HIGHEST)
    first_im = -jnp.einsum("...qp,qk->...kp", padded, sin_small, precision=HIGHEST)
    turned_re = first_re * cos_twist + first_im * sin_twist
    turned_im = first_im * cos_twist - first_re * sin_twist
    out_re = jnp.einsum("...kp,pj->...kj", turned_re, cos_large, precision=HIGHEST) + jnp.einsum(
        "...kp,pj->...kj", turned_im, sin_large, precision=HIGHEST
    )
    out_im = jnp.einsum("...kp,pj->...kj", turned_im, cos_large, precision=HIGHEST) - jnp.einsum(
        "...kp,pj->...kj", turned_re, sin_large, precision=HIGHEST
    )
    return (out_re, out_im)


def from_spectrum(real_part, imag_part, tables):
    cos_small, sin_small, cos_twist, sin_twist, cos_large, sin_large = tables
    span = cos_small.shape[0]
    back_re = jnp.einsum("...kj,pj->...kp", real_part, cos_large, precision=HIGHEST) - jnp.einsum(
        "...kj,pj->...kp", imag_part, sin_large, precision=HIGHEST
    )
    back_im = jnp.einsum("...kj,pj->...kp", imag_part, cos_large, precision=HIGHEST) + jnp.einsum(
        "...kj,pj->...kp", real_part, sin_large, precision=HIGHEST
    )
    turned_re = back_re * cos_twist - back_im * sin_twist
    turned_im = back_im * cos_twist + back_re * sin_twist
    signal = (
        jnp.einsum("...kp,qk->...qp", turned_re, cos_small, precision=HIGHEST)
        - jnp.einsum("...kp,qk->...qp", turned_im, sin_small, precision=HIGHEST)
    ) / (span * 128)
    signal = signal.reshape(signal.shape[:-2] + (span * 128,))
    return signal[..., : span * 64]


def position_features(length):
    places = jnp.arange(length, dtype=jnp.float32)
    angle = places * (2.0 * math.pi / length)
    return jnp.stack(
        [
            places / length,
            jnp.cos(angle),
            jnp.sin(angle),
            jnp.cos(2.0 * angle),
            jnp.sin(2.0 * angle),
        ],
        axis=1,
    )


def decay_factors(channel_ids, length):
    rank = (channel_ids * 5 % D).astype(jnp.float32) / D
    lowest = math.log(0.25 / length)
    highest = math.log(1.0 / 30.0)
    rate = jnp.exp(lowest + rank * (highest - lowest))
    places = jnp.arange(length, dtype=jnp.float32)
    return jnp.exp(-rate[:, None] * places[None, :]) * jnp.sqrt(2.0 * rate)[:, None]


def channel_order(data, nwide, nnarrow, rows_half):
    count = data.shape[0]
    return data.reshape(count, nnarrow, nwide, rows_half).transpose(0, 2, 1, 3).reshape(count, -1)


def row_order(data, nwide, nnarrow):
    total = data.shape[0]
    rows_half = data.shape[1]
    count = total // (nwide * nnarrow)
    return (
        data.reshape(nnarrow, nwide, count, rows_half)
        .transpose(1, 0, 2, 3)
        .reshape(total, rows_half)
        .T
    )


def body(
    hidden_in,
    gainfirst,
    shiftfirst,
    valueright,
    valueleft,
    shaperight,
    shapeleft,
    convtaps,
    posweight,
    posbias,
    sinefreq,
    midweight,
    midbias,
    filterout,
    outright,
    outleft,
    gainsecond,
    shiftsecond,
    gateright,
    gateleft,
    liftright,
    liftleft,
    lowerright,
    lowerleft,
    grad_out,
):
    rowcount = hidden_in.shape[0]
    local_groups = gateright.shape[1] // gateleft.shape[0]
    nwide = lax.axis_size("wide")
    nnarrow = lax.axis_size("narrow")
    narrow_index = lax.axis_index("narrow")
    rows_half = rowcount // nnarrow
    row_start = narrow_index * rows_half
    combined = lax.axis_index("wide") * nnarrow + narrow_index
    resid = lax.dynamic_slice_in_dim(hidden_in, row_start, rows_half, 0).astype(jnp.float32)
    normone, hat_one, inv_one = norm_forward(resid, gainfirst, shiftfirst)
    normone = normone.astype(jnp.bfloat16)
    mid_value = section_one(normone, valueright, BLOCKS, False)
    signal = section_two(mid_value, valueleft).astype(jnp.bfloat16)
    mid_shape = section_one(normone, shaperight, BLOCKS, False)
    shaping = section_two(mid_shape, shapeleft)
    group = nwide // SEQS * nnarrow
    place = combined % group
    before = from_behind(signal[-2:], ("wide", "narrow"), 1)
    before = jnp.where(place == 0, jnp.zeros_like(before), before)
    extended = jnp.concatenate([before, signal], axis=0).astype(jnp.float32)
    shortconv = (
        convtaps[0] * extended[2:] + convtaps[1] * extended[1:-1] + convtaps[2] * extended[:-2]
    ).astype(jnp.bfloat16)
    channels = lax.all_to_all(
        lax.all_to_all(shortconv.T, "wide", split_axis=0, concat_axis=1, tiled=True),
        "narrow",
        split_axis=0,
        concat_axis=1,
        tiled=True,
    )
    channels = channel_order(channels, nwide, nnarrow, rows_half)
    count = channels.shape[0]
    length = channels.shape[1] // SEQS
    feats = position_features(length)
    lin_one = jnp.dot(feats, posweight, precision=HIGHEST) + posbias
    act_one = jnp.sin(sinefreq * lin_one)
    lin_two = jnp.dot(act_one, midweight, precision=HIGHEST) + midbias
    act_two = jnp.sin(sinefreq * lin_two)
    own_cols = lax.dynamic_slice_in_dim(filterout, combined * count, count, 1)
    channel_ids = combined * count + jnp.arange(count, dtype=jnp.int32)
    modulation = decay_factors(channel_ids, length)
    taps = jnp.dot(act_two, own_cols, precision=HIGHEST).T * modulation
    tables = fourier_tables(2 * length)
    sig_re, sig_im = to_spectrum(channels.astype(jnp.float32).reshape(count, SEQS, length), tables)
    fil_re, fil_im = to_spectrum(taps.reshape(count, 1, length), tables)
    conv_chan = from_spectrum(
        sig_re * fil_re - sig_im * fil_im, sig_re * fil_im + sig_im * fil_re, tables
    )
    conv_chan = conv_chan.reshape(count, SEQS * length).astype(jnp.bfloat16)
    longconv = lax.all_to_all(
        lax.all_to_all(conv_chan, "wide", split_axis=1, concat_axis=0, tiled=True),
        "narrow",
        split_axis=1,
        concat_axis=0,
        tiled=True,
    )
    longconv = row_order(longconv, nwide, nnarrow)
    mixed = (shaping * longconv.astype(jnp.float32)).astype(jnp.bfloat16)
    mid_out = section_one(mixed, outright, BLOCKS, False)
    middle = resid + section_two(mid_out, outleft)
    normtwo, hat_two, inv_two = norm_forward(middle, gainsecond, shiftsecond)
    normtwo = normtwo.astype(jnp.bfloat16)
    norm_all = lax.all_gather(normtwo, "narrow", axis=0, tiled=True)
    mid_gate = section_one(norm_all, gateright, local_groups, True)
    pregate = section_two(mid_gate, gateleft)
    mid_lift = section_one(norm_all, liftright, local_groups, True)
    prelift = section_two(mid_lift, liftleft)
    cumulative = 0.5 * (1.0 + lax.erf(pregate * (1.0 / math.sqrt(2.0))))
    activated = pregate * cumulative
    hidden = (activated * prelift).astype(jnp.bfloat16)
    mid_lower = section_one(hidden, lowerright, BLOCKS, False)
    partial_sum = section_two(mid_lower, lowerleft)
    partial_sum = partial_sum + lax.dynamic_update_slice_in_dim(
        jnp.zeros_like(partial_sum), middle, row_start, 0
    )
    hidden_out = lax.psum_scatter(
        partial_sum.astype(jnp.bfloat16), "narrow", scatter_dimension=1, tiled=True
    )
    upstream = lax.all_gather(grad_out, "narrow", axis=1, tiled=True)
    grad_lowerleft, grad_mid_lower = back_two(
        mid_lower, lowerleft, upstream.reshape(rowcount, BLOCKS, -1)
    )
    grad_lowerright, grad_hidden = back_one(hidden, lowerright, grad_mid_lower, False)
    density = jnp.exp(-0.5 * pregate * pregate) * (1.0 / math.sqrt(2.0 * math.pi))
    grad_pregate = (grad_hidden * prelift * (cumulative + pregate * density)).astype(jnp.bfloat16)
    grad_prelift = (grad_hidden * activated).astype(jnp.bfloat16)
    grad_gateleft, grad_mid_gate = back_two(
        mid_gate, gateleft, grad_pregate.reshape(rowcount, local_groups, -1)
    )
    grad_gateright, into_gate = back_one(norm_all, gateright, grad_mid_gate, True)
    grad_liftleft, grad_mid_lift = back_two(
        mid_lift, liftleft, grad_prelift.reshape(rowcount, local_groups, -1)
    )
    grad_liftright, into_lift = back_one(norm_all, liftright, grad_mid_lift, True)
    ffn_local = (
        grad_gateright,
        grad_gateleft,
        grad_liftright,
        grad_liftleft,
        grad_lowerright,
        grad_lowerleft,
    )
    dnormtwo = lax.psum_scatter(
        (into_gate + into_lift).astype(jnp.bfloat16), "narrow", scatter_dimension=0, tiled=True
    ).astype(jnp.float32)
    back_two_norm, grad_gainsecond, grad_shiftsecond = norm_backward(
        dnormtwo, hat_two, inv_two, gainsecond
    )
    up_rows = lax.dynamic_slice_in_dim(upstream, row_start, rows_half, 0)
    dmiddle = up_rows.astype(jnp.float32) + back_two_norm
    dbranch = dmiddle.astype(jnp.bfloat16)
    grad_outleft, grad_mid_out = back_two(mid_out, outleft, dbranch.reshape(rows_half, BLOCKS, -1))
    grad_outright, dmixed = back_one(mixed, outright, grad_mid_out, False)
    dshaping = (dmixed * longconv.astype(jnp.float32)).astype(jnp.bfloat16)
    dlong = (dmixed * shaping).astype(jnp.bfloat16)
    grad_chan = lax.all_to_all(
        lax.all_to_all(dlong.T, "wide", split_axis=0, concat_axis=1, tiled=True),
        "narrow",
        split_axis=0,
        concat_axis=1,
        tiled=True,
    )
    grad_chan = channel_order(grad_chan, nwide, nnarrow, rows_half)
    dlong_re, dlong_im = to_spectrum(
        grad_chan.astype(jnp.float32).reshape(count, SEQS, length), tables
    )
    dshort_chan = from_spectrum(
        dlong_re * fil_re + dlong_im * fil_im, dlong_im * fil_re - dlong_re * fil_im, tables
    )
    dshort_chan = dshort_chan.reshape(count, SEQS * length).astype(jnp.bfloat16)
    filt_re = jnp.sum(dlong_re * sig_re + dlong_im * sig_im, axis=1, keepdims=True)
    filt_im = jnp.sum(dlong_im * sig_re - dlong_re * sig_im, axis=1, keepdims=True)
    grad_taps = from_spectrum(filt_re, filt_im, tables).reshape(count, length)
    dshort = lax.all_to_all(
        lax.all_to_all(dshort_chan, "wide", split_axis=1, concat_axis=0, tiled=True),
        "narrow",
        split_axis=1,
        concat_axis=0,
        tiled=True,
    )
    dshort = row_order(dshort, nwide, nnarrow)
    grad_modded = grad_taps * modulation
    grad_filterout = jnp.dot(act_two.T, grad_modded.T, precision=HIGHEST)
    dact_two = jnp.dot(grad_modded.T, own_cols.T, precision=HIGHEST)
    dlin_two = dact_two * jnp.cos(sinefreq * lin_two)
    scaled_two = dlin_two * sinefreq
    grad_midweight = jnp.dot(act_one.T, scaled_two, precision=HIGHEST)
    grad_midbias = jnp.sum(scaled_two, axis=0)
    dact_one = jnp.dot(scaled_two, midweight.T, precision=HIGHEST)
    dlin_one = dact_one * jnp.cos(sinefreq * lin_one)
    scaled_one = dlin_one * sinefreq
    grad_posweight = jnp.dot(feats.T, scaled_one, precision=HIGHEST)
    grad_posbias = jnp.sum(scaled_one, axis=0)
    grad_sinefreq = jnp.sum(dlin_one * lin_one, axis=0) + jnp.sum(dlin_two * lin_two, axis=0)
    after = from_behind(dshort[:2], ("wide", "narrow"), -1)
    after = jnp.where(place == group - 1, jnp.zeros_like(after), after)
    ext_grad = jnp.concatenate([dshort, after], axis=0).astype(jnp.float32)
    dsignal = (
        convtaps[0] * ext_grad[:-2] + convtaps[1] * ext_grad[1:-1] + convtaps[2] * ext_grad[2:]
    ).astype(jnp.bfloat16)
    short_grad = dshort.astype(jnp.float32)
    grad_convtaps = jnp.stack(
        [
            jnp.sum(extended[2:] * short_grad, axis=0),
            jnp.sum(extended[1:-1] * short_grad, axis=0),
            jnp.sum(extended[:-2] * short_grad, axis=0),
        ]
    )
    grad_valueleft, grad_mid_value = back_two(
        mid_value, valueleft, dsignal.reshape(rows_half, BLOCKS, -1)
    )
    grad_valueright, into_value = back_one(normone, valueright, grad_mid_value, False)
    grad_shapeleft, grad_mid_shape = back_two(
        mid_shape, shapeleft, dshaping.reshape(rows_half, BLOCKS, -1)
    )
    grad_shaperight, into_shape = back_one(normone, shaperight, grad_mid_shape, False)
    back_one_norm, grad_gainfirst, grad_shiftfirst = norm_backward(
        into_value + into_shape, hat_one, inv_one, gainfirst
    )
    full_grad = (dmiddle + back_one_norm).astype(jnp.bfloat16)
    hidden_grad = lax.all_to_all(full_grad, "narrow", split_axis=1, concat_axis=0, tiled=True)
    mixer_grads = lax.psum(
        (
            grad_gainfirst,
            grad_shiftfirst,
            grad_valueright,
            grad_valueleft,
            grad_shaperight,
            grad_shapeleft,
            grad_convtaps,
            grad_posweight,
            grad_posbias,
            grad_sinefreq,
            grad_midweight,
            grad_midbias,
            grad_outright,
            grad_outleft,
            grad_gainsecond,
            grad_shiftsecond,
        ),
        ("wide", "narrow"),
    )
    ffn_grads = lax.psum(
        (ffn_local[0], ffn_local[1], ffn_local[2], ffn_local[3], ffn_local[4], ffn_local[5]), "wide"
    )
    return (
        hidden_out,
        hidden_grad,
        mixer_grads[0],
        mixer_grads[1],
        mixer_grads[2],
        mixer_grads[3],
        mixer_grads[4],
        mixer_grads[5],
        mixer_grads[6],
        mixer_grads[7],
        mixer_grads[8],
        mixer_grads[9],
        mixer_grads[10],
        mixer_grads[11],
        grad_filterout,
        mixer_grads[12],
        mixer_grads[13],
        mixer_grads[14],
        mixer_grads[15],
        ffn_grads[0],
        ffn_grads[1],
        ffn_grads[2],
        ffn_grads[3],
        ffn_grads[4],
        ffn_grads[5],
    )


F32 = jnp.float32
BF16 = jnp.bfloat16
MESH = pl.DeviceIdType.MESH
TILE = 256
PAD = 256


def mm(a, b, precision=None):
    return lax.dot_general(
        a, b, (((1,), (0,)), ((), ())), precision=precision, preferred_element_type=F32
    )


def mm_nt(a, b, precision=None):
    return lax.dot_general(
        a, b, (((1,), (1,)), ((), ())), precision=precision, preferred_element_type=F32
    )


def mm_tn(a, b, precision=None):
    return lax.dot_general(
        a, b, (((0,), (0,)), ((), ())), precision=precision, preferred_element_type=F32
    )


def lanes(width):
    return lax.broadcasted_iota(jnp.int32, (1, width), 1)


def mask(condition, dtype=BF16):
    return jnp.where(condition, 1.0, 0.0).astype(dtype)


def between(width, low, high, dtype=BF16):
    lane = lanes(width)
    return mask((lane >= low) & (lane < high), dtype)


def join(first, second):
    return jnp.concatenate(
        [first[:, :128], first[:, 128:] + second[:, :128], second[:, 128:]], axis=1
    )


def sine_cosine(angle):
    turns = jnp.floor(angle * (1.0 / math.pi) + 0.5)
    rest = angle - turns * 3.140625
    rest = rest - turns * 9.67502593994140625e-4
    rest = rest - turns * 1.509957990978376e-7
    flip = 1.0 - 2.0 * (turns - 2.0 * jnp.floor(turns * 0.5))
    square = rest * rest
    sine = 1.0
    for divisor in (110.0, 72.0, 42.0, 20.0, 6.0):
        sine = 1.0 - square * (1.0 / divisor) * sine
    cosine = 1.0
    for divisor in (132.0, 90.0, 56.0, 30.0, 12.0, 2.0):
        cosine = 1.0 - square * (1.0 / divisor) * cosine
    return (sine * rest * flip, cosine * flip)


def fold(whole, side):
    return [
        whole[192 * b + 96 * side : 192 * b + 96 * side + 48, :] * between(384, 0, 192, F32)
        + whole[192 * b + 96 * side + 48 : 192 * b + 96 * side + 96, :] * between(384, 192, 384, F32)
        for b in range(2)
    ]


STRIDES = (1, 2, 4, 8)
PART = 768
STEP_ROWS = (0, 384, 576, 672, 720)
ORDERS = ((0, 1, 2, 3), (0, 2, 3, 1), (0, 1, 2, 3), (0, 1, 2, 3), (0, 1, 2, 3))
CHUNK = 48
LOWER_RIGHT, LOWER_LEFT, GATE_RIGHT, LIFT_RIGHT, GATE_LEFT, LIFT_LEFT, CHANNEL_ROWS = (
    0,
    768,
    960,
    1152,
    1344,
    2112,
    4 * PART,
)
OUT_LEFT, SHAPE_RIGHT, SHAPE_LEFT = (0, 384, 576)
VALUE_RIGHT, VALUE_LEFT, FILTER_OUT, VECTORS, FILTER, OUT_RIGHT = (0, 192, 384, 512, 528, 576)


def tile_rows(index, size=TILE):
    return pl.ds(pl.multiple_of(index * size, size), size)


def whole_kernel(
    hidden_in,
    upstream,
    hbm_cos,
    hbm_sin,
    place,
    place_parts,
    gainfirst,
    shiftfirst,
    gainsecond,
    shiftsecond,
    convtaps,
    posweight,
    posbias,
    midbias,
    sinefreq,
    midweight,
    filterout,
    valueright,
    valueleft,
    shaperight,
    shapeleft,
    outright,
    outleft,
    gateright,
    gateleft,
    liftright,
    liftleft,
    lowerright,
    lowerleft,
    hidden_out,
    hidden_grad,
    sums_channel,
    sums_mixer,
    inputs,
    table_cos,
    table_sin,
    vectors,
    filter_vectors,
    w_first,
    w_value,
    w_shape,
    w_out_first,
    w_out_second,
    w_glu,
    w_gate,
    w_lift,
    w_lower,
    w_lower_second,
    up_halves,
    stats,
    norm_one,
    inner_one,
    sig_halves,
    sig_rows,
    shaping,
    sig_pad,
    short,
    act_one,
    cos_one,
    lin_one,
    act_two,
    cos_two,
    lin_two,
    fil_spec,
    sig_spec,
    prod_spec,
    long_rows,
    long_halves,
    inner_out,
    hat_two,
    norm_two,
    inner_glu,
    factor_gate,
    factor_lift,
    hid,
    inner_lower,
    out_own,
    part_send,
    part_recv,
    d_inner_lower,
    d_gate,
    d_lift,
    d_inner_glu,
    dn_own,
    dn_send,
    dn_recv,
    d_inner_out,
    d_shaping,
    dl_rows,
    ds_pad,
    ds_halves,
    d_inner_one,
    cross_send,
    mid_send,
    mid_recv,
    d_middle,
    branch,
    shape_send,
    shape_recv,
    value_send,
    value_recv,
    w_cross,
    through,
    d_lin,
    own_out,
    grad_vectors,
    grad_filter,
    gain_sums,
    send_sem,
    recv_sem,
    load_sem,
    got,
    sum_send,
    sum_recv,
    sum_free,
    late,
    late_core,
    late_slots,
    late_send,
    late_recv,
):
    rows = inputs.shape[0]
    tiles = rows // TILE
    length = 2 * rows
    spans = length // TILE
    wide = lax.axis_index("wide")
    narrow = lax.axis_index("narrow")
    bits = [lax.rem(wide // stride, 2) for stride in STRIDES]
    core = bits[0]
    sibling = (wide + 1 - 2 * core, narrow)
    partner = (wide, 1 - narrow)
    quarter = 2 * narrow + core
    own_half = pl.ds(pl.multiple_of(narrow * 384, 384), 384)
    other_half = pl.ds(pl.multiple_of((1 - narrow) * 384, 384), 384)

    loads = {}

    def load(name, source, target):
        loads[name] = pltpu.make_async_copy(source, target, load_sem.at[len(loads)])
        loads[name].start()

    load("inputs", hidden_in, inputs)
    load("valueright", valueright, hid.at[0, pl.ds(0, 192)])
    load("shaperight", shaperight, hid.at[0, pl.ds(192, 192)])
    load("valueleft", valueleft, hid.at[1, pl.ds(0, 192)])
    load("shapeleft", shapeleft, hid.at[1, pl.ds(192, 192)])
    load("filterout", filterout, factor_gate.at[0, pl.ds(0, 128)])
    load("cos", hbm_cos, table_cos)
    load("sin", hbm_sin, table_sin)
    load("outright", outright, d_gate.at[0, pl.ds(0, 192)])
    load("outleft", outleft, d_gate.at[0, pl.ds(192, 192)])
    load("gateright", gateright, d_lift.at[1, pl.ds(96, 192), pl.ds(0, 384)])
    load("liftright", liftright, d_lift.at[1, pl.ds(96, 192), pl.ds(384, 384)])
    load("lowerleft", lowerleft, d_lift.at[1, pl.ds(0, 96)])
    load("lower_top", lowerright.at[pl.ds(0, 512)], d_lift.at[0, :, pl.ds(0, 384)])
    load("lower_end", lowerright.at[pl.ds(512, 256)], d_lift.at[0, pl.ds(0, 256), pl.ds(384, 384)])
    for k in range(2):
        at = pl.ds(64 * k, 192)
        load(("gate", k), gateleft.at[:, pl.ds(D * k, D)], w_gate.at[k, at])
        load(("lift", k), liftleft.at[:, pl.ds(D * k, D)], w_lift.at[k, at])
    load("upstream", upstream, up_halves.at[narrow])

    barrier = pltpu.get_barrier_semaphore()
    others = [(wide + stride * (1 - 2 * bit), narrow) for stride, bit in zip(STRIDES, bits)]
    chip = wide // 2
    fellows = [(2 * lax.rem(chip + t, 8) + core, narrow) for t in range(8)]
    for device in [sibling, partner] + fellows[1:]:
        pl.semaphore_signal(barrier, inc=1, device_id=device, device_id_type=MESH)

    for i, source in enumerate((gainfirst, shiftfirst, gainsecond, shiftsecond)):
        vectors[i : i + 1, :] = source[...].reshape(1, D)
    vectors[4:7, :] = convtaps[...]
    vectors[7:8, :] = jnp.zeros((1, D), F32)
    filter_vectors[...] = jnp.zeros(filter_vectors.shape, F32)
    filter_vectors[0:5, :] = posweight[...]
    for i, source in enumerate((posbias, midbias, sinefreq)):
        filter_vectors[8 + i : 9 + i, :] = source[...].reshape(1, 128)

    pl.semaphore_wait(barrier, 9)

    def send(source, target, device, index):
        return pltpu.make_async_remote_copy(
            src_ref=source,
            dst_ref=target,
            send_sem=send_sem.at[index],
            recv_sem=recv_sem.at[index],
            device_id=device,
            device_id_type=MESH,
        )

    mixer_slab = sums_mixer.at[narrow]
    parts_of = [sums_channel.at[pl.ds(PART * i, PART)] for i in range(4)] + [mixer_slab.at[pl.ds(0, PART)]]
    offsets = []
    for order in ORDERS:
        found = [0]
        for step in range(4):
            found.append(pl.multiple_of(found[step] + bits[order[step]] * (PART >> (step + 1)), 16))
        offsets.append(found)

    def sum_copy(source, target, i, step, back):
        index = 8 * i + 4 * back + step
        return pltpu.make_async_remote_copy(
            src_ref=source,
            dst_ref=target,
            send_sem=sum_send.at[index],
            recv_sem=sum_recv.at[index],
            device_id=others[ORDERS[i][step]],
            device_id_type=MESH,
        )

    def scatter(i, step):
        size = PART >> (step + 1)
        away = pl.multiple_of(offsets[i][step] + (1 - bits[ORDERS[i][step]]) * size, 16)
        return sum_copy(
            parts_of[i].at[pl.ds(away, size)], got.at[i, pl.ds(STEP_ROWS[step], size)], i, step, 0
        )

    def gather(i, step):
        at = pl.ds(offsets[i][step + 1], PART >> (step + 1))
        return sum_copy(parts_of[i].at[at], parts_of[i].at[at], i, step, 1)

    def hand_back(i, step):
        pl.semaphore_wait(sum_free.at[4 * i + step], 1)
        gather(i, step).start()

    def advance(i, step):
        scatter(i, step).wait()

        @pl.loop(0, (PART >> (step + 1)) // CHUNK)
        def _(index):
            own = pl.ds(pl.multiple_of(offsets[i][step + 1] + index * CHUNK, 16), CHUNK)
            came = got[i, pl.ds(pl.multiple_of(STEP_ROWS[step] + index * CHUNK, 16), CHUNK), :]
            parts_of[i][own, :] = (parts_of[i][own, :].astype(F32) + came.astype(F32)).astype(BF16)

        pl.semaphore_signal(
            sum_free.at[4 * i + step],
            inc=1,
            device_id=others[ORDERS[i][step]],
            device_id_type=MESH,
        )
        if step < 3:
            scatter(i, step + 1).start()
        else:
            hand_back(i, 3)

    def retreat(i, step):
        gather(i, step).wait()
        if step > 0:
            hand_back(i, step - 1)

    def late_copy(source, target, device, index):
        return pltpu.make_async_remote_copy(
            src_ref=source,
            dst_ref=target,
            send_sem=late_send.at[index],
            recv_sem=late_recv.at[index],
            device_id=device,
            device_id_type=MESH,
        )

    up_copy = send(upstream, up_halves.at[narrow], partner, 0)
    up_copy.start()

    row = lax.broadcasted_iota(jnp.int32, (D, 384), 0)
    lane = lax.broadcasted_iota(jnp.int32, (D, 384), 1)
    step = jnp.where(lane >= 96, 96, 0) + jnp.where(lane >= 192, 96, 0) + jnp.where(lane >= 288, 96, 0)
    select = mask(row == lane + step + narrow * 96)
    for name in ("valueright", "shaperight", "valueleft", "shapeleft"):
        loads[name].wait()
    right_half = mm(hid[0, 0:192, :], select).astype(BF16)
    shape_half = mm(hid[0, 192:384, :], select).astype(BF16)
    for b in range(4):
        kept = between(384, 96 * b, 96 * b + 96)
        w_first[192 * b : 192 * b + 192, 0:384] = right_half * kept
        w_first[192 * b : 192 * b + 192, 384:768] = shape_half * kept
    row = lax.broadcasted_iota(jnp.int32, (D, 2 * PAD), 0)
    lane = lax.broadcasted_iota(jnp.int32, (D, 2 * PAD), 1)
    group = jnp.where(lane >= PAD, 1, 0)
    entry = lane - PAD * group
    spread = mask((row == (2 * narrow + group) * 192 + entry) & (entry < 192))
    for source, target in ((0, w_value), (192, w_shape)):
        wider = mm(hid[1, source : source + 192, :], spread).astype(BF16)
        for b in range(4):
            for k in range(2):
                target[96 * b + 48 * k : 96 * b + 48 * k + 48, :] = wider[
                    48 * b : 48 * b + 48, :
                ] * between(2 * PAD, PAD * k, PAD * k + PAD)
    row = lax.broadcasted_iota(jnp.int32, (D, 192), 0)
    lane = lax.broadcasted_iota(jnp.int32, (D, 192), 1)
    start = (2 * narrow) * 192 + (1 - narrow) * 96
    cross = mask(row == start + lane + jnp.where(lane >= 96, 96, 0))
    for i in range(2):
        part = mm(hid[0, 192 * i : 192 * i + 192, :], cross).astype(BF16)
        for b in range(2):
            w_cross[i, 192 * b : 192 * b + 192, :] = part * between(192, 96 * b, 96 * b + 96)
    first = vectors[0:1, :]
    shift_first = vectors[1:2, :]

    coarse = vectors[...].astype(BF16)
    fine = (vectors[...] - coarse.astype(F32)).astype(BF16)
    through[...] = mm(coarse, w_first[...]) + mm(fine, w_first[...])
    loads["inputs"].wait()

    @pl.loop(0, tiles)
    def _(index):
        at = tile_rows(index)
        values = inputs[at, :].astype(F32)
        average = jnp.mean(values, axis=-1, keepdims=True)
        center = values - average
        inverse = lax.rsqrt(jnp.mean(center * center, axis=-1, keepdims=True) + EPSILON)
        hat = center * inverse
        stats[at, 0:1] = average
        stats[at, 1:2] = inverse
        normed = (hat * first + shift_first).astype(BF16)
        norm_one[at, :] = normed
        inner = mm(normed, w_first[...]).astype(BF16)
        inner_one[at, :] = inner
        signal = mm(inner[:, :384], w_value[...]).astype(BF16)
        sig_halves[0, at, :] = signal[:, :PAD]
        sig_halves[1, at, :] = signal[:, PAD:]
        shaped = mm(inner[:, 384:], w_shape[...])
        shaping[0, at, :] = shaped[:, :PAD]
        shaping[1, at, :] = shaped[:, PAD:]

    sig_copy = send(sig_halves.at[1 - core], sig_rows.at[core], sibling, 1)
    sig_copy.start()
    sig_rows[core] = sig_halves[core]

    row = lax.broadcasted_iota(jnp.int32, (D, PAD), 0)
    lane = lax.broadcasted_iota(jnp.int32, (D, PAD), 1)
    pick = mask((row == quarter * 192 + lane) & (lane < 192))
    conv = mm(coarse, pick) + mm(fine, pick)
    loads["filterout"].wait()
    own_out[...] = mm(factor_gate[0, 0:128, :].astype(BF16), pick).astype(BF16)
    pos_bias = filter_vectors[8:9, :]
    mid_bias = filter_vectors[9:10, :]
    frequency = filter_vectors[10:11, :]
    mid_high = midweight[...].astype(BF16)
    mid_low = (midweight[...] - mid_high.astype(F32)).astype(BF16)
    pos_high = filter_vectors[0:8, :].astype(BF16).astype(F32)
    pos_parts = jnp.concatenate(
        [pos_high, pos_high, filter_vectors[0:8, :] - pos_high, jnp.zeros((8, 128), F32)], axis=0
    ).astype(BF16)
    ranks = 5 * (quarter * 192 + lanes(PAD))
    for bound in range(5):
        ranks = jnp.where(ranks >= D, ranks - D, ranks)
    lowest = math.log(0.25 / length)
    highest = math.log(1.0 / 30.0)
    rate = jnp.exp(lowest + ranks.astype(F32) * (1.0 / D) * (highest - lowest))
    loud = jnp.sqrt(2.0 * rate)

    def decay(index):
        places = (lax.broadcasted_iota(jnp.int32, (TILE, PAD), 0) + index * TILE).astype(F32)
        return jnp.exp(-rate * places) * loud

    @pl.loop(0, spans)
    def _(index):
        at = tile_rows(index)
        one = mm(place_parts[at, :], pos_parts) + pos_bias
        sine, cosine = sine_cosine(frequency * one)
        high = sine.astype(BF16)
        low = (sine - high.astype(F32)).astype(BF16)
        lin_one[at, :] = one.astype(BF16)
        act_one[at, :] = high
        cos_one[at, :] = cosine.astype(BF16)
        two = mm(high, mid_high) + mm(low, mid_high) + mm(high, mid_low) + mid_bias
        sine, cosine = sine_cosine(frequency * two)
        high = sine.astype(BF16)
        lin_two[at, :] = two.astype(BF16)
        act_two[at, :] = high
        cos_two[at, :] = cosine.astype(BF16)
        short[at, :] = (mm(high, own_out[...]) * decay(index)).astype(BF16)

    loads["cos"].wait()
    loads["sin"].wait()

    @pl.loop(0, spans)
    def _(index):
        at = tile_rows(index)
        real = mm(table_cos[at, :], short[...])
        imag = mm(table_sin[at, :], short[...])
        turn_cos = place[at, 5:6] * (1.0 / length)
        turn_sin = place[at, 6:7] * (1.0 / length)
        fil_spec[0, at, :] = real * turn_cos + imag * turn_sin
        fil_spec[1, at, :] = imag * turn_cos - real * turn_sin

    for name in ("outright", "outleft", "gateright", "liftright", "lowerleft", "lower_top", "lower_end"):
        loads[name].wait()
    out_half = d_gate[0, 0:192, own_half]
    w_out_first[0:192, :] = out_half * between(384, 0, 192)
    w_out_first[192:256, :] = jnp.zeros((64, 384), BF16)
    w_out_first[256:448, :] = out_half * between(384, 192, 384)
    w_out_first[448:512, :] = jnp.zeros((64, 384), BF16)
    for b in range(4):
        for k in range(4):
            w_out_second[b // 2, 192 * (b % 2) + 48 * k : 192 * (b % 2) + 48 * k + 48, :] = d_gate[
                0, 192 + 48 * b : 240 + 48 * b, :
            ] * between(D, 192 * k, 192 * k + 192)
    lane = lanes(384)
    inside = lane - jnp.where(lane >= 192, 192, 0)
    for b in range(4):
        kept = mask((inside >= 48 * b) & (inside < 48 * b + 48))
        w_glu[192 * b : 192 * b + 192, 0:384] = d_lift[1, 96:288, 0:384] * kept
        w_glu[192 * b : 192 * b + 192, 384:768] = d_lift[1, 96:288, 384:768] * kept
    for target in (w_gate, w_lift):
        target[0, 192:256, :] = jnp.zeros((64, D), BF16)
        target[1, 0:64, :] = jnp.zeros((64, D), BF16)
    w_lower[0, 0:512, :] = d_lift[0, :, 0:256] * between(256, 0, 192)
    w_lower[0, 512:768, :] = d_lift[0, 0:256, 384:640] * between(256, 0, 192)
    w_lower[1, 0:512, :] = d_lift[0, :, 128:384] * between(256, 64, 256)
    w_lower[1, 512:768, :] = d_lift[0, 0:256, 512:768] * between(256, 64, 256)
    for b in range(2):
        for k in range(4):
            w_lower_second[192 * b + 48 * k : 192 * b + 48 * k + 48, :] = d_lift[
                1, 48 * b : 48 * b + 48, :
            ] * between(D, 192 * k, 192 * k + 192)

    sig_copy.wait_recv()
    sig_pad[0:8, :] = jnp.zeros((8, PAD), F32)
    for part in range(2):
        sig_pad[8 + part * rows : 8 + part * rows + rows, :] = sig_rows[part].astype(F32)
    for index in range(spans):
        start = 8 + index * TILE
        total = conv[4:5, :] * sig_pad[start : start + TILE, :]
        total += conv[5:6, :] * sig_pad[start - 1 : start - 1 + TILE, :]
        total += conv[6:7, :] * sig_pad[start - 2 : start - 2 + TILE, :]
        short[index * TILE : index * TILE + TILE, :] = total.astype(BF16)

    @pl.loop(0, spans)
    def _(index):
        at = tile_rows(index)
        real = mm(table_cos[at, :], short[...])
        imag = mm(table_sin[at, :], short[...])
        sig_spec[0, at, :] = real.astype(BF16)
        sig_spec[1, at, :] = imag.astype(BF16)
        fil_re = fil_spec[0, at, :]
        fil_im = fil_spec[1, at, :]
        prod_spec[0, at, :] = (real * fil_re - imag * fil_im).astype(BF16)
        prod_spec[1, at, :] = (real * fil_im + imag * fil_re).astype(BF16)

    per_half = rows // TILE

    @pl.loop(0, spans)
    def _(index):
        at = tile_rows(index)
        result = mm(table_cos[at, :], prod_spec[0]) + mm(table_sin[at, :], prod_spec[1])
        long_rows[index // per_half, tile_rows(lax.rem(index, per_half)), :] = result.astype(BF16)

    long_copy = send(long_rows.at[1 - core], long_halves.at[core], sibling, 2)
    long_copy.start()
    long_halves[core] = long_rows[core]
    long_copy.wait_recv()
    sig_copy.wait_send()
    long_copy.wait_send()

    def inner_copy(index):
        at = tile_rows(index)
        return send(inner_out.at[narrow, at], inner_out.at[narrow, at], partner, 3 + index)

    dn_copy = send(dn_send, dn_recv, partner, 5)
    own_rows = tile_rows(narrow)
    cross_copy = send(cross_send, d_inner_out.at[own_rows], partner, 6)
    middle_copy = send(mid_send, mid_recv, partner, 11)

    def part_copy(index):
        at = tile_rows(index)
        return send(part_send.at[at], part_recv.at[at], partner, 7 + index)

    def shape_copy(index):
        at = tile_rows(index)
        return send(shape_send.at[at], shape_recv.at[at], partner, 12 + index)

    def value_copy(index):
        at = tile_rows(index)
        return send(value_send.at[at], value_recv.at[at], partner, 14 + index)

    def first_other(index):
        return 1 - narrow + index * (2 * narrow - 1)

    @pl.loop(0, tiles)
    def _(order):
        index = narrow + order * (1 - 2 * narrow)
        at = tile_rows(index)
        inner = None
        for k in range(2):
            product = (shaping[k, at, :] * long_halves[k, at, :].astype(F32)).astype(BF16)
            term = mm(product, w_out_first[k * PAD : k * PAD + PAD, :])
            inner = term if inner is None else inner + term
        inner_out[narrow, at, :] = inner.astype(BF16)

        @pl.when(order == 1)
        def _():
            inner_copy(narrow).wait_send()

        inner_copy(index).start()

    up_copy.wait_recv()
    for k in range(2):
        loads["gate", k].wait()
        loads["lift", k].wait()
    loads["upstream"].wait()

    gain_second = vectors[2:3, :]
    shift_second = vectors[3:4, :]

    @pl.loop(0, tiles)
    def _(order):
        index = first_other(order)
        at = tile_rows(index)
        inner_copy(index).wait_recv()
        mid = inputs[at, :].astype(F32)
        mid += mm(inner_out[0, at, :], w_out_second[0])
        mid += mm(inner_out[1, at, :], w_out_second[1])
        dn_own[...] = mid
        center = mid - jnp.mean(mid, axis=-1, keepdims=True)
        inverse = lax.rsqrt(jnp.mean(center * center, axis=-1, keepdims=True) + EPSILON)
        hat = center * inverse
        hat_two[...] = hat
        stats[0:TILE, 2:3] = inverse
        normed = (hat * gain_second + shift_second).astype(BF16)
        norm_two[at, :] = normed
        inner = mm(normed, w_glu[...]).astype(BF16)
        inner_glu[at, :] = inner
        lower = [None, None]
        for k in range(2):
            for columns in (slice(0, 256), slice(256, 512), slice(512, 768)):
                gate = mm(inner[:, 128 * k : 128 * k + 256], w_gate[k, :, columns])
                lift = mm(inner[:, 384 + 128 * k : 384 + 128 * k + 256], w_lift[k, :, columns])
                cumulative = 0.5 * (1.0 + lax.erf(gate * (1.0 / math.sqrt(2.0))))
                density = jnp.exp(-0.5 * gate * gate) * (1.0 / math.sqrt(2.0 * math.pi))
                activated = gate * cumulative
                unit = (activated * lift).astype(BF16)
                hid[k, at, columns] = unit
                factor_lift[k, :, columns] = activated
                factor_gate[k, :, columns] = lift * (cumulative + gate * density)
                term = mm(unit, w_lower[k, columns, :])
                lower[k] = term if lower[k] is None else lower[k] + term
        inner_low = join(*lower).astype(BF16)
        inner_lower[at, :] = inner_low
        out_own[at, :] = dn_own[:, own_half] + mm(inner_low, w_lower_second[:, own_half])
        part_send[at, :] = mm(inner_low, w_lower_second[:, other_half]).astype(BF16)

        above = jnp.concatenate([up_halves[0, at, :], up_halves[1, at, :]], axis=1)
        d_low = mm_nt(above, w_lower_second[...]).astype(BF16)
        d_inner_lower[at, :] = d_low
        gates = [None, None]
        lifts = [None, None]
        for k in range(2):
            for columns in (slice(0, 256), slice(256, 512), slice(512, 768)):
                d_hidden = mm_nt(d_low[:, 128 * k : 128 * k + 256], w_lower[k, columns, :])
                to_gate = (d_hidden * factor_gate[k, :, columns]).astype(BF16)
                to_lift = (d_hidden * factor_lift[k, :, columns]).astype(BF16)
                d_gate[k, at, columns] = to_gate
                d_lift[k, at, columns] = to_lift
                term = mm_nt(to_gate, w_gate[k, :, columns])
                gates[k] = term if gates[k] is None else gates[k] + term
                term = mm_nt(to_lift, w_lift[k, :, columns])
                lifts[k] = term if lifts[k] is None else lifts[k] + term
        d_glu = jnp.concatenate([join(*gates), join(*lifts)], axis=1).astype(BF16)
        d_inner_glu[at, :] = d_glu
        into = mm_nt(d_glu, w_glu[...])
        dn_own[...] = into

        @pl.when(order == 0)
        def _():
            dn_send[...] = dn_own[...].astype(BF16)
            dn_copy.start()

    low_lanes = lanes(128) < 64
    for columns in (slice(0, 384), slice(384, 768)):
        columns_at = slice(LOWER_RIGHT + columns.start, LOWER_RIGHT + columns.stop)
        parts = [
            mm_tn(hid[k, :, columns], d_inner_lower[:, 128 * k : 128 * k + 256]) for k in range(2)
        ]
        sums_channel[columns_at, 0:128] = parts[0][:, 0:128].astype(BF16)
        sums_channel[columns_at, 128:256] = jnp.where(
            low_lanes, parts[0][:, 128:256], parts[1][:, 0:128]
        ).astype(BF16)
        sums_channel[columns_at, 256:384] = parts[1][:, 128:256].astype(BF16)
    scatter(0, 0).start()
    for side in range(2):
        columns = slice(384 * side, 384 * side + 384)
        folded = fold(mm_tn(inner_lower[...], up_halves[side]), side)
        for b in range(2):
            first_row = LOWER_LEFT + 96 * side + 48 * b
            sums_channel[first_row : first_row + 48, :] = folded[b].astype(BF16)
    for offset, target in ((0, GATE_RIGHT), (384, LIFT_RIGHT)):
        whole = mm_tn(norm_two[...], d_inner_glu[:, offset : offset + 384])
        total = None
        for b in range(4):
            term = whole[192 * b : 192 * b + 192, :] * mask(
                (inside >= 48 * b) & (inside < 48 * b + 48), F32
            )
            total = term if total is None else total + term
        sums_channel[target : target + 192, :] = total.astype(BF16)

    for offset, upper, target in ((0, d_gate, GATE_LEFT), (384, d_lift, LIFT_LEFT)):
        for k in range(2):
            for start in (0, 384):
                whole = mm_tn(
                    inner_glu[:, offset + 128 * k : offset + 128 * k + 256],
                    upper[k, :, start : start + 384],
                )
                first_row = target + 384 * k + start // 2
                sums_channel[first_row : first_row + 192, :] = whole[
                    64 * k : 64 * k + 192, :
                ].astype(BF16)
        if upper is d_gate:
            scatter(1, 0).start()
    sums_channel[2880:3072, :] = jnp.zeros((192, 384), BF16)
    scatter(2, 0).start()
    scatter(3, 0).start()

    dn_copy.wait_recv()
    into = dn_own[...] + dn_recv[...].astype(F32)
    hat = hat_two[...]
    gain_sums[...] = jnp.zeros(gain_sums.shape, F32)
    gain_sums[0:1, :] = jnp.sum(into * hat, axis=0, keepdims=True)
    gain_sums[1:2, :] = jnp.sum(into, axis=0, keepdims=True)
    scaled = into * gain_second
    above = jnp.concatenate([up_halves[0, own_rows, :], up_halves[1, own_rows, :]], axis=1)
    d_mid = above.astype(F32) + stats[0:TILE, 2:3] * (
        scaled
        - jnp.mean(scaled, axis=-1, keepdims=True)
        - hat * jnp.mean(scaled * hat, axis=-1, keepdims=True)
    )
    hat_two[...] = d_mid
    branch[...] = d_mid.astype(BF16)
    cross_send[...] = mm_nt(branch[...], w_out_second[1 - narrow]).astype(BF16)
    cross_copy.start()
    mid_send[...] = hat_two[:, other_half].astype(BF16)
    d_inner_out[own_rows, :] = mm_nt(branch[...], w_out_second[narrow]).astype(BF16)
    for i in range(4):
        advance(i, 0)
    for h in range(2):
        for side in range(2):
            columns = slice(384 * side, 384 * side + 384)
            folded = fold(mm_tn(inner_out[h, own_rows, :], branch[:, columns]), side)
            for b in range(2):
                first_row = OUT_LEFT + 192 * h + 96 * side + 48 * b
                mixer_slab[first_row : first_row + 48, :] = folded[b].astype(BF16)

    @pl.loop(0, tiles)
    def _(order):
        index = narrow + order * (1 - 2 * narrow)
        at = tile_rows(index)

        @pl.when(order == 1)
        def _():
            cross_copy.wait_recv()
            middle_copy.start()

        d_inner = d_inner_out[at, :]
        for k in range(2):
            d_mixed = mm_nt(d_inner, w_out_first[k * PAD : k * PAD + PAD, :])
            d_shaping[k, at, :] = (d_mixed * long_halves[k, at, :].astype(F32)).astype(BF16)
            sig_halves[k, at, :] = (d_mixed * shaping[k, at, :]).astype(BF16)

    dl_copy = send(sig_halves.at[1 - core], dl_rows.at[core], sibling, 9)
    dl_copy.start()
    dl_rows[core] = sig_halves[core]

    @pl.loop(0, tiles)
    def _(index):
        at = tile_rows(index)
        to_shape = jnp.concatenate([d_shaping[0, at, :], d_shaping[1, at, :]], axis=1)
        d_inner_one[at, 384:768] = mm_nt(to_shape, w_shape[...]).astype(BF16)
        shape_send[at, :] = mm_nt(
            to_shape, w_shape[pl.ds(pl.multiple_of((1 - narrow) * 192, 192), 192), :]
        ).astype(BF16)
        shape_copy(index).start()

    @pl.loop(0, tiles)
    def _(index):
        part_copy(index).start()

    advance(1, 1)
    advance(0, 1)

    lane = lax.broadcasted_iota(jnp.int32, (2 * PAD, 384), 1)
    row = lax.broadcasted_iota(jnp.int32, (2 * PAD, 384), 0)
    squeeze = mask(row == lane + jnp.where(lane >= 192, 64, 0))

    def first_gradient(offset):
        whole = mm_tn(norm_one[...], d_inner_one[:, offset : offset + 384])
        total = None
        for b in range(4):
            term = whole[192 * b : 192 * b + 192, :] * between(384, 96 * b, 96 * b + 96, F32)
            total = term if total is None else total + term
        return total.astype(BF16)

    def second_gradient(offset, upper):
        above = jnp.concatenate([upper[0], upper[1]], axis=1)
        whole = mm_tn(inner_one[:, offset : offset + 384], above)
        pieces = []
        for b in range(4):
            total = None
            for k in range(2):
                term = whole[96 * b + 48 * k : 96 * b + 48 * k + 48, :] * between(
                    2 * PAD, PAD * k, PAD * k + PAD, F32
                )
                total = term if total is None else total + term
            pieces.append(total)
        return mm(jnp.concatenate(pieces, axis=0).astype(BF16), squeeze).astype(BF16)

    mixer_slab[SHAPE_RIGHT : SHAPE_RIGHT + 192, :] = first_gradient(384)
    mixer_slab[SHAPE_LEFT : SHAPE_LEFT + 192, :] = second_gradient(384, d_shaping)
    scatter(4, 0).start()
    parts = []
    for k in range(2):
        product = (shaping[k] * long_halves[k].astype(F32)).astype(BF16)
        parts.append(mm_tn(product, d_inner_out[...]))
    late[OUT_RIGHT : OUT_RIGHT + 192, :] = jnp.where(
        lanes(384) < 192, parts[0][0:192, :], parts[1][0:192, :]
    ).astype(BF16)
    advance(2, 1)
    advance(1, 2)
    advance(0, 2)

    dl_copy.wait_recv()

    @pl.loop(0, spans)
    def _(index):
        at = tile_rows(index)
        upper = dl_rows[...].reshape(length, PAD)
        real = mm(table_cos[at, :], upper)
        imag = mm(table_sin[at, :], upper)
        fil_re = fil_spec[0, at, :]
        fil_im = fil_spec[1, at, :]
        prod_spec[0, at, :] = (real * fil_re + imag * fil_im).astype(BF16)
        prod_spec[1, at, :] = (imag * fil_re - real * fil_im).astype(BF16)
        sig_re = sig_spec[0, at, :].astype(F32)
        sig_im = sig_spec[1, at, :].astype(F32)
        turn_cos = place[at, 5:6] * (1.0 / length)
        turn_sin = place[at, 6:7] * (1.0 / length)
        both_re = real * sig_re + imag * sig_im
        both_im = imag * sig_re - real * sig_im
        sig_spec[0, at, :] = (both_re * turn_cos - both_im * turn_sin).astype(BF16)
        sig_spec[1, at, :] = (both_im * turn_cos + both_re * turn_sin).astype(BF16)

    advance(4, 0)
    advance(3, 1)
    advance(1, 3)
    advance(2, 2)
    advance(0, 3)
    ds_pad[length : length + 8, :] = jnp.zeros((8, PAD), F32)

    @pl.loop(0, spans)
    def _(index):
        at = tile_rows(index)
        result = mm(table_cos[at, :], prod_spec[0]) + mm(table_sin[at, :], prod_spec[1])
        ds_pad[at, :] = result.astype(BF16).astype(F32)

    for index in range(spans):
        start = index * TILE
        total = conv[4:5, :] * ds_pad[start : start + TILE, :]
        total += conv[5:6, :] * ds_pad[start + 1 : start + 1 + TILE, :]
        total += conv[6:7, :] * ds_pad[start + 2 : start + 2 + TILE, :]
        part, inner_start = divmod(start, rows)
        long_rows[part, inner_start : inner_start + TILE, :] = total.astype(BF16)
    ds_copy = send(long_rows.at[1 - core], ds_halves.at[core], sibling, 10)
    ds_copy.start()
    ds_halves[core] = long_rows[core]

    advance(3, 2)
    advance(2, 3)
    retreat(1, 3)
    retreat(0, 3)
    grad_vectors[...] = jnp.zeros(grad_vectors.shape, F32)
    sums = [jnp.zeros((1, PAD), F32) for _ in range(3)]
    for index in range(spans):
        start = index * TILE
        upper = ds_pad[start : start + TILE, :]
        for j in range(3):
            sums[j] += jnp.sum(
                upper * sig_pad[8 + start - j : 8 + start - j + TILE, :], axis=0, keepdims=True
            )
    sums = jnp.concatenate(sums + [jnp.zeros((5, PAD), F32)], axis=0)
    lane = lax.broadcasted_iota(jnp.int32, (PAD, 384), 1)
    row = lax.broadcasted_iota(jnp.int32, (PAD, 384), 0)
    place_core = mask((lane == core * 192 + row) & (row < 192))
    conv_sums = mm(sums.astype(BF16), place_core)
    grad_vectors[4:7, :] = conv_sums[0:3, :]

    d_lin[...] = jnp.zeros(d_lin.shape, F32)
    grad_filter[...] = jnp.zeros(grad_filter.shape, F32)

    def filter_back(index):
        at = tile_rows(index)
        d_taps = mm(table_cos[at, :], sig_spec[0]) + mm(table_sin[at, :], sig_spec[1])
        d_mod = d_taps * decay(index)
        d_mod = d_mod.astype(BF16)
        d_lin[...] += mm_tn(act_two[at, :], d_mod)
        two = mm_nt(d_mod, own_out[...]) * cos_two[at, :].astype(F32)
        scaled_two = two * frequency
        coarse_two = scaled_two.astype(BF16)
        grad_filter[0:128, :] += mm_tn(act_one[at, :], coarse_two)
        one = mm_nt(coarse_two, mid_high) * cos_one[at, :].astype(F32)
        scaled_one = one * frequency
        grad_filter[128:136, :] += mm_tn(place_parts[at, :], scaled_one.astype(BF16))[0:8, :]
        grad_filter[136:137, :] += jnp.sum(scaled_one, axis=0, keepdims=True)
        grad_filter[137:138, :] += jnp.sum(scaled_two, axis=0, keepdims=True)
        grad_filter[138:139, :] += jnp.sum(
            one * lin_one[at, :].astype(F32) + two * lin_two[at, :].astype(F32), axis=0, keepdims=True
        )

    pl.loop(0, spans // 2)(filter_back)
    advance(4, 1)
    retreat(1, 2)
    pl.loop(spans // 2, spans)(filter_back)
    late[FILTER_OUT : FILTER_OUT + 128, :] = mm(d_lin[...].astype(BF16), place_core).astype(BF16)
    for i in range(3):
        late[FILTER : FILTER + 48, 128 * i : 128 * i + 128] = grad_filter[
            48 * i : 48 * i + 48, :
        ].astype(BF16)


    advance(4, 2)
    advance(3, 3)
    retreat(0, 2)
    retreat(2, 3)

    ds_copy.wait_recv()
    other_blocks = pl.ds(pl.multiple_of((1 - narrow) * 192, 192), 192)

    @pl.loop(0, tiles)
    def _(index):
        at = tile_rows(index)
        to_value = jnp.concatenate([ds_halves[0, at, :], ds_halves[1, at, :]], axis=1)
        d_inner = mm_nt(to_value, w_value[...]).astype(BF16)
        d_inner_one[at, 0:384] = d_inner
        against = inner_one[at, :].astype(F32) - through[1:2, :]
        d_inner = d_inner_one[at, :].astype(F32)
        plain = jnp.sum(d_inner * through[0:1, :], axis=-1, keepdims=True)
        along = jnp.sum(d_inner * against, axis=-1, keepdims=True)
        stats[at, 2:3] = plain
        stats[at, 3:4] = along
        lane = lanes(128)
        tail = jnp.where(lane == 64, plain, jnp.where(lane == 65, along, 0.0))
        away = mm_nt(to_value, w_value[other_blocks, :])
        value_send[at, 0:128] = away[:, 0:128].astype(BF16)
        value_send[at, 128:192] = away[:, 128:192].astype(BF16)
        value_send[at, 192:256] = tail[:, 64:128].astype(BF16)
        value_copy(index).start()

    @pl.loop(0, tiles)
    def _(index):
        at = tile_rows(index)
        into = mm_nt(d_inner_one[at, :], w_first[...])
        hat = (inputs[at, :].astype(F32) - stats[at, 0:1]) * stats[at, 1:2]
        gain_sums[2:3, :] += jnp.sum(into * hat, axis=0, keepdims=True)
        gain_sums[3:4, :] += jnp.sum(into, axis=0, keepdims=True)

    advance(4, 3)
    retreat(3, 3)
    late[VALUE_RIGHT : VALUE_RIGHT + 192, :] = first_gradient(0)
    late[VALUE_LEFT : VALUE_LEFT + 192, :] = second_gradient(0, ds_halves)
    grad_vectors[0:4, :] = gain_sums[0:4, 0:384]
    grad_vectors[8:12, :] = gain_sums[0:4, 384:768]
    late[VECTORS : VECTORS + 16, :] = grad_vectors[...].astype(BF16)

    to_core = late_copy(
        late.at[pl.ds(pl.multiple_of((1 - core) * 384, 16), 384)], late_core, sibling, 0
    )
    to_core.start()
    retreat(4, 3)
    to_core.wait()

    @pl.loop(0, 384 // CHUNK)
    def _(index):
        at = pl.ds(pl.multiple_of(core * 384 + index * CHUNK, 16), CHUNK)
        came = late_core[pl.ds(pl.multiple_of(index * CHUNK, 16), CHUNK), :]
        late[at, :] = (late[at, :].astype(F32) + came.astype(F32)).astype(BF16)

    def share(t):
        return pl.multiple_of(core * 384 + lax.rem(chip + 8 - t, 8) * CHUNK, 16)

    direct = [
        late_copy(late.at[pl.ds(share(8 - t), CHUNK)], late_slots.at[t - 1], fellows[t], t)
        for t in range(1, 8)
    ]
    for copy in direct:
        copy.start()

    first_half = vectors[0:1, own_half]
    middle_copy.wait_recv()
    d_middle[own_rows, :] = hat_two[:, own_half]
    d_middle[tile_rows(1 - narrow), :] = mid_recv[...].astype(F32)
    @pl.loop(0, tiles)
    def _(index):
        at = tile_rows(index)
        part_copy(index).wait_recv()
        hidden_out[at, :] = (out_own[at, :] + part_recv[at, :].astype(F32)).astype(BF16)
        shape_copy(index).wait_recv()
        value_copy(index).wait_recv()
        into = mm_nt(d_inner_one[at, :], w_first[own_half, :])
        into += mm_nt(value_recv[at, 0:192], w_cross[0])
        into += mm_nt(shape_recv[at, :], w_cross[1])
        plain = (stats[at, 2:3] + value_recv[at, 192:193].astype(F32)) * (1.0 / D)
        along = (stats[at, 3:4] + value_recv[at, 193:194].astype(F32)) * (1.0 / D)
        hat = (inputs[at, own_half].astype(F32) - stats[at, 0:1]) * stats[at, 1:2]
        hidden_grad[at, :] = (
            d_middle[at, :] + stats[at, 1:2] * (into * first_half - plain - hat * along)
        ).astype(BF16)

    retreat(4, 2)
    retreat(1, 1)
    retreat(0, 1)
    total = late[pl.ds(share(0), CHUNK), :].astype(F32)
    for t in range(1, 8):
        direct[t - 1].wait()
        total += late_slots[t - 1].astype(F32)
    own_share = pl.ds(pl.multiple_of(PART + share(0), 16), CHUNK)
    mixer_slab[own_share, :] = total.astype(BF16)
    spread_out = [
        late_copy(mixer_slab.at[own_share], mixer_slab.at[own_share], fellows[t], 8 + t)
        for t in range(1, 8)
    ]
    for copy in spread_out:
        copy.start()
    retreat(4, 1)
    early_rows = pl.ds(offsets[4][1], PART // 2)
    across_early = late_copy(mixer_slab.at[early_rows], mixer_slab.at[early_rows], partner, 40)
    across_early.start()
    retreat(2, 2)
    retreat(3, 2)
    across = []
    along_own = []
    for t in range(8):
        if t > 0:
            spread_out[t - 1].wait()
        at = pl.ds(pl.multiple_of(PART + share(t), 16), CHUNK)
        across.append(late_copy(mixer_slab.at[at], mixer_slab.at[at], partner, 16 + t))
        across[t].start()
        along_own.append(late_copy(mixer_slab.at[at], mixer_slab.at[at], sibling, 24 + t))
        along_own[t].start()
    across_early.wait()
    other = sums_mixer.at[1 - narrow, early_rows]
    along_early = late_copy(other, other, sibling, 41)
    along_early.start()
    retreat(2, 1)
    along_other = []
    for t in range(8):
        across[t].wait()
        at = pl.ds(pl.multiple_of(PART + share(t), 16), CHUNK)
        other = sums_mixer.at[1 - narrow, at]
        along_other.append(late_copy(other, other, sibling, 32 + t))
        along_other[t].start()
    retreat(3, 1)
    for i in range(5):
        retreat(i, 0)
    for copy in along_own + along_other + [along_early]:
        copy.wait()

    inner_copy(1 - narrow).wait_send()
    for copy in (up_copy, dl_copy, ds_copy, dn_copy, cross_copy, middle_copy):
        copy.wait_send()

    @pl.loop(0, tiles)
    def _(index):
        for copy in (part_copy, shape_copy, value_copy):
            copy(index).wait_send()


def finish_kernel(
    hidden_in,
    hidden_grad_in,
    hbm_channel,
    hbm_mixer,
    hidden_out,
    hidden_grad,
    grad_gainfirst,
    grad_shiftfirst,
    grad_valueright,
    grad_valueleft,
    grad_shaperight,
    grad_shapeleft,
    grad_convtaps,
    grad_posweight,
    grad_posbias,
    grad_sinefreq,
    grad_midweight,
    grad_midbias,
    grad_filterout,
    grad_outright,
    grad_outleft,
    grad_gainsecond,
    grad_shiftsecond,
    grad_gateright,
    grad_gateleft,
    grad_liftright,
    grad_liftleft,
    grad_lowerright,
    grad_lowerleft,
    channel,
    mixer,
    gateright,
    gateleft,
    liftright,
    liftleft,
    lowerright,
    lowerleft,
    both_filter,
    in_sem,
    out_sem,
):
    ins = []
    outs = []

    def fetch(source, target):
        ins.append(pltpu.make_async_copy(source, target, in_sem.at[len(ins)]))
        ins[-1].start()

    def store(source, target):
        outs.append(pltpu.make_async_copy(source, target, out_sem.at[len(outs)]))
        outs[-1].start()

    for i in range(4):
        at = pl.ds(PART * i, PART)
        fetch(hbm_channel.at[at], channel.at[at])
    fetch(hbm_mixer, mixer)
    hidden_out[...] = hidden_in[...]
    hidden_grad[...] = hidden_grad_in[...]

    ins[0].wait()
    lowerright[...] = channel[LOWER_RIGHT : LOWER_RIGHT + D, :].astype(F32)
    store(lowerright, grad_lowerright)
    ins[1].wait()
    for h in range(2):
        columns = slice(384 * h, 384 * h + 384)
        lowerleft[:, columns] = channel[LOWER_LEFT + 96 * h : LOWER_LEFT + 96 * h + 96, :].astype(F32)
    gateright[...] = channel[GATE_RIGHT : GATE_RIGHT + 192, :].astype(F32)
    liftright[...] = channel[LIFT_RIGHT : LIFT_RIGHT + 192, :].astype(F32)
    store(lowerleft, grad_lowerleft)
    store(gateright, grad_gateright)
    store(liftright, grad_liftright)
    ins[2].wait()
    for i in range(4):
        first_row = GATE_LEFT + 192 * i
        gateleft[:, 384 * i : 384 * i + 384] = channel[first_row : first_row + 192, :].astype(F32)
    store(gateleft, grad_gateleft)
    ins[3].wait()
    for i in range(4):
        first_row = LIFT_LEFT + 192 * i
        liftleft[:, 384 * i : 384 * i + 384] = channel[first_row : first_row + 192, :].astype(F32)
    store(liftleft, grad_liftleft)
    ins[4].wait()

    lane = lax.broadcasted_iota(jnp.int32, (384, D), 1)
    row = lax.broadcasted_iota(jnp.int32, (384, D), 0)
    step = jnp.where(row >= 96, 96, 0) + jnp.where(row >= 192, 96, 0) + jnp.where(row >= 288, 96, 0)
    unselect = [mask(lane == row + step + 96 * h) for h in range(2)]
    for first_row, target in ((PART + VALUE_RIGHT, grad_valueright), (SHAPE_RIGHT, grad_shaperight)):
        target[...] = mm(mixer[0, first_row : first_row + 192, :], unselect[0]) + mm(
            mixer[1, first_row : first_row + 192, :], unselect[1]
        )
    for h in range(2):
        columns = slice(384 * h, 384 * h + 384)
        for first_row, target in (
            (PART + OUT_RIGHT, grad_outright),
            (SHAPE_LEFT, grad_shapeleft),
            (PART + VALUE_LEFT, grad_valueleft),
        ):
            target[:, columns] = mixer[h, first_row : first_row + 192, :].astype(F32)
        for side in range(2):
            at = slice(OUT_LEFT + 192 * h + 96 * side, OUT_LEFT + 192 * h + 96 * side + 96)
            grad_outleft[96 * h : 96 * h + 96, 384 * side : 384 * side + 384] = mixer[
                0, at, :
            ].astype(F32) + mixer[1, at, :].astype(F32)
    vectors = [mixer[h, PART + VECTORS : PART + VECTORS + 16, :].astype(F32) for h in range(2)]
    whole = jnp.concatenate(vectors, axis=1)
    both = vectors[0] + vectors[1]
    grad_convtaps[...] = whole[4:7, :]
    for i, target in enumerate((grad_gainsecond, grad_shiftsecond, grad_gainfirst, grad_shiftfirst)):
        target[...] = jnp.concatenate([both[i : i + 1, :], both[8 + i : 9 + i, :]], axis=1).reshape(D)
    for i in range(3):
        columns = slice(128 * i, 128 * i + 128)
        at = slice(PART + FILTER, PART + FILTER + 48)
        both_filter[48 * i : 48 * i + 48, :] = mixer[0, at, columns].astype(F32) + mixer[
            1, at, columns
        ].astype(F32)
    grad_midweight[...] = both_filter[0:128, :]
    grad_posweight[...] = both_filter[128:133, :]
    grad_posbias[...] = both_filter[136:137, :].reshape(128)
    grad_midbias[...] = both_filter[137:138, :].reshape(128)
    grad_sinefreq[...] = both_filter[138:139, :].reshape(128)
    count = grad_filterout.shape[0]
    first = (lax.axis_index("wide") * 2 + lax.axis_index("narrow")) * count
    total = jnp.zeros(grad_filterout.shape, F32)
    row = lax.broadcasted_iota(jnp.int32, (count, 384), 0)
    lane = lax.broadcasted_iota(jnp.int32, (count, 384), 1)
    for h in range(2):
        total += mm_nt(
            mask(lane + 384 * h == first + row),
            mixer[h, PART + FILTER_OUT : PART + FILTER_OUT + 128, :],
        )
    grad_filterout[...] = total
    for copy in outs:
        copy.wait()


def transform_tables(length):
    index = np.arange(length, dtype=np.float64) + 0.5
    angle = np.outer(index, index) * (math.pi / length)
    return (np.cos(angle).astype(jnp.bfloat16), np.sin(angle).astype(jnp.bfloat16))


def place_table(length):
    places = np.arange(length, dtype=np.float64)
    angle = places * (2.0 * math.pi / length)
    turn = (places + 0.5) * (math.pi / (2.0 * length))
    columns = [
        places / length,
        np.cos(angle),
        np.sin(angle),
        np.cos(2.0 * angle),
        np.sin(2.0 * angle),
        np.cos(turn),
        np.sin(turn),
        np.zeros(length),
    ]
    table = np.stack(columns, axis=1).astype(np.float32)
    feats = np.concatenate([table[:, :5], np.zeros((length, 3), np.float32)], axis=1)
    high = feats.astype(jnp.bfloat16)
    low = (feats - high.astype(np.float32)).astype(jnp.bfloat16)
    return (table, np.concatenate([high, low, high, np.zeros_like(high)], axis=1))


def pair_body(
    hidden_in,
    gainfirst,
    shiftfirst,
    valueright,
    valueleft,
    shaperight,
    shapeleft,
    convtaps,
    posweight,
    posbias,
    sinefreq,
    midweight,
    midbias,
    filterout,
    outright,
    outleft,
    gainsecond,
    shiftsecond,
    gateright,
    gateleft,
    liftright,
    liftleft,
    lowerright,
    lowerleft,
    grad_out,
):
    rows = hidden_in.shape[0]
    length = 2 * rows
    table_cos, table_sin = transform_tables(length)
    def out(extent, dtype=BF16):
        return jax.ShapeDtypeStruct(extent, dtype)

    def buf(*extent, dtype=BF16):
        return pltpu.VMEM(extent, dtype)

    vmem = pl.BlockSpec(memory_space=pltpu.VMEM)
    hbm = pl.BlockSpec(memory_space=pl.ANY)
    results = pl.pallas_call(
        whole_kernel,
        out_shape=(
            out((rows, 384)),
            out((rows, 384)),
            out((CHANNEL_ROWS, 384)),
            out((2, 2 * PART, 384)),
        ),
        in_specs=[hbm] * 4 + [vmem] * 12 + [hbm] * 13,
        out_specs=[vmem] * 4,
        scratch_shapes=[
            buf(rows, D),
            buf(length, length),
            buf(length, length),
            buf(8, D, dtype=F32),
            buf(16, 128, dtype=F32),
            buf(D, D),
            buf(384, 512),
            buf(384, 512),
            buf(512, 384),
            buf(2, 384, D),
            buf(D, D),
            buf(2, 256, D),
            buf(2, 256, D),
            buf(2, D, 256),
            buf(384, D),
            buf(2, rows, 384),
            buf(rows, 128, dtype=F32),
            buf(rows, D),
            buf(rows, D),
            buf(2, rows, PAD),
            buf(2, rows, PAD),
            buf(2, rows, PAD, dtype=F32),
            buf(length + 8, PAD, dtype=F32),
            buf(length, PAD),
            buf(length, 128),
            buf(length, 128),
            buf(length, 128),
            buf(length, 128),
            buf(length, 128),
            buf(length, 128),
            buf(2, length, PAD, dtype=F32),
            buf(2, length, PAD),
            buf(2, length, PAD),
            buf(2, rows, PAD),
            buf(2, rows, PAD),
            buf(2, rows, 384),
            buf(TILE, D, dtype=F32),
            buf(rows, D),
            buf(rows, D),
            buf(2, TILE, D, dtype=F32),
            buf(2, TILE, D, dtype=F32),
            buf(2, rows, D),
            buf(rows, 384),
            buf(rows, 384, dtype=F32),
            buf(rows, 384),
            buf(rows, 384),
            buf(rows, 384),
            buf(2, rows, D),
            buf(2, rows, D),
            buf(rows, D),
            buf(TILE, D, dtype=F32),
            buf(TILE, D),
            buf(TILE, D),
            buf(rows, 384),
            buf(2, rows, PAD),
            buf(2, rows, PAD),
            buf(length + 8, PAD, dtype=F32),
            buf(2, rows, PAD),
            buf(rows, D),
            buf(TILE, 384),
            buf(TILE, 384),
            buf(TILE, 384),
            buf(rows, 384, dtype=F32),
            buf(TILE, D),
            buf(rows, 192),
            buf(rows, 192),
            buf(rows, 256),
            buf(rows, 256),
            buf(2, 384, 192),
            buf(8, D, dtype=F32),
            buf(128, PAD, dtype=F32),
            buf(128, PAD),
            buf(16, 384, dtype=F32),
            buf(144, 128, dtype=F32),
            buf(8, D, dtype=F32),
            pltpu.SemaphoreType.DMA((16,)),
            pltpu.SemaphoreType.DMA((16,)),
            pltpu.SemaphoreType.DMA((20,)),
            buf(5, STEP_ROWS[4], 384),
            pltpu.SemaphoreType.DMA((40,)),
            pltpu.SemaphoreType.DMA((40,)),
            pltpu.SemaphoreType.REGULAR((20,)),
            buf(PART, 384),
            buf(PART // 2, 384),
            buf(7, CHUNK, 384),
            pltpu.SemaphoreType.DMA((42,)),
            pltpu.SemaphoreType.DMA((42,)),
        ],
        compiler_params=pltpu.CompilerParams(
            collective_id=0, has_side_effects=True, vmem_limit_bytes=63 * 1024 * 1024
        ),
    )(
        hidden_in,
        grad_out,
        table_cos,
        table_sin,
        *place_table(length),
        gainfirst,
        shiftfirst,
        gainsecond,
        shiftsecond,
        convtaps,
        posweight,
        posbias,
        midbias,
        sinefreq,
        midweight,
        filterout,
        valueright,
        valueleft,
        shaperight,
        shapeleft,
        outright,
        outleft,
        gateright,
        gateleft,
        liftright,
        liftleft,
        lowerright,
        lowerleft,
    )
    count = D // (lax.axis_size("wide") * lax.axis_size("narrow"))
    square = out((192, D), F32)
    grads = pl.pallas_call(
        finish_kernel,
        out_shape=(
            out((rows, 384)),
            out((rows, 384)),
            out((D,), F32),
            out((D,), F32),
            square,
            square,
            square,
            square,
            out((3, D), F32),
            out((5, 128), F32),
            out((128,), F32),
            out((128,), F32),
            out((128, 128), F32),
            out((128,), F32),
            out((count, 128), F32),
            square,
            square,
            out((D,), F32),
            out((D,), F32),
            out(gateright.shape, F32),
            out(gateleft.shape, F32),
            out(liftright.shape, F32),
            out(liftleft.shape, F32),
            out(lowerright.shape, F32),
            out(lowerleft.shape, F32),
        ),
        in_specs=[vmem] * 2 + [hbm] * 2,
        out_specs=[vmem] * 19 + [hbm] * 6,
        scratch_shapes=[
            buf(CHANNEL_ROWS, 384),
            buf(2, 2 * PART, 384),
            buf(*gateright.shape, dtype=F32),
            buf(*gateleft.shape, dtype=F32),
            buf(*liftright.shape, dtype=F32),
            buf(*liftleft.shape, dtype=F32),
            buf(*lowerright.shape, dtype=F32),
            buf(*lowerleft.shape, dtype=F32),
            buf(144, 128, dtype=F32),
            pltpu.SemaphoreType.DMA((5,)),
            pltpu.SemaphoreType.DMA((6,)),
        ],
        compiler_params=pltpu.CompilerParams(vmem_limit_bytes=60 * 1024 * 1024),
    )(*results)
    return (*grads[:14], grads[14].T, *grads[15:])


def solution(mesh):
    pairs = mesh.shape["wide"] == 2 * SEQS and mesh.shape["narrow"] == 2
    return jax.shard_map(
        pair_body if pairs else body,
        mesh=mesh,
        in_specs=(
            P("wide", None),
            P(),
            P(),
            P(),
            P(),
            P(),
            P(),
            P(),
            P(),
            P(),
            P(),
            P(),
            P(),
            P(),
            P(),
            P(),
            P(),
            P(),
            P(None, "narrow"),
            P(None, "narrow"),
            P(None, "narrow"),
            P(None, "narrow"),
            P(None, "narrow"),
            P("narrow", None),
            P("wide", "narrow"),
        ),
        out_specs=(
            P("wide", "narrow"),
            P("wide", "narrow"),
            P(),
            P(),
            P(),
            P(),
            P(),
            P(),
            P(),
            P(),
            P(),
            P(),
            P(),
            P(),
            P(None, ("wide", "narrow")),
            P(),
            P(),
            P(),
            P(),
            P(None, "narrow"),
            P(None, "narrow"),
            P(None, "narrow"),
            P(None, "narrow"),
            P(None, "narrow"),
            P("narrow", None),
        ),
        check_vma=False,
    )
```

```python
import math

import jax
import jax.numpy as jnp
import numpy as np
from jax import lax
from jax.experimental import pallas as pl
from jax.experimental.pallas import tpu as pltpu
from jax.sharding import PartitionSpec as P

D = 768
BLOCKS = 4
SEQS = 8


EPSILON = 1e-05
HIGHEST = lax.Precision.HIGHEST


def from_behind(x, axis, by):
    length = lax.axis_size(axis)
    pairs = [(i, i + by) for i in range(length) if 0 <= i + by < length]
    return lax.ppermute(x, axis, pairs)


def norm_forward(values, gain, shift):
    center = values - jnp.mean(values, axis=-1, keepdims=True)
    inverse = lax.rsqrt(jnp.mean(center * center, axis=-1, keepdims=True) + EPSILON)
    normed = center * inverse
    return (normed * gain + shift, normed, inverse)


def norm_backward(upstream, normed, inverse, gain):
    scaled = upstream * gain
    result = inverse * (
        scaled
        - jnp.mean(scaled, axis=-1, keepdims=True)
        - normed * jnp.mean(scaled * normed, axis=-1, keepdims=True)
    )
    return (result, jnp.sum(upstream * normed, axis=0), jnp.sum(upstream, axis=0))


def right_view(right, nblocks, groups, group_first):
    width_in = right.shape[0]
    piece = right.shape[1] // (nblocks * groups)
    if group_first:
        return (right.reshape(width_in, groups, nblocks, piece), "ikbc")
    return (right.reshape(width_in, nblocks, groups, piece), "ibkc")


def section_one(inputs, right, groups, group_first):
    rowcount = inputs.shape[0]
    width_in = right.shape[0]
    nblocks = inputs.shape[1] // width_in
    factor, letters = right_view(right, nblocks, groups, group_first)
    first = jnp.einsum(
        "tbi," + letters + "->tkbc",
        inputs.reshape(rowcount, nblocks, width_in),
        factor,
        preferred_element_type=jnp.float32,
    )
    return first.reshape(rowcount, groups, -1).astype(jnp.bfloat16)


def section_two(middle_part, left):
    groups = middle_part.shape[1]
    result = jnp.einsum(
        "tkj,jke->tke",
        middle_part,
        left.reshape(left.shape[0], groups, -1),
        preferred_element_type=jnp.float32,
    )
    return result.reshape(result.shape[0], -1)


def back_two(middle_part, left, upstream):
    groups = middle_part.shape[1]
    left_view = left.reshape(left.shape[0], groups, -1)
    grad_left = jnp.einsum(
        "tkj,tke->jke", middle_part, upstream, preferred_element_type=jnp.float32
    )
    grad_middle = jnp.einsum(
        "tke,jke->tkj", upstream, left_view, preferred_element_type=jnp.float32
    )
    return (grad_left.reshape(left.shape[0], -1), grad_middle.astype(jnp.bfloat16))


def back_one(inputs, right, grad_middle, group_first):
    rowcount = inputs.shape[0]
    width_in = right.shape[0]
    nblocks = inputs.shape[1] // width_in
    groups = grad_middle.shape[1]
    factor, letters = right_view(right, nblocks, groups, group_first)
    spread_back = grad_middle.reshape(rowcount, groups, nblocks, -1)
    blocked = inputs.reshape(rowcount, nblocks, width_in)
    grad_right = jnp.einsum(
        "tbi,tkbc->" + letters, blocked, spread_back, preferred_element_type=jnp.float32
    )
    grad_inputs = jnp.einsum(
        "tkbc," + letters + "->tbi", spread_back, factor, preferred_element_type=jnp.float32
    )
    return (grad_right.reshape(width_in, -1), grad_inputs.reshape(rowcount, -1))


def fourier_tables(length):
    span = length // 128
    slow_index = jnp.arange(span, dtype=jnp.int32)
    fast_index = jnp.arange(128, dtype=jnp.int32)
    small = (slow_index[:, None] * slow_index[None, :] % span).astype(jnp.float32) * (
        2.0 * math.pi / span
    )
    twist = (slow_index[:, None] * fast_index[None, :] % length).astype(jnp.float32) * (
        2.0 * math.pi / length
    )
    large = (fast_index[:, None] * fast_index[None, :] % 128).astype(jnp.float32) * (
        2.0 * math.pi / 128
    )
    return (
        jnp.cos(small),
        jnp.sin(small),
        jnp.cos(twist),
        jnp.sin(twist),
        jnp.cos(large),
        jnp.sin(large),
    )


def to_spectrum(signal, tables):
    cos_small, sin_small, cos_twist, sin_twist, cos_large, sin_large = tables
    span = cos_small.shape[0]
    padded = jnp.concatenate([signal, jnp.zeros_like(signal)], axis=-1)
    padded = padded.reshape(signal.shape[:-1] + (span, 128))
    first_re = jnp.einsum("...qp,qk->...kp", padded, cos_small, precision=HIGHEST)
    first_im = -jnp.einsum("...qp,qk->...kp", padded, sin_small, precision=HIGHEST)
    turned_re = first_re * cos_twist + first_im * sin_twist
    turned_im = first_im * cos_twist - first_re * sin_twist
    out_re = jnp.einsum("...kp,pj->...kj", turned_re, cos_large, precision=HIGHEST) + jnp.einsum(
        "...kp,pj->...kj", turned_im, sin_large, precision=HIGHEST
    )
    out_im = jnp.einsum("...kp,pj->...kj", turned_im, cos_large, precision=HIGHEST) - jnp.einsum(
        "...kp,pj->...kj", turned_re, sin_large, precision=HIGHEST
    )
    return (out_re, out_im)


def from_spectrum(real_part, imag_part, tables):
    cos_small, sin_small, cos_twist, sin_twist, cos_large, sin_large = tables
    span = cos_small.shape[0]
    back_re = jnp.einsum("...kj,pj->...kp", real_part, cos_large, precision=HIGHEST) - jnp.einsum(
        "...kj,pj->...kp", imag_part, sin_large, precision=HIGHEST
    )
    back_im = jnp.einsum("...kj,pj->...kp", imag_part, cos_large, precision=HIGHEST) + jnp.einsum(
        "...kj,pj->...kp", real_part, sin_large, precision=HIGHEST
    )
    turned_re = back_re * cos_twist - back_im * sin_twist
    turned_im = back_im * cos_twist + back_re * sin_twist
    signal = (
        jnp.einsum("...kp,qk->...qp", turned_re, cos_small, precision=HIGHEST)
        - jnp.einsum("...kp,qk->...qp", turned_im, sin_small, precision=HIGHEST)
    ) / (span * 128)
    signal = signal.reshape(signal.shape[:-2] + (span * 128,))
    return signal[..., : span * 64]


def position_features(length):
    places = jnp.arange(length, dtype=jnp.float32)
    angle = places * (2.0 * math.pi / length)
    return jnp.stack(
        [
            places / length,
            jnp.cos(angle),
            jnp.sin(angle),
            jnp.cos(2.0 * angle),
            jnp.sin(2.0 * angle),
        ],
        axis=1,
    )


def decay_factors(channel_ids, length):
    rank = (channel_ids * 5 % D).astype(jnp.float32) / D
    lowest = math.log(0.25 / length)
    highest = math.log(1.0 / 30.0)
    rate = jnp.exp(lowest + rank * (highest - lowest))
    places = jnp.arange(length, dtype=jnp.float32)
    return jnp.exp(-rate[:, None] * places[None, :]) * jnp.sqrt(2.0 * rate)[:, None]


def channel_order(data, nwide, nnarrow, rows_half):
    count = data.shape[0]
    return data.reshape(count, nnarrow, nwide, rows_half).transpose(0, 2, 1, 3).reshape(count, -1)


def row_order(data, nwide, nnarrow):
    total = data.shape[0]
    rows_half = data.shape[1]
    count = total // (nwide * nnarrow)
    return (
        data.reshape(nnarrow, nwide, count, rows_half)
        .transpose(1, 0, 2, 3)
        .reshape(total, rows_half)
        .T
    )


def body(
    hidden_in,
    gainfirst,
    shiftfirst,
    valueright,
    valueleft,
    shaperight,
    shapeleft,
    convtaps,
    posweight,
    posbias,
    sinefreq,
    midweight,
    midbias,
    filterout,
    outright,
    outleft,
    gainsecond,
    shiftsecond,
    gateright,
    gateleft,
    liftright,
    liftleft,
    lowerright,
    lowerleft,
    grad_out,
):
    rowcount = hidden_in.shape[0]
    local_groups = gateright.shape[1] // gateleft.shape[0]
    nwide = lax.axis_size("wide")
    nnarrow = lax.axis_size("narrow")
    narrow_index = lax.axis_index("narrow")
    rows_half = rowcount // nnarrow
    row_start = narrow_index * rows_half
    combined = lax.axis_index("wide") * nnarrow + narrow_index
    resid = lax.dynamic_slice_in_dim(hidden_in, row_start, rows_half, 0).astype(jnp.float32)
    normone, hat_one, inv_one = norm_forward(resid, gainfirst, shiftfirst)
    normone = normone.astype(jnp.bfloat16)
    mid_value = section_one(normone, valueright, BLOCKS, False)
    signal = section_two(mid_value, valueleft).astype(jnp.bfloat16)
    mid_shape = section_one(normone, shaperight, BLOCKS, False)
    shaping = section_two(mid_shape, shapeleft)
    group = nwide // SEQS * nnarrow
    place = combined % group
    before = from_behind(signal[-2:], ("wide", "narrow"), 1)
    before = jnp.where(place == 0, jnp.zeros_like(before), before)
    extended = jnp.concatenate([before, signal], axis=0).astype(jnp.float32)
    shortconv = (
        convtaps[0] * extended[2:] + convtaps[1] * extended[1:-1] + convtaps[2] * extended[:-2]
    ).astype(jnp.bfloat16)
    channels = lax.all_to_all(
        lax.all_to_all(shortconv.T, "wide", split_axis=0, concat_axis=1, tiled=True),
        "narrow",
        split_axis=0,
        concat_axis=1,
        tiled=True,
    )
    channels = channel_order(channels, nwide, nnarrow, rows_half)
    count = channels.shape[0]
    length = channels.shape[1] // SEQS
    feats = position_features(length)
    lin_one = jnp.dot(feats, posweight, precision=HIGHEST) + posbias
    act_one = jnp.sin(sinefreq * lin_one)
    lin_two = jnp.dot(act_one, midweight, precision=HIGHEST) + midbias
    act_two = jnp.sin(sinefreq * lin_two)
    own_cols = lax.dynamic_slice_in_dim(filterout, combined * count, count, 1)
    channel_ids = combined * count + jnp.arange(count, dtype=jnp.int32)
    modulation = decay_factors(channel_ids, length)
    taps = jnp.dot(act_two, own_cols, precision=HIGHEST).T * modulation
    tables = fourier_tables(2 * length)
    sig_re, sig_im = to_spectrum(channels.astype(jnp.float32).reshape(count, SEQS, length), tables)
    fil_re, fil_im = to_spectrum(taps.reshape(count, 1, length), tables)
    conv_chan = from_spectrum(
        sig_re * fil_re - sig_im * fil_im, sig_re * fil_im + sig_im * fil_re, tables
    )
    conv_chan = conv_chan.reshape(count, SEQS * length).astype(jnp.bfloat16)
    longconv = lax.all_to_all(
        lax.all_to_all(conv_chan, "wide", split_axis=1, concat_axis=0, tiled=True),
        "narrow",
        split_axis=1,
        concat_axis=0,
        tiled=True,
    )
    longconv = row_order(longconv, nwide, nnarrow)
    mixed = (shaping * longconv.astype(jnp.float32)).astype(jnp.bfloat16)
    mid_out = section_one(mixed, outright, BLOCKS, False)
    middle = resid + section_two(mid_out, outleft)
    normtwo, hat_two, inv_two = norm_forward(middle, gainsecond, shiftsecond)
    normtwo = normtwo.astype(jnp.bfloat16)
    norm_all = lax.all_gather(normtwo, "narrow", axis=0, tiled=True)
    mid_gate = section_one(norm_all, gateright, local_groups, True)
    pregate = section_two(mid_gate, gateleft)
    mid_lift = section_one(norm_all, liftright, local_groups, True)
    prelift = section_two(mid_lift, liftleft)
    cumulative = 0.5 * (1.0 + lax.erf(pregate * (1.0 / math.sqrt(2.0))))
    activated = pregate * cumulative
    hidden = (activated * prelift).astype(jnp.bfloat16)
    mid_lower = section_one(hidden, lowerright, BLOCKS, False)
    partial_sum = section_two(mid_lower, lowerleft)
    partial_sum = partial_sum + lax.dynamic_update_slice_in_dim(
        jnp.zeros_like(partial_sum), middle, row_start, 0
    )
    hidden_out = lax.psum_scatter(
        partial_sum.astype(jnp.bfloat16), "narrow", scatter_dimension=1, tiled=True
    )
    upstream = lax.all_gather(grad_out, "narrow", axis=1, tiled=True)
    grad_lowerleft, grad_mid_lower = back_two(
        mid_lower, lowerleft, upstream.reshape(rowcount, BLOCKS, -1)
    )
    grad_lowerright, grad_hidden = back_one(hidden, lowerright, grad_mid_lower, False)
    density = jnp.exp(-0.5 * pregate * pregate) * (1.0 / math.sqrt(2.0 * math.pi))
    grad_pregate = (grad_hidden * prelift * (cumulative + pregate * density)).astype(jnp.bfloat16)
    grad_prelift = (grad_hidden * activated).astype(jnp.bfloat16)
    grad_gateleft, grad_mid_gate = back_two(
        mid_gate, gateleft, grad_pregate.reshape(rowcount, local_groups, -1)
    )
    grad_gateright, into_gate = back_one(norm_all, gateright, grad_mid_gate, True)
    grad_liftleft, grad_mid_lift = back_two(
        mid_lift, liftleft, grad_prelift.reshape(rowcount, local_groups, -1)
    )
    grad_liftright, into_lift = back_one(norm_all, liftright, grad_mid_lift, True)
    ffn_local = (
        grad_gateright,
        grad_gateleft,
        grad_liftright,
        grad_liftleft,
        grad_lowerright,
        grad_lowerleft,
    )
    dnormtwo = lax.psum_scatter(
        (into_gate + into_lift).astype(jnp.bfloat16), "narrow", scatter_dimension=0, tiled=True
    ).astype(jnp.float32)
    back_two_norm, grad_gainsecond, grad_shiftsecond = norm_backward(
        dnormtwo, hat_two, inv_two, gainsecond
    )
    up_rows = lax.dynamic_slice_in_dim(upstream, row_start, rows_half, 0)
    dmiddle = up_rows.astype(jnp.float32) + back_two_norm
    dbranch = dmiddle.astype(jnp.bfloat16)
    grad_outleft, grad_mid_out = back_two(mid_out, outleft, dbranch.reshape(rows_half, BLOCKS, -1))
    grad_outright, dmixed = back_one(mixed, outright, grad_mid_out, False)
    dshaping = (dmixed * longconv.astype(jnp.float32)).astype(jnp.bfloat16)
    dlong = (dmixed * shaping).astype(jnp.bfloat16)
    grad_chan = lax.all_to_all(
        lax.all_to_all(dlong.T, "wide", split_axis=0, concat_axis=1, tiled=True),
        "narrow",
        split_axis=0,
        concat_axis=1,
        tiled=True,
    )
    grad_chan = channel_order(grad_chan, nwide, nnarrow, rows_half)
    dlong_re, dlong_im = to_spectrum(
        grad_chan.astype(jnp.float32).reshape(count, SEQS, length), tables
    )
    dshort_chan = from_spectrum(
        dlong_re * fil_re + dlong_im * fil_im, dlong_im * fil_re - dlong_re * fil_im, tables
    )
    dshort_chan = dshort_chan.reshape(count, SEQS * length).astype(jnp.bfloat16)
    filt_re = jnp.sum(dlong_re * sig_re + dlong_im * sig_im, axis=1, keepdims=True)
    filt_im = jnp.sum(dlong_im * sig_re - dlong_re * sig_im, axis=1, keepdims=True)
    grad_taps = from_spectrum(filt_re, filt_im, tables).reshape(count, length)
    dshort = lax.all_to_all(
        lax.all_to_all(dshort_chan, "wide", split_axis=1, concat_axis=0, tiled=True),
        "narrow",
        split_axis=1,
        concat_axis=0,
        tiled=True,
    )
    dshort = row_order(dshort, nwide, nnarrow)
    grad_modded = grad_taps * modulation
    grad_filterout = jnp.dot(act_two.T, grad_modded.T, precision=HIGHEST)
    dact_two = jnp.dot(grad_modded.T, own_cols.T, precision=HIGHEST)
    dlin_two = dact_two * jnp.cos(sinefreq * lin_two)
    scaled_two = dlin_two * sinefreq
    grad_midweight = jnp.dot(act_one.T, scaled_two, precision=HIGHEST)
    grad_midbias = jnp.sum(scaled_two, axis=0)
    dact_one = jnp.dot(scaled_two, midweight.T, precision=HIGHEST)
    dlin_one = dact_one * jnp.cos(sinefreq * lin_one)
    scaled_one = dlin_one * sinefreq
    grad_posweight = jnp.dot(feats.T, scaled_one, precision=HIGHEST)
    grad_posbias = jnp.sum(scaled_one, axis=0)
    grad_sinefreq = jnp.sum(dlin_one * lin_one, axis=0) + jnp.sum(dlin_two * lin_two, axis=0)
    after = from_behind(dshort[:2], ("wide", "narrow"), -1)
    after = jnp.where(place == group - 1, jnp.zeros_like(after), after)
    ext_grad = jnp.concatenate([dshort, after], axis=0).astype(jnp.float32)
    dsignal = (
        convtaps[0] * ext_grad[:-2] + convtaps[1] * ext_grad[1:-1] + convtaps[2] * ext_grad[2:]
    ).astype(jnp.bfloat16)
    short_grad = dshort.astype(jnp.float32)
    grad_convtaps = jnp.stack(
        [
            jnp.sum(extended[2:] * short_grad, axis=0),
            jnp.sum(extended[1:-1] * short_grad, axis=0),
            jnp.sum(extended[:-2] * short_grad, axis=0),
        ]
    )
    grad_valueleft, grad_mid_value = back_two(
        mid_value, valueleft, dsignal.reshape(rows_half, BLOCKS, -1)
    )
    grad_valueright, into_value = back_one(normone, valueright, grad_mid_value, False)
    grad_shapeleft, grad_mid_shape = back_two(
        mid_shape, shapeleft, dshaping.reshape(rows_half, BLOCKS, -1)
    )
    grad_shaperight, into_shape = back_one(normone, shaperight, grad_mid_shape, False)
    back_one_norm, grad_gainfirst, grad_shiftfirst = norm_backward(
        into_value + into_shape, hat_one, inv_one, gainfirst
    )
    full_grad = (dmiddle + back_one_norm).astype(jnp.bfloat16)
    hidden_grad = lax.all_to_all(full_grad, "narrow", split_axis=1, concat_axis=0, tiled=True)
    mixer_grads = lax.psum(
        (
            grad_gainfirst,
            grad_shiftfirst,
            grad_valueright,
            grad_valueleft,
            grad_shaperight,
            grad_shapeleft,
            grad_convtaps,
            grad_posweight,
            grad_posbias,
            grad_sinefreq,
            grad_midweight,
            grad_midbias,
            grad_outright,
            grad_outleft,
            grad_gainsecond,
            grad_shiftsecond,
        ),
        ("wide", "narrow"),
    )
    ffn_grads = lax.psum(
        (ffn_local[0], ffn_local[1], ffn_local[2], ffn_local[3], ffn_local[4], ffn_local[5]), "wide"
    )
    return (
        hidden_out,
        hidden_grad,
        mixer_grads[0],
        mixer_grads[1],
        mixer_grads[2],
        mixer_grads[3],
        mixer_grads[4],
        mixer_grads[5],
        mixer_grads[6],
        mixer_grads[7],
        mixer_grads[8],
        mixer_grads[9],
        mixer_grads[10],
        mixer_grads[11],
        grad_filterout,
        mixer_grads[12],
        mixer_grads[13],
        mixer_grads[14],
        mixer_grads[15],
        ffn_grads[0],
        ffn_grads[1],
        ffn_grads[2],
        ffn_grads[3],
        ffn_grads[4],
        ffn_grads[5],
    )


F32 = jnp.float32
BF16 = jnp.bfloat16
MESH = pl.DeviceIdType.MESH
TILE = 256
PAD = 256


def mm(a, b, precision=None):
    return lax.dot_general(
        a, b, (((1,), (0,)), ((), ())), precision=precision, preferred_element_type=F32
    )


def mm_nt(a, b, precision=None):
    return lax.dot_general(
        a, b, (((1,), (1,)), ((), ())), precision=precision, preferred_element_type=F32
    )


def mm_tn(a, b, precision=None):
    return lax.dot_general(
        a, b, (((0,), (0,)), ((), ())), precision=precision, preferred_element_type=F32
    )


def lanes(width):
    return lax.broadcasted_iota(jnp.int32, (1, width), 1)


def mask(condition, dtype=BF16):
    return jnp.where(condition, 1.0, 0.0).astype(dtype)


def between(width, low, high, dtype=BF16):
    lane = lanes(width)
    return mask((lane >= low) & (lane < high), dtype)


def join(first, second):
    return jnp.concatenate(
        [first[:, :128], first[:, 128:] + second[:, :128], second[:, 128:]], axis=1
    )


def sine_cosine(angle):
    turns = jnp.floor(angle * (1.0 / math.pi) + 0.5)
    rest = angle - turns * 3.140625
    rest = rest - turns * 9.67502593994140625e-4
    rest = rest - turns * 1.509957990978376e-7
    flip = 1.0 - 2.0 * (turns - 2.0 * jnp.floor(turns * 0.5))
    square = rest * rest
    sine = 1.0
    for divisor in (110.0, 72.0, 42.0, 20.0, 6.0):
        sine = 1.0 - square * (1.0 / divisor) * sine
    cosine = 1.0
    for divisor in (132.0, 90.0, 56.0, 30.0, 12.0, 2.0):
        cosine = 1.0 - square * (1.0 / divisor) * cosine
    return (sine * rest * flip, cosine * flip)


def fold(whole, side):
    return [
        whole[192 * b + 96 * side : 192 * b + 96 * side + 48, :] * between(384, 0, 192, F32)
        + whole[192 * b + 96 * side + 48 : 192 * b + 96 * side + 96, :] * between(384, 192, 384, F32)
        for b in range(2)
    ]


STRIDES = (1, 2, 4, 8)
PART = 768
STEP_ROWS = (0, 384, 576, 672, 720)
ORDERS = ((0, 1, 2, 3), (0, 2, 3, 1), (0, 1, 2, 3), (0, 1, 2, 3), (0, 1, 2, 3))
CHUNK = 48
LOWER_RIGHT, LOWER_LEFT, GATE_RIGHT, LIFT_RIGHT, GATE_LEFT, LIFT_LEFT, CHANNEL_ROWS = (
    0,
    768,
    960,
    1152,
    1344,
    2112,
    4 * PART,
)
OUT_LEFT, SHAPE_RIGHT, SHAPE_LEFT = (0, 384, 576)
VALUE_RIGHT, VALUE_LEFT, FILTER_OUT, VECTORS, FILTER, OUT_RIGHT = (0, 192, 384, 512, 528, 576)


def tile_rows(index, size=TILE):
    return pl.ds(pl.multiple_of(index * size, size), size)


def whole_kernel(
    hidden_in,
    upstream,
    hbm_cos,
    hbm_sin,
    place,
    place_parts,
    gainfirst,
    shiftfirst,
    gainsecond,
    shiftsecond,
    convtaps,
    posweight,
    posbias,
    midbias,
    sinefreq,
    midweight,
    filterout,
    valueright,
    valueleft,
    shaperight,
    shapeleft,
    outright,
    outleft,
    gateright,
    gateleft,
    liftright,
    liftleft,
    lowerright,
    lowerleft,
    result_out,
    result_grad,
    result_channel,
    result_mixer,
    hidden_out,
    hidden_grad,
    sums_channel,
    sums_mixer,
    store_sem,
    inputs,
    table_cos,
    table_sin,
    vectors,
    filter_vectors,
    w_first,
    w_value,
    w_shape,
    w_out_first,
    w_out_second,
    w_glu,
    w_gate,
    w_lift,
    w_lower,
    w_lower_second,
    up_halves,
    stats,
    norm_one,
    inner_one,
    sig_halves,
    sig_rows,
    shaping,
    sig_pad,
    short,
    act_one,
    cos_one,
    lin_one,
    act_two,
    cos_two,
    lin_two,
    fil_spec,
    sig_spec,
    prod_spec,
    long_rows,
    long_halves,
    inner_out,
    hat_two,
    norm_two,
    inner_glu,
    factor_gate,
    factor_lift,
    hid,
    inner_lower,
    out_own,
    part_send,
    part_recv,
    d_inner_lower,
    d_gate,
    d_lift,
    d_inner_glu,
    dn_own,
    dn_send,
    dn_recv,
    d_inner_out,
    d_shaping,
    dl_rows,
    ds_pad,
    ds_halves,
    d_inner_one,
    cross_send,
    mid_send,
    mid_recv,
    d_middle,
    branch,
    shape_send,
    shape_recv,
    value_send,
    value_recv,
    w_cross,
    through,
    d_lin,
    own_out,
    grad_vectors,
    grad_filter,
    gain_sums,
    send_sem,
    recv_sem,
    load_sem,
    got,
    sum_send,
    sum_recv,
    sum_free,
    late,
    late_core,
    late_slots,
    late_send,
    late_recv,
):
    rows = inputs.shape[0]
    tiles = rows // TILE
    length = 2 * rows
    spans = length // TILE
    wide = lax.axis_index("wide")
    narrow = lax.axis_index("narrow")
    bits = [lax.rem(wide // stride, 2) for stride in STRIDES]
    core = bits[0]
    sibling = (wide + 1 - 2 * core, narrow)
    partner = (wide, 1 - narrow)
    quarter = 2 * narrow + core
    own_half = pl.ds(pl.multiple_of(narrow * 384, 384), 384)
    other_half = pl.ds(pl.multiple_of((1 - narrow) * 384, 384), 384)

    loads = {}

    def load(name, source, target):
        loads[name] = pltpu.make_async_copy(source, target, load_sem.at[len(loads)])
        loads[name].start()

    load("inputs", hidden_in, inputs)
    load("valueright", valueright, hid.at[0, pl.ds(0, 192)])
    load("shaperight", shaperight, hid.at[0, pl.ds(192, 192)])
    load("valueleft", valueleft, hid.at[1, pl.ds(0, 192)])
    load("shapeleft", shapeleft, hid.at[1, pl.ds(192, 192)])
    load("filterout", filterout, factor_gate.at[0, pl.ds(0, 128)])
    load("cos", hbm_cos, table_cos)
    load("sin", hbm_sin, table_sin)
    load("outright", outright, d_gate.at[0, pl.ds(0, 192)])
    load("outleft", outleft, d_gate.at[0, pl.ds(192, 192)])
    load("gateright", gateright, d_lift.at[1, pl.ds(96, 192), pl.ds(0, 384)])
    load("liftright", liftright, d_lift.at[1, pl.ds(96, 192), pl.ds(384, 384)])
    load("lowerleft", lowerleft, d_lift.at[1, pl.ds(0, 96)])
    load("lower_top", lowerright.at[pl.ds(0, 512)], d_lift.at[0, :, pl.ds(0, 384)])
    load("lower_end", lowerright.at[pl.ds(512, 256)], d_lift.at[0, pl.ds(0, 256), pl.ds(384, 384)])
    for k in range(2):
        at = pl.ds(64 * k, 192)
        load(("gate", k), gateleft.at[:, pl.ds(D * k, D)], w_gate.at[k, at])
        load(("lift", k), liftleft.at[:, pl.ds(D * k, D)], w_lift.at[k, at])
    load("upstream", upstream, up_halves.at[narrow])

    stores = []

    def store(source, target):
        stores.append(pltpu.make_async_copy(source, target, store_sem.at[len(stores)]))
        stores[-1].start()

    barrier = pltpu.get_barrier_semaphore()
    others = [(wide + stride * (1 - 2 * bit), narrow) for stride, bit in zip(STRIDES, bits)]
    chip = wide // 2
    fellows = [(2 * lax.rem(chip + t, 8) + core, narrow) for t in range(8)]
    for device in [sibling, partner] + fellows[1:]:
        pl.semaphore_signal(barrier, inc=1, device_id=device, device_id_type=MESH)

    for i, source in enumerate((gainfirst, shiftfirst, gainsecond, shiftsecond)):
        vectors[i : i + 1, :] = source[...].reshape(1, D)
    vectors[4:7, :] = convtaps[...]
    vectors[7:8, :] = jnp.zeros((1, D), F32)
    filter_vectors[...] = jnp.zeros(filter_vectors.shape, F32)
    filter_vectors[0:5, :] = posweight[...]
    for i, source in enumerate((posbias, midbias, sinefreq)):
        filter_vectors[8 + i : 9 + i, :] = source[...].reshape(1, 128)

    def send(source, target, device, index):
        return pltpu.make_async_remote_copy(
            src_ref=source,
            dst_ref=target,
            send_sem=send_sem.at[index],
            recv_sem=recv_sem.at[index],
            device_id=device,
            device_id_type=MESH,
        )

    mixer_slab = sums_mixer.at[narrow]
    parts_of = [sums_channel.at[pl.ds(PART * i, PART)] for i in range(4)] + [mixer_slab.at[pl.ds(0, PART)]]
    offsets = []
    for order in ORDERS:
        found = [0]
        for step in range(4):
            found.append(pl.multiple_of(found[step] + bits[order[step]] * (PART >> (step + 1)), 16))
        offsets.append(found)

    def sum_copy(source, target, i, step, back):
        index = 8 * i + 4 * back + step
        return pltpu.make_async_remote_copy(
            src_ref=source,
            dst_ref=target,
            send_sem=sum_send.at[index],
            recv_sem=sum_recv.at[index],
            device_id=others[ORDERS[i][step]],
            device_id_type=MESH,
        )

    def scatter(i, step):
        size = PART >> (step + 1)
        away = pl.multiple_of(offsets[i][step] + (1 - bits[ORDERS[i][step]]) * size, 16)
        return sum_copy(
            parts_of[i].at[pl.ds(away, size)], got.at[i, pl.ds(STEP_ROWS[step], size)], i, step, 0
        )

    def gather(i, step):
        at = pl.ds(offsets[i][step + 1], PART >> (step + 1))
        return sum_copy(parts_of[i].at[at], parts_of[i].at[at], i, step, 1)

    def hand_back(i, step):
        pl.semaphore_wait(sum_free.at[4 * i + step], 1)
        gather(i, step).start()

    def advance(i, step):
        scatter(i, step).wait()

        @pl.loop(0, (PART >> (step + 1)) // CHUNK)
        def _(index):
            own = pl.ds(pl.multiple_of(offsets[i][step + 1] + index * CHUNK, 16), CHUNK)
            came = got[i, pl.ds(pl.multiple_of(STEP_ROWS[step] + index * CHUNK, 16), CHUNK), :]
            parts_of[i][own, :] = (parts_of[i][own, :].astype(F32) + came.astype(F32)).astype(BF16)

        pl.semaphore_signal(
            sum_free.at[4 * i + step],
            inc=1,
            device_id=others[ORDERS[i][step]],
            device_id_type=MESH,
        )
        if step < 3:
            scatter(i, step + 1).start()
        else:
            hand_back(i, 3)

    def retreat(i, step):
        gather(i, step).wait()
        if step > 0:
            hand_back(i, step - 1)

    def late_copy(source, target, device, index):
        return pltpu.make_async_remote_copy(
            src_ref=source,
            dst_ref=target,
            send_sem=late_send.at[index],
            recv_sem=late_recv.at[index],
            device_id=device,
            device_id_type=MESH,
        )

    row = lax.broadcasted_iota(jnp.int32, (D, 384), 0)
    lane = lax.broadcasted_iota(jnp.int32, (D, 384), 1)
    step = jnp.where(lane >= 96, 96, 0) + jnp.where(lane >= 192, 96, 0) + jnp.where(lane >= 288, 96, 0)
    select = mask(row == lane + step + narrow * 96)
    for name in ("valueright", "shaperight", "valueleft", "shapeleft"):
        loads[name].wait()
    right_half = mm(hid[0, 0:192, :], select).astype(BF16)
    shape_half = mm(hid[0, 192:384, :], select).astype(BF16)
    for b in range(4):
        kept = between(384, 96 * b, 96 * b + 96)
        w_first[192 * b : 192 * b + 192, 0:384] = right_half * kept
        w_first[192 * b : 192 * b + 192, 384:768] = shape_half * kept
    row = lax.broadcasted_iota(jnp.int32, (D, 2 * PAD), 0)
    lane = lax.broadcasted_iota(jnp.int32, (D, 2 * PAD), 1)
    group = jnp.where(lane >= PAD, 1, 0)
    entry = lane - PAD * group
    spread = mask((row == (2 * narrow + group) * 192 + entry) & (entry < 192))
    for source, target in ((0, w_value), (192, w_shape)):
        wider = mm(hid[1, source : source + 192, :], spread).astype(BF16)
        for b in range(4):
            for k in range(2):
                target[96 * b + 48 * k : 96 * b + 48 * k + 48, :] = wider[
                    48 * b : 48 * b + 48, :
                ] * between(2 * PAD, PAD * k, PAD * k + PAD)
    row = lax.broadcasted_iota(jnp.int32, (D, 192), 0)
    lane = lax.broadcasted_iota(jnp.int32, (D, 192), 1)
    start = (2 * narrow) * 192 + (1 - narrow) * 96
    cross = mask(row == start + lane + jnp.where(lane >= 96, 96, 0))
    for i in range(2):
        part = mm(hid[0, 192 * i : 192 * i + 192, :], cross).astype(BF16)
        for b in range(2):
            w_cross[i, 192 * b : 192 * b + 192, :] = part * between(192, 96 * b, 96 * b + 96)
    first = vectors[0:1, :]
    shift_first = vectors[1:2, :]

    coarse = vectors[...].astype(BF16)
    fine = (vectors[...] - coarse.astype(F32)).astype(BF16)
    through[...] = mm(coarse, w_first[...]) + mm(fine, w_first[...])
    loads["inputs"].wait()

    @pl.loop(0, tiles)
    def _(index):
        at = tile_rows(index)
        values = inputs[at, :].astype(F32)
        average = jnp.mean(values, axis=-1, keepdims=True)
        center = values - average
        inverse = lax.rsqrt(jnp.mean(center * center, axis=-1, keepdims=True) + EPSILON)
        hat = center * inverse
        stats[at, 0:1] = average
        stats[at, 1:2] = inverse
        normed = (hat * first + shift_first).astype(BF16)
        norm_one[at, :] = normed
        inner = mm(normed, w_first[...]).astype(BF16)
        inner_one[at, :] = inner
        signal = mm(inner[:, :384], w_value[...]).astype(BF16)
        sig_halves[0, at, :] = signal[:, :PAD]
        sig_halves[1, at, :] = signal[:, PAD:]
        shaped = mm(inner[:, 384:], w_shape[...])
        shaping[0, at, :] = shaped[:, :PAD]
        shaping[1, at, :] = shaped[:, PAD:]

    pl.semaphore_wait(barrier, 9)
    sig_copy = send(sig_halves.at[1 - core], sig_rows.at[core], sibling, 1)
    sig_copy.start()
    up_copy = send(upstream, up_halves.at[narrow], partner, 0)
    up_copy.start()
    sig_rows[core] = sig_halves[core]

    row = lax.broadcasted_iota(jnp.int32, (D, PAD), 0)
    lane = lax.broadcasted_iota(jnp.int32, (D, PAD), 1)
    pick = mask((row == quarter * 192 + lane) & (lane < 192))
    conv = mm(coarse, pick) + mm(fine, pick)
    loads["filterout"].wait()
    own_out[...] = mm(factor_gate[0, 0:128, :].astype(BF16), pick).astype(BF16)
    pos_bias = filter_vectors[8:9, :]
    mid_bias = filter_vectors[9:10, :]
    frequency = filter_vectors[10:11, :]
    mid_high = midweight[...].astype(BF16)
    mid_low = (midweight[...] - mid_high.astype(F32)).astype(BF16)
    pos_high = filter_vectors[0:8, :].astype(BF16).astype(F32)
    pos_parts = jnp.concatenate(
        [pos_high, pos_high, filter_vectors[0:8, :] - pos_high, jnp.zeros((8, 128), F32)], axis=0
    ).astype(BF16)
    ranks = 5 * (quarter * 192 + lanes(PAD))
    for bound in range(5):
        ranks = jnp.where(ranks >= D, ranks - D, ranks)
    lowest = math.log(0.25 / length)
    highest = math.log(1.0 / 30.0)
    rate = jnp.exp(lowest + ranks.astype(F32) * (1.0 / D) * (highest - lowest))
    loud = jnp.sqrt(2.0 * rate)

    def decay(index):
        places = (lax.broadcasted_iota(jnp.int32, (TILE, PAD), 0) + index * TILE).astype(F32)
        return jnp.exp(-rate * places) * loud

    @pl.loop(0, spans)
    def _(index):
        at = tile_rows(index)
        one = mm(place_parts[at, :], pos_parts) + pos_bias
        sine, cosine = sine_cosine(frequency * one)
        high = sine.astype(BF16)
        low = (sine - high.astype(F32)).astype(BF16)
        lin_one[at, :] = one.astype(BF16)
        act_one[at, :] = high
        cos_one[at, :] = cosine.astype(BF16)
        two = mm(high, mid_high) + mm(low, mid_high) + mm(high, mid_low) + mid_bias
        sine, cosine = sine_cosine(frequency * two)
        high = sine.astype(BF16)
        lin_two[at, :] = two.astype(BF16)
        act_two[at, :] = high
        cos_two[at, :] = cosine.astype(BF16)
        short[at, :] = (mm(high, own_out[...]) * decay(index)).astype(BF16)

    loads["cos"].wait()
    loads["sin"].wait()

    @pl.loop(0, spans)
    def _(index):
        at = tile_rows(index)
        real = mm(table_cos[at, :], short[...])
        imag = mm(table_sin[at, :], short[...])
        turn_cos = place[at, 5:6] * (1.0 / length)
        turn_sin = place[at, 6:7] * (1.0 / length)
        fil_spec[0, at, :] = real * turn_cos + imag * turn_sin
        fil_spec[1, at, :] = imag * turn_cos - real * turn_sin

    for name in ("outright", "outleft", "gateright", "liftright", "lowerleft", "lower_top", "lower_end"):
        loads[name].wait()
    out_half = d_gate[0, 0:192, own_half]
    w_out_first[0:192, :] = out_half * between(384, 0, 192)
    w_out_first[192:256, :] = jnp.zeros((64, 384), BF16)
    w_out_first[256:448, :] = out_half * between(384, 192, 384)
    w_out_first[448:512, :] = jnp.zeros((64, 384), BF16)
    for b in range(4):
        for k in range(4):
            w_out_second[b // 2, 192 * (b % 2) + 48 * k : 192 * (b % 2) + 48 * k + 48, :] = d_gate[
                0, 192 + 48 * b : 240 + 48 * b, :
            ] * between(D, 192 * k, 192 * k + 192)
    lane = lanes(384)
    inside = lane - jnp.where(lane >= 192, 192, 0)
    for b in range(4):
        kept = mask((inside >= 48 * b) & (inside < 48 * b + 48))
        w_glu[192 * b : 192 * b + 192, 0:384] = d_lift[1, 96:288, 0:384] * kept
        w_glu[192 * b : 192 * b + 192, 384:768] = d_lift[1, 96:288, 384:768] * kept
    for target in (w_gate, w_lift):
        target[0, 192:256, :] = jnp.zeros((64, D), BF16)
        target[1, 0:64, :] = jnp.zeros((64, D), BF16)
    w_lower[0, 0:512, :] = d_lift[0, :, 0:256] * between(256, 0, 192)
    w_lower[0, 512:768, :] = d_lift[0, 0:256, 384:640] * between(256, 0, 192)
    w_lower[1, 0:512, :] = d_lift[0, :, 128:384] * between(256, 64, 256)
    w_lower[1, 512:768, :] = d_lift[0, 0:256, 512:768] * between(256, 64, 256)
    for b in range(2):
        for k in range(4):
            w_lower_second[192 * b + 48 * k : 192 * b + 48 * k + 48, :] = d_lift[
                1, 48 * b : 48 * b + 48, :
            ] * between(D, 192 * k, 192 * k + 192)

    sig_copy.wait_recv()
    sig_pad[0:8, :] = jnp.zeros((8, PAD), F32)
    for part in range(2):
        sig_pad[8 + part * rows : 8 + part * rows + rows, :] = sig_rows[part].astype(F32)
    for index in range(spans):
        start = 8 + index * TILE
        total = conv[4:5, :] * sig_pad[start : start + TILE, :]
        total += conv[5:6, :] * sig_pad[start - 1 : start - 1 + TILE, :]
        total += conv[6:7, :] * sig_pad[start - 2 : start - 2 + TILE, :]
        short[index * TILE : index * TILE + TILE, :] = total.astype(BF16)

    @pl.loop(0, spans)
    def _(index):
        at = tile_rows(index)
        real = mm(table_cos[at, :], short[...])
        imag = mm(table_sin[at, :], short[...])
        sig_spec[0, at, :] = real.astype(BF16)
        sig_spec[1, at, :] = imag.astype(BF16)
        fil_re = fil_spec[0, at, :]
        fil_im = fil_spec[1, at, :]
        prod_spec[0, at, :] = (real * fil_re - imag * fil_im).astype(BF16)
        prod_spec[1, at, :] = (real * fil_im + imag * fil_re).astype(BF16)

    per_half = rows // TILE

    def long_tile(part, index):
        at = tile_rows(part * per_half + index)
        result = mm(table_cos[at, :], prod_spec[0]) + mm(table_sin[at, :], prod_spec[1])
        return result.astype(BF16)

    @pl.loop(0, per_half)
    def _(index):
        long_rows[1 - core, tile_rows(index), :] = long_tile(1 - core, index)

    long_copy = send(long_rows.at[1 - core], long_halves.at[core], sibling, 2)
    long_copy.start()

    @pl.loop(0, per_half)
    def _(index):
        long_halves[core, tile_rows(index), :] = long_tile(core, index)

    long_copy.wait_recv()
    sig_copy.wait_send()
    long_copy.wait_send()

    def inner_copy(index):
        at = tile_rows(index)
        return send(inner_out.at[narrow, at], inner_out.at[narrow, at], partner, 3 + index)

    dn_copy = send(dn_send, dn_recv, partner, 5)
    own_rows = tile_rows(narrow)
    cross_copy = send(cross_send, d_inner_out.at[own_rows], partner, 6)
    middle_copy = send(mid_send, mid_recv, partner, 11)

    def part_copy(index):
        at = tile_rows(index)
        return send(part_send.at[at], part_recv.at[at], partner, 7 + index)

    def shape_copy(index):
        at = tile_rows(index)
        return send(shape_send.at[at], shape_recv.at[at], partner, 12 + index)

    def value_copy(index):
        at = tile_rows(index)
        return send(value_send.at[at], value_recv.at[at], partner, 14 + index)

    def first_other(index):
        return 1 - narrow + index * (2 * narrow - 1)

    @pl.loop(0, tiles)
    def _(order):
        index = narrow + order * (1 - 2 * narrow)
        at = tile_rows(index)
        inner = None
        for k in range(2):
            product = (shaping[k, at, :] * long_halves[k, at, :].astype(F32)).astype(BF16)
            term = mm(product, w_out_first[k * PAD : k * PAD + PAD, :])
            inner = term if inner is None else inner + term
        inner_out[narrow, at, :] = inner.astype(BF16)

        @pl.when(order == 1)
        def _():
            inner_copy(narrow).wait_send()

        inner_copy(index).start()

    up_copy.wait_recv()
    for k in range(2):
        loads["gate", k].wait()
        loads["lift", k].wait()
    loads["upstream"].wait()

    gain_second = vectors[2:3, :]
    shift_second = vectors[3:4, :]

    @pl.loop(0, tiles)
    def _(order):
        index = first_other(order)
        at = tile_rows(index)
        inner_copy(index).wait_recv()
        mid = inputs[at, :].astype(F32)
        mid += mm(inner_out[0, at, :], w_out_second[0])
        mid += mm(inner_out[1, at, :], w_out_second[1])
        dn_own[...] = mid
        center = mid - jnp.mean(mid, axis=-1, keepdims=True)
        inverse = lax.rsqrt(jnp.mean(center * center, axis=-1, keepdims=True) + EPSILON)
        hat = center * inverse
        hat_two[...] = hat
        stats[0:TILE, 2:3] = inverse
        normed = (hat * gain_second + shift_second).astype(BF16)
        norm_two[at, :] = normed
        inner = mm(normed, w_glu[...]).astype(BF16)
        inner_glu[at, :] = inner
        lower = [None, None]
        for k in range(2):
            for columns in (slice(0, 256), slice(256, 512), slice(512, 768)):
                gate = mm(inner[:, 128 * k : 128 * k + 256], w_gate[k, :, columns])
                lift = mm(inner[:, 384 + 128 * k : 384 + 128 * k + 256], w_lift[k, :, columns])
                cumulative = 0.5 * (1.0 + lax.erf(gate * (1.0 / math.sqrt(2.0))))
                density = jnp.exp(-0.5 * gate * gate) * (1.0 / math.sqrt(2.0 * math.pi))
                activated = gate * cumulative
                unit = (activated * lift).astype(BF16)
                hid[k, at, columns] = unit
                factor_lift[k, :, columns] = activated
                factor_gate[k, :, columns] = lift * (cumulative + gate * density)
                term = mm(unit, w_lower[k, columns, :])
                lower[k] = term if lower[k] is None else lower[k] + term
        inner_low = join(*lower).astype(BF16)
        inner_lower[at, :] = inner_low
        out_own[at, :] = dn_own[:, own_half] + mm(inner_low, w_lower_second[:, own_half])
        part_send[at, :] = mm(inner_low, w_lower_second[:, other_half]).astype(BF16)

        above = jnp.concatenate([up_halves[0, at, :], up_halves[1, at, :]], axis=1)
        d_low = mm_nt(above, w_lower_second[...]).astype(BF16)
        d_inner_lower[at, :] = d_low
        gates = [None, None]
        lifts = [None, None]
        for k in range(2):
            for columns in (slice(0, 256), slice(256, 512), slice(512, 768)):
                d_hidden = mm_nt(d_low[:, 128 * k : 128 * k + 256], w_lower[k, columns, :])
                to_gate = (d_hidden * factor_gate[k, :, columns]).astype(BF16)
                to_lift = (d_hidden * factor_lift[k, :, columns]).astype(BF16)
                d_gate[k, at, columns] = to_gate
                d_lift[k, at, columns] = to_lift
                term = mm_nt(to_gate, w_gate[k, :, columns])
                gates[k] = term if gates[k] is None else gates[k] + term
                term = mm_nt(to_lift, w_lift[k, :, columns])
                lifts[k] = term if lifts[k] is None else lifts[k] + term
        d_glu = jnp.concatenate([join(*gates), join(*lifts)], axis=1).astype(BF16)
        d_inner_glu[at, :] = d_glu
        into = mm_nt(d_glu, w_glu[...])
        dn_own[...] = into

        @pl.when(order == 0)
        def _():
            dn_send[...] = dn_own[...].astype(BF16)
            dn_copy.start()

    low_lanes = lanes(128) < 64
    for columns in (slice(0, 384), slice(384, 768)):
        columns_at = slice(LOWER_RIGHT + columns.start, LOWER_RIGHT + columns.stop)
        parts = [
            mm_tn(hid[k, :, columns], d_inner_lower[:, 128 * k : 128 * k + 256]) for k in range(2)
        ]
        sums_channel[columns_at, 0:128] = parts[0][:, 0:128].astype(BF16)
        sums_channel[columns_at, 128:256] = jnp.where(
            low_lanes, parts[0][:, 128:256], parts[1][:, 0:128]
        ).astype(BF16)
        sums_channel[columns_at, 256:384] = parts[1][:, 128:256].astype(BF16)
    scatter(0, 0).start()
    for side in range(2):
        columns = slice(384 * side, 384 * side + 384)
        folded = fold(mm_tn(inner_lower[...], up_halves[side]), side)
        for b in range(2):
            first_row = LOWER_LEFT + 96 * side + 48 * b
            sums_channel[first_row : first_row + 48, :] = folded[b].astype(BF16)
    for offset, target in ((0, GATE_RIGHT), (384, LIFT_RIGHT)):
        whole = mm_tn(norm_two[...], d_inner_glu[:, offset : offset + 384])
        total = None
        for b in range(4):
            term = whole[192 * b : 192 * b + 192, :] * mask(
                (inside >= 48 * b) & (inside < 48 * b + 48), F32
            )
            total = term if total is None else total + term
        sums_channel[target : target + 192, :] = total.astype(BF16)

    for offset, upper, target in ((0, d_gate, GATE_LEFT), (384, d_lift, LIFT_LEFT)):
        for k in range(2):
            for start in (0, 384):
                whole = mm_tn(
                    inner_glu[:, offset + 128 * k : offset + 128 * k + 256],
                    upper[k, :, start : start + 384],
                )
                first_row = target + 384 * k + start // 2
                sums_channel[first_row : first_row + 192, :] = whole[
                    64 * k : 64 * k + 192, :
                ].astype(BF16)
        if upper is d_gate:
            scatter(1, 0).start()
    sums_channel[2880:3072, :] = jnp.zeros((192, 384), BF16)
    scatter(2, 0).start()
    scatter(3, 0).start()

    dn_copy.wait_recv()
    into = dn_own[...] + dn_recv[...].astype(F32)
    hat = hat_two[...]
    gain_sums[...] = jnp.zeros(gain_sums.shape, F32)
    gain_sums[0:1, :] = jnp.sum(into * hat, axis=0, keepdims=True)
    gain_sums[1:2, :] = jnp.sum(into, axis=0, keepdims=True)
    scaled = into * gain_second
    above = jnp.concatenate([up_halves[0, own_rows, :], up_halves[1, own_rows, :]], axis=1)
    d_mid = above.astype(F32) + stats[0:TILE, 2:3] * (
        scaled
        - jnp.mean(scaled, axis=-1, keepdims=True)
        - hat * jnp.mean(scaled * hat, axis=-1, keepdims=True)
    )
    hat_two[...] = d_mid
    branch[...] = d_mid.astype(BF16)
    cross_send[...] = mm_nt(branch[...], w_out_second[1 - narrow]).astype(BF16)
    cross_copy.start()
    mid_send[...] = hat_two[:, other_half].astype(BF16)
    d_inner_out[own_rows, :] = mm_nt(branch[...], w_out_second[narrow]).astype(BF16)
    for i in range(4):
        advance(i, 0)
    for h in range(2):
        for side in range(2):
            columns = slice(384 * side, 384 * side + 384)
            folded = fold(mm_tn(inner_out[h, own_rows, :], branch[:, columns]), side)
            for b in range(2):
                first_row = OUT_LEFT + 192 * h + 96 * side + 48 * b
                mixer_slab[first_row : first_row + 48, :] = folded[b].astype(BF16)

    @pl.loop(0, tiles)
    def _(order):
        index = narrow + order * (1 - 2 * narrow)
        at = tile_rows(index)

        @pl.when(order == 1)
        def _():
            cross_copy.wait_recv()
            middle_copy.start()

        d_inner = d_inner_out[at, :]
        for k in range(2):
            d_mixed = mm_nt(d_inner, w_out_first[k * PAD : k * PAD + PAD, :])
            d_shaping[k, at, :] = (d_mixed * long_halves[k, at, :].astype(F32)).astype(BF16)
            sig_halves[k, at, :] = (d_mixed * shaping[k, at, :]).astype(BF16)

    dl_copy = send(sig_halves.at[1 - core], dl_rows.at[core], sibling, 9)
    dl_copy.start()
    dl_rows[core] = sig_halves[core]

    @pl.loop(0, tiles)
    def _(index):
        at = tile_rows(index)
        to_shape = jnp.concatenate([d_shaping[0, at, :], d_shaping[1, at, :]], axis=1)
        d_inner_one[at, 384:768] = mm_nt(to_shape, w_shape[...]).astype(BF16)
        shape_send[at, :] = mm_nt(
            to_shape, w_shape[pl.ds(pl.multiple_of((1 - narrow) * 192, 192), 192), :]
        ).astype(BF16)
        shape_copy(index).start()

    @pl.loop(0, tiles)
    def _(index):
        part_copy(index).start()

    advance(1, 1)
    advance(0, 1)

    lane = lax.broadcasted_iota(jnp.int32, (2 * PAD, 384), 1)
    row = lax.broadcasted_iota(jnp.int32, (2 * PAD, 384), 0)
    squeeze = mask(row == lane + jnp.where(lane >= 192, 64, 0))

    def first_gradient(offset):
        whole = mm_tn(norm_one[...], d_inner_one[:, offset : offset + 384])
        total = None
        for b in range(4):
            term = whole[192 * b : 192 * b + 192, :] * between(384, 96 * b, 96 * b + 96, F32)
            total = term if total is None else total + term
        return total.astype(BF16)

    def second_gradient(offset, upper):
        above = jnp.concatenate([upper[0], upper[1]], axis=1)
        whole = mm_tn(inner_one[:, offset : offset + 384], above)
        pieces = []
        for b in range(4):
            total = None
            for k in range(2):
                term = whole[96 * b + 48 * k : 96 * b + 48 * k + 48, :] * between(
                    2 * PAD, PAD * k, PAD * k + PAD, F32
                )
                total = term if total is None else total + term
            pieces.append(total)
        return mm(jnp.concatenate(pieces, axis=0).astype(BF16), squeeze).astype(BF16)

    mixer_slab[SHAPE_RIGHT : SHAPE_RIGHT + 192, :] = first_gradient(384)
    mixer_slab[SHAPE_LEFT : SHAPE_LEFT + 192, :] = second_gradient(384, d_shaping)
    scatter(4, 0).start()
    parts = []
    for k in range(2):
        product = (shaping[k] * long_halves[k].astype(F32)).astype(BF16)
        parts.append(mm_tn(product, d_inner_out[...]))
    late[OUT_RIGHT : OUT_RIGHT + 192, :] = jnp.where(
        lanes(384) < 192, parts[0][0:192, :], parts[1][0:192, :]
    ).astype(BF16)
    advance(2, 1)
    advance(1, 2)
    advance(0, 2)

    dl_copy.wait_recv()

    @pl.loop(0, spans)
    def _(index):
        at = tile_rows(index)
        upper = dl_rows[...].reshape(length, PAD)
        real = mm(table_cos[at, :], upper)
        imag = mm(table_sin[at, :], upper)
        fil_re = fil_spec[0, at, :]
        fil_im = fil_spec[1, at, :]
        prod_spec[0, at, :] = (real * fil_re + imag * fil_im).astype(BF16)
        prod_spec[1, at, :] = (imag * fil_re - real * fil_im).astype(BF16)
        sig_re = sig_spec[0, at, :].astype(F32)
        sig_im = sig_spec[1, at, :].astype(F32)
        turn_cos = place[at, 5:6] * (1.0 / length)
        turn_sin = place[at, 6:7] * (1.0 / length)
        both_re = real * sig_re + imag * sig_im
        both_im = imag * sig_re - real * sig_im
        sig_spec[0, at, :] = (both_re * turn_cos - both_im * turn_sin).astype(BF16)
        sig_spec[1, at, :] = (both_im * turn_cos + both_re * turn_sin).astype(BF16)

    advance(4, 0)
    advance(3, 1)
    advance(1, 3)
    advance(2, 2)
    advance(0, 3)
    ds_pad[length : length + 8, :] = jnp.zeros((8, PAD), F32)

    @pl.loop(0, spans)
    def _(index):
        at = tile_rows(index)
        result = mm(table_cos[at, :], prod_spec[0]) + mm(table_sin[at, :], prod_spec[1])
        ds_pad[at, :] = result.astype(BF16).astype(F32)

    for index in range(spans):
        start = index * TILE
        total = conv[4:5, :] * ds_pad[start : start + TILE, :]
        total += conv[5:6, :] * ds_pad[start + 1 : start + 1 + TILE, :]
        total += conv[6:7, :] * ds_pad[start + 2 : start + 2 + TILE, :]
        part, inner_start = divmod(start, rows)
        long_rows[part, inner_start : inner_start + TILE, :] = total.astype(BF16)
    ds_copy = send(long_rows.at[1 - core], ds_halves.at[core], sibling, 10)
    ds_copy.start()
    ds_halves[core] = long_rows[core]

    advance(4, 1)
    advance(3, 2)
    advance(2, 3)
    retreat(1, 3)
    retreat(0, 3)
    grad_vectors[...] = jnp.zeros(grad_vectors.shape, F32)
    sums = [jnp.zeros((1, PAD), F32) for _ in range(3)]
    for index in range(spans):
        start = index * TILE
        upper = ds_pad[start : start + TILE, :]
        for j in range(3):
            sums[j] += jnp.sum(
                upper * sig_pad[8 + start - j : 8 + start - j + TILE, :], axis=0, keepdims=True
            )
    sums = jnp.concatenate(sums + [jnp.zeros((5, PAD), F32)], axis=0)
    lane = lax.broadcasted_iota(jnp.int32, (PAD, 384), 1)
    row = lax.broadcasted_iota(jnp.int32, (PAD, 384), 0)
    place_core = mask((lane == core * 192 + row) & (row < 192))
    conv_sums = mm(sums.astype(BF16), place_core)
    grad_vectors[4:7, :] = conv_sums[0:3, :]

    d_lin[...] = jnp.zeros(d_lin.shape, F32)
    grad_filter[...] = jnp.zeros(grad_filter.shape, F32)

    def filter_back(index):
        at = tile_rows(index)
        d_taps = mm(table_cos[at, :], sig_spec[0]) + mm(table_sin[at, :], sig_spec[1])
        d_mod = d_taps * decay(index)
        d_mod = d_mod.astype(BF16)
        d_lin[...] += mm_tn(act_two[at, :], d_mod)
        two = mm_nt(d_mod, own_out[...]) * cos_two[at, :].astype(F32)
        scaled_two = two * frequency
        coarse_two = scaled_two.astype(BF16)
        grad_filter[0:128, :] += mm_tn(act_one[at, :], coarse_two)
        one = mm_nt(coarse_two, mid_high) * cos_one[at, :].astype(F32)
        scaled_one = one * frequency
        grad_filter[128:136, :] += mm_tn(place_parts[at, :], scaled_one.astype(BF16))[0:8, :]
        grad_filter[136:137, :] += jnp.sum(scaled_one, axis=0, keepdims=True)
        grad_filter[137:138, :] += jnp.sum(scaled_two, axis=0, keepdims=True)
        grad_filter[138:139, :] += jnp.sum(
            one * lin_one[at, :].astype(F32) + two * lin_two[at, :].astype(F32), axis=0, keepdims=True
        )

    pl.loop(0, spans // 2)(filter_back)
    advance(4, 2)
    pl.loop(spans // 2, spans)(filter_back)
    late[FILTER_OUT : FILTER_OUT + 128, :] = mm(d_lin[...].astype(BF16), place_core).astype(BF16)
    for i in range(3):
        late[FILTER : FILTER + 48, 128 * i : 128 * i + 128] = grad_filter[
            48 * i : 48 * i + 48, :
        ].astype(BF16)


    advance(4, 3)
    advance(3, 3)
    retreat(1, 2)
    retreat(0, 2)
    retreat(2, 3)

    ds_copy.wait_recv()
    other_blocks = pl.ds(pl.multiple_of((1 - narrow) * 192, 192), 192)

    @pl.loop(0, tiles)
    def _(index):
        at = tile_rows(index)
        to_value = jnp.concatenate([ds_halves[0, at, :], ds_halves[1, at, :]], axis=1)
        d_inner = mm_nt(to_value, w_value[...]).astype(BF16)
        d_inner_one[at, 0:384] = d_inner
        against = inner_one[at, :].astype(F32) - through[1:2, :]
        d_inner = d_inner_one[at, :].astype(F32)
        plain = jnp.sum(d_inner * through[0:1, :], axis=-1, keepdims=True)
        along = jnp.sum(d_inner * against, axis=-1, keepdims=True)
        stats[at, 2:3] = plain
        stats[at, 3:4] = along
        lane = lanes(128)
        tail = jnp.where(lane == 64, plain, jnp.where(lane == 65, along, 0.0))
        away = mm_nt(to_value, w_value[other_blocks, :])
        value_send[at, 0:128] = away[:, 0:128].astype(BF16)
        value_send[at, 128:192] = away[:, 128:192].astype(BF16)
        value_send[at, 192:256] = tail[:, 64:128].astype(BF16)
        value_copy(index).start()

    @pl.loop(0, tiles)
    def _(index):
        at = tile_rows(index)
        into = mm_nt(d_inner_one[at, :], w_first[...])
        hat = (inputs[at, :].astype(F32) - stats[at, 0:1]) * stats[at, 1:2]
        gain_sums[2:3, :] += jnp.sum(into * hat, axis=0, keepdims=True)
        gain_sums[3:4, :] += jnp.sum(into, axis=0, keepdims=True)

    retreat(4, 3)
    retreat(3, 3)
    late[VALUE_RIGHT : VALUE_RIGHT + 192, :] = first_gradient(0)
    late[VALUE_LEFT : VALUE_LEFT + 192, :] = second_gradient(0, ds_halves)
    grad_vectors[0:4, :] = gain_sums[0:4, 0:384]
    grad_vectors[8:12, :] = gain_sums[0:4, 384:768]
    late[VECTORS : VECTORS + 16, :] = grad_vectors[...].astype(BF16)

    to_core = late_copy(
        late.at[pl.ds(pl.multiple_of((1 - core) * 384, 16), 384)], late_core, sibling, 0
    )
    to_core.start()
    retreat(4, 2)
    to_core.wait()

    @pl.loop(0, 384 // CHUNK)
    def _(index):
        at = pl.ds(pl.multiple_of(core * 384 + index * CHUNK, 16), CHUNK)
        came = late_core[pl.ds(pl.multiple_of(index * CHUNK, 16), CHUNK), :]
        late[at, :] = (late[at, :].astype(F32) + came.astype(F32)).astype(BF16)

    def share(t):
        return pl.multiple_of(core * 384 + lax.rem(chip + 8 - t, 8) * CHUNK, 16)

    direct = [
        late_copy(late.at[pl.ds(share(8 - t), CHUNK)], late_slots.at[t - 1], fellows[t], t)
        for t in range(1, 8)
    ]
    for copy in direct:
        copy.start()

    first_half = vectors[0:1, own_half]
    middle_copy.wait_recv()
    d_middle[own_rows, :] = hat_two[:, own_half]
    d_middle[tile_rows(1 - narrow), :] = mid_recv[...].astype(F32)
    @pl.loop(0, tiles)
    def _(index):
        at = tile_rows(index)
        part_copy(index).wait_recv()
        hidden_out[at, :] = (out_own[at, :] + part_recv[at, :].astype(F32)).astype(BF16)
        shape_copy(index).wait_recv()
        value_copy(index).wait_recv()
        into = mm_nt(d_inner_one[at, :], w_first[own_half, :])
        into += mm_nt(value_recv[at, 0:192], w_cross[0])
        into += mm_nt(shape_recv[at, :], w_cross[1])
        plain = (stats[at, 2:3] + value_recv[at, 192:193].astype(F32)) * (1.0 / D)
        along = (stats[at, 3:4] + value_recv[at, 193:194].astype(F32)) * (1.0 / D)
        hat = (inputs[at, own_half].astype(F32) - stats[at, 0:1]) * stats[at, 1:2]
        hidden_grad[at, :] = (
            d_middle[at, :] + stats[at, 1:2] * (into * first_half - plain - hat * along)
        ).astype(BF16)

    retreat(4, 1)
    early_rows = pl.ds(offsets[4][1], PART // 2)
    across_early = late_copy(mixer_slab.at[early_rows], mixer_slab.at[early_rows], partner, 40)
    across_early.start()
    retreat(1, 1)
    retreat(0, 1)
    store(hidden_out, result_out)
    store(hidden_grad, result_grad)
    total = late[pl.ds(share(0), CHUNK), :].astype(F32)
    for t in range(1, 8):
        direct[t - 1].wait()
        total += late_slots[t - 1].astype(F32)
    own_share = pl.ds(pl.multiple_of(PART + share(0), 16), CHUNK)
    mixer_slab[own_share, :] = total.astype(BF16)
    spread_out = [
        late_copy(mixer_slab.at[own_share], mixer_slab.at[own_share], fellows[t], 8 + t)
        for t in range(1, 8)
    ]
    for copy in spread_out:
        copy.start()
    retreat(2, 2)
    retreat(3, 2)
    across = []
    along_own = []
    for t in range(8):
        if t > 0:
            spread_out[t - 1].wait()
        at = pl.ds(pl.multiple_of(PART + share(t), 16), CHUNK)
        across.append(late_copy(mixer_slab.at[at], mixer_slab.at[at], partner, 16 + t))
        across[t].start()
        along_own.append(late_copy(mixer_slab.at[at], mixer_slab.at[at], sibling, 24 + t))
        along_own[t].start()
    across_early.wait()
    other = sums_mixer.at[1 - narrow, early_rows]
    along_early = late_copy(other, other, sibling, 41)
    along_early.start()
    retreat(2, 1)
    along_other = []
    for t in range(8):
        across[t].wait()
        at = pl.ds(pl.multiple_of(PART + share(t), 16), CHUNK)
        other = sums_mixer.at[1 - narrow, at]
        along_other.append(late_copy(other, other, sibling, 32 + t))
        along_other[t].start()
    retreat(3, 1)
    for i in (1, 0, 2, 3):
        retreat(i, 0)
        at = pl.ds(PART * i, PART)
        store(sums_channel.at[at], result_channel.at[at])
    retreat(4, 0)
    along_early.wait()
    early = pl.ds(0, PART)
    store(sums_mixer.at[:, early], result_mixer.at[:, early])
    for copy in along_own + along_other:
        copy.wait()
    rest = pl.ds(PART, PART)
    store(sums_mixer.at[:, rest], result_mixer.at[:, rest])

    inner_copy(1 - narrow).wait_send()
    for copy in (up_copy, dl_copy, ds_copy, dn_copy, cross_copy, middle_copy):
        copy.wait_send()

    @pl.loop(0, tiles)
    def _(index):
        for copy in (part_copy, shape_copy, value_copy):
            copy(index).wait_send()

    for copy in stores:
        copy.wait()


def finish_kernel(
    hidden_in,
    hidden_grad_in,
    hbm_channel,
    hbm_mixer,
    hidden_out,
    hidden_grad,
    grad_gainfirst,
    grad_shiftfirst,
    grad_valueright,
    grad_valueleft,
    grad_shaperight,
    grad_shapeleft,
    grad_convtaps,
    grad_posweight,
    grad_posbias,
    grad_sinefreq,
    grad_midweight,
    grad_midbias,
    grad_filterout,
    grad_outright,
    grad_outleft,
    grad_gainsecond,
    grad_shiftsecond,
    grad_gateright,
    grad_gateleft,
    grad_liftright,
    grad_liftleft,
    grad_lowerright,
    grad_lowerleft,
    channel,
    mixer,
    pass_out,
    pass_grad,
    valueright,
    valueleft,
    shaperight,
    shapeleft,
    outright,
    outleft,
    gateright,
    gateleft,
    liftright,
    liftleft,
    lowerright,
    lowerleft,
    both_filter,
    in_sem,
    out_sem,
):
    ins = []
    outs = []

    def fetch(source, target):
        ins.append(pltpu.make_async_copy(source, target, in_sem.at[len(ins)]))
        ins[-1].start()

    def store(source, target):
        outs.append(pltpu.make_async_copy(source, target, out_sem.at[len(outs)]))
        outs[-1].start()

    for i in range(4):
        at = pl.ds(PART * i, PART)
        fetch(hbm_channel.at[at], channel.at[at])
    fetch(hbm_mixer, mixer)
    fetch(hidden_in, pass_out)
    fetch(hidden_grad_in, pass_grad)

    ins[0].wait()
    lowerright[...] = channel[LOWER_RIGHT : LOWER_RIGHT + D, :].astype(F32)
    store(lowerright, grad_lowerright)
    ins[1].wait()
    for h in range(2):
        columns = slice(384 * h, 384 * h + 384)
        lowerleft[:, columns] = channel[LOWER_LEFT + 96 * h : LOWER_LEFT + 96 * h + 96, :].astype(F32)
    gateright[...] = channel[GATE_RIGHT : GATE_RIGHT + 192, :].astype(F32)
    liftright[...] = channel[LIFT_RIGHT : LIFT_RIGHT + 192, :].astype(F32)
    store(lowerleft, grad_lowerleft)
    store(gateright, grad_gateright)
    store(liftright, grad_liftright)
    ins[2].wait()
    for i in range(4):
        first_row = GATE_LEFT + 192 * i
        gateleft[:, 384 * i : 384 * i + 384] = channel[first_row : first_row + 192, :].astype(F32)
    store(gateleft, grad_gateleft)
    ins[3].wait()
    for i in range(4):
        first_row = LIFT_LEFT + 192 * i
        liftleft[:, 384 * i : 384 * i + 384] = channel[first_row : first_row + 192, :].astype(F32)
    store(liftleft, grad_liftleft)
    ins[4].wait()

    lane = lax.broadcasted_iota(jnp.int32, (384, D), 1)
    row = lax.broadcasted_iota(jnp.int32, (384, D), 0)
    step = jnp.where(row >= 96, 96, 0) + jnp.where(row >= 192, 96, 0) + jnp.where(row >= 288, 96, 0)
    unselect = [mask(lane == row + step + 96 * h) for h in range(2)]
    for first_row, target, result in (
        (PART + VALUE_RIGHT, valueright, grad_valueright),
        (SHAPE_RIGHT, shaperight, grad_shaperight),
    ):
        target[...] = mm(mixer[0, first_row : first_row + 192, :], unselect[0]) + mm(
            mixer[1, first_row : first_row + 192, :], unselect[1]
        )
        store(target, result)
    for first_row, target, result in (
        (PART + OUT_RIGHT, outright, grad_outright),
        (SHAPE_LEFT, shapeleft, grad_shapeleft),
        (PART + VALUE_LEFT, valueleft, grad_valueleft),
    ):
        for h in range(2):
            target[:, 384 * h : 384 * h + 384] = mixer[h, first_row : first_row + 192, :].astype(F32)
        store(target, result)
    for h in range(2):
        for side in range(2):
            at = slice(OUT_LEFT + 192 * h + 96 * side, OUT_LEFT + 192 * h + 96 * side + 96)
            outleft[96 * h : 96 * h + 96, 384 * side : 384 * side + 384] = mixer[0, at, :].astype(
                F32
            ) + mixer[1, at, :].astype(F32)
    store(outleft, grad_outleft)
    vectors = [mixer[h, PART + VECTORS : PART + VECTORS + 16, :].astype(F32) for h in range(2)]
    whole = jnp.concatenate(vectors, axis=1)
    both = vectors[0] + vectors[1]
    grad_convtaps[...] = whole[4:7, :]
    for i, target in enumerate((grad_gainsecond, grad_shiftsecond, grad_gainfirst, grad_shiftfirst)):
        target[...] = jnp.concatenate([both[i : i + 1, :], both[8 + i : 9 + i, :]], axis=1).reshape(D)
    for i in range(3):
        columns = slice(128 * i, 128 * i + 128)
        at = slice(PART + FILTER, PART + FILTER + 48)
        both_filter[48 * i : 48 * i + 48, :] = mixer[0, at, columns].astype(F32) + mixer[
            1, at, columns
        ].astype(F32)
    grad_midweight[...] = both_filter[0:128, :]
    grad_posweight[...] = both_filter[128:133, :]
    grad_posbias[...] = both_filter[136:137, :].reshape(128)
    grad_midbias[...] = both_filter[137:138, :].reshape(128)
    grad_sinefreq[...] = both_filter[138:139, :].reshape(128)
    count = grad_filterout.shape[0]
    first = (lax.axis_index("wide") * 2 + lax.axis_index("narrow")) * count
    total = jnp.zeros(grad_filterout.shape, F32)
    row = lax.broadcasted_iota(jnp.int32, (count, 384), 0)
    lane = lax.broadcasted_iota(jnp.int32, (count, 384), 1)
    for h in range(2):
        total += mm_nt(
            mask(lane + 384 * h == first + row),
            mixer[h, PART + FILTER_OUT : PART + FILTER_OUT + 128, :],
        )
    grad_filterout[...] = total
    ins[5].wait()
    store(pass_out, hidden_out)
    ins[6].wait()
    store(pass_grad, hidden_grad)
    for copy in outs:
        copy.wait()


def transform_tables(length):
    index = np.arange(length, dtype=np.float64) + 0.5
    angle = np.outer(index, index) * (math.pi / length)
    return (np.cos(angle).astype(jnp.bfloat16), np.sin(angle).astype(jnp.bfloat16))


def place_table(length):
    places = np.arange(length, dtype=np.float64)
    angle = places * (2.0 * math.pi / length)
    turn = (places + 0.5) * (math.pi / (2.0 * length))
    columns = [
        places / length,
        np.cos(angle),
        np.sin(angle),
        np.cos(2.0 * angle),
        np.sin(2.0 * angle),
        np.cos(turn),
        np.sin(turn),
        np.zeros(length),
    ]
    table = np.stack(columns, axis=1).astype(np.float32)
    feats = np.concatenate([table[:, :5], np.zeros((length, 3), np.float32)], axis=1)
    high = feats.astype(jnp.bfloat16)
    low = (feats - high.astype(np.float32)).astype(jnp.bfloat16)
    return (table, np.concatenate([high, low, high, np.zeros_like(high)], axis=1))


def pair_body(
    hidden_in,
    gainfirst,
    shiftfirst,
    valueright,
    valueleft,
    shaperight,
    shapeleft,
    convtaps,
    posweight,
    posbias,
    sinefreq,
    midweight,
    midbias,
    filterout,
    outright,
    outleft,
    gainsecond,
    shiftsecond,
    gateright,
    gateleft,
    liftright,
    liftleft,
    lowerright,
    lowerleft,
    grad_out,
):
    rows = hidden_in.shape[0]
    length = 2 * rows
    table_cos, table_sin = transform_tables(length)
    def out(extent, dtype=BF16):
        return jax.ShapeDtypeStruct(extent, dtype)

    def buf(*extent, dtype=BF16):
        return pltpu.VMEM(extent, dtype)

    vmem = pl.BlockSpec(memory_space=pltpu.VMEM)
    hbm = pl.BlockSpec(memory_space=pl.ANY)
    results = pl.pallas_call(
        whole_kernel,
        out_shape=(
            out((rows, 384)),
            out((rows, 384)),
            out((CHANNEL_ROWS, 384)),
            out((2, 2 * PART, 384)),
        ),
        in_specs=[hbm] * 4 + [vmem] * 12 + [hbm] * 13,
        out_specs=[hbm] * 4,
        scratch_shapes=[
            buf(rows, 384),
            buf(rows, 384),
            buf(CHANNEL_ROWS, 384),
            buf(2, 2 * PART, 384),
            pltpu.SemaphoreType.DMA((8,)),
            buf(rows, D),
            buf(length, length),
            buf(length, length),
            buf(8, D, dtype=F32),
            buf(16, 128, dtype=F32),
            buf(D, D),
            buf(384, 512),
            buf(384, 512),
            buf(512, 384),
            buf(2, 384, D),
            buf(D, D),
            buf(2, 256, D),
            buf(2, 256, D),
            buf(2, D, 256),
            buf(384, D),
            buf(2, rows, 384),
            buf(rows, 128, dtype=F32),
            buf(rows, D),
            buf(rows, D),
            buf(2, rows, PAD),
            buf(2, rows, PAD),
            buf(2, rows, PAD, dtype=F32),
            buf(length + 8, PAD, dtype=F32),
            buf(length, PAD),
            buf(length, 128),
            buf(length, 128),
            buf(length, 128),
            buf(length, 128),
            buf(length, 128),
            buf(length, 128),
            buf(2, length, PAD, dtype=F32),
            buf(2, length, PAD),
            buf(2, length, PAD),
            buf(2, rows, PAD),
            buf(2, rows, PAD),
            buf(2, rows, 384),
            buf(TILE, D, dtype=F32),
            buf(rows, D),
            buf(rows, D),
            buf(2, TILE, D, dtype=F32),
            buf(2, TILE, D, dtype=F32),
            buf(2, rows, D),
            buf(rows, 384),
            buf(rows, 384, dtype=F32),
            buf(rows, 384),
            buf(rows, 384),
            buf(rows, 384),
            buf(2, rows, D),
            buf(2, rows, D),
            buf(rows, D),
            buf(TILE, D, dtype=F32),
            buf(TILE, D),
            buf(TILE, D),
            buf(rows, 384),
            buf(2, rows, PAD),
            buf(2, rows, PAD),
            buf(length + 8, PAD, dtype=F32),
            buf(2, rows, PAD),
            buf(rows, D),
            buf(TILE, 384),
            buf(TILE, 384),
            buf(TILE, 384),
            buf(rows, 384, dtype=F32),
            buf(TILE, D),
            buf(rows, 192),
            buf(rows, 192),
            buf(rows, 256),
            buf(rows, 256),
            buf(2, 384, 192),
            buf(8, D, dtype=F32),
            buf(128, PAD, dtype=F32),
            buf(128, PAD),
            buf(16, 384, dtype=F32),
            buf(144, 128, dtype=F32),
            buf(8, D, dtype=F32),
            pltpu.SemaphoreType.DMA((16,)),
            pltpu.SemaphoreType.DMA((16,)),
            pltpu.SemaphoreType.DMA((20,)),
            buf(5, STEP_ROWS[4], 384),
            pltpu.SemaphoreType.DMA((40,)),
            pltpu.SemaphoreType.DMA((40,)),
            pltpu.SemaphoreType.REGULAR((20,)),
            buf(PART, 384),
            buf(PART // 2, 384),
            buf(7, CHUNK, 384),
            pltpu.SemaphoreType.DMA((42,)),
            pltpu.SemaphoreType.DMA((42,)),
        ],
        compiler_params=pltpu.CompilerParams(
            collective_id=0, has_side_effects=True, vmem_limit_bytes=63 * 1024 * 1024
        ),
    )(
        hidden_in,
        grad_out,
        table_cos,
        table_sin,
        *place_table(length),
        gainfirst,
        shiftfirst,
        gainsecond,
        shiftsecond,
        convtaps,
        posweight,
        posbias,
        midbias,
        sinefreq,
        midweight,
        filterout,
        valueright,
        valueleft,
        shaperight,
        shapeleft,
        outright,
        outleft,
        gateright,
        gateleft,
        liftright,
        liftleft,
        lowerright,
        lowerleft,
    )
    count = D // (lax.axis_size("wide") * lax.axis_size("narrow"))
    square = out((192, D), F32)
    grads = pl.pallas_call(
        finish_kernel,
        out_shape=(
            out((rows, 384)),
            out((rows, 384)),
            out((D,), F32),
            out((D,), F32),
            square,
            square,
            square,
            square,
            out((3, D), F32),
            out((5, 128), F32),
            out((128,), F32),
            out((128,), F32),
            out((128, 128), F32),
            out((128,), F32),
            out((count, 128), F32),
            square,
            square,
            out((D,), F32),
            out((D,), F32),
            out(gateright.shape, F32),
            out(gateleft.shape, F32),
            out(liftright.shape, F32),
            out(liftleft.shape, F32),
            out(lowerright.shape, F32),
            out(lowerleft.shape, F32),
        ),
        in_specs=[hbm] * 4,
        out_specs=[hbm] * 2 + [vmem] * 2 + [hbm] * 4 + [vmem] * 7 + [hbm] * 2 + [vmem] * 2 + [hbm] * 6,
        scratch_shapes=[
            buf(CHANNEL_ROWS, 384),
            buf(2, 2 * PART, 384),
            buf(rows, 384),
            buf(rows, 384),
            *[buf(192, D, dtype=F32)] * 6,
            buf(*gateright.shape, dtype=F32),
            buf(*gateleft.shape, dtype=F32),
            buf(*liftright.shape, dtype=F32),
            buf(*liftleft.shape, dtype=F32),
            buf(*lowerright.shape, dtype=F32),
            buf(*lowerleft.shape, dtype=F32),
            buf(144, 128, dtype=F32),
            pltpu.SemaphoreType.DMA((7,)),
            pltpu.SemaphoreType.DMA((14,)),
        ],
        compiler_params=pltpu.CompilerParams(vmem_limit_bytes=60 * 1024 * 1024),
    )(*results)
    return (*grads[:14], grads[14].T, *grads[15:])


def solution(mesh):
    pairs = mesh.shape["wide"] == 2 * SEQS and mesh.shape["narrow"] == 2
    return jax.shard_map(
        pair_body if pairs else body,
        mesh=mesh,
        in_specs=(
            P("wide", None),
            P(),
            P(),
            P(),
            P(),
            P(),
            P(),
            P(),
            P(),
            P(),
            P(),
            P(),
            P(),
            P(),
            P(),
            P(),
            P(),
            P(),
            P(None, "narrow"),
            P(None, "narrow"),
            P(None, "narrow"),
            P(None, "narrow"),
            P(None, "narrow"),
            P("narrow", None),
            P("wide", "narrow"),
        ),
        out_specs=(
            P("wide", "narrow"),
            P("wide", "narrow"),
            P(),
            P(),
            P(),
            P(),
            P(),
            P(),
            P(),
            P(),
            P(),
            P(),
            P(),
            P(),
            P(None, ("wide", "narrow")),
            P(),
            P(),
            P(),
            P(),
            P(None, "narrow"),
            P(None, "narrow"),
            P(None, "narrow"),
            P(None, "narrow"),
            P(None, "narrow"),
            P("narrow", None),
        ),
        check_vma=False,
    )
```

```python
import math

import jax
import jax.numpy as jnp
import numpy as np
from jax import lax
from jax.experimental import pallas as pl
from jax.experimental.pallas import tpu as pltpu
from jax.sharding import PartitionSpec as P

D = 768
BLOCKS = 4
SEQS = 8


EPSILON = 1e-05
HIGHEST = lax.Precision.HIGHEST


def from_behind(x, axis, by):
    length = lax.axis_size(axis)
    pairs = [(i, i + by) for i in range(length) if 0 <= i + by < length]
    return lax.ppermute(x, axis, pairs)


def norm_forward(values, gain, shift):
    center = values - jnp.mean(values, axis=-1, keepdims=True)
    inverse = lax.rsqrt(jnp.mean(center * center, axis=-1, keepdims=True) + EPSILON)
    normed = center * inverse
    return (normed * gain + shift, normed, inverse)


def norm_backward(upstream, normed, inverse, gain):
    scaled = upstream * gain
    result = inverse * (
        scaled
        - jnp.mean(scaled, axis=-1, keepdims=True)
        - normed * jnp.mean(scaled * normed, axis=-1, keepdims=True)
    )
    return (result, jnp.sum(upstream * normed, axis=0), jnp.sum(upstream, axis=0))


def right_view(right, nblocks, groups, group_first):
    width_in = right.shape[0]
    piece = right.shape[1] // (nblocks * groups)
    if group_first:
        return (right.reshape(width_in, groups, nblocks, piece), "ikbc")
    return (right.reshape(width_in, nblocks, groups, piece), "ibkc")


def section_one(inputs, right, groups, group_first):
    rowcount = inputs.shape[0]
    width_in = right.shape[0]
    nblocks = inputs.shape[1] // width_in
    factor, letters = right_view(right, nblocks, groups, group_first)
    first = jnp.einsum(
        "tbi," + letters + "->tkbc",
        inputs.reshape(rowcount, nblocks, width_in),
        factor,
        preferred_element_type=jnp.float32,
    )
    return first.reshape(rowcount, groups, -1).astype(jnp.bfloat16)


def section_two(middle_part, left):
    groups = middle_part.shape[1]
    result = jnp.einsum(
        "tkj,jke->tke",
        middle_part,
        left.reshape(left.shape[0], groups, -1),
        preferred_element_type=jnp.float32,
    )
    return result.reshape(result.shape[0], -1)


def back_two(middle_part, left, upstream):
    groups = middle_part.shape[1]
    left_view = left.reshape(left.shape[0], groups, -1)
    grad_left = jnp.einsum(
        "tkj,tke->jke", middle_part, upstream, preferred_element_type=jnp.float32
    )
    grad_middle = jnp.einsum(
        "tke,jke->tkj", upstream, left_view, preferred_element_type=jnp.float32
    )
    return (grad_left.reshape(left.shape[0], -1), grad_middle.astype(jnp.bfloat16))


def back_one(inputs, right, grad_middle, group_first):
    rowcount = inputs.shape[0]
    width_in = right.shape[0]
    nblocks = inputs.shape[1] // width_in
    groups = grad_middle.shape[1]
    factor, letters = right_view(right, nblocks, groups, group_first)
    spread_back = grad_middle.reshape(rowcount, groups, nblocks, -1)
    blocked = inputs.reshape(rowcount, nblocks, width_in)
    grad_right = jnp.einsum(
        "tbi,tkbc->" + letters, blocked, spread_back, preferred_element_type=jnp.float32
    )
    grad_inputs = jnp.einsum(
        "tkbc," + letters + "->tbi", spread_back, factor, preferred_element_type=jnp.float32
    )
    return (grad_right.reshape(width_in, -1), grad_inputs.reshape(rowcount, -1))


def fourier_tables(length):
    span = length // 128
    slow_index = jnp.arange(span, dtype=jnp.int32)
    fast_index = jnp.arange(128, dtype=jnp.int32)
    small = (slow_index[:, None] * slow_index[None, :] % span).astype(jnp.float32) * (
        2.0 * math.pi / span
    )
    twist = (slow_index[:, None] * fast_index[None, :] % length).astype(jnp.float32) * (
        2.0 * math.pi / length
    )
    large = (fast_index[:, None] * fast_index[None, :] % 128).astype(jnp.float32) * (
        2.0 * math.pi / 128
    )
    return (
        jnp.cos(small),
        jnp.sin(small),
        jnp.cos(twist),
        jnp.sin(twist),
        jnp.cos(large),
        jnp.sin(large),
    )


def to_spectrum(signal, tables):
    cos_small, sin_small, cos_twist, sin_twist, cos_large, sin_large = tables
    span = cos_small.shape[0]
    padded = jnp.concatenate([signal, jnp.zeros_like(signal)], axis=-1)
    padded = padded.reshape(signal.shape[:-1] + (span, 128))
    first_re = jnp.einsum("...qp,qk->...kp", padded, cos_small, precision=HIGHEST)
    first_im = -jnp.einsum("...qp,qk->...kp", padded, sin_small, precision=HIGHEST)
    turned_re = first_re * cos_twist + first_im * sin_twist
    turned_im = first_im * cos_twist - first_re * sin_twist
    out_re = jnp.einsum("...kp,pj->...kj", turned_re, cos_large, precision=HIGHEST) + jnp.einsum(
        "...kp,pj->...kj", turned_im, sin_large, precision=HIGHEST
    )
    out_im = jnp.einsum("...kp,pj->...kj", turned_im, cos_large, precision=HIGHEST) - jnp.einsum(
        "...kp,pj->...kj", turned_re, sin_large, precision=HIGHEST
    )
    return (out_re, out_im)


def from_spectrum(real_part, imag_part, tables):
    cos_small, sin_small, cos_twist, sin_twist, cos_large, sin_large = tables
    span = cos_small.shape[0]
    back_re = jnp.einsum("...kj,pj->...kp", real_part, cos_large, precision=HIGHEST) - jnp.einsum(
        "...kj,pj->...kp", imag_part, sin_large, precision=HIGHEST
    )
    back_im = jnp.einsum("...kj,pj->...kp", imag_part, cos_large, precision=HIGHEST) + jnp.einsum(
        "...kj,pj->...kp", real_part, sin_large, precision=HIGHEST
    )
    turned_re = back_re * cos_twist - back_im * sin_twist
    turned_im = back_im * cos_twist + back_re * sin_twist
    signal = (
        jnp.einsum("...kp,qk->...qp", turned_re, cos_small, precision=HIGHEST)
        - jnp.einsum("...kp,qk->...qp", turned_im, sin_small, precision=HIGHEST)
    ) / (span * 128)
    signal = signal.reshape(signal.shape[:-2] + (span * 128,))
    return signal[..., : span * 64]


def position_features(length):
    places = jnp.arange(length, dtype=jnp.float32)
    angle = places * (2.0 * math.pi / length)
    return jnp.stack(
        [
            places / length,
            jnp.cos(angle),
            jnp.sin(angle),
            jnp.cos(2.0 * angle),
            jnp.sin(2.0 * angle),
        ],
        axis=1,
    )


def decay_factors(channel_ids, length):
    rank = (channel_ids * 5 % D).astype(jnp.float32) / D
    lowest = math.log(0.25 / length)
    highest = math.log(1.0 / 30.0)
    rate = jnp.exp(lowest + rank * (highest - lowest))
    places = jnp.arange(length, dtype=jnp.float32)
    return jnp.exp(-rate[:, None] * places[None, :]) * jnp.sqrt(2.0 * rate)[:, None]


def channel_order(data, nwide, nnarrow, rows_half):
    count = data.shape[0]
    return data.reshape(count, nnarrow, nwide, rows_half).transpose(0, 2, 1, 3).reshape(count, -1)


def row_order(data, nwide, nnarrow):
    total = data.shape[0]
    rows_half = data.shape[1]
    count = total // (nwide * nnarrow)
    return (
        data.reshape(nnarrow, nwide, count, rows_half)
        .transpose(1, 0, 2, 3)
        .reshape(total, rows_half)
        .T
    )


def body(
    hidden_in,
    gainfirst,
    shiftfirst,
    valueright,
    valueleft,
    shaperight,
    shapeleft,
    convtaps,
    posweight,
    posbias,
    sinefreq,
    midweight,
    midbias,
    filterout,
    outright,
    outleft,
    gainsecond,
    shiftsecond,
    gateright,
    gateleft,
    liftright,
    liftleft,
    lowerright,
    lowerleft,
    grad_out,
):
    rowcount = hidden_in.shape[0]
    local_groups = gateright.shape[1] // gateleft.shape[0]
    nwide = lax.axis_size("wide")
    nnarrow = lax.axis_size("narrow")
    narrow_index = lax.axis_index("narrow")
    rows_half = rowcount // nnarrow
    row_start = narrow_index * rows_half
    combined = lax.axis_index("wide") * nnarrow + narrow_index
    resid = lax.dynamic_slice_in_dim(hidden_in, row_start, rows_half, 0).astype(jnp.float32)
    normone, hat_one, inv_one = norm_forward(resid, gainfirst, shiftfirst)
    normone = normone.astype(jnp.bfloat16)
    mid_value = section_one(normone, valueright, BLOCKS, False)
    signal = section_two(mid_value, valueleft).astype(jnp.bfloat16)
    mid_shape = section_one(normone, shaperight, BLOCKS, False)
    shaping = section_two(mid_shape, shapeleft)
    group = nwide // SEQS * nnarrow
    place = combined % group
    before = from_behind(signal[-2:], ("wide", "narrow"), 1)
    before = jnp.where(place == 0, jnp.zeros_like(before), before)
    extended = jnp.concatenate([before, signal], axis=0).astype(jnp.float32)
    shortconv = (
        convtaps[0] * extended[2:] + convtaps[1] * extended[1:-1] + convtaps[2] * extended[:-2]
    ).astype(jnp.bfloat16)
    channels = lax.all_to_all(
        lax.all_to_all(shortconv.T, "wide", split_axis=0, concat_axis=1, tiled=True),
        "narrow",
        split_axis=0,
        concat_axis=1,
        tiled=True,
    )
    channels = channel_order(channels, nwide, nnarrow, rows_half)
    count = channels.shape[0]
    length = channels.shape[1] // SEQS
    feats = position_features(length)
    lin_one = jnp.dot(feats, posweight, precision=HIGHEST) + posbias
    act_one = jnp.sin(sinefreq * lin_one)
    lin_two = jnp.dot(act_one, midweight, precision=HIGHEST) + midbias
    act_two = jnp.sin(sinefreq * lin_two)
    own_cols = lax.dynamic_slice_in_dim(filterout, combined * count, count, 1)
    channel_ids = combined * count + jnp.arange(count, dtype=jnp.int32)
    modulation = decay_factors(channel_ids, length)
    taps = jnp.dot(act_two, own_cols, precision=HIGHEST).T * modulation
    tables = fourier_tables(2 * length)
    sig_re, sig_im = to_spectrum(channels.astype(jnp.float32).reshape(count, SEQS, length), tables)
    fil_re, fil_im = to_spectrum(taps.reshape(count, 1, length), tables)
    conv_chan = from_spectrum(
        sig_re * fil_re - sig_im * fil_im, sig_re * fil_im + sig_im * fil_re, tables
    )
    conv_chan = conv_chan.reshape(count, SEQS * length).astype(jnp.bfloat16)
    longconv = lax.all_to_all(
        lax.all_to_all(conv_chan, "wide", split_axis=1, concat_axis=0, tiled=True),
        "narrow",
        split_axis=1,
        concat_axis=0,
        tiled=True,
    )
    longconv = row_order(longconv, nwide, nnarrow)
    mixed = (shaping * longconv.astype(jnp.float32)).astype(jnp.bfloat16)
    mid_out = section_one(mixed, outright, BLOCKS, False)
    middle = resid + section_two(mid_out, outleft)
    normtwo, hat_two, inv_two = norm_forward(middle, gainsecond, shiftsecond)
    normtwo = normtwo.astype(jnp.bfloat16)
    norm_all = lax.all_gather(normtwo, "narrow", axis=0, tiled=True)
    mid_gate = section_one(norm_all, gateright, local_groups, True)
    pregate = section_two(mid_gate, gateleft)
    mid_lift = section_one(norm_all, liftright, local_groups, True)
    prelift = section_two(mid_lift, liftleft)
    cumulative = 0.5 * (1.0 + lax.erf(pregate * (1.0 / math.sqrt(2.0))))
    activated = pregate * cumulative
    hidden = (activated * prelift).astype(jnp.bfloat16)
    mid_lower = section_one(hidden, lowerright, BLOCKS, False)
    partial_sum = section_two(mid_lower, lowerleft)
    partial_sum = partial_sum + lax.dynamic_update_slice_in_dim(
        jnp.zeros_like(partial_sum), middle, row_start, 0
    )
    hidden_out = lax.psum_scatter(
        partial_sum.astype(jnp.bfloat16), "narrow", scatter_dimension=1, tiled=True
    )
    upstream = lax.all_gather(grad_out, "narrow", axis=1, tiled=True)
    grad_lowerleft, grad_mid_lower = back_two(
        mid_lower, lowerleft, upstream.reshape(rowcount, BLOCKS, -1)
    )
    grad_lowerright, grad_hidden = back_one(hidden, lowerright, grad_mid_lower, False)
    density = jnp.exp(-0.5 * pregate * pregate) * (1.0 / math.sqrt(2.0 * math.pi))
    grad_pregate = (grad_hidden * prelift * (cumulative + pregate * density)).astype(jnp.bfloat16)
    grad_prelift = (grad_hidden * activated).astype(jnp.bfloat16)
    grad_gateleft, grad_mid_gate = back_two(
        mid_gate, gateleft, grad_pregate.reshape(rowcount, local_groups, -1)
    )
    grad_gateright, into_gate = back_one(norm_all, gateright, grad_mid_gate, True)
    grad_liftleft, grad_mid_lift = back_two(
        mid_lift, liftleft, grad_prelift.reshape(rowcount, local_groups, -1)
    )
    grad_liftright, into_lift = back_one(norm_all, liftright, grad_mid_lift, True)
    ffn_local = (
        grad_gateright,
        grad_gateleft,
        grad_liftright,
        grad_liftleft,
        grad_lowerright,
        grad_lowerleft,
    )
    dnormtwo = lax.psum_scatter(
        (into_gate + into_lift).astype(jnp.bfloat16), "narrow", scatter_dimension=0, tiled=True
    ).astype(jnp.float32)
    back_two_norm, grad_gainsecond, grad_shiftsecond = norm_backward(
        dnormtwo, hat_two, inv_two, gainsecond
    )
    up_rows = lax.dynamic_slice_in_dim(upstream, row_start, rows_half, 0)
    dmiddle = up_rows.astype(jnp.float32) + back_two_norm
    dbranch = dmiddle.astype(jnp.bfloat16)
    grad_outleft, grad_mid_out = back_two(mid_out, outleft, dbranch.reshape(rows_half, BLOCKS, -1))
    grad_outright, dmixed = back_one(mixed, outright, grad_mid_out, False)
    dshaping = (dmixed * longconv.astype(jnp.float32)).astype(jnp.bfloat16)
    dlong = (dmixed * shaping).astype(jnp.bfloat16)
    grad_chan = lax.all_to_all(
        lax.all_to_all(dlong.T, "wide", split_axis=0, concat_axis=1, tiled=True),
        "narrow",
        split_axis=0,
        concat_axis=1,
        tiled=True,
    )
    grad_chan = channel_order(grad_chan, nwide, nnarrow, rows_half)
    dlong_re, dlong_im = to_spectrum(
        grad_chan.astype(jnp.float32).reshape(count, SEQS, length), tables
    )
    dshort_chan = from_spectrum(
        dlong_re * fil_re + dlong_im * fil_im, dlong_im * fil_re - dlong_re * fil_im, tables
    )
    dshort_chan = dshort_chan.reshape(count, SEQS * length).astype(jnp.bfloat16)
    filt_re = jnp.sum(dlong_re * sig_re + dlong_im * sig_im, axis=1, keepdims=True)
    filt_im = jnp.sum(dlong_im * sig_re - dlong_re * sig_im, axis=1, keepdims=True)
    grad_taps = from_spectrum(filt_re, filt_im, tables).reshape(count, length)
    dshort = lax.all_to_all(
        lax.all_to_all(dshort_chan, "wide", split_axis=1, concat_axis=0, tiled=True),
        "narrow",
        split_axis=1,
        concat_axis=0,
        tiled=True,
    )
    dshort = row_order(dshort, nwide, nnarrow)
    grad_modded = grad_taps * modulation
    grad_filterout = jnp.dot(act_two.T, grad_modded.T, precision=HIGHEST)
    dact_two = jnp.dot(grad_modded.T, own_cols.T, precision=HIGHEST)
    dlin_two = dact_two * jnp.cos(sinefreq * lin_two)
    scaled_two = dlin_two * sinefreq
    grad_midweight = jnp.dot(act_one.T, scaled_two, precision=HIGHEST)
    grad_midbias = jnp.sum(scaled_two, axis=0)
    dact_one = jnp.dot(scaled_two, midweight.T, precision=HIGHEST)
    dlin_one = dact_one * jnp.cos(sinefreq * lin_one)
    scaled_one = dlin_one * sinefreq
    grad_posweight = jnp.dot(feats.T, scaled_one, precision=HIGHEST)
    grad_posbias = jnp.sum(scaled_one, axis=0)
    grad_sinefreq = jnp.sum(dlin_one * lin_one, axis=0) + jnp.sum(dlin_two * lin_two, axis=0)
    after = from_behind(dshort[:2], ("wide", "narrow"), -1)
    after = jnp.where(place == group - 1, jnp.zeros_like(after), after)
    ext_grad = jnp.concatenate([dshort, after], axis=0).astype(jnp.float32)
    dsignal = (
        convtaps[0] * ext_grad[:-2] + convtaps[1] * ext_grad[1:-1] + convtaps[2] * ext_grad[2:]
    ).astype(jnp.bfloat16)
    short_grad = dshort.astype(jnp.float32)
    grad_convtaps = jnp.stack(
        [
            jnp.sum(extended[2:] * short_grad, axis=0),
            jnp.sum(extended[1:-1] * short_grad, axis=0),
            jnp.sum(extended[:-2] * short_grad, axis=0),
        ]
    )
    grad_valueleft, grad_mid_value = back_two(
        mid_value, valueleft, dsignal.reshape(rows_half, BLOCKS, -1)
    )
    grad_valueright, into_value = back_one(normone, valueright, grad_mid_value, False)
    grad_shapeleft, grad_mid_shape = back_two(
        mid_shape, shapeleft, dshaping.reshape(rows_half, BLOCKS, -1)
    )
    grad_shaperight, into_shape = back_one(normone, shaperight, grad_mid_shape, False)
    back_one_norm, grad_gainfirst, grad_shiftfirst = norm_backward(
        into_value + into_shape, hat_one, inv_one, gainfirst
    )
    full_grad = (dmiddle + back_one_norm).astype(jnp.bfloat16)
    hidden_grad = lax.all_to_all(full_grad, "narrow", split_axis=1, concat_axis=0, tiled=True)
    mixer_grads = lax.psum(
        (
            grad_gainfirst,
            grad_shiftfirst,
            grad_valueright,
            grad_valueleft,
            grad_shaperight,
            grad_shapeleft,
            grad_convtaps,
            grad_posweight,
            grad_posbias,
            grad_sinefreq,
            grad_midweight,
            grad_midbias,
            grad_outright,
            grad_outleft,
            grad_gainsecond,
            grad_shiftsecond,
        ),
        ("wide", "narrow"),
    )
    ffn_grads = lax.psum(
        (ffn_local[0], ffn_local[1], ffn_local[2], ffn_local[3], ffn_local[4], ffn_local[5]), "wide"
    )
    return (
        hidden_out,
        hidden_grad,
        mixer_grads[0],
        mixer_grads[1],
        mixer_grads[2],
        mixer_grads[3],
        mixer_grads[4],
        mixer_grads[5],
        mixer_grads[6],
        mixer_grads[7],
        mixer_grads[8],
        mixer_grads[9],
        mixer_grads[10],
        mixer_grads[11],
        grad_filterout,
        mixer_grads[12],
        mixer_grads[13],
        mixer_grads[14],
        mixer_grads[15],
        ffn_grads[0],
        ffn_grads[1],
        ffn_grads[2],
        ffn_grads[3],
        ffn_grads[4],
        ffn_grads[5],
    )


F32 = jnp.float32
BF16 = jnp.bfloat16
MESH = pl.DeviceIdType.MESH
TILE = 256
PAD = 256


def mm(a, b, precision=None):
    return lax.dot_general(
        a, b, (((1,), (0,)), ((), ())), precision=precision, preferred_element_type=F32
    )


def mm_nt(a, b, precision=None):
    return lax.dot_general(
        a, b, (((1,), (1,)), ((), ())), precision=precision, preferred_element_type=F32
    )


def mm_tn(a, b, precision=None):
    return lax.dot_general(
        a, b, (((0,), (0,)), ((), ())), precision=precision, preferred_element_type=F32
    )


def lanes(width):
    return lax.broadcasted_iota(jnp.int32, (1, width), 1)


def mask(condition, dtype=BF16):
    return jnp.where(condition, 1.0, 0.0).astype(dtype)


def between(width, low, high, dtype=BF16):
    lane = lanes(width)
    return mask((lane >= low) & (lane < high), dtype)


def join(first, second):
    return jnp.concatenate(
        [first[:, :128], first[:, 128:] + second[:, :128], second[:, 128:]], axis=1
    )


def sine_cosine(angle):
    turns = jnp.floor(angle * (1.0 / math.pi) + 0.5)
    rest = angle - turns * 3.140625
    rest = rest - turns * 9.67502593994140625e-4
    rest = rest - turns * 1.509957990978376e-7
    flip = 1.0 - 2.0 * (turns - 2.0 * jnp.floor(turns * 0.5))
    square = rest * rest
    sine = 1.0
    for divisor in (110.0, 72.0, 42.0, 20.0, 6.0):
        sine = 1.0 - square * (1.0 / divisor) * sine
    cosine = 1.0
    for divisor in (132.0, 90.0, 56.0, 30.0, 12.0, 2.0):
        cosine = 1.0 - square * (1.0 / divisor) * cosine
    return (sine * rest * flip, cosine * flip)


def fold(whole, side):
    return [
        whole[192 * b + 96 * side : 192 * b + 96 * side + 48, :] * between(384, 0, 192, F32)
        + whole[192 * b + 96 * side + 48 : 192 * b + 96 * side + 96, :] * between(384, 192, 384, F32)
        for b in range(2)
    ]


STRIDES = (1, 2, 4, 8)
PART = 768
STEP_ROWS = (0, 384, 576, 672, 720)
ORDERS = ((0, 1, 2, 3), (0, 2, 3, 1), (0, 1, 2, 3), (0, 1, 2, 3), (0, 1, 2, 3))
CHUNK = 48
LOWER_RIGHT, LOWER_LEFT, GATE_RIGHT, LIFT_RIGHT, GATE_LEFT, LIFT_LEFT, CHANNEL_ROWS = (
    0,
    768,
    960,
    1152,
    1344,
    2112,
    4 * PART,
)
OUT_LEFT, SHAPE_RIGHT, SHAPE_LEFT = (0, 384, 576)
VALUE_RIGHT, VALUE_LEFT, FILTER_OUT, VECTORS, FILTER, OUT_RIGHT = (0, 192, 384, 512, 528, 576)


def tile_rows(index, size=TILE):
    return pl.ds(pl.multiple_of(index * size, size), size)


def whole_kernel(
    hidden_in,
    upstream,
    hbm_cos,
    hbm_sin,
    place,
    place_parts,
    gainfirst,
    shiftfirst,
    gainsecond,
    shiftsecond,
    convtaps,
    posweight,
    posbias,
    midbias,
    sinefreq,
    midweight,
    filterout,
    valueright,
    valueleft,
    shaperight,
    shapeleft,
    outright,
    outleft,
    gateright,
    gateleft,
    liftright,
    liftleft,
    lowerright,
    lowerleft,
    result_out,
    result_grad,
    result_channel,
    result_mixer,
    hidden_out,
    hidden_grad,
    sums_channel,
    sums_mixer,
    store_sem,
    inputs,
    table_cos,
    table_sin,
    vectors,
    filter_vectors,
    w_first,
    w_value,
    w_shape,
    w_out_first,
    w_out_second,
    w_glu,
    w_gate,
    w_lift,
    w_lower,
    w_lower_second,
    up_halves,
    stats,
    norm_one,
    inner_one,
    sig_halves,
    sig_rows,
    shaping,
    sig_pad,
    short,
    act_one,
    cos_one,
    lin_one,
    act_two,
    cos_two,
    lin_two,
    fil_spec,
    sig_spec,
    prod_spec,
    long_rows,
    long_halves,
    inner_out,
    hat_two,
    norm_two,
    inner_glu,
    factor_gate,
    factor_lift,
    hid,
    inner_lower,
    out_own,
    part_send,
    part_recv,
    d_inner_lower,
    d_gate,
    d_lift,
    d_inner_glu,
    dn_own,
    dn_send,
    dn_recv,
    d_inner_out,
    d_shaping,
    dl_rows,
    ds_pad,
    ds_halves,
    d_inner_one,
    cross_send,
    mid_send,
    mid_recv,
    d_middle,
    branch,
    shape_send,
    shape_recv,
    value_send,
    value_recv,
    w_cross,
    through,
    d_lin,
    own_out,
    grad_vectors,
    grad_filter,
    gain_sums,
    send_sem,
    recv_sem,
    load_sem,
    got,
    sum_send,
    sum_recv,
    sum_free,
    late,
    late_core,
    late_slots,
    late_send,
    late_recv,
):
    rows = inputs.shape[0]
    tiles = rows // TILE
    length = 2 * rows
    spans = length // TILE
    wide = lax.axis_index("wide")
    narrow = lax.axis_index("narrow")
    bits = [lax.rem(wide // stride, 2) for stride in STRIDES]
    core = bits[0]
    sibling = (wide + 1 - 2 * core, narrow)
    partner = (wide, 1 - narrow)
    quarter = 2 * narrow + core
    own_half = pl.ds(pl.multiple_of(narrow * 384, 384), 384)
    other_half = pl.ds(pl.multiple_of((1 - narrow) * 384, 384), 384)

    loads = {}

    def load(name, source, target):
        loads[name] = pltpu.make_async_copy(source, target, load_sem.at[len(loads)])
        loads[name].start()

    load("inputs", hidden_in, inputs)
    load("valueright", valueright, hid.at[0, pl.ds(0, 192)])
    load("shaperight", shaperight, hid.at[0, pl.ds(192, 192)])
    load("valueleft", valueleft, hid.at[1, pl.ds(0, 192)])
    load("shapeleft", shapeleft, hid.at[1, pl.ds(192, 192)])
    load("filterout", filterout, factor_gate.at[0, pl.ds(0, 128)])
    load("cos", hbm_cos, table_cos)
    load("sin", hbm_sin, table_sin)
    load("outright", outright, d_gate.at[0, pl.ds(0, 192)])
    load("outleft", outleft, d_gate.at[0, pl.ds(192, 192)])
    load("gateright", gateright, d_lift.at[1, pl.ds(96, 192), pl.ds(0, 384)])
    load("liftright", liftright, d_lift.at[1, pl.ds(96, 192), pl.ds(384, 384)])
    load("lowerleft", lowerleft, d_lift.at[1, pl.ds(0, 96)])
    load("lower_top", lowerright.at[pl.ds(0, 512)], d_lift.at[0, :, pl.ds(0, 384)])
    load("lower_end", lowerright.at[pl.ds(512, 256)], d_lift.at[0, pl.ds(0, 256), pl.ds(384, 384)])
    for k in range(2):
        at = pl.ds(64 * k, 192)
        load(("gate", k), gateleft.at[:, pl.ds(D * k, D)], w_gate.at[k, at])
        load(("lift", k), liftleft.at[:, pl.ds(D * k, D)], w_lift.at[k, at])
    load("upstream", upstream, up_halves.at[narrow])

    stores = []

    def store(source, target):
        stores.append(pltpu.make_async_copy(source, target, store_sem.at[len(stores)]))
        stores[-1].start()

    barrier = pltpu.get_barrier_semaphore()
    others = [(wide + stride * (1 - 2 * bit), narrow) for stride, bit in zip(STRIDES, bits)]
    chip = wide // 2
    fellows = [(2 * lax.rem(chip + t, 8) + core, narrow) for t in range(8)]
    for device in [sibling, partner] + fellows[1:]:
        pl.semaphore_signal(barrier, inc=1, device_id=device, device_id_type=MESH)

    for i, source in enumerate((gainfirst, shiftfirst, gainsecond, shiftsecond)):
        vectors[i : i + 1, :] = source[...].reshape(1, D)
    vectors[4:7, :] = convtaps[...]
    vectors[7:8, :] = jnp.zeros((1, D), F32)
    filter_vectors[...] = jnp.zeros(filter_vectors.shape, F32)
    filter_vectors[0:5, :] = posweight[...]
    for i, source in enumerate((posbias, midbias, sinefreq)):
        filter_vectors[8 + i : 9 + i, :] = source[...].reshape(1, 128)

    def send(source, target, device, index):
        return pltpu.make_async_remote_copy(
            src_ref=source,
            dst_ref=target,
            send_sem=send_sem.at[index],
            recv_sem=recv_sem.at[index],
            device_id=device,
            device_id_type=MESH,
        )

    mixer_slab = sums_mixer.at[narrow]
    parts_of = [sums_channel.at[pl.ds(PART * i, PART)] for i in range(4)] + [mixer_slab.at[pl.ds(0, PART)]]
    offsets = []
    for order in ORDERS:
        found = [0]
        for step in range(4):
            found.append(pl.multiple_of(found[step] + bits[order[step]] * (PART >> (step + 1)), 16))
        offsets.append(found)

    def sum_copy(source, target, i, step, back):
        index = 8 * i + 4 * back + step
        return pltpu.make_async_remote_copy(
            src_ref=source,
            dst_ref=target,
            send_sem=sum_send.at[index],
            recv_sem=sum_recv.at[index],
            device_id=others[ORDERS[i][step]],
            device_id_type=MESH,
        )

    def scatter(i, step):
        size = PART >> (step + 1)
        away = pl.multiple_of(offsets[i][step] + (1 - bits[ORDERS[i][step]]) * size, 16)
        return sum_copy(
            parts_of[i].at[pl.ds(away, size)], got.at[i, pl.ds(STEP_ROWS[step], size)], i, step, 0
        )

    def gather(i, step):
        at = pl.ds(offsets[i][step + 1], PART >> (step + 1))
        return sum_copy(parts_of[i].at[at], parts_of[i].at[at], i, step, 1)

    def hand_back(i, step):
        pl.semaphore_wait(sum_free.at[4 * i + step], 1)
        gather(i, step).start()

    def advance(i, step):
        scatter(i, step).wait()

        @pl.loop(0, (PART >> (step + 1)) // CHUNK)
        def _(index):
            own = pl.ds(pl.multiple_of(offsets[i][step + 1] + index * CHUNK, 16), CHUNK)
            came = got[i, pl.ds(pl.multiple_of(STEP_ROWS[step] + index * CHUNK, 16), CHUNK), :]
            parts_of[i][own, :] = (parts_of[i][own, :].astype(F32) + came.astype(F32)).astype(BF16)

        pl.semaphore_signal(
            sum_free.at[4 * i + step],
            inc=1,
            device_id=others[ORDERS[i][step]],
            device_id_type=MESH,
        )
        if step < 3:
            scatter(i, step + 1).start()
        else:
            hand_back(i, 3)

    def retreat(i, step):
        gather(i, step).wait()
        if step > 0:
            hand_back(i, step - 1)

    def late_copy(source, target, device, index):
        return pltpu.make_async_remote_copy(
            src_ref=source,
            dst_ref=target,
            send_sem=late_send.at[index],
            recv_sem=late_recv.at[index],
            device_id=device,
            device_id_type=MESH,
        )

    row = lax.broadcasted_iota(jnp.int32, (D, 384), 0)
    lane = lax.broadcasted_iota(jnp.int32, (D, 384), 1)
    step = jnp.where(lane >= 96, 96, 0) + jnp.where(lane >= 192, 96, 0) + jnp.where(lane >= 288, 96, 0)
    select = mask(row == lane + step + narrow * 96)
    for name in ("valueright", "shaperight", "valueleft", "shapeleft"):
        loads[name].wait()
    right_half = mm(hid[0, 0:192, :], select).astype(BF16)
    shape_half = mm(hid[0, 192:384, :], select).astype(BF16)
    for b in range(4):
        kept = between(384, 96 * b, 96 * b + 96)
        w_first[192 * b : 192 * b + 192, 0:384] = right_half * kept
        w_first[192 * b : 192 * b + 192, 384:768] = shape_half * kept
    row = lax.broadcasted_iota(jnp.int32, (D, 2 * PAD), 0)
    lane = lax.broadcasted_iota(jnp.int32, (D, 2 * PAD), 1)
    group = jnp.where(lane >= PAD, 1, 0)
    entry = lane - PAD * group
    spread = mask((row == (2 * narrow + group) * 192 + entry) & (entry < 192))
    for source, target in ((0, w_value), (192, w_shape)):
        wider = mm(hid[1, source : source + 192, :], spread).astype(BF16)
        for b in range(4):
            for k in range(2):
                target[96 * b + 48 * k : 96 * b + 48 * k + 48, :] = wider[
                    48 * b : 48 * b + 48, :
                ] * between(2 * PAD, PAD * k, PAD * k + PAD)
    row = lax.broadcasted_iota(jnp.int32, (D, 192), 0)
    lane = lax.broadcasted_iota(jnp.int32, (D, 192), 1)
    start = (2 * narrow) * 192 + (1 - narrow) * 96
    cross = mask(row == start + lane + jnp.where(lane >= 96, 96, 0))
    for i in range(2):
        part = mm(hid[0, 192 * i : 192 * i + 192, :], cross).astype(BF16)
        for b in range(2):
            w_cross[i, 192 * b : 192 * b + 192, :] = part * between(192, 96 * b, 96 * b + 96)
    first = vectors[0:1, :]
    shift_first = vectors[1:2, :]

    coarse = vectors[...].astype(BF16)
    fine = (vectors[...] - coarse.astype(F32)).astype(BF16)
    through[...] = mm(coarse, w_first[...]) + mm(fine, w_first[...])
    loads["inputs"].wait()

    @pl.loop(0, tiles)
    def _(index):
        at = tile_rows(index)
        values = inputs[at, :].astype(F32)
        average = jnp.mean(values, axis=-1, keepdims=True)
        center = values - average
        inverse = lax.rsqrt(jnp.mean(center * center, axis=-1, keepdims=True) + EPSILON)
        hat = center * inverse
        stats[at, 0:1] = average
        stats[at, 1:2] = inverse
        normed = (hat * first + shift_first).astype(BF16)
        norm_one[at, :] = normed
        inner = mm(normed, w_first[...]).astype(BF16)
        inner_one[at, :] = inner
        signal = mm(inner[:, :384], w_value[...]).astype(BF16)
        sig_halves[0, at, :] = signal[:, :PAD]
        sig_halves[1, at, :] = signal[:, PAD:]
        shaped = mm(inner[:, 384:], w_shape[...])
        shaping[0, at, :] = shaped[:, :PAD]
        shaping[1, at, :] = shaped[:, PAD:]

    pl.semaphore_wait(barrier, 9)
    sig_copy = send(sig_halves.at[1 - core], sig_rows.at[core], sibling, 1)
    sig_copy.start()
    up_copy = send(upstream, up_halves.at[narrow], partner, 0)
    up_copy.start()
    sig_rows[core] = sig_halves[core]

    row = lax.broadcasted_iota(jnp.int32, (D, PAD), 0)
    lane = lax.broadcasted_iota(jnp.int32, (D, PAD), 1)
    pick = mask((row == quarter * 192 + lane) & (lane < 192))
    conv = mm(coarse, pick) + mm(fine, pick)
    loads["filterout"].wait()
    own_out[...] = mm(factor_gate[0, 0:128, :].astype(BF16), pick).astype(BF16)
    pos_bias = filter_vectors[8:9, :]
    mid_bias = filter_vectors[9:10, :]
    frequency = filter_vectors[10:11, :]
    mid_high = midweight[...].astype(BF16)
    mid_low = (midweight[...] - mid_high.astype(F32)).astype(BF16)
    pos_high = filter_vectors[0:8, :].astype(BF16).astype(F32)
    pos_parts = jnp.concatenate(
        [pos_high, pos_high, filter_vectors[0:8, :] - pos_high, jnp.zeros((8, 128), F32)], axis=0
    ).astype(BF16)
    ranks = 5 * (quarter * 192 + lanes(PAD))
    for bound in range(5):
        ranks = jnp.where(ranks >= D, ranks - D, ranks)
    lowest = math.log(0.25 / length)
    highest = math.log(1.0 / 30.0)
    rate = jnp.exp(lowest + ranks.astype(F32) * (1.0 / D) * (highest - lowest))
    loud = jnp.sqrt(2.0 * rate)

    def decay(index):
        places = (lax.broadcasted_iota(jnp.int32, (TILE, PAD), 0) + index * TILE).astype(F32)
        return jnp.exp(-rate * places) * loud

    @pl.loop(0, spans)
    def _(index):
        at = tile_rows(index)
        one = mm(place_parts[at, :], pos_parts) + pos_bias
        sine, cosine = sine_cosine(frequency * one)
        high = sine.astype(BF16)
        low = (sine - high.astype(F32)).astype(BF16)
        lin_one[at, :] = one.astype(BF16)
        act_one[at, :] = high
        cos_one[at, :] = cosine.astype(BF16)
        two = mm(high, mid_high) + mm(low, mid_high) + mm(high, mid_low) + mid_bias
        sine, cosine = sine_cosine(frequency * two)
        high = sine.astype(BF16)
        lin_two[at, :] = two.astype(BF16)
        act_two[at, :] = high
        cos_two[at, :] = cosine.astype(BF16)
        short[at, :] = (mm(high, own_out[...]) * decay(index)).astype(BF16)

    loads["cos"].wait()
    loads["sin"].wait()

    @pl.loop(0, spans)
    def _(index):
        at = tile_rows(index)
        real = mm(table_cos[at, :], short[...])
        imag = mm(table_sin[at, :], short[...])
        turn_cos = place[at, 5:6] * (1.0 / length)
        turn_sin = place[at, 6:7] * (1.0 / length)
        fil_spec[0, at, :] = real * turn_cos + imag * turn_sin
        fil_spec[1, at, :] = imag * turn_cos - real * turn_sin

    for name in ("outright", "outleft", "gateright", "liftright", "lowerleft", "lower_top", "lower_end"):
        loads[name].wait()
    out_half = d_gate[0, 0:192, own_half]
    w_out_first[0:192, :] = out_half * between(384, 0, 192)
    w_out_first[192:256, :] = jnp.zeros((64, 384), BF16)
    w_out_first[256:448, :] = out_half * between(384, 192, 384)
    w_out_first[448:512, :] = jnp.zeros((64, 384), BF16)
    for b in range(4):
        for k in range(4):
            w_out_second[b // 2, 192 * (b % 2) + 48 * k : 192 * (b % 2) + 48 * k + 48, :] = d_gate[
                0, 192 + 48 * b : 240 + 48 * b, :
            ] * between(D, 192 * k, 192 * k + 192)
    lane = lanes(384)
    inside = lane - jnp.where(lane >= 192, 192, 0)
    for b in range(4):
        kept = mask((inside >= 48 * b) & (inside < 48 * b + 48))
        w_glu[192 * b : 192 * b + 192, 0:384] = d_lift[1, 96:288, 0:384] * kept
        w_glu[192 * b : 192 * b + 192, 384:768] = d_lift[1, 96:288, 384:768] * kept
    for target in (w_gate, w_lift):
        target[0, 192:256, :] = jnp.zeros((64, D), BF16)
        target[1, 0:64, :] = jnp.zeros((64, D), BF16)
    w_lower[0, 0:512, :] = d_lift[0, :, 0:256] * between(256, 0, 192)
    w_lower[0, 512:768, :] = d_lift[0, 0:256, 384:640] * between(256, 0, 192)
    w_lower[1, 0:512, :] = d_lift[0, :, 128:384] * between(256, 64, 256)
    w_lower[1, 512:768, :] = d_lift[0, 0:256, 512:768] * between(256, 64, 256)
    for b in range(2):
        for k in range(4):
            w_lower_second[192 * b + 48 * k : 192 * b + 48 * k + 48, :] = d_lift[
                1, 48 * b : 48 * b + 48, :
            ] * between(D, 192 * k, 192 * k + 192)

    sig_copy.wait_recv()
    sig_pad[0:8, :] = jnp.zeros((8, PAD), F32)
    for part in range(2):
        sig_pad[8 + part * rows : 8 + part * rows + rows, :] = sig_rows[part].astype(F32)
    for index in range(spans):
        start = 8 + index * TILE
        total = conv[4:5, :] * sig_pad[start : start + TILE, :]
        total += conv[5:6, :] * sig_pad[start - 1 : start - 1 + TILE, :]
        total += conv[6:7, :] * sig_pad[start - 2 : start - 2 + TILE, :]
        short[index * TILE : index * TILE + TILE, :] = total.astype(BF16)

    @pl.loop(0, spans)
    def _(index):
        at = tile_rows(index)
        real = mm(table_cos[at, :], short[...])
        imag = mm(table_sin[at, :], short[...])
        sig_spec[0, at, :] = real.astype(BF16)
        sig_spec[1, at, :] = imag.astype(BF16)
        fil_re = fil_spec[0, at, :]
        fil_im = fil_spec[1, at, :]
        prod_spec[0, at, :] = (real * fil_re - imag * fil_im).astype(BF16)
        prod_spec[1, at, :] = (real * fil_im + imag * fil_re).astype(BF16)

    per_half = rows // TILE

    def long_tile(part, index):
        at = tile_rows(part * per_half + index)
        result = mm(table_cos[at, :], prod_spec[0]) + mm(table_sin[at, :], prod_spec[1])
        return result.astype(BF16)

    @pl.loop(0, per_half)
    def _(index):
        long_rows[1 - core, tile_rows(index), :] = long_tile(1 - core, index)

    long_copy = send(long_rows.at[1 - core], long_halves.at[core], sibling, 2)
    long_copy.start()

    @pl.loop(0, per_half)
    def _(index):
        long_halves[core, tile_rows(index), :] = long_tile(core, index)

    long_copy.wait_recv()
    sig_copy.wait_send()
    long_copy.wait_send()

    def inner_copy(index):
        at = tile_rows(index)
        return send(inner_out.at[narrow, at], inner_out.at[narrow, at], partner, 3 + index)

    dn_copy = send(dn_send, dn_recv, partner, 5)
    own_rows = tile_rows(narrow)
    cross_copy = send(cross_send, d_inner_out.at[own_rows], partner, 6)
    middle_copy = send(mid_send, mid_recv, partner, 11)

    def part_copy(index):
        at = tile_rows(index)
        return send(part_send.at[at], part_recv.at[at], partner, 7 + index)

    def shape_copy(index):
        at = tile_rows(index)
        return send(shape_send.at[at], shape_recv.at[at], partner, 12 + index)

    def value_copy(index):
        at = tile_rows(index)
        return send(value_send.at[at], value_recv.at[at], partner, 14 + index)

    def first_other(index):
        return 1 - narrow + index * (2 * narrow - 1)

    @pl.loop(0, tiles)
    def _(order):
        index = narrow + order * (1 - 2 * narrow)
        at = tile_rows(index)
        inner = None
        for k in range(2):
            product = (shaping[k, at, :] * long_halves[k, at, :].astype(F32)).astype(BF16)
            term = mm(product, w_out_first[k * PAD : k * PAD + PAD, :])
            inner = term if inner is None else inner + term
        inner_out[narrow, at, :] = inner.astype(BF16)

        @pl.when(order == 1)
        def _():
            inner_copy(narrow).wait_send()

        inner_copy(index).start()

    up_copy.wait_recv()
    for k in range(2):
        loads["gate", k].wait()
        loads["lift", k].wait()
    loads["upstream"].wait()

    gain_second = vectors[2:3, :]
    shift_second = vectors[3:4, :]

    @pl.loop(0, tiles)
    def _(index):
        at = tile_rows(index)
        above = jnp.concatenate([up_halves[0, at, :], up_halves[1, at, :]], axis=1)
        d_inner_lower[at, :] = mm_nt(above, w_lower_second[...]).astype(BF16)

    @pl.loop(0, tiles)
    def _(order):
        index = first_other(order)
        at = tile_rows(index)
        inner_copy(index).wait_recv()
        mid = inputs[at, :].astype(F32)
        mid += mm(inner_out[0, at, :], w_out_second[0])
        mid += mm(inner_out[1, at, :], w_out_second[1])
        dn_own[...] = mid
        center = mid - jnp.mean(mid, axis=-1, keepdims=True)
        inverse = lax.rsqrt(jnp.mean(center * center, axis=-1, keepdims=True) + EPSILON)
        hat = center * inverse
        hat_two[...] = hat
        stats[0:TILE, 2:3] = inverse
        normed = (hat * gain_second + shift_second).astype(BF16)
        norm_two[at, :] = normed
        inner = mm(normed, w_glu[...]).astype(BF16)
        inner_glu[at, :] = inner
        lower = [None, None]
        for k in range(2):
            for columns in (slice(0, 256), slice(256, 512), slice(512, 768)):
                gate = mm(inner[:, 128 * k : 128 * k + 256], w_gate[k, :, columns])
                lift = mm(inner[:, 384 + 128 * k : 384 + 128 * k + 256], w_lift[k, :, columns])
                cumulative = 0.5 * (1.0 + lax.erf(gate * (1.0 / math.sqrt(2.0))))
                density = jnp.exp(-0.5 * gate * gate) * (1.0 / math.sqrt(2.0 * math.pi))
                activated = gate * cumulative
                unit = (activated * lift).astype(BF16)
                hid[k, at, columns] = unit
                factor_lift[k, :, columns] = activated
                factor_gate[k, :, columns] = lift * (cumulative + gate * density)
                term = mm(unit, w_lower[k, columns, :])
                lower[k] = term if lower[k] is None else lower[k] + term
        inner_low = join(*lower).astype(BF16)
        inner_lower[at, :] = inner_low
        out_own[at, :] = dn_own[:, own_half] + mm(inner_low, w_lower_second[:, own_half])
        part_send[at, :] = mm(inner_low, w_lower_second[:, other_half]).astype(BF16)

        d_low = d_inner_lower[at, :]
        gates = [None, None]
        lifts = [None, None]
        for k in range(2):
            for columns in (slice(0, 256), slice(256, 512), slice(512, 768)):
                d_hidden = mm_nt(d_low[:, 128 * k : 128 * k + 256], w_lower[k, columns, :])
                to_gate = (d_hidden * factor_gate[k, :, columns]).astype(BF16)
                to_lift = (d_hidden * factor_lift[k, :, columns]).astype(BF16)
                d_gate[k, at, columns] = to_gate
                d_lift[k, at, columns] = to_lift
                term = mm_nt(to_gate, w_gate[k, :, columns])
                gates[k] = term if gates[k] is None else gates[k] + term
                term = mm_nt(to_lift, w_lift[k, :, columns])
                lifts[k] = term if lifts[k] is None else lifts[k] + term
        d_glu = jnp.concatenate([join(*gates), join(*lifts)], axis=1).astype(BF16)
        d_inner_glu[at, :] = d_glu
        into = mm_nt(d_glu, w_glu[...])
        dn_own[...] = into

        @pl.when(order == 0)
        def _():
            dn_send[...] = dn_own[...].astype(BF16)
            dn_copy.start()

    low_lanes = lanes(128) < 64
    for columns in (slice(0, 384), slice(384, 768)):
        columns_at = slice(LOWER_RIGHT + columns.start, LOWER_RIGHT + columns.stop)
        parts = [
            mm_tn(hid[k, :, columns], d_inner_lower[:, 128 * k : 128 * k + 256]) for k in range(2)
        ]
        sums_channel[columns_at, 0:128] = parts[0][:, 0:128].astype(BF16)
        sums_channel[columns_at, 128:256] = jnp.where(
            low_lanes, parts[0][:, 128:256], parts[1][:, 0:128]
        ).astype(BF16)
        sums_channel[columns_at, 256:384] = parts[1][:, 128:256].astype(BF16)
    scatter(0, 0).start()
    for side in range(2):
        columns = slice(384 * side, 384 * side + 384)
        folded = fold(mm_tn(inner_lower[...], up_halves[side]), side)
        for b in range(2):
            first_row = LOWER_LEFT + 96 * side + 48 * b
            sums_channel[first_row : first_row + 48, :] = folded[b].astype(BF16)
    for offset, target in ((0, GATE_RIGHT), (384, LIFT_RIGHT)):
        whole = mm_tn(norm_two[...], d_inner_glu[:, offset : offset + 384])
        total = None
        for b in range(4):
            term = whole[192 * b : 192 * b + 192, :] * mask(
                (inside >= 48 * b) & (inside < 48 * b + 48), F32
            )
            total = term if total is None else total + term
        sums_channel[target : target + 192, :] = total.astype(BF16)

    for offset, upper, target in ((0, d_gate, GATE_LEFT), (384, d_lift, LIFT_LEFT)):
        for k in range(2):
            for start in (0, 384):
                whole = mm_tn(
                    inner_glu[:, offset + 128 * k : offset + 128 * k + 256],
                    upper[k, :, start : start + 384],
                )
                first_row = target + 384 * k + start // 2
                sums_channel[first_row : first_row + 192, :] = whole[
                    64 * k : 64 * k + 192, :
                ].astype(BF16)
        if upper is d_gate:
            scatter(1, 0).start()
    sums_channel[2880:3072, :] = jnp.zeros((192, 384), BF16)
    scatter(2, 0).start()
    scatter(3, 0).start()

    dn_copy.wait_recv()
    into = dn_own[...] + dn_recv[...].astype(F32)
    hat = hat_two[...]
    gain_sums[...] = jnp.zeros(gain_sums.shape, F32)
    gain_sums[0:1, :] = jnp.sum(into * hat, axis=0, keepdims=True)
    gain_sums[1:2, :] = jnp.sum(into, axis=0, keepdims=True)
    scaled = into * gain_second
    above = jnp.concatenate([up_halves[0, own_rows, :], up_halves[1, own_rows, :]], axis=1)
    d_mid = above.astype(F32) + stats[0:TILE, 2:3] * (
        scaled
        - jnp.mean(scaled, axis=-1, keepdims=True)
        - hat * jnp.mean(scaled * hat, axis=-1, keepdims=True)
    )
    hat_two[...] = d_mid
    branch[...] = d_mid.astype(BF16)
    cross_send[...] = mm_nt(branch[...], w_out_second[1 - narrow]).astype(BF16)
    cross_copy.start()
    mid_send[...] = hat_two[:, other_half].astype(BF16)
    d_inner_out[own_rows, :] = mm_nt(branch[...], w_out_second[narrow]).astype(BF16)
    for i in range(4):
        advance(i, 0)
    for h in range(2):
        for side in range(2):
            columns = slice(384 * side, 384 * side + 384)
            folded = fold(mm_tn(inner_out[h, own_rows, :], branch[:, columns]), side)
            for b in range(2):
                first_row = OUT_LEFT + 192 * h + 96 * side + 48 * b
                mixer_slab[first_row : first_row + 48, :] = folded[b].astype(BF16)

    @pl.loop(0, tiles)
    def _(order):
        index = narrow + order * (1 - 2 * narrow)
        at = tile_rows(index)

        @pl.when(order == 1)
        def _():
            cross_copy.wait_recv()
            middle_copy.start()

        d_inner = d_inner_out[at, :]
        for k in range(2):
            d_mixed = mm_nt(d_inner, w_out_first[k * PAD : k * PAD + PAD, :])
            d_shaping[k, at, :] = (d_mixed * long_halves[k, at, :].astype(F32)).astype(BF16)
            sig_halves[k, at, :] = (d_mixed * shaping[k, at, :]).astype(BF16)

    dl_copy = send(sig_halves.at[1 - core], dl_rows.at[core], sibling, 9)
    dl_copy.start()
    dl_rows[core] = sig_halves[core]

    @pl.loop(0, tiles)
    def _(index):
        at = tile_rows(index)
        to_shape = jnp.concatenate([d_shaping[0, at, :], d_shaping[1, at, :]], axis=1)
        d_inner_one[at, 384:768] = mm_nt(to_shape, w_shape[...]).astype(BF16)
        shape_send[at, :] = mm_nt(
            to_shape, w_shape[pl.ds(pl.multiple_of((1 - narrow) * 192, 192), 192), :]
        ).astype(BF16)
        shape_copy(index).start()

    @pl.loop(0, tiles)
    def _(index):
        part_copy(index).start()

    advance(1, 1)
    advance(0, 1)

    lane = lax.broadcasted_iota(jnp.int32, (2 * PAD, 384), 1)
    row = lax.broadcasted_iota(jnp.int32, (2 * PAD, 384), 0)
    squeeze = mask(row == lane + jnp.where(lane >= 192, 64, 0))

    def first_gradient(offset):
        whole = mm_tn(norm_one[...], d_inner_one[:, offset : offset + 384])
        total = None
        for b in range(4):
            term = whole[192 * b : 192 * b + 192, :] * between(384, 96 * b, 96 * b + 96, F32)
            total = term if total is None else total + term
        return total.astype(BF16)

    def second_gradient(offset, upper):
        above = jnp.concatenate([upper[0], upper[1]], axis=1)
        whole = mm_tn(inner_one[:, offset : offset + 384], above)
        pieces = []
        for b in range(4):
            total = None
            for k in range(2):
                term = whole[96 * b + 48 * k : 96 * b + 48 * k + 48, :] * between(
                    2 * PAD, PAD * k, PAD * k + PAD, F32
                )
                total = term if total is None else total + term
            pieces.append(total)
        return mm(jnp.concatenate(pieces, axis=0).astype(BF16), squeeze).astype(BF16)

    mixer_slab[SHAPE_RIGHT : SHAPE_RIGHT + 192, :] = first_gradient(384)
    mixer_slab[SHAPE_LEFT : SHAPE_LEFT + 192, :] = second_gradient(384, d_shaping)
    scatter(4, 0).start()
    parts = []
    for k in range(2):
        product = (shaping[k] * long_halves[k].astype(F32)).astype(BF16)
        parts.append(mm_tn(product, d_inner_out[...]))
    late[OUT_RIGHT : OUT_RIGHT + 192, :] = jnp.where(
        lanes(384) < 192, parts[0][0:192, :], parts[1][0:192, :]
    ).astype(BF16)
    advance(2, 1)
    advance(1, 2)
    advance(0, 2)

    dl_copy.wait_recv()

    @pl.loop(0, spans)
    def _(index):
        at = tile_rows(index)
        upper = dl_rows[...].reshape(length, PAD)
        real = mm(table_cos[at, :], upper)
        imag = mm(table_sin[at, :], upper)
        fil_re = fil_spec[0, at, :]
        fil_im = fil_spec[1, at, :]
        prod_spec[0, at, :] = (real * fil_re + imag * fil_im).astype(BF16)
        prod_spec[1, at, :] = (imag * fil_re - real * fil_im).astype(BF16)
        sig_re = sig_spec[0, at, :].astype(F32)
        sig_im = sig_spec[1, at, :].astype(F32)
        turn_cos = place[at, 5:6] * (1.0 / length)
        turn_sin = place[at, 6:7] * (1.0 / length)
        both_re = real * sig_re + imag * sig_im
        both_im = imag * sig_re - real * sig_im
        sig_spec[0, at, :] = (both_re * turn_cos - both_im * turn_sin).astype(BF16)
        sig_spec[1, at, :] = (both_im * turn_cos + both_re * turn_sin).astype(BF16)

    advance(4, 0)
    advance(3, 1)
    advance(1, 3)
    advance(2, 2)
    advance(0, 3)
    ds_pad[length : length + 8, :] = jnp.zeros((8, PAD), F32)

    @pl.loop(0, spans)
    def _(index):
        at = tile_rows(index)
        result = mm(table_cos[at, :], prod_spec[0]) + mm(table_sin[at, :], prod_spec[1])
        ds_pad[at, :] = result.astype(BF16).astype(F32)

    for index in range(spans):
        start = index * TILE
        total = conv[4:5, :] * ds_pad[start : start + TILE, :]
        total += conv[5:6, :] * ds_pad[start + 1 : start + 1 + TILE, :]
        total += conv[6:7, :] * ds_pad[start + 2 : start + 2 + TILE, :]
        part, inner_start = divmod(start, rows)
        long_rows[part, inner_start : inner_start + TILE, :] = total.astype(BF16)
    ds_copy = send(long_rows.at[1 - core], ds_halves.at[core], sibling, 10)
    ds_copy.start()
    ds_halves[core] = long_rows[core]

    advance(4, 1)
    advance(3, 2)
    advance(2, 3)
    retreat(1, 3)
    retreat(0, 3)
    grad_vectors[...] = jnp.zeros(grad_vectors.shape, F32)
    sums = [jnp.zeros((1, PAD), F32) for _ in range(3)]
    for index in range(spans):
        start = index * TILE
        upper = ds_pad[start : start + TILE, :]
        for j in range(3):
            sums[j] += jnp.sum(
                upper * sig_pad[8 + start - j : 8 + start - j + TILE, :], axis=0, keepdims=True
            )
    sums = jnp.concatenate(sums + [jnp.zeros((5, PAD), F32)], axis=0)
    lane = lax.broadcasted_iota(jnp.int32, (PAD, 384), 1)
    row = lax.broadcasted_iota(jnp.int32, (PAD, 384), 0)
    place_core = mask((lane == core * 192 + row) & (row < 192))
    conv_sums = mm(sums.astype(BF16), place_core)
    grad_vectors[4:7, :] = conv_sums[0:3, :]

    d_lin[...] = jnp.zeros(d_lin.shape, F32)
    grad_filter[...] = jnp.zeros(grad_filter.shape, F32)

    def filter_back(index):
        at = tile_rows(index)
        d_taps = mm(table_cos[at, :], sig_spec[0]) + mm(table_sin[at, :], sig_spec[1])
        d_mod = d_taps * decay(index)
        d_mod = d_mod.astype(BF16)
        d_lin[...] += mm_tn(act_two[at, :], d_mod)
        two = mm_nt(d_mod, own_out[...]) * cos_two[at, :].astype(F32)
        scaled_two = two * frequency
        coarse_two = scaled_two.astype(BF16)
        grad_filter[0:128, :] += mm_tn(act_one[at, :], coarse_two)
        one = mm_nt(coarse_two, mid_high) * cos_one[at, :].astype(F32)
        scaled_one = one * frequency
        grad_filter[128:136, :] += mm_tn(place_parts[at, :], scaled_one.astype(BF16))[0:8, :]
        grad_filter[136:137, :] += jnp.sum(scaled_one, axis=0, keepdims=True)
        grad_filter[137:138, :] += jnp.sum(scaled_two, axis=0, keepdims=True)
        grad_filter[138:139, :] += jnp.sum(
            one * lin_one[at, :].astype(F32) + two * lin_two[at, :].astype(F32), axis=0, keepdims=True
        )

    pl.loop(0, spans // 2)(filter_back)
    advance(4, 2)
    pl.loop(spans // 2, spans)(filter_back)
    late[FILTER_OUT : FILTER_OUT + 128, :] = mm(d_lin[...].astype(BF16), place_core).astype(BF16)
    for i in range(3):
        late[FILTER : FILTER + 48, 128 * i : 128 * i + 128] = grad_filter[
            48 * i : 48 * i + 48, :
        ].astype(BF16)


    advance(4, 3)
    advance(3, 3)
    retreat(1, 2)
    retreat(0, 2)
    retreat(2, 3)

    ds_copy.wait_recv()
    other_blocks = pl.ds(pl.multiple_of((1 - narrow) * 192, 192), 192)

    @pl.loop(0, tiles)
    def _(index):
        at = tile_rows(index)
        to_value = jnp.concatenate([ds_halves[0, at, :], ds_halves[1, at, :]], axis=1)
        d_inner = mm_nt(to_value, w_value[...]).astype(BF16)
        d_inner_one[at, 0:384] = d_inner
        against = inner_one[at, :].astype(F32) - through[1:2, :]
        d_inner = d_inner_one[at, :].astype(F32)
        plain = jnp.sum(d_inner * through[0:1, :], axis=-1, keepdims=True)
        along = jnp.sum(d_inner * against, axis=-1, keepdims=True)
        stats[at, 2:3] = plain
        stats[at, 3:4] = along
        lane = lanes(128)
        tail = jnp.where(lane == 64, plain, jnp.where(lane == 65, along, 0.0))
        away = mm_nt(to_value, w_value[other_blocks, :])
        value_send[at, 0:128] = away[:, 0:128].astype(BF16)
        value_send[at, 128:192] = away[:, 128:192].astype(BF16)
        value_send[at, 192:256] = tail[:, 64:128].astype(BF16)
        value_copy(index).start()

    @pl.loop(0, tiles)
    def _(index):
        at = tile_rows(index)
        into = mm_nt(d_inner_one[at, :], w_first[...])
        hat = (inputs[at, :].astype(F32) - stats[at, 0:1]) * stats[at, 1:2]
        gain_sums[2:3, :] += jnp.sum(into * hat, axis=0, keepdims=True)
        gain_sums[3:4, :] += jnp.sum(into, axis=0, keepdims=True)

    retreat(4, 3)
    retreat(3, 3)
    late[VALUE_RIGHT : VALUE_RIGHT + 192, :] = first_gradient(0)
    late[VALUE_LEFT : VALUE_LEFT + 192, :] = second_gradient(0, ds_halves)
    grad_vectors[0:4, :] = gain_sums[0:4, 0:384]
    grad_vectors[8:12, :] = gain_sums[0:4, 384:768]
    late[VECTORS : VECTORS + 16, :] = grad_vectors[...].astype(BF16)

    to_core = late_copy(
        late.at[pl.ds(pl.multiple_of((1 - core) * 384, 16), 384)], late_core, sibling, 0
    )
    to_core.start()
    retreat(4, 2)
    to_core.wait()

    @pl.loop(0, 384 // CHUNK)
    def _(index):
        at = pl.ds(pl.multiple_of(core * 384 + index * CHUNK, 16), CHUNK)
        came = late_core[pl.ds(pl.multiple_of(index * CHUNK, 16), CHUNK), :]
        late[at, :] = (late[at, :].astype(F32) + came.astype(F32)).astype(BF16)

    def share(t):
        return pl.multiple_of(core * 384 + lax.rem(chip + 8 - t, 8) * CHUNK, 16)

    direct = [
        late_copy(late.at[pl.ds(share(8 - t), CHUNK)], late_slots.at[t - 1], fellows[t], t)
        for t in range(1, 8)
    ]
    for copy in direct:
        copy.start()

    first_half = vectors[0:1, own_half]
    middle_copy.wait_recv()
    d_middle[own_rows, :] = hat_two[:, own_half]
    d_middle[tile_rows(1 - narrow), :] = mid_recv[...].astype(F32)
    @pl.loop(0, tiles)
    def _(index):
        at = tile_rows(index)
        part_copy(index).wait_recv()
        hidden_out[at, :] = (out_own[at, :] + part_recv[at, :].astype(F32)).astype(BF16)
        shape_copy(index).wait_recv()
        value_copy(index).wait_recv()
        into = mm_nt(d_inner_one[at, :], w_first[own_half, :])
        into += mm_nt(value_recv[at, 0:192], w_cross[0])
        into += mm_nt(shape_recv[at, :], w_cross[1])
        plain = (stats[at, 2:3] + value_recv[at, 192:193].astype(F32)) * (1.0 / D)
        along = (stats[at, 3:4] + value_recv[at, 193:194].astype(F32)) * (1.0 / D)
        hat = (inputs[at, own_half].astype(F32) - stats[at, 0:1]) * stats[at, 1:2]
        hidden_grad[at, :] = (
            d_middle[at, :] + stats[at, 1:2] * (into * first_half - plain - hat * along)
        ).astype(BF16)

    retreat(4, 1)
    early_rows = pl.ds(offsets[4][1], PART // 2)
    across_early = late_copy(mixer_slab.at[early_rows], mixer_slab.at[early_rows], partner, 40)
    across_early.start()
    retreat(1, 1)
    retreat(0, 1)
    store(hidden_out, result_out)
    store(hidden_grad, result_grad)
    total = late[pl.ds(share(0), CHUNK), :].astype(F32)
    for t in range(1, 8):
        direct[t - 1].wait()
        total += late_slots[t - 1].astype(F32)
    own_share = pl.ds(pl.multiple_of(PART + share(0), 16), CHUNK)
    mixer_slab[own_share, :] = total.astype(BF16)
    spread_out = [
        late_copy(mixer_slab.at[own_share], mixer_slab.at[own_share], fellows[t], 8 + t)
        for t in range(1, 8)
    ]
    for copy in spread_out:
        copy.start()
    retreat(2, 2)
    retreat(3, 2)
    across = []
    along_own = []
    for t in range(8):
        if t > 0:
            spread_out[t - 1].wait()
        at = pl.ds(pl.multiple_of(PART + share(t), 16), CHUNK)
        across.append(late_copy(mixer_slab.at[at], mixer_slab.at[at], partner, 16 + t))
        across[t].start()
        along_own.append(late_copy(mixer_slab.at[at], mixer_slab.at[at], sibling, 24 + t))
        along_own[t].start()
    across_early.wait()
    other = sums_mixer.at[1 - narrow, early_rows]
    along_early = late_copy(other, other, sibling, 41)
    along_early.start()
    retreat(2, 1)
    along_other = []
    for t in range(8):
        across[t].wait()
        at = pl.ds(pl.multiple_of(PART + share(t), 16), CHUNK)
        other = sums_mixer.at[1 - narrow, at]
        along_other.append(late_copy(other, other, sibling, 32 + t))
        along_other[t].start()
    retreat(3, 1)
    for i in (1, 0, 2, 3):
        retreat(i, 0)
        at = pl.ds(PART * i, PART)
        store(sums_channel.at[at], result_channel.at[at])
    retreat(4, 0)
    along_early.wait()
    early = pl.ds(0, PART)
    store(sums_mixer.at[:, early], result_mixer.at[:, early])
    for copy in along_own + along_other:
        copy.wait()
    rest = pl.ds(PART, PART)
    store(sums_mixer.at[:, rest], result_mixer.at[:, rest])

    inner_copy(1 - narrow).wait_send()
    for copy in (up_copy, dl_copy, ds_copy, dn_copy, cross_copy, middle_copy):
        copy.wait_send()

    @pl.loop(0, tiles)
    def _(index):
        for copy in (part_copy, shape_copy, value_copy):
            copy(index).wait_send()

    for copy in stores:
        copy.wait()


def finish_kernel(
    hidden_in,
    hidden_grad_in,
    hbm_channel,
    hbm_mixer,
    hidden_out,
    hidden_grad,
    grad_gainfirst,
    grad_shiftfirst,
    grad_valueright,
    grad_valueleft,
    grad_shaperight,
    grad_shapeleft,
    grad_convtaps,
    grad_posweight,
    grad_posbias,
    grad_sinefreq,
    grad_midweight,
    grad_midbias,
    grad_filterout,
    grad_outright,
    grad_outleft,
    grad_gainsecond,
    grad_shiftsecond,
    grad_gateright,
    grad_gateleft,
    grad_liftright,
    grad_liftleft,
    grad_lowerright,
    grad_lowerleft,
    channel,
    mixer,
    pass_out,
    pass_grad,
    valueright,
    valueleft,
    shaperight,
    shapeleft,
    outright,
    outleft,
    gateright,
    gateleft,
    liftright,
    liftleft,
    lowerright,
    lowerleft,
    both_filter,
    in_sem,
    out_sem,
):
    ins = []
    outs = []

    def fetch(source, target):
        ins.append(pltpu.make_async_copy(source, target, in_sem.at[len(ins)]))
        ins[-1].start()

    def store(source, target):
        outs.append(pltpu.make_async_copy(source, target, out_sem.at[len(outs)]))
        outs[-1].start()

    for i in range(4):
        at = pl.ds(PART * i, PART)
        fetch(hbm_channel.at[at], channel.at[at])
    fetch(hbm_mixer, mixer)
    fetch(hidden_in, pass_out)
    fetch(hidden_grad_in, pass_grad)

    ins[0].wait()
    lowerright[...] = channel[LOWER_RIGHT : LOWER_RIGHT + D, :].astype(F32)
    store(lowerright, grad_lowerright)
    ins[1].wait()
    for h in range(2):
        columns = slice(384 * h, 384 * h + 384)
        lowerleft[:, columns] = channel[LOWER_LEFT + 96 * h : LOWER_LEFT + 96 * h + 96, :].astype(F32)
    gateright[...] = channel[GATE_RIGHT : GATE_RIGHT + 192, :].astype(F32)
    liftright[...] = channel[LIFT_RIGHT : LIFT_RIGHT + 192, :].astype(F32)
    store(lowerleft, grad_lowerleft)
    store(gateright, grad_gateright)
    store(liftright, grad_liftright)
    ins[2].wait()
    for i in range(4):
        first_row = GATE_LEFT + 192 * i
        gateleft[:, 384 * i : 384 * i + 384] = channel[first_row : first_row + 192, :].astype(F32)
    store(gateleft, grad_gateleft)
    ins[3].wait()
    for i in range(4):
        first_row = LIFT_LEFT + 192 * i
        liftleft[:, 384 * i : 384 * i + 384] = channel[first_row : first_row + 192, :].astype(F32)
    store(liftleft, grad_liftleft)
    ins[4].wait()

    lane = lax.broadcasted_iota(jnp.int32, (384, D), 1)
    row = lax.broadcasted_iota(jnp.int32, (384, D), 0)
    step = jnp.where(row >= 96, 96, 0) + jnp.where(row >= 192, 96, 0) + jnp.where(row >= 288, 96, 0)
    unselect = [mask(lane == row + step + 96 * h) for h in range(2)]
    for first_row, target, result in (
        (PART + VALUE_RIGHT, valueright, grad_valueright),
        (SHAPE_RIGHT, shaperight, grad_shaperight),
    ):
        target[...] = mm(mixer[0, first_row : first_row + 192, :], unselect[0]) + mm(
            mixer[1, first_row : first_row + 192, :], unselect[1]
        )
        store(target, result)
    for first_row, target, result in (
        (PART + OUT_RIGHT, outright, grad_outright),
        (SHAPE_LEFT, shapeleft, grad_shapeleft),
        (PART + VALUE_LEFT, valueleft, grad_valueleft),
    ):
        for h in range(2):
            target[:, 384 * h : 384 * h + 384] = mixer[h, first_row : first_row + 192, :].astype(F32)
        store(target, result)
    for h in range(2):
        for side in range(2):
            at = slice(OUT_LEFT + 192 * h + 96 * side, OUT_LEFT + 192 * h + 96 * side + 96)
            outleft[96 * h : 96 * h + 96, 384 * side : 384 * side + 384] = mixer[0, at, :].astype(
                F32
            ) + mixer[1, at, :].astype(F32)
    store(outleft, grad_outleft)
    vectors = [mixer[h, PART + VECTORS : PART + VECTORS + 16, :].astype(F32) for h in range(2)]
    whole = jnp.concatenate(vectors, axis=1)
    both = vectors[0] + vectors[1]
    grad_convtaps[...] = whole[4:7, :]
    for i, target in enumerate((grad_gainsecond, grad_shiftsecond, grad_gainfirst, grad_shiftfirst)):
        target[...] = jnp.concatenate([both[i : i + 1, :], both[8 + i : 9 + i, :]], axis=1).reshape(D)
    for i in range(3):
        columns = slice(128 * i, 128 * i + 128)
        at = slice(PART + FILTER, PART + FILTER + 48)
        both_filter[48 * i : 48 * i + 48, :] = mixer[0, at, columns].astype(F32) + mixer[
            1, at, columns
        ].astype(F32)
    grad_midweight[...] = both_filter[0:128, :]
    grad_posweight[...] = both_filter[128:133, :]
    grad_posbias[...] = both_filter[136:137, :].reshape(128)
    grad_midbias[...] = both_filter[137:138, :].reshape(128)
    grad_sinefreq[...] = both_filter[138:139, :].reshape(128)
    count = grad_filterout.shape[0]
    first = (lax.axis_index("wide") * 2 + lax.axis_index("narrow")) * count
    total = jnp.zeros(grad_filterout.shape, F32)
    row = lax.broadcasted_iota(jnp.int32, (count, 384), 0)
    lane = lax.broadcasted_iota(jnp.int32, (count, 384), 1)
    for h in range(2):
        total += mm_nt(
            mask(lane + 384 * h == first + row),
            mixer[h, PART + FILTER_OUT : PART + FILTER_OUT + 128, :],
        )
    grad_filterout[...] = total
    ins[5].wait()
    store(pass_out, hidden_out)
    ins[6].wait()
    store(pass_grad, hidden_grad)
    for copy in outs:
        copy.wait()


def transform_tables(length):
    index = np.arange(length, dtype=np.float64) + 0.5
    angle = np.outer(index, index) * (math.pi / length)
    return (np.cos(angle).astype(jnp.bfloat16), np.sin(angle).astype(jnp.bfloat16))


def place_table(length):
    places = np.arange(length, dtype=np.float64)
    angle = places * (2.0 * math.pi / length)
    turn = (places + 0.5) * (math.pi / (2.0 * length))
    columns = [
        places / length,
        np.cos(angle),
        np.sin(angle),
        np.cos(2.0 * angle),
        np.sin(2.0 * angle),
        np.cos(turn),
        np.sin(turn),
        np.zeros(length),
    ]
    table = np.stack(columns, axis=1).astype(np.float32)
    feats = np.concatenate([table[:, :5], np.zeros((length, 3), np.float32)], axis=1)
    high = feats.astype(jnp.bfloat16)
    low = (feats - high.astype(np.float32)).astype(jnp.bfloat16)
    return (table, np.concatenate([high, low, high, np.zeros_like(high)], axis=1))


def pair_body(
    hidden_in,
    gainfirst,
    shiftfirst,
    valueright,
    valueleft,
    shaperight,
    shapeleft,
    convtaps,
    posweight,
    posbias,
    sinefreq,
    midweight,
    midbias,
    filterout,
    outright,
    outleft,
    gainsecond,
    shiftsecond,
    gateright,
    gateleft,
    liftright,
    liftleft,
    lowerright,
    lowerleft,
    grad_out,
):
    rows = hidden_in.shape[0]
    length = 2 * rows
    table_cos, table_sin = transform_tables(length)
    def out(extent, dtype=BF16):
        return jax.ShapeDtypeStruct(extent, dtype)

    def buf(*extent, dtype=BF16):
        return pltpu.VMEM(extent, dtype)

    vmem = pl.BlockSpec(memory_space=pltpu.VMEM)
    hbm = pl.BlockSpec(memory_space=pl.ANY)
    results = pl.pallas_call(
        whole_kernel,
        out_shape=(
            out((rows, 384)),
            out((rows, 384)),
            out((CHANNEL_ROWS, 384)),
            out((2, 2 * PART, 384)),
        ),
        in_specs=[hbm] * 4 + [vmem] * 12 + [hbm] * 13,
        out_specs=[hbm] * 4,
        scratch_shapes=[
            buf(rows, 384),
            buf(rows, 384),
            buf(CHANNEL_ROWS, 384),
            buf(2, 2 * PART, 384),
            pltpu.SemaphoreType.DMA((8,)),
            buf(rows, D),
            buf(length, length),
            buf(length, length),
            buf(8, D, dtype=F32),
            buf(16, 128, dtype=F32),
            buf(D, D),
            buf(384, 512),
            buf(384, 512),
            buf(512, 384),
            buf(2, 384, D),
            buf(D, D),
            buf(2, 256, D),
            buf(2, 256, D),
            buf(2, D, 256),
            buf(384, D),
            buf(2, rows, 384),
            buf(rows, 128, dtype=F32),
            buf(rows, D),
            buf(rows, D),
            buf(2, rows, PAD),
            buf(2, rows, PAD),
            buf(2, rows, PAD, dtype=F32),
            buf(length + 8, PAD, dtype=F32),
            buf(length, PAD),
            buf(length, 128),
            buf(length, 128),
            buf(length, 128),
            buf(length, 128),
            buf(length, 128),
            buf(length, 128),
            buf(2, length, PAD, dtype=F32),
            buf(2, length, PAD),
            buf(2, length, PAD),
            buf(2, rows, PAD),
            buf(2, rows, PAD),
            buf(2, rows, 384),
            buf(TILE, D, dtype=F32),
            buf(rows, D),
            buf(rows, D),
            buf(2, TILE, D, dtype=F32),
            buf(2, TILE, D, dtype=F32),
            buf(2, rows, D),
            buf(rows, 384),
            buf(rows, 384, dtype=F32),
            buf(rows, 384),
            buf(rows, 384),
            buf(rows, 384),
            buf(2, rows, D),
            buf(2, rows, D),
            buf(rows, D),
            buf(TILE, D, dtype=F32),
            buf(TILE, D),
            buf(TILE, D),
            buf(rows, 384),
            buf(2, rows, PAD),
            buf(2, rows, PAD),
            buf(length + 8, PAD, dtype=F32),
            buf(2, rows, PAD),
            buf(rows, D),
            buf(TILE, 384),
            buf(TILE, 384),
            buf(TILE, 384),
            buf(rows, 384, dtype=F32),
            buf(TILE, D),
            buf(rows, 192),
            buf(rows, 192),
            buf(rows, 256),
            buf(rows, 256),
            buf(2, 384, 192),
            buf(8, D, dtype=F32),
            buf(128, PAD, dtype=F32),
            buf(128, PAD),
            buf(16, 384, dtype=F32),
            buf(144, 128, dtype=F32),
            buf(8, D, dtype=F32),
            pltpu.SemaphoreType.DMA((16,)),
            pltpu.SemaphoreType.DMA((16,)),
            pltpu.SemaphoreType.DMA((20,)),
            buf(5, STEP_ROWS[4], 384),
            pltpu.SemaphoreType.DMA((40,)),
            pltpu.SemaphoreType.DMA((40,)),
            pltpu.SemaphoreType.REGULAR((20,)),
            buf(PART, 384),
            buf(PART // 2, 384),
            buf(7, CHUNK, 384),
            pltpu.SemaphoreType.DMA((42,)),
            pltpu.SemaphoreType.DMA((42,)),
        ],
        compiler_params=pltpu.CompilerParams(
            collective_id=0, has_side_effects=True, vmem_limit_bytes=63 * 1024 * 1024
        ),
    )(
        hidden_in,
        grad_out,
        table_cos,
        table_sin,
        *place_table(length),
        gainfirst,
        shiftfirst,
        gainsecond,
        shiftsecond,
        convtaps,
        posweight,
        posbias,
        midbias,
        sinefreq,
        midweight,
        filterout,
        valueright,
        valueleft,
        shaperight,
        shapeleft,
        outright,
        outleft,
        gateright,
        gateleft,
        liftright,
        liftleft,
        lowerright,
        lowerleft,
    )
    count = D // (lax.axis_size("wide") * lax.axis_size("narrow"))
    square = out((192, D), F32)
    grads = pl.pallas_call(
        finish_kernel,
        out_shape=(
            out((rows, 384)),
            out((rows, 384)),
            out((D,), F32),
            out((D,), F32),
            square,
            square,
            square,
            square,
            out((3, D), F32),
            out((5, 128), F32),
            out((128,), F32),
            out((128,), F32),
            out((128, 128), F32),
            out((128,), F32),
            out((count, 128), F32),
            square,
            square,
            out((D,), F32),
            out((D,), F32),
            out(gateright.shape, F32),
            out(gateleft.shape, F32),
            out(liftright.shape, F32),
            out(liftleft.shape, F32),
            out(lowerright.shape, F32),
            out(lowerleft.shape, F32),
        ),
        in_specs=[hbm] * 4,
        out_specs=[hbm] * 2 + [vmem] * 2 + [hbm] * 4 + [vmem] * 7 + [hbm] * 2 + [vmem] * 2 + [hbm] * 6,
        scratch_shapes=[
            buf(CHANNEL_ROWS, 384),
            buf(2, 2 * PART, 384),
            buf(rows, 384),
            buf(rows, 384),
            *[buf(192, D, dtype=F32)] * 6,
            buf(*gateright.shape, dtype=F32),
            buf(*gateleft.shape, dtype=F32),
            buf(*liftright.shape, dtype=F32),
            buf(*liftleft.shape, dtype=F32),
            buf(*lowerright.shape, dtype=F32),
            buf(*lowerleft.shape, dtype=F32),
            buf(144, 128, dtype=F32),
            pltpu.SemaphoreType.DMA((7,)),
            pltpu.SemaphoreType.DMA((14,)),
        ],
        compiler_params=pltpu.CompilerParams(vmem_limit_bytes=60 * 1024 * 1024),
    )(*results)
    return (*grads[:14], grads[14].T, *grads[15:])


def solution(mesh):
    pairs = mesh.shape["wide"] == 2 * SEQS and mesh.shape["narrow"] == 2
    return jax.shard_map(
        pair_body if pairs else body,
        mesh=mesh,
        in_specs=(
            P("wide", None),
            P(),
            P(),
            P(),
            P(),
            P(),
            P(),
            P(),
            P(),
            P(),
            P(),
            P(),
            P(),
            P(),
            P(),
            P(),
            P(),
            P(),
            P(None, "narrow"),
            P(None, "narrow"),
            P(None, "narrow"),
            P(None, "narrow"),
            P(None, "narrow"),
            P("narrow", None),
            P("wide", "narrow"),
        ),
        out_specs=(
            P("wide", "narrow"),
            P("wide", "narrow"),
            P(),
            P(),
            P(),
            P(),
            P(),
            P(),
            P(),
            P(),
            P(),
            P(),
            P(),
            P(),
            P(None, ("wide", "narrow")),
            P(),
            P(),
            P(),
            P(),
            P(None, "narrow"),
            P(None, "narrow"),
            P(None, "narrow"),
            P(None, "narrow"),
            P(None, "narrow"),
            P("narrow", None),
        ),
        check_vma=False,
    )
```

```python
import math

import jax
import jax.numpy as jnp
import numpy as np
from jax import lax
from jax.experimental import pallas as pl
from jax.experimental.pallas import tpu as pltpu
from jax.sharding import PartitionSpec as P

D = 768
BLOCKS = 4
SEQS = 8


EPSILON = 1e-05
HIGHEST = lax.Precision.HIGHEST


def from_behind(x, axis, by):
    length = lax.axis_size(axis)
    pairs = [(i, i + by) for i in range(length) if 0 <= i + by < length]
    return lax.ppermute(x, axis, pairs)


def norm_forward(values, gain, shift):
    center = values - jnp.mean(values, axis=-1, keepdims=True)
    inverse = lax.rsqrt(jnp.mean(center * center, axis=-1, keepdims=True) + EPSILON)
    normed = center * inverse
    return (normed * gain + shift, normed, inverse)


def norm_backward(upstream, normed, inverse, gain):
    scaled = upstream * gain
    result = inverse * (
        scaled
        - jnp.mean(scaled, axis=-1, keepdims=True)
        - normed * jnp.mean(scaled * normed, axis=-1, keepdims=True)
    )
    return (result, jnp.sum(upstream * normed, axis=0), jnp.sum(upstream, axis=0))


def right_view(right, nblocks, groups, group_first):
    width_in = right.shape[0]
    piece = right.shape[1] // (nblocks * groups)
    if group_first:
        return (right.reshape(width_in, groups, nblocks, piece), "ikbc")
    return (right.reshape(width_in, nblocks, groups, piece), "ibkc")


def section_one(inputs, right, groups, group_first):
    rowcount = inputs.shape[0]
    width_in = right.shape[0]
    nblocks = inputs.shape[1] // width_in
    factor, letters = right_view(right, nblocks, groups, group_first)
    first = jnp.einsum(
        "tbi," + letters + "->tkbc",
        inputs.reshape(rowcount, nblocks, width_in),
        factor,
        preferred_element_type=jnp.float32,
    )
    return first.reshape(rowcount, groups, -1).astype(jnp.bfloat16)


def section_two(middle_part, left):
    groups = middle_part.shape[1]
    result = jnp.einsum(
        "tkj,jke->tke",
        middle_part,
        left.reshape(left.shape[0], groups, -1),
        preferred_element_type=jnp.float32,
    )
    return result.reshape(result.shape[0], -1)


def back_two(middle_part, left, upstream):
    groups = middle_part.shape[1]
    left_view = left.reshape(left.shape[0], groups, -1)
    grad_left = jnp.einsum(
        "tkj,tke->jke", middle_part, upstream, preferred_element_type=jnp.float32
    )
    grad_middle = jnp.einsum(
        "tke,jke->tkj", upstream, left_view, preferred_element_type=jnp.float32
    )
    return (grad_left.reshape(left.shape[0], -1), grad_middle.astype(jnp.bfloat16))


def back_one(inputs, right, grad_middle, group_first):
    rowcount = inputs.shape[0]
    width_in = right.shape[0]
    nblocks = inputs.shape[1] // width_in
    groups = grad_middle.shape[1]
    factor, letters = right_view(right, nblocks, groups, group_first)
    spread_back = grad_middle.reshape(rowcount, groups, nblocks, -1)
    blocked = inputs.reshape(rowcount, nblocks, width_in)
    grad_right = jnp.einsum(
        "tbi,tkbc->" + letters, blocked, spread_back, preferred_element_type=jnp.float32
    )
    grad_inputs = jnp.einsum(
        "tkbc," + letters + "->tbi", spread_back, factor, preferred_element_type=jnp.float32
    )
    return (grad_right.reshape(width_in, -1), grad_inputs.reshape(rowcount, -1))


def fourier_tables(length):
    span = length // 128
    slow_index = jnp.arange(span, dtype=jnp.int32)
    fast_index = jnp.arange(128, dtype=jnp.int32)
    small = (slow_index[:, None] * slow_index[None, :] % span).astype(jnp.float32) * (
        2.0 * math.pi / span
    )
    twist = (slow_index[:, None] * fast_index[None, :] % length).astype(jnp.float32) * (
        2.0 * math.pi / length
    )
    large = (fast_index[:, None] * fast_index[None, :] % 128).astype(jnp.float32) * (
        2.0 * math.pi / 128
    )
    return (
        jnp.cos(small),
        jnp.sin(small),
        jnp.cos(twist),
        jnp.sin(twist),
        jnp.cos(large),
        jnp.sin(large),
    )


def to_spectrum(signal, tables):
    cos_small, sin_small, cos_twist, sin_twist, cos_large, sin_large = tables
    span = cos_small.shape[0]
    padded = jnp.concatenate([signal, jnp.zeros_like(signal)], axis=-1)
    padded = padded.reshape(signal.shape[:-1] + (span, 128))
    first_re = jnp.einsum("...qp,qk->...kp", padded, cos_small, precision=HIGHEST)
    first_im = -jnp.einsum("...qp,qk->...kp", padded, sin_small, precision=HIGHEST)
    turned_re = first_re * cos_twist + first_im * sin_twist
    turned_im = first_im * cos_twist - first_re * sin_twist
    out_re = jnp.einsum("...kp,pj->...kj", turned_re, cos_large, precision=HIGHEST) + jnp.einsum(
        "...kp,pj->...kj", turned_im, sin_large, precision=HIGHEST
    )
    out_im = jnp.einsum("...kp,pj->...kj", turned_im, cos_large, precision=HIGHEST) - jnp.einsum(
        "...kp,pj->...kj", turned_re, sin_large, precision=HIGHEST
    )
    return (out_re, out_im)


def from_spectrum(real_part, imag_part, tables):
    cos_small, sin_small, cos_twist, sin_twist, cos_large, sin_large = tables
    span = cos_small.shape[0]
    back_re = jnp.einsum("...kj,pj->...kp", real_part, cos_large, precision=HIGHEST) - jnp.einsum(
        "...kj,pj->...kp", imag_part, sin_large, precision=HIGHEST
    )
    back_im = jnp.einsum("...kj,pj->...kp", imag_part, cos_large, precision=HIGHEST) + jnp.einsum(
        "...kj,pj->...kp", real_part, sin_large, precision=HIGHEST
    )
    turned_re = back_re * cos_twist - back_im * sin_twist
    turned_im = back_im * cos_twist + back_re * sin_twist
    signal = (
        jnp.einsum("...kp,qk->...qp", turned_re, cos_small, precision=HIGHEST)
        - jnp.einsum("...kp,qk->...qp", turned_im, sin_small, precision=HIGHEST)
    ) / (span * 128)
    signal = signal.reshape(signal.shape[:-2] + (span * 128,))
    return signal[..., : span * 64]


def position_features(length):
    places = jnp.arange(length, dtype=jnp.float32)
    angle = places * (2.0 * math.pi / length)
    return jnp.stack(
        [
            places / length,
            jnp.cos(angle),
            jnp.sin(angle),
            jnp.cos(2.0 * angle),
            jnp.sin(2.0 * angle),
        ],
        axis=1,
    )


def decay_factors(channel_ids, length):
    rank = (channel_ids * 5 % D).astype(jnp.float32) / D
    lowest = math.log(0.25 / length)
    highest = math.log(1.0 / 30.0)
    rate = jnp.exp(lowest + rank * (highest - lowest))
    places = jnp.arange(length, dtype=jnp.float32)
    return jnp.exp(-rate[:, None] * places[None, :]) * jnp.sqrt(2.0 * rate)[:, None]


def channel_order(data, nwide, nnarrow, rows_half):
    count = data.shape[0]
    return data.reshape(count, nnarrow, nwide, rows_half).transpose(0, 2, 1, 3).reshape(count, -1)


def row_order(data, nwide, nnarrow):
    total = data.shape[0]
    rows_half = data.shape[1]
    count = total // (nwide * nnarrow)
    return (
        data.reshape(nnarrow, nwide, count, rows_half)
        .transpose(1, 0, 2, 3)
        .reshape(total, rows_half)
        .T
    )


def body(
    hidden_in,
    gainfirst,
    shiftfirst,
    valueright,
    valueleft,
    shaperight,
    shapeleft,
    convtaps,
    posweight,
    posbias,
    sinefreq,
    midweight,
    midbias,
    filterout,
    outright,
    outleft,
    gainsecond,
    shiftsecond,
    gateright,
    gateleft,
    liftright,
    liftleft,
    lowerright,
    lowerleft,
    grad_out,
):
    rowcount = hidden_in.shape[0]
    local_groups = gateright.shape[1] // gateleft.shape[0]
    nwide = lax.axis_size("wide")
    nnarrow = lax.axis_size("narrow")
    narrow_index = lax.axis_index("narrow")
    rows_half = rowcount // nnarrow
    row_start = narrow_index * rows_half
    combined = lax.axis_index("wide") * nnarrow + narrow_index
    resid = lax.dynamic_slice_in_dim(hidden_in, row_start, rows_half, 0).astype(jnp.float32)
    normone, hat_one, inv_one = norm_forward(resid, gainfirst, shiftfirst)
    normone = normone.astype(jnp.bfloat16)
    mid_value = section_one(normone, valueright, BLOCKS, False)
    signal = section_two(mid_value, valueleft).astype(jnp.bfloat16)
    mid_shape = section_one(normone, shaperight, BLOCKS, False)
    shaping = section_two(mid_shape, shapeleft)
    group = nwide // SEQS * nnarrow
    place = combined % group
    before = from_behind(signal[-2:], ("wide", "narrow"), 1)
    before = jnp.where(place == 0, jnp.zeros_like(before), before)
    extended = jnp.concatenate([before, signal], axis=0).astype(jnp.float32)
    shortconv = (
        convtaps[0] * extended[2:] + convtaps[1] * extended[1:-1] + convtaps[2] * extended[:-2]
    ).astype(jnp.bfloat16)
    channels = lax.all_to_all(
        lax.all_to_all(shortconv.T, "wide", split_axis=0, concat_axis=1, tiled=True),
        "narrow",
        split_axis=0,
        concat_axis=1,
        tiled=True,
    )
    channels = channel_order(channels, nwide, nnarrow, rows_half)
    count = channels.shape[0]
    length = channels.shape[1] // SEQS
    feats = position_features(length)
    lin_one = jnp.dot(feats, posweight, precision=HIGHEST) + posbias
    act_one = jnp.sin(sinefreq * lin_one)
    lin_two = jnp.dot(act_one, midweight, precision=HIGHEST) + midbias
    act_two = jnp.sin(sinefreq * lin_two)
    own_cols = lax.dynamic_slice_in_dim(filterout, combined * count, count, 1)
    channel_ids = combined * count + jnp.arange(count, dtype=jnp.int32)
    modulation = decay_factors(channel_ids, length)
    taps = jnp.dot(act_two, own_cols, precision=HIGHEST).T * modulation
    tables = fourier_tables(2 * length)
    sig_re, sig_im = to_spectrum(channels.astype(jnp.float32).reshape(count, SEQS, length), tables)
    fil_re, fil_im = to_spectrum(taps.reshape(count, 1, length), tables)
    conv_chan = from_spectrum(
        sig_re * fil_re - sig_im * fil_im, sig_re * fil_im + sig_im * fil_re, tables
    )
    conv_chan = conv_chan.reshape(count, SEQS * length).astype(jnp.bfloat16)
    longconv = lax.all_to_all(
        lax.all_to_all(conv_chan, "wide", split_axis=1, concat_axis=0, tiled=True),
        "narrow",
        split_axis=1,
        concat_axis=0,
        tiled=True,
    )
    longconv = row_order(longconv, nwide, nnarrow)
    mixed = (shaping * longconv.astype(jnp.float32)).astype(jnp.bfloat16)
    mid_out = section_one(mixed, outright, BLOCKS, False)
    middle = resid + section_two(mid_out, outleft)
    normtwo, hat_two, inv_two = norm_forward(middle, gainsecond, shiftsecond)
    normtwo = normtwo.astype(jnp.bfloat16)
    norm_all = lax.all_gather(normtwo, "narrow", axis=0, tiled=True)
    mid_gate = section_one(norm_all, gateright, local_groups, True)
    pregate = section_two(mid_gate, gateleft)
    mid_lift = section_one(norm_all, liftright, local_groups, True)
    prelift = section_two(mid_lift, liftleft)
    cumulative = 0.5 * (1.0 + lax.erf(pregate * (1.0 / math.sqrt(2.0))))
    activated = pregate * cumulative
    hidden = (activated * prelift).astype(jnp.bfloat16)
    mid_lower = section_one(hidden, lowerright, BLOCKS, False)
    partial_sum = section_two(mid_lower, lowerleft)
    partial_sum = partial_sum + lax.dynamic_update_slice_in_dim(
        jnp.zeros_like(partial_sum), middle, row_start, 0
    )
    hidden_out = lax.psum_scatter(
        partial_sum.astype(jnp.bfloat16), "narrow", scatter_dimension=1, tiled=True
    )
    upstream = lax.all_gather(grad_out, "narrow", axis=1, tiled=True)
    grad_lowerleft, grad_mid_lower = back_two(
        mid_lower, lowerleft, upstream.reshape(rowcount, BLOCKS, -1)
    )
    grad_lowerright, grad_hidden = back_one(hidden, lowerright, grad_mid_lower, False)
    density = jnp.exp(-0.5 * pregate * pregate) * (1.0 / math.sqrt(2.0 * math.pi))
    grad_pregate = (grad_hidden * prelift * (cumulative + pregate * density)).astype(jnp.bfloat16)
    grad_prelift = (grad_hidden * activated).astype(jnp.bfloat16)
    grad_gateleft, grad_mid_gate = back_two(
        mid_gate, gateleft, grad_pregate.reshape(rowcount, local_groups, -1)
    )
    grad_gateright, into_gate = back_one(norm_all, gateright, grad_mid_gate, True)
    grad_liftleft, grad_mid_lift = back_two(
        mid_lift, liftleft, grad_prelift.reshape(rowcount, local_groups, -1)
    )
    grad_liftright, into_lift = back_one(norm_all, liftright, grad_mid_lift, True)
    ffn_local = (
        grad_gateright,
        grad_gateleft,
        grad_liftright,
        grad_liftleft,
        grad_lowerright,
        grad_lowerleft,
    )
    dnormtwo = lax.psum_scatter(
        (into_gate + into_lift).astype(jnp.bfloat16), "narrow", scatter_dimension=0, tiled=True
    ).astype(jnp.float32)
    back_two_norm, grad_gainsecond, grad_shiftsecond = norm_backward(
        dnormtwo, hat_two, inv_two, gainsecond
    )
    up_rows = lax.dynamic_slice_in_dim(upstream, row_start, rows_half, 0)
    dmiddle = up_rows.astype(jnp.float32) + back_two_norm
    dbranch = dmiddle.astype(jnp.bfloat16)
    grad_outleft, grad_mid_out = back_two(mid_out, outleft, dbranch.reshape(rows_half, BLOCKS, -1))
    grad_outright, dmixed = back_one(mixed, outright, grad_mid_out, False)
    dshaping = (dmixed * longconv.astype(jnp.float32)).astype(jnp.bfloat16)
    dlong = (dmixed * shaping).astype(jnp.bfloat16)
    grad_chan = lax.all_to_all(
        lax.all_to_all(dlong.T, "wide", split_axis=0, concat_axis=1, tiled=True),
        "narrow",
        split_axis=0,
        concat_axis=1,
        tiled=True,
    )
    grad_chan = channel_order(grad_chan, nwide, nnarrow, rows_half)
    dlong_re, dlong_im = to_spectrum(
        grad_chan.astype(jnp.float32).reshape(count, SEQS, length), tables
    )
    dshort_chan = from_spectrum(
        dlong_re * fil_re + dlong_im * fil_im, dlong_im * fil_re - dlong_re * fil_im, tables
    )
    dshort_chan = dshort_chan.reshape(count, SEQS * length).astype(jnp.bfloat16)
    filt_re = jnp.sum(dlong_re * sig_re + dlong_im * sig_im, axis=1, keepdims=True)
    filt_im = jnp.sum(dlong_im * sig_re - dlong_re * sig_im, axis=1, keepdims=True)
    grad_taps = from_spectrum(filt_re, filt_im, tables).reshape(count, length)
    dshort = lax.all_to_all(
        lax.all_to_all(dshort_chan, "wide", split_axis=1, concat_axis=0, tiled=True),
        "narrow",
        split_axis=1,
        concat_axis=0,
        tiled=True,
    )
    dshort = row_order(dshort, nwide, nnarrow)
    grad_modded = grad_taps * modulation
    grad_filterout = jnp.dot(act_two.T, grad_modded.T, precision=HIGHEST)
    dact_two = jnp.dot(grad_modded.T, own_cols.T, precision=HIGHEST)
    dlin_two = dact_two * jnp.cos(sinefreq * lin_two)
    scaled_two = dlin_two * sinefreq
    grad_midweight = jnp.dot(act_one.T, scaled_two, precision=HIGHEST)
    grad_midbias = jnp.sum(scaled_two, axis=0)
    dact_one = jnp.dot(scaled_two, midweight.T, precision=HIGHEST)
    dlin_one = dact_one * jnp.cos(sinefreq * lin_one)
    scaled_one = dlin_one * sinefreq
    grad_posweight = jnp.dot(feats.T, scaled_one, precision=HIGHEST)
    grad_posbias = jnp.sum(scaled_one, axis=0)
    grad_sinefreq = jnp.sum(dlin_one * lin_one, axis=0) + jnp.sum(dlin_two * lin_two, axis=0)
    after = from_behind(dshort[:2], ("wide", "narrow"), -1)
    after = jnp.where(place == group - 1, jnp.zeros_like(after), after)
    ext_grad = jnp.concatenate([dshort, after], axis=0).astype(jnp.float32)
    dsignal = (
        convtaps[0] * ext_grad[:-2] + convtaps[1] * ext_grad[1:-1] + convtaps[2] * ext_grad[2:]
    ).astype(jnp.bfloat16)
    short_grad = dshort.astype(jnp.float32)
    grad_convtaps = jnp.stack(
        [
            jnp.sum(extended[2:] * short_grad, axis=0),
            jnp.sum(extended[1:-1] * short_grad, axis=0),
            jnp.sum(extended[:-2] * short_grad, axis=0),
        ]
    )
    grad_valueleft, grad_mid_value = back_two(
        mid_value, valueleft, dsignal.reshape(rows_half, BLOCKS, -1)
    )
    grad_valueright, into_value = back_one(normone, valueright, grad_mid_value, False)
    grad_shapeleft, grad_mid_shape = back_two(
        mid_shape, shapeleft, dshaping.reshape(rows_half, BLOCKS, -1)
    )
    grad_shaperight, into_shape = back_one(normone, shaperight, grad_mid_shape, False)
    back_one_norm, grad_gainfirst, grad_shiftfirst = norm_backward(
        into_value + into_shape, hat_one, inv_one, gainfirst
    )
    full_grad = (dmiddle + back_one_norm).astype(jnp.bfloat16)
    hidden_grad = lax.all_to_all(full_grad, "narrow", split_axis=1, concat_axis=0, tiled=True)
    mixer_grads = lax.psum(
        (
            grad_gainfirst,
            grad_shiftfirst,
            grad_valueright,
            grad_valueleft,
            grad_shaperight,
            grad_shapeleft,
            grad_convtaps,
            grad_posweight,
            grad_posbias,
            grad_sinefreq,
            grad_midweight,
            grad_midbias,
            grad_outright,
            grad_outleft,
            grad_gainsecond,
            grad_shiftsecond,
        ),
        ("wide", "narrow"),
    )
    ffn_grads = lax.psum(
        (ffn_local[0], ffn_local[1], ffn_local[2], ffn_local[3], ffn_local[4], ffn_local[5]), "wide"
    )
    return (
        hidden_out,
        hidden_grad,
        mixer_grads[0],
        mixer_grads[1],
        mixer_grads[2],
        mixer_grads[3],
        mixer_grads[4],
        mixer_grads[5],
        mixer_grads[6],
        mixer_grads[7],
        mixer_grads[8],
        mixer_grads[9],
        mixer_grads[10],
        mixer_grads[11],
        grad_filterout,
        mixer_grads[12],
        mixer_grads[13],
        mixer_grads[14],
        mixer_grads[15],
        ffn_grads[0],
        ffn_grads[1],
        ffn_grads[2],
        ffn_grads[3],
        ffn_grads[4],
        ffn_grads[5],
    )


F32 = jnp.float32
BF16 = jnp.bfloat16
MESH = pl.DeviceIdType.MESH
TILE = 256
PAD = 256


def mm(a, b, precision=None):
    return lax.dot_general(
        a, b, (((1,), (0,)), ((), ())), precision=precision, preferred_element_type=F32
    )


def mm_nt(a, b, precision=None):
    return lax.dot_general(
        a, b, (((1,), (1,)), ((), ())), precision=precision, preferred_element_type=F32
    )


def mm_tn(a, b, precision=None):
    return lax.dot_general(
        a, b, (((0,), (0,)), ((), ())), precision=precision, preferred_element_type=F32
    )


def lanes(width):
    return lax.broadcasted_iota(jnp.int32, (1, width), 1)


def mask(condition, dtype=BF16):
    return jnp.where(condition, 1.0, 0.0).astype(dtype)


def between(width, low, high, dtype=BF16):
    lane = lanes(width)
    return mask((lane >= low) & (lane < high), dtype)


def join(first, second):
    return jnp.concatenate(
        [first[:, :128], first[:, 128:] + second[:, :128], second[:, 128:]], axis=1
    )


def sine_cosine(angle):
    turns = jnp.floor(angle * (1.0 / math.pi) + 0.5)
    rest = angle - turns * 3.140625
    rest = rest - turns * 9.67502593994140625e-4
    rest = rest - turns * 1.509957990978376e-7
    flip = 1.0 - 2.0 * (turns - 2.0 * jnp.floor(turns * 0.5))
    square = rest * rest
    sine = 1.0
    for divisor in (110.0, 72.0, 42.0, 20.0, 6.0):
        sine = 1.0 - square * (1.0 / divisor) * sine
    cosine = 1.0
    for divisor in (132.0, 90.0, 56.0, 30.0, 12.0, 2.0):
        cosine = 1.0 - square * (1.0 / divisor) * cosine
    return (sine * rest * flip, cosine * flip)


def fold(whole, side):
    return [
        whole[192 * b + 96 * side : 192 * b + 96 * side + 48, :] * between(384, 0, 192, F32)
        + whole[192 * b + 96 * side + 48 : 192 * b + 96 * side + 96, :] * between(384, 192, 384, F32)
        for b in range(2)
    ]


STRIDES = (1, 2, 4, 8)
PART = 768
STEP_ROWS = (0, 384, 576, 672, 720)
ORDERS = ((0, 1, 2, 3), (0, 2, 3, 1), (0, 1, 2, 3), (0, 1, 2, 3), (0, 1, 2, 3))
CHUNK = 48
LOWER_RIGHT, LOWER_LEFT, GATE_RIGHT, LIFT_RIGHT, GATE_LEFT, LIFT_LEFT, CHANNEL_ROWS = (
    0,
    768,
    960,
    1152,
    1344,
    2112,
    4 * PART,
)
OUT_LEFT, SHAPE_RIGHT, SHAPE_LEFT = (0, 384, 576)
VALUE_RIGHT, VALUE_LEFT, FILTER_OUT, VECTORS, FILTER, OUT_RIGHT = (0, 192, 384, 512, 528, 576)


def tile_rows(index, size=TILE):
    return pl.ds(pl.multiple_of(index * size, size), size)


def whole_kernel(
    hidden_in,
    upstream,
    hbm_cos,
    hbm_sin,
    place,
    place_parts,
    gainfirst,
    shiftfirst,
    gainsecond,
    shiftsecond,
    convtaps,
    posweight,
    posbias,
    midbias,
    sinefreq,
    midweight,
    filterout,
    valueright,
    valueleft,
    shaperight,
    shapeleft,
    outright,
    outleft,
    gateright,
    gateleft,
    liftright,
    liftleft,
    lowerright,
    lowerleft,
    result_out,
    result_grad,
    result_channel,
    result_mixer,
    hidden_out,
    hidden_grad,
    sums_channel,
    sums_mixer,
    store_sem,
    inputs,
    table_cos,
    table_sin,
    vectors,
    filter_vectors,
    w_first,
    w_value,
    w_shape,
    w_out_first,
    w_out_second,
    w_glu,
    w_gate,
    w_lift,
    w_lower,
    w_lower_second,
    up_halves,
    stats,
    norm_one,
    inner_one,
    sig_halves,
    sig_rows,
    shaping,
    sig_pad,
    short,
    act_one,
    cos_one,
    lin_one,
    act_two,
    cos_two,
    lin_two,
    fil_spec,
    sig_spec,
    prod_spec,
    long_rows,
    long_halves,
    inner_out,
    hat_two,
    norm_two,
    inner_glu,
    factor_gate,
    factor_lift,
    hid,
    inner_lower,
    out_own,
    part_send,
    part_recv,
    d_inner_lower,
    d_gate,
    d_lift,
    d_inner_glu,
    dn_own,
    dn_send,
    dn_recv,
    d_inner_out,
    d_shaping,
    dl_rows,
    ds_pad,
    ds_halves,
    d_inner_one,
    cross_send,
    mid_send,
    mid_recv,
    d_middle,
    branch,
    shape_send,
    shape_recv,
    value_send,
    value_recv,
    w_cross,
    through,
    d_lin,
    own_out,
    grad_vectors,
    grad_filter,
    gain_sums,
    send_sem,
    recv_sem,
    load_sem,
    got,
    sum_send,
    sum_recv,
    sum_free,
    late,
    late_core,
    late_slots,
    late_send,
    late_recv,
):
    rows = inputs.shape[0]
    tiles = rows // TILE
    length = 2 * rows
    spans = length // TILE
    wide = lax.axis_index("wide")
    narrow = lax.axis_index("narrow")
    bits = [lax.rem(wide // stride, 2) for stride in STRIDES]
    core = bits[0]
    sibling = (wide + 1 - 2 * core, narrow)
    partner = (wide, 1 - narrow)
    quarter = 2 * narrow + core
    own_half = pl.ds(pl.multiple_of(narrow * 384, 384), 384)
    other_half = pl.ds(pl.multiple_of((1 - narrow) * 384, 384), 384)

    loads = {}

    def load(name, source, target):
        loads[name] = pltpu.make_async_copy(source, target, load_sem.at[len(loads)])
        loads[name].start()

    load("inputs", hidden_in, inputs)
    load("valueright", valueright, hid.at[0, pl.ds(0, 192)])
    load("shaperight", shaperight, hid.at[0, pl.ds(192, 192)])
    load("valueleft", valueleft, hid.at[1, pl.ds(0, 192)])
    load("shapeleft", shapeleft, hid.at[1, pl.ds(192, 192)])
    load("filterout", filterout, factor_gate.at[0, pl.ds(0, 128)])
    load("cos", hbm_cos, table_cos)
    load("sin", hbm_sin, table_sin)
    load("outright", outright, d_gate.at[0, pl.ds(0, 192)])
    load("outleft", outleft, d_gate.at[0, pl.ds(192, 192)])
    load("gateright", gateright, d_lift.at[1, pl.ds(96, 192), pl.ds(0, 384)])
    load("liftright", liftright, d_lift.at[1, pl.ds(96, 192), pl.ds(384, 384)])
    load("lowerleft", lowerleft, d_lift.at[1, pl.ds(0, 96)])
    load("lower_top", lowerright.at[pl.ds(0, 512)], d_lift.at[0, :, pl.ds(0, 384)])
    load("lower_end", lowerright.at[pl.ds(512, 256)], d_lift.at[0, pl.ds(0, 256), pl.ds(384, 384)])
    for k in range(2):
        at = pl.ds(64 * k, 192)
        load(("gate", k), gateleft.at[:, pl.ds(D * k, D)], w_gate.at[k, at])
        load(("lift", k), liftleft.at[:, pl.ds(D * k, D)], w_lift.at[k, at])
    load("upstream", upstream, up_halves.at[narrow])

    stores = []

    def store(source, target):
        stores.append(pltpu.make_async_copy(source, target, store_sem.at[len(stores)]))
        stores[-1].start()

    barrier = pltpu.get_barrier_semaphore()
    others = [(wide + stride * (1 - 2 * bit), narrow) for stride, bit in zip(STRIDES, bits)]
    chip = wide // 2
    fellows = [(2 * lax.rem(chip + t, 8) + core, narrow) for t in range(8)]
    for device in [sibling, partner] + fellows[1:]:
        pl.semaphore_signal(barrier, inc=1, device_id=device, device_id_type=MESH)

    for i, source in enumerate((gainfirst, shiftfirst, gainsecond, shiftsecond)):
        vectors[i : i + 1, :] = source[...].reshape(1, D)
    vectors[4:7, :] = convtaps[...]
    vectors[7:8, :] = jnp.zeros((1, D), F32)
    filter_vectors[...] = jnp.zeros(filter_vectors.shape, F32)
    filter_vectors[0:5, :] = posweight[...]
    for i, source in enumerate((posbias, midbias, sinefreq)):
        filter_vectors[8 + i : 9 + i, :] = source[...].reshape(1, 128)

    def send(source, target, device, index):
        return pltpu.make_async_remote_copy(
            src_ref=source,
            dst_ref=target,
            send_sem=send_sem.at[index],
            recv_sem=recv_sem.at[index],
            device_id=device,
            device_id_type=MESH,
        )

    mixer_slab = sums_mixer.at[narrow]
    parts_of = [sums_channel.at[pl.ds(PART * i, PART)] for i in range(4)] + [mixer_slab.at[pl.ds(0, PART)]]
    offsets = []
    for order in ORDERS:
        found = [0]
        for step in range(4):
            found.append(pl.multiple_of(found[step] + bits[order[step]] * (PART >> (step + 1)), 16))
        offsets.append(found)

    def sum_copy(source, target, i, step, back):
        index = 8 * i + 4 * back + step
        return pltpu.make_async_remote_copy(
            src_ref=source,
            dst_ref=target,
            send_sem=sum_send.at[index],
            recv_sem=sum_recv.at[index],
            device_id=others[ORDERS[i][step]],
            device_id_type=MESH,
        )

    def scatter(i, step):
        size = PART >> (step + 1)
        away = pl.multiple_of(offsets[i][step] + (1 - bits[ORDERS[i][step]]) * size, 16)
        return sum_copy(
            parts_of[i].at[pl.ds(away, size)], got.at[i, pl.ds(STEP_ROWS[step], size)], i, step, 0
        )

    def gather(i, step):
        at = pl.ds(offsets[i][step + 1], PART >> (step + 1))
        return sum_copy(parts_of[i].at[at], parts_of[i].at[at], i, step, 1)

    def hand_back(i, step):
        pl.semaphore_wait(sum_free.at[4 * i + step], 1)
        gather(i, step).start()

    def advance(i, step):
        scatter(i, step).wait()

        @pl.loop(0, (PART >> (step + 1)) // CHUNK)
        def _(index):
            own = pl.ds(pl.multiple_of(offsets[i][step + 1] + index * CHUNK, 16), CHUNK)
            came = got[i, pl.ds(pl.multiple_of(STEP_ROWS[step] + index * CHUNK, 16), CHUNK), :]
            parts_of[i][own, :] = (parts_of[i][own, :].astype(F32) + came.astype(F32)).astype(BF16)

        pl.semaphore_signal(
            sum_free.at[4 * i + step],
            inc=1,
            device_id=others[ORDERS[i][step]],
            device_id_type=MESH,
        )
        if step < 3:
            scatter(i, step + 1).start()
        else:
            hand_back(i, 3)

    def retreat(i, step):
        gather(i, step).wait()
        if step > 0:
            hand_back(i, step - 1)

    def late_copy(source, target, device, index):
        return pltpu.make_async_remote_copy(
            src_ref=source,
            dst_ref=target,
            send_sem=late_send.at[index],
            recv_sem=late_recv.at[index],
            device_id=device,
            device_id_type=MESH,
        )

    row = lax.broadcasted_iota(jnp.int32, (D, 384), 0)
    lane = lax.broadcasted_iota(jnp.int32, (D, 384), 1)
    step = jnp.where(lane >= 96, 96, 0) + jnp.where(lane >= 192, 96, 0) + jnp.where(lane >= 288, 96, 0)
    select = mask(row == lane + step + narrow * 96)
    for name in ("valueright", "shaperight", "valueleft", "shapeleft"):
        loads[name].wait()
    right_half = mm(hid[0, 0:192, :], select).astype(BF16)
    shape_half = mm(hid[0, 192:384, :], select).astype(BF16)
    for b in range(4):
        kept = between(384, 96 * b, 96 * b + 96)
        w_first[192 * b : 192 * b + 192, 0:384] = right_half * kept
        w_first[192 * b : 192 * b + 192, 384:768] = shape_half * kept
    row = lax.broadcasted_iota(jnp.int32, (D, 2 * PAD), 0)
    lane = lax.broadcasted_iota(jnp.int32, (D, 2 * PAD), 1)
    group = jnp.where(lane >= PAD, 1, 0)
    entry = lane - PAD * group
    spread = mask((row == (2 * narrow + group) * 192 + entry) & (entry < 192))
    for source, target in ((0, w_value), (192, w_shape)):
        wider = mm(hid[1, source : source + 192, :], spread).astype(BF16)
        for b in range(4):
            for k in range(2):
                target[96 * b + 48 * k : 96 * b + 48 * k + 48, :] = wider[
                    48 * b : 48 * b + 48, :
                ] * between(2 * PAD, PAD * k, PAD * k + PAD)
    row = lax.broadcasted_iota(jnp.int32, (D, 192), 0)
    lane = lax.broadcasted_iota(jnp.int32, (D, 192), 1)
    start = (2 * narrow) * 192 + (1 - narrow) * 96
    cross = mask(row == start + lane + jnp.where(lane >= 96, 96, 0))
    for i in range(2):
        part = mm(hid[0, 192 * i : 192 * i + 192, :], cross).astype(BF16)
        for b in range(2):
            w_cross[i, 192 * b : 192 * b + 192, :] = part * between(192, 96 * b, 96 * b + 96)
    first = vectors[0:1, :]
    shift_first = vectors[1:2, :]

    coarse = vectors[...].astype(BF16)
    fine = (vectors[...] - coarse.astype(F32)).astype(BF16)
    through[...] = mm(coarse, w_first[...]) + mm(fine, w_first[...])
    loads["inputs"].wait()

    @pl.loop(0, tiles)
    def _(index):
        at = tile_rows(index)
        values = inputs[at, :].astype(F32)
        average = jnp.mean(values, axis=-1, keepdims=True)
        center = values - average
        inverse = lax.rsqrt(jnp.mean(center * center, axis=-1, keepdims=True) + EPSILON)
        hat = center * inverse
        stats[at, 0:1] = average
        stats[at, 1:2] = inverse
        normed = (hat * first + shift_first).astype(BF16)
        norm_one[at, :] = normed
        inner = mm(normed, w_first[...]).astype(BF16)
        inner_one[at, :] = inner
        signal = mm(inner[:, :384], w_value[...]).astype(BF16)
        sig_halves[0, at, :] = signal[:, :PAD]
        sig_halves[1, at, :] = signal[:, PAD:]
        shaped = mm(inner[:, 384:], w_shape[...])
        shaping[0, at, :] = shaped[:, :PAD]
        shaping[1, at, :] = shaped[:, PAD:]

    pl.semaphore_wait(barrier, 9)
    sig_copy = send(sig_halves.at[1 - core], sig_rows.at[core], sibling, 1)
    sig_copy.start()
    up_copy = send(upstream, up_halves.at[narrow], partner, 0)
    up_copy.start()
    sig_rows[core] = sig_halves[core]

    row = lax.broadcasted_iota(jnp.int32, (D, PAD), 0)
    lane = lax.broadcasted_iota(jnp.int32, (D, PAD), 1)
    pick = mask((row == quarter * 192 + lane) & (lane < 192))
    conv = mm(coarse, pick) + mm(fine, pick)
    loads["filterout"].wait()
    own_out[...] = mm(factor_gate[0, 0:128, :].astype(BF16), pick).astype(BF16)
    pos_bias = filter_vectors[8:9, :]
    mid_bias = filter_vectors[9:10, :]
    frequency = filter_vectors[10:11, :]
    mid_high = midweight[...].astype(BF16)
    mid_low = (midweight[...] - mid_high.astype(F32)).astype(BF16)
    pos_high = filter_vectors[0:8, :].astype(BF16).astype(F32)
    pos_parts = jnp.concatenate(
        [pos_high, pos_high, filter_vectors[0:8, :] - pos_high, jnp.zeros((8, 128), F32)], axis=0
    ).astype(BF16)
    ranks = 5 * (quarter * 192 + lanes(PAD))
    for bound in range(5):
        ranks = jnp.where(ranks >= D, ranks - D, ranks)
    lowest = math.log(0.25 / length)
    highest = math.log(1.0 / 30.0)
    rate = jnp.exp(lowest + ranks.astype(F32) * (1.0 / D) * (highest - lowest))
    loud = jnp.sqrt(2.0 * rate)

    def decay(index):
        places = (lax.broadcasted_iota(jnp.int32, (TILE, PAD), 0) + index * TILE).astype(F32)
        return jnp.exp(-rate * places) * loud

    @pl.loop(0, spans)
    def _(index):
        at = tile_rows(index)
        one = mm(place_parts[at, :], pos_parts) + pos_bias
        sine, cosine = sine_cosine(frequency * one)
        high = sine.astype(BF16)
        low = (sine - high.astype(F32)).astype(BF16)
        lin_one[at, :] = one.astype(BF16)
        act_one[at, :] = high
        cos_one[at, :] = cosine.astype(BF16)
        two = mm(high, mid_high) + mm(low, mid_high) + mm(high, mid_low) + mid_bias
        sine, cosine = sine_cosine(frequency * two)
        high = sine.astype(BF16)
        lin_two[at, :] = two.astype(BF16)
        act_two[at, :] = high
        cos_two[at, :] = cosine.astype(BF16)
        short[at, :] = (mm(high, own_out[...]) * decay(index)).astype(BF16)

    loads["cos"].wait()
    loads["sin"].wait()

    @pl.loop(0, spans)
    def _(index):
        at = tile_rows(index)
        real = mm(table_cos[at, :], short[...])
        imag = mm(table_sin[at, :], short[...])
        turn_cos = place[at, 5:6] * (1.0 / length)
        turn_sin = place[at, 6:7] * (1.0 / length)
        fil_spec[0, at, :] = real * turn_cos + imag * turn_sin
        fil_spec[1, at, :] = imag * turn_cos - real * turn_sin

    for name in ("outright", "outleft", "gateright", "liftright", "lowerleft", "lower_top", "lower_end"):
        loads[name].wait()
    out_half = d_gate[0, 0:192, own_half]
    w_out_first[0:192, :] = out_half * between(384, 0, 192)
    w_out_first[192:256, :] = jnp.zeros((64, 384), BF16)
    w_out_first[256:448, :] = out_half * between(384, 192, 384)
    w_out_first[448:512, :] = jnp.zeros((64, 384), BF16)
    for b in range(4):
        for k in range(4):
            w_out_second[b // 2, 192 * (b % 2) + 48 * k : 192 * (b % 2) + 48 * k + 48, :] = d_gate[
                0, 192 + 48 * b : 240 + 48 * b, :
            ] * between(D, 192 * k, 192 * k + 192)
    lane = lanes(384)
    inside = lane - jnp.where(lane >= 192, 192, 0)
    for b in range(4):
        kept = mask((inside >= 48 * b) & (inside < 48 * b + 48))
        w_glu[192 * b : 192 * b + 192, 0:384] = d_lift[1, 96:288, 0:384] * kept
        w_glu[192 * b : 192 * b + 192, 384:768] = d_lift[1, 96:288, 384:768] * kept
    for target in (w_gate, w_lift):
        target[0, 192:256, :] = jnp.zeros((64, D), BF16)
        target[1, 0:64, :] = jnp.zeros((64, D), BF16)
    w_lower[0, 0:512, :] = d_lift[0, :, 0:256] * between(256, 0, 192)
    w_lower[0, 512:768, :] = d_lift[0, 0:256, 384:640] * between(256, 0, 192)
    w_lower[1, 0:512, :] = d_lift[0, :, 128:384] * between(256, 64, 256)
    w_lower[1, 512:768, :] = d_lift[0, 0:256, 512:768] * between(256, 64, 256)
    for b in range(2):
        for k in range(4):
            w_lower_second[192 * b + 48 * k : 192 * b + 48 * k + 48, :] = d_lift[
                1, 48 * b : 48 * b + 48, :
            ] * between(D, 192 * k, 192 * k + 192)

    sig_copy.wait_recv()
    sig_pad[0:8, :] = jnp.zeros((8, PAD), F32)
    for part in range(2):
        sig_pad[8 + part * rows : 8 + part * rows + rows, :] = sig_rows[part].astype(F32)
    for index in range(spans):
        start = 8 + index * TILE
        total = conv[4:5, :] * sig_pad[start : start + TILE, :]
        total += conv[5:6, :] * sig_pad[start - 1 : start - 1 + TILE, :]
        total += conv[6:7, :] * sig_pad[start - 2 : start - 2 + TILE, :]
        short[index * TILE : index * TILE + TILE, :] = total.astype(BF16)

    @pl.loop(0, spans)
    def _(index):
        at = tile_rows(index)
        real = mm(table_cos[at, :], short[...])
        imag = mm(table_sin[at, :], short[...])
        sig_spec[0, at, :] = real.astype(BF16)
        sig_spec[1, at, :] = imag.astype(BF16)
        fil_re = fil_spec[0, at, :]
        fil_im = fil_spec[1, at, :]
        prod_spec[0, at, :] = (real * fil_re - imag * fil_im).astype(BF16)
        prod_spec[1, at, :] = (real * fil_im + imag * fil_re).astype(BF16)

    per_half = rows // TILE

    def long_tile(part, index):
        at = tile_rows(part * per_half + index)
        result = mm(table_cos[at, :], prod_spec[0]) + mm(table_sin[at, :], prod_spec[1])
        return result.astype(BF16)

    @pl.loop(0, per_half)
    def _(index):
        long_rows[1 - core, tile_rows(index), :] = long_tile(1 - core, index)

    long_copy = send(long_rows.at[1 - core], long_halves.at[core], sibling, 2)
    long_copy.start()

    @pl.loop(0, per_half)
    def _(index):
        long_halves[core, tile_rows(index), :] = long_tile(core, index)

    long_copy.wait_recv()
    sig_copy.wait_send()
    long_copy.wait_send()

    def inner_copy(index):
        at = tile_rows(index)
        return send(inner_out.at[narrow, at], inner_out.at[narrow, at], partner, 3 + index)

    dn_copy = send(dn_send, dn_recv, partner, 5)
    own_rows = tile_rows(narrow)
    cross_copy = send(cross_send, d_inner_out.at[own_rows], partner, 6)
    middle_copy = send(mid_send, mid_recv, partner, 11)

    def part_copy(index):
        at = tile_rows(index)
        return send(part_send.at[at], part_recv.at[at], partner, 7 + index)

    def shape_copy(index):
        at = tile_rows(index)
        return send(shape_send.at[at], shape_recv.at[at], partner, 12 + index)

    def value_copy(index):
        at = tile_rows(index)
        return send(value_send.at[at], value_recv.at[at], partner, 14 + index)

    def first_other(index):
        return 1 - narrow + index * (2 * narrow - 1)

    @pl.loop(0, tiles)
    def _(order):
        index = narrow + order * (1 - 2 * narrow)
        at = tile_rows(index)
        inner = None
        for k in range(2):
            product = (shaping[k, at, :] * long_halves[k, at, :].astype(F32)).astype(BF16)
            term = mm(product, w_out_first[k * PAD : k * PAD + PAD, :])
            inner = term if inner is None else inner + term
        inner_out[narrow, at, :] = inner.astype(BF16)

        @pl.when(order == 1)
        def _():
            inner_copy(narrow).wait_send()

        inner_copy(index).start()

    up_copy.wait_recv()
    for k in range(2):
        loads["gate", k].wait()
        loads["lift", k].wait()
    loads["upstream"].wait()

    gain_second = vectors[2:3, :]
    shift_second = vectors[3:4, :]

    @pl.loop(0, tiles)
    def _(order):
        index = first_other(order)
        at = tile_rows(index)
        inner_copy(index).wait_recv()
        mid = inputs[at, :].astype(F32)
        mid += mm(inner_out[0, at, :], w_out_second[0])
        mid += mm(inner_out[1, at, :], w_out_second[1])
        dn_own[...] = mid
        center = mid - jnp.mean(mid, axis=-1, keepdims=True)
        inverse = lax.rsqrt(jnp.mean(center * center, axis=-1, keepdims=True) + EPSILON)
        hat = center * inverse
        hat_two[...] = hat
        stats[0:TILE, 2:3] = inverse
        normed = (hat * gain_second + shift_second).astype(BF16)
        norm_two[at, :] = normed
        inner = mm(normed, w_glu[...]).astype(BF16)
        inner_glu[at, :] = inner
        lower = [None, None]
        for k in range(2):
            for columns in (slice(0, 256), slice(256, 512), slice(512, 768)):
                gate = mm(inner[:, 128 * k : 128 * k + 256], w_gate[k, :, columns])
                lift = mm(inner[:, 384 + 128 * k : 384 + 128 * k + 256], w_lift[k, :, columns])
                cumulative = 0.5 * (1.0 + lax.erf(gate * (1.0 / math.sqrt(2.0))))
                density = jnp.exp(-0.5 * gate * gate) * (1.0 / math.sqrt(2.0 * math.pi))
                activated = gate * cumulative
                unit = (activated * lift).astype(BF16)
                hid[k, at, columns] = unit
                factor_lift[k, :, columns] = activated
                factor_gate[k, :, columns] = lift * (cumulative + gate * density)
                term = mm(unit, w_lower[k, columns, :])
                lower[k] = term if lower[k] is None else lower[k] + term
        inner_low = join(*lower).astype(BF16)
        inner_lower[at, :] = inner_low
        out_own[at, :] = dn_own[:, own_half] + mm(inner_low, w_lower_second[:, own_half])
        part_send[at, :] = mm(inner_low, w_lower_second[:, other_half]).astype(BF16)

        above = jnp.concatenate([up_halves[0, at, :], up_halves[1, at, :]], axis=1)
        d_low = mm_nt(above, w_lower_second[...]).astype(BF16)
        d_inner_lower[at, :] = d_low
        gates = [None, None]
        lifts = [None, None]
        for k in range(2):
            for columns in (slice(0, 256), slice(256, 512), slice(512, 768)):
                d_hidden = mm_nt(d_low[:, 128 * k : 128 * k + 256], w_lower[k, columns, :])
                to_gate = (d_hidden * factor_gate[k, :, columns]).astype(BF16)
                to_lift = (d_hidden * factor_lift[k, :, columns]).astype(BF16)
                d_gate[k, at, columns] = to_gate
                d_lift[k, at, columns] = to_lift
                term = mm_nt(to_gate, w_gate[k, :, columns])
                gates[k] = term if gates[k] is None else gates[k] + term
                term = mm_nt(to_lift, w_lift[k, :, columns])
                lifts[k] = term if lifts[k] is None else lifts[k] + term
        d_glu = jnp.concatenate([join(*gates), join(*lifts)], axis=1).astype(BF16)
        d_inner_glu[at, :] = d_glu
        into = mm_nt(d_glu, w_glu[...])
        dn_own[...] = into

        @pl.when(order == 0)
        def _():
            dn_send[...] = dn_own[...].astype(BF16)
            dn_copy.start()

    low_lanes = lanes(128) < 64
    for columns in (slice(0, 384), slice(384, 768)):
        columns_at = slice(LOWER_RIGHT + columns.start, LOWER_RIGHT + columns.stop)
        parts = [
            mm_tn(hid[k, :, columns], d_inner_lower[:, 128 * k : 128 * k + 256]) for k in range(2)
        ]
        sums_channel[columns_at, 0:128] = parts[0][:, 0:128].astype(BF16)
        sums_channel[columns_at, 128:256] = jnp.where(
            low_lanes, parts[0][:, 128:256], parts[1][:, 0:128]
        ).astype(BF16)
        sums_channel[columns_at, 256:384] = parts[1][:, 128:256].astype(BF16)
    scatter(0, 0).start()
    for side in range(2):
        columns = slice(384 * side, 384 * side + 384)
        folded = fold(mm_tn(inner_lower[...], up_halves[side]), side)
        for b in range(2):
            first_row = LOWER_LEFT + 96 * side + 48 * b
            sums_channel[first_row : first_row + 48, :] = folded[b].astype(BF16)
    for offset, target in ((0, GATE_RIGHT), (384, LIFT_RIGHT)):
        whole = mm_tn(norm_two[...], d_inner_glu[:, offset : offset + 384])
        total = None
        for b in range(4):
            term = whole[192 * b : 192 * b + 192, :] * mask(
                (inside >= 48 * b) & (inside < 48 * b + 48), F32
            )
            total = term if total is None else total + term
        sums_channel[target : target + 192, :] = total.astype(BF16)

    for offset, upper, target in ((0, d_gate, GATE_LEFT), (384, d_lift, LIFT_LEFT)):
        for k in range(2):
            for start in (0, 384):
                whole = mm_tn(
                    inner_glu[:, offset + 128 * k : offset + 128 * k + 256],
                    upper[k, :, start : start + 384],
                )
                first_row = target + 384 * k + start // 2
                sums_channel[first_row : first_row + 192, :] = whole[
                    64 * k : 64 * k + 192, :
                ].astype(BF16)
        if upper is d_gate:
            scatter(1, 0).start()
    sums_channel[2880:3072, :] = jnp.zeros((192, 384), BF16)
    scatter(2, 0).start()
    scatter(3, 0).start()

    dn_copy.wait_recv()
    into = dn_own[...] + dn_recv[...].astype(F32)
    hat = hat_two[...]
    gain_sums[...] = jnp.zeros(gain_sums.shape, F32)
    gain_sums[0:1, :] = jnp.sum(into * hat, axis=0, keepdims=True)
    gain_sums[1:2, :] = jnp.sum(into, axis=0, keepdims=True)
    scaled = into * gain_second
    above = jnp.concatenate([up_halves[0, own_rows, :], up_halves[1, own_rows, :]], axis=1)
    d_mid = above.astype(F32) + stats[0:TILE, 2:3] * (
        scaled
        - jnp.mean(scaled, axis=-1, keepdims=True)
        - hat * jnp.mean(scaled * hat, axis=-1, keepdims=True)
    )
    hat_two[...] = d_mid
    branch[...] = d_mid.astype(BF16)
    cross_send[...] = mm_nt(branch[...], w_out_second[1 - narrow]).astype(BF16)
    cross_copy.start()
    mid_send[...] = hat_two[:, other_half].astype(BF16)
    d_inner_out[own_rows, :] = mm_nt(branch[...], w_out_second[narrow]).astype(BF16)
    for i in range(4):
        advance(i, 0)
    for h in range(2):
        for side in range(2):
            columns = slice(384 * side, 384 * side + 384)
            folded = fold(mm_tn(inner_out[h, own_rows, :], branch[:, columns]), side)
            for b in range(2):
                first_row = OUT_LEFT + 192 * h + 96 * side + 48 * b
                mixer_slab[first_row : first_row + 48, :] = folded[b].astype(BF16)

    @pl.loop(0, tiles)
    def _(order):
        index = narrow + order * (1 - 2 * narrow)
        at = tile_rows(index)

        @pl.when(order == 1)
        def _():
            cross_copy.wait_recv()
            middle_copy.start()

        d_inner = d_inner_out[at, :]
        for k in range(2):
            d_mixed = mm_nt(d_inner, w_out_first[k * PAD : k * PAD + PAD, :])
            d_shaping[k, at, :] = (d_mixed * long_halves[k, at, :].astype(F32)).astype(BF16)
            sig_halves[k, at, :] = (d_mixed * shaping[k, at, :]).astype(BF16)

    dl_copy = send(sig_halves.at[1 - core], dl_rows.at[core], sibling, 9)
    dl_copy.start()
    dl_rows[core] = sig_halves[core]

    @pl.loop(0, tiles)
    def _(index):
        at = tile_rows(index)
        to_shape = jnp.concatenate([d_shaping[0, at, :], d_shaping[1, at, :]], axis=1)
        d_inner_one[at, 384:768] = mm_nt(to_shape, w_shape[...]).astype(BF16)
        shape_send[at, :] = mm_nt(
            to_shape, w_shape[pl.ds(pl.multiple_of((1 - narrow) * 192, 192), 192), :]
        ).astype(BF16)
        shape_copy(index).start()

    @pl.loop(0, tiles)
    def _(index):
        part_copy(index).start()

    advance(1, 1)
    advance(0, 1)

    lane = lax.broadcasted_iota(jnp.int32, (2 * PAD, 384), 1)
    row = lax.broadcasted_iota(jnp.int32, (2 * PAD, 384), 0)
    squeeze = mask(row == lane + jnp.where(lane >= 192, 64, 0))

    def first_gradient(offset):
        whole = mm_tn(norm_one[...], d_inner_one[:, offset : offset + 384])
        total = None
        for b in range(4):
            term = whole[192 * b : 192 * b + 192, :] * between(384, 96 * b, 96 * b + 96, F32)
            total = term if total is None else total + term
        return total.astype(BF16)

    def second_gradient(offset, upper):
        above = jnp.concatenate([upper[0], upper[1]], axis=1)
        whole = mm_tn(inner_one[:, offset : offset + 384], above)
        pieces = []
        for b in range(4):
            total = None
            for k in range(2):
                term = whole[96 * b + 48 * k : 96 * b + 48 * k + 48, :] * between(
                    2 * PAD, PAD * k, PAD * k + PAD, F32
                )
                total = term if total is None else total + term
            pieces.append(total)
        return mm(jnp.concatenate(pieces, axis=0).astype(BF16), squeeze).astype(BF16)

    mixer_slab[SHAPE_RIGHT : SHAPE_RIGHT + 192, :] = first_gradient(384)
    mixer_slab[SHAPE_LEFT : SHAPE_LEFT + 192, :] = second_gradient(384, d_shaping)
    scatter(4, 0).start()
    parts = []
    for k in range(2):
        product = (shaping[k] * long_halves[k].astype(F32)).astype(BF16)
        parts.append(mm_tn(product, d_inner_out[...]))
    late[OUT_RIGHT : OUT_RIGHT + 192, :] = jnp.where(
        lanes(384) < 192, parts[0][0:192, :], parts[1][0:192, :]
    ).astype(BF16)

    dl_copy.wait_recv()

    @pl.loop(0, spans)
    def _(index):
        at = tile_rows(index)
        upper = dl_rows[...].reshape(length, PAD)
        real = mm(table_cos[at, :], upper)
        imag = mm(table_sin[at, :], upper)
        fil_re = fil_spec[0, at, :]
        fil_im = fil_spec[1, at, :]
        prod_spec[0, at, :] = (real * fil_re + imag * fil_im).astype(BF16)
        prod_spec[1, at, :] = (imag * fil_re - real * fil_im).astype(BF16)
        sig_re = sig_spec[0, at, :].astype(F32)
        sig_im = sig_spec[1, at, :].astype(F32)
        turn_cos = place[at, 5:6] * (1.0 / length)
        turn_sin = place[at, 6:7] * (1.0 / length)
        both_re = real * sig_re + imag * sig_im
        both_im = imag * sig_re - real * sig_im
        sig_spec[0, at, :] = (both_re * turn_cos - both_im * turn_sin).astype(BF16)
        sig_spec[1, at, :] = (both_im * turn_cos + both_re * turn_sin).astype(BF16)

    advance(2, 1)
    advance(1, 2)
    advance(0, 2)
    advance(4, 0)
    advance(3, 1)
    ds_pad[length : length + 8, :] = jnp.zeros((8, PAD), F32)

    @pl.loop(0, spans)
    def _(index):
        at = tile_rows(index)
        result = mm(table_cos[at, :], prod_spec[0]) + mm(table_sin[at, :], prod_spec[1])
        ds_pad[at, :] = result.astype(BF16).astype(F32)

    for index in range(spans):
        start = index * TILE
        total = conv[4:5, :] * ds_pad[start : start + TILE, :]
        total += conv[5:6, :] * ds_pad[start + 1 : start + 1 + TILE, :]
        total += conv[6:7, :] * ds_pad[start + 2 : start + 2 + TILE, :]
        part, inner_start = divmod(start, rows)
        long_rows[part, inner_start : inner_start + TILE, :] = total.astype(BF16)
    ds_copy = send(long_rows.at[1 - core], ds_halves.at[core], sibling, 10)
    ds_copy.start()
    ds_halves[core] = long_rows[core]

    advance(1, 3)
    advance(2, 2)
    advance(0, 3)
    advance(4, 1)
    advance(3, 2)
    retreat(1, 3)
    grad_vectors[...] = jnp.zeros(grad_vectors.shape, F32)
    sums = [jnp.zeros((1, PAD), F32) for _ in range(3)]
    for index in range(spans):
        start = index * TILE
        upper = ds_pad[start : start + TILE, :]
        for j in range(3):
            sums[j] += jnp.sum(
                upper * sig_pad[8 + start - j : 8 + start - j + TILE, :], axis=0, keepdims=True
            )
    sums = jnp.concatenate(sums + [jnp.zeros((5, PAD), F32)], axis=0)
    lane = lax.broadcasted_iota(jnp.int32, (PAD, 384), 1)
    row = lax.broadcasted_iota(jnp.int32, (PAD, 384), 0)
    place_core = mask((lane == core * 192 + row) & (row < 192))
    conv_sums = mm(sums.astype(BF16), place_core)
    grad_vectors[4:7, :] = conv_sums[0:3, :]

    d_lin[...] = jnp.zeros(d_lin.shape, F32)
    grad_filter[...] = jnp.zeros(grad_filter.shape, F32)

    def filter_back(index):
        at = tile_rows(index)
        d_taps = mm(table_cos[at, :], sig_spec[0]) + mm(table_sin[at, :], sig_spec[1])
        d_mod = d_taps * decay(index)
        d_mod = d_mod.astype(BF16)
        d_lin[...] += mm_tn(act_two[at, :], d_mod)
        two = mm_nt(d_mod, own_out[...]) * cos_two[at, :].astype(F32)
        scaled_two = two * frequency
        coarse_two = scaled_two.astype(BF16)
        grad_filter[0:128, :] += mm_tn(act_one[at, :], coarse_two)
        one = mm_nt(coarse_two, mid_high) * cos_one[at, :].astype(F32)
        scaled_one = one * frequency
        grad_filter[128:136, :] += mm_tn(place_parts[at, :], scaled_one.astype(BF16))[0:8, :]
        grad_filter[136:137, :] += jnp.sum(scaled_one, axis=0, keepdims=True)
        grad_filter[137:138, :] += jnp.sum(scaled_two, axis=0, keepdims=True)
        grad_filter[138:139, :] += jnp.sum(
            one * lin_one[at, :].astype(F32) + two * lin_two[at, :].astype(F32), axis=0, keepdims=True
        )

    pl.loop(0, spans // 2)(filter_back)
    advance(4, 2)
    advance(2, 3)
    retreat(0, 3)
    pl.loop(spans // 2, spans)(filter_back)
    late[FILTER_OUT : FILTER_OUT + 128, :] = mm(d_lin[...].astype(BF16), place_core).astype(BF16)
    for i in range(3):
        late[FILTER : FILTER + 48, 128 * i : 128 * i + 128] = grad_filter[
            48 * i : 48 * i + 48, :
        ].astype(BF16)


    advance(4, 3)
    advance(3, 3)
    retreat(1, 2)
    retreat(0, 2)
    retreat(2, 3)
    ds_copy.wait_recv()
    other_blocks = pl.ds(pl.multiple_of((1 - narrow) * 192, 192), 192)

    @pl.loop(0, tiles)
    def _(index):
        at = tile_rows(index)
        to_value = jnp.concatenate([ds_halves[0, at, :], ds_halves[1, at, :]], axis=1)
        d_inner = mm_nt(to_value, w_value[...]).astype(BF16)
        d_inner_one[at, 0:384] = d_inner
        against = inner_one[at, :].astype(F32) - through[1:2, :]
        d_inner = d_inner_one[at, :].astype(F32)
        plain = jnp.sum(d_inner * through[0:1, :], axis=-1, keepdims=True)
        along = jnp.sum(d_inner * against, axis=-1, keepdims=True)
        stats[at, 2:3] = plain
        stats[at, 3:4] = along
        lane = lanes(128)
        tail = jnp.where(lane == 64, plain, jnp.where(lane == 65, along, 0.0))
        away = mm_nt(to_value, w_value[other_blocks, :])
        value_send[at, 0:128] = away[:, 0:128].astype(BF16)
        value_send[at, 128:192] = away[:, 128:192].astype(BF16)
        value_send[at, 192:256] = tail[:, 64:128].astype(BF16)
        value_copy(index).start()

    @pl.loop(0, tiles)
    def _(index):
        at = tile_rows(index)
        into = mm_nt(d_inner_one[at, :], w_first[...])
        hat = (inputs[at, :].astype(F32) - stats[at, 0:1]) * stats[at, 1:2]
        gain_sums[2:3, :] += jnp.sum(into * hat, axis=0, keepdims=True)
        gain_sums[3:4, :] += jnp.sum(into, axis=0, keepdims=True)

    retreat(4, 3)
    retreat(3, 3)
    late[VALUE_RIGHT : VALUE_RIGHT + 192, :] = first_gradient(0)
    late[VALUE_LEFT : VALUE_LEFT + 192, :] = second_gradient(0, ds_halves)
    grad_vectors[0:4, :] = gain_sums[0:4, 0:384]
    grad_vectors[8:12, :] = gain_sums[0:4, 384:768]
    late[VECTORS : VECTORS + 16, :] = grad_vectors[...].astype(BF16)

    to_core = late_copy(
        late.at[pl.ds(pl.multiple_of((1 - core) * 384, 16), 384)], late_core, sibling, 0
    )
    to_core.start()
    retreat(4, 2)
    to_core.wait()

    @pl.loop(0, 384 // CHUNK)
    def _(index):
        at = pl.ds(pl.multiple_of(core * 384 + index * CHUNK, 16), CHUNK)
        came = late_core[pl.ds(pl.multiple_of(index * CHUNK, 16), CHUNK), :]
        late[at, :] = (late[at, :].astype(F32) + came.astype(F32)).astype(BF16)

    def share(t):
        return pl.multiple_of(core * 384 + lax.rem(chip + 8 - t, 8) * CHUNK, 16)

    direct = [
        late_copy(late.at[pl.ds(share(8 - t), CHUNK)], late_slots.at[t - 1], fellows[t], t)
        for t in range(1, 8)
    ]
    for copy in direct:
        copy.start()

    first_half = vectors[0:1, own_half]
    middle_copy.wait_recv()
    d_middle[own_rows, :] = hat_two[:, own_half]
    d_middle[tile_rows(1 - narrow), :] = mid_recv[...].astype(F32)
    @pl.loop(0, tiles)
    def _(index):
        at = tile_rows(index)
        part_copy(index).wait_recv()
        hidden_out[at, :] = (out_own[at, :] + part_recv[at, :].astype(F32)).astype(BF16)
        shape_copy(index).wait_recv()
        value_copy(index).wait_recv()
        into = mm_nt(d_inner_one[at, :], w_first[own_half, :])
        into += mm_nt(value_recv[at, 0:192], w_cross[0])
        into += mm_nt(shape_recv[at, :], w_cross[1])
        plain = (stats[at, 2:3] + value_recv[at, 192:193].astype(F32)) * (1.0 / D)
        along = (stats[at, 3:4] + value_recv[at, 193:194].astype(F32)) * (1.0 / D)
        hat = (inputs[at, own_half].astype(F32) - stats[at, 0:1]) * stats[at, 1:2]
        hidden_grad[at, :] = (
            d_middle[at, :] + stats[at, 1:2] * (into * first_half - plain - hat * along)
        ).astype(BF16)

    store(hidden_out, result_out)
    store(hidden_grad, result_grad)
    retreat(4, 1)
    early_rows = pl.ds(offsets[4][1], PART // 2)
    across_early = late_copy(mixer_slab.at[early_rows], mixer_slab.at[early_rows], partner, 40)
    across_early.start()
    retreat(1, 1)
    retreat(0, 1)
    total = late[pl.ds(share(0), CHUNK), :].astype(F32)
    for t in range(1, 8):
        direct[t - 1].wait()
        total += late_slots[t - 1].astype(F32)
    own_share = pl.ds(pl.multiple_of(PART + share(0), 16), CHUNK)
    mixer_slab[own_share, :] = total.astype(BF16)
    spread_out = [
        late_copy(mixer_slab.at[own_share], mixer_slab.at[own_share], fellows[t], 8 + t)
        for t in range(1, 8)
    ]
    for copy in spread_out:
        copy.start()
    retreat(2, 2)
    retreat(3, 2)
    across = []
    along_own = []
    for t in range(8):
        if t > 0:
            spread_out[t - 1].wait()
        at = pl.ds(pl.multiple_of(PART + share(t), 16), CHUNK)
        across.append(late_copy(mixer_slab.at[at], mixer_slab.at[at], partner, 16 + t))
        across[t].start()
        along_own.append(late_copy(mixer_slab.at[at], mixer_slab.at[at], sibling, 24 + t))
        along_own[t].start()
    across_early.wait()
    other = sums_mixer.at[1 - narrow, early_rows]
    along_early = late_copy(other, other, sibling, 41)
    along_early.start()
    retreat(2, 1)
    along_other = []
    for t in range(8):
        across[t].wait()
        at = pl.ds(pl.multiple_of(PART + share(t), 16), CHUNK)
        other = sums_mixer.at[1 - narrow, at]
        along_other.append(late_copy(other, other, sibling, 32 + t))
        along_other[t].start()
    retreat(3, 1)
    for i in (1, 0, 2, 3):
        retreat(i, 0)
        at = pl.ds(PART * i, PART)
        store(sums_channel.at[at], result_channel.at[at])
    retreat(4, 0)
    along_early.wait()
    early = pl.ds(0, PART)
    store(sums_mixer.at[:, early], result_mixer.at[:, early])
    for copy in along_own + along_other:
        copy.wait()
    rest = pl.ds(PART, PART)
    store(sums_mixer.at[:, rest], result_mixer.at[:, rest])

    inner_copy(1 - narrow).wait_send()
    for copy in (up_copy, dl_copy, ds_copy, dn_copy, cross_copy, middle_copy):
        copy.wait_send()

    @pl.loop(0, tiles)
    def _(index):
        for copy in (part_copy, shape_copy, value_copy):
            copy(index).wait_send()

    for copy in stores:
        copy.wait()


def finish_kernel(
    hidden_in,
    hidden_grad_in,
    hbm_channel,
    hbm_mixer,
    hidden_out,
    hidden_grad,
    grad_gainfirst,
    grad_shiftfirst,
    grad_valueright,
    grad_valueleft,
    grad_shaperight,
    grad_shapeleft,
    grad_convtaps,
    grad_posweight,
    grad_posbias,
    grad_sinefreq,
    grad_midweight,
    grad_midbias,
    grad_filterout,
    grad_outright,
    grad_outleft,
    grad_gainsecond,
    grad_shiftsecond,
    grad_gateright,
    grad_gateleft,
    grad_liftright,
    grad_liftleft,
    grad_lowerright,
    grad_lowerleft,
    channel,
    mixer,
    pass_out,
    pass_grad,
    valueright,
    valueleft,
    shaperight,
    shapeleft,
    outright,
    outleft,
    gateright,
    gateleft,
    liftright,
    liftleft,
    lowerright,
    lowerleft,
    both_filter,
    in_sem,
    out_sem,
):
    ins = []
    outs = []

    def fetch(source, target):
        ins.append(pltpu.make_async_copy(source, target, in_sem.at[len(ins)]))
        ins[-1].start()

    def store(source, target):
        outs.append(pltpu.make_async_copy(source, target, out_sem.at[len(outs)]))
        outs[-1].start()

    for i in range(4):
        at = pl.ds(PART * i, PART)
        fetch(hbm_channel.at[at], channel.at[at])
    fetch(hbm_mixer, mixer)
    fetch(hidden_in, pass_out)
    fetch(hidden_grad_in, pass_grad)

    ins[0].wait()
    lowerright[...] = channel[LOWER_RIGHT : LOWER_RIGHT + D, :].astype(F32)
    store(lowerright, grad_lowerright)
    ins[1].wait()
    for h in range(2):
        columns = slice(384 * h, 384 * h + 384)
        lowerleft[:, columns] = channel[LOWER_LEFT + 96 * h : LOWER_LEFT + 96 * h + 96, :].astype(F32)
    gateright[...] = channel[GATE_RIGHT : GATE_RIGHT + 192, :].astype(F32)
    liftright[...] = channel[LIFT_RIGHT : LIFT_RIGHT + 192, :].astype(F32)
    store(lowerleft, grad_lowerleft)
    store(gateright, grad_gateright)
    store(liftright, grad_liftright)
    ins[2].wait()
    for i in range(4):
        first_row = GATE_LEFT + 192 * i
        gateleft[:, 384 * i : 384 * i + 384] = channel[first_row : first_row + 192, :].astype(F32)
    store(gateleft, grad_gateleft)
    ins[3].wait()
    for i in range(4):
        first_row = LIFT_LEFT + 192 * i
        liftleft[:, 384 * i : 384 * i + 384] = channel[first_row : first_row + 192, :].astype(F32)
    store(liftleft, grad_liftleft)
    ins[4].wait()

    lane = lax.broadcasted_iota(jnp.int32, (384, D), 1)
    row = lax.broadcasted_iota(jnp.int32, (384, D), 0)
    step = jnp.where(row >= 96, 96, 0) + jnp.where(row >= 192, 96, 0) + jnp.where(row >= 288, 96, 0)
    unselect = [mask(lane == row + step + 96 * h) for h in range(2)]
    for first_row, target, result in (
        (PART + VALUE_RIGHT, valueright, grad_valueright),
        (SHAPE_RIGHT, shaperight, grad_shaperight),
    ):
        target[...] = mm(mixer[0, first_row : first_row + 192, :], unselect[0]) + mm(
            mixer[1, first_row : first_row + 192, :], unselect[1]
        )
        store(target, result)
    for first_row, target, result in (
        (PART + OUT_RIGHT, outright, grad_outright),
        (SHAPE_LEFT, shapeleft, grad_shapeleft),
        (PART + VALUE_LEFT, valueleft, grad_valueleft),
    ):
        for h in range(2):
            target[:, 384 * h : 384 * h + 384] = mixer[h, first_row : first_row + 192, :].astype(F32)
        store(target, result)
    for h in range(2):
        for side in range(2):
            at = slice(OUT_LEFT + 192 * h + 96 * side, OUT_LEFT + 192 * h + 96 * side + 96)
            outleft[96 * h : 96 * h + 96, 384 * side : 384 * side + 384] = mixer[0, at, :].astype(
                F32
            ) + mixer[1, at, :].astype(F32)
    store(outleft, grad_outleft)
    vectors = [mixer[h, PART + VECTORS : PART + VECTORS + 16, :].astype(F32) for h in range(2)]
    whole = jnp.concatenate(vectors, axis=1)
    both = vectors[0] + vectors[1]
    grad_convtaps[...] = whole[4:7, :]
    for i, target in enumerate((grad_gainsecond, grad_shiftsecond, grad_gainfirst, grad_shiftfirst)):
        target[...] = jnp.concatenate([both[i : i + 1, :], both[8 + i : 9 + i, :]], axis=1).reshape(D)
    for i in range(3):
        columns = slice(128 * i, 128 * i + 128)
        at = slice(PART + FILTER, PART + FILTER + 48)
        both_filter[48 * i : 48 * i + 48, :] = mixer[0, at, columns].astype(F32) + mixer[
            1, at, columns
        ].astype(F32)
    grad_midweight[...] = both_filter[0:128, :]
    grad_posweight[...] = both_filter[128:133, :]
    grad_posbias[...] = both_filter[136:137, :].reshape(128)
    grad_midbias[...] = both_filter[137:138, :].reshape(128)
    grad_sinefreq[...] = both_filter[138:139, :].reshape(128)
    count = grad_filterout.shape[0]
    first = (lax.axis_index("wide") * 2 + lax.axis_index("narrow")) * count
    total = jnp.zeros(grad_filterout.shape, F32)
    row = lax.broadcasted_iota(jnp.int32, (count, 384), 0)
    lane = lax.broadcasted_iota(jnp.int32, (count, 384), 1)
    for h in range(2):
        total += mm_nt(
            mask(lane + 384 * h == first + row),
            mixer[h, PART + FILTER_OUT : PART + FILTER_OUT + 128, :],
        )
    grad_filterout[...] = total
    ins[5].wait()
    store(pass_out, hidden_out)
    ins[6].wait()
    store(pass_grad, hidden_grad)
    for copy in outs:
        copy.wait()


def transform_tables(length):
    index = np.arange(length, dtype=np.float64) + 0.5
    angle = np.outer(index, index) * (math.pi / length)
    return (np.cos(angle).astype(jnp.bfloat16), np.sin(angle).astype(jnp.bfloat16))


def place_table(length):
    places = np.arange(length, dtype=np.float64)
    angle = places * (2.0 * math.pi / length)
    turn = (places + 0.5) * (math.pi / (2.0 * length))
    columns = [
        places / length,
        np.cos(angle),
        np.sin(angle),
        np.cos(2.0 * angle),
        np.sin(2.0 * angle),
        np.cos(turn),
        np.sin(turn),
        np.zeros(length),
    ]
    table = np.stack(columns, axis=1).astype(np.float32)
    feats = np.concatenate([table[:, :5], np.zeros((length, 3), np.float32)], axis=1)
    high = feats.astype(jnp.bfloat16)
    low = (feats - high.astype(np.float32)).astype(jnp.bfloat16)
    return (table, np.concatenate([high, low, high, np.zeros_like(high)], axis=1))


def pair_body(
    hidden_in,
    gainfirst,
    shiftfirst,
    valueright,
    valueleft,
    shaperight,
    shapeleft,
    convtaps,
    posweight,
    posbias,
    sinefreq,
    midweight,
    midbias,
    filterout,
    outright,
    outleft,
    gainsecond,
    shiftsecond,
    gateright,
    gateleft,
    liftright,
    liftleft,
    lowerright,
    lowerleft,
    grad_out,
):
    rows = hidden_in.shape[0]
    length = 2 * rows
    table_cos, table_sin = transform_tables(length)
    def out(extent, dtype=BF16):
        return jax.ShapeDtypeStruct(extent, dtype)

    def buf(*extent, dtype=BF16):
        return pltpu.VMEM(extent, dtype)

    vmem = pl.BlockSpec(memory_space=pltpu.VMEM)
    hbm = pl.BlockSpec(memory_space=pl.ANY)
    results = pl.pallas_call(
        whole_kernel,
        out_shape=(
            out((rows, 384)),
            out((rows, 384)),
            out((CHANNEL_ROWS, 384)),
            out((2, 2 * PART, 384)),
        ),
        in_specs=[hbm] * 4 + [vmem] * 12 + [hbm] * 13,
        out_specs=[hbm] * 4,
        scratch_shapes=[
            buf(rows, 384),
            buf(rows, 384),
            buf(CHANNEL_ROWS, 384),
            buf(2, 2 * PART, 384),
            pltpu.SemaphoreType.DMA((8,)),
            buf(rows, D),
            buf(length, length),
            buf(length, length),
            buf(8, D, dtype=F32),
            buf(16, 128, dtype=F32),
            buf(D, D),
            buf(384, 512),
            buf(384, 512),
            buf(512, 384),
            buf(2, 384, D),
            buf(D, D),
            buf(2, 256, D),
            buf(2, 256, D),
            buf(2, D, 256),
            buf(384, D),
            buf(2, rows, 384),
            buf(rows, 128, dtype=F32),
            buf(rows, D),
            buf(rows, D),
            buf(2, rows, PAD),
            buf(2, rows, PAD),
            buf(2, rows, PAD, dtype=F32),
            buf(length + 8, PAD, dtype=F32),
            buf(length, PAD),
            buf(length, 128),
            buf(length, 128),
            buf(length, 128),
            buf(length, 128),
            buf(length, 128),
            buf(length, 128),
            buf(2, length, PAD, dtype=F32),
            buf(2, length, PAD),
            buf(2, length, PAD),
            buf(2, rows, PAD),
            buf(2, rows, PAD),
            buf(2, rows, 384),
            buf(TILE, D, dtype=F32),
            buf(rows, D),
            buf(rows, D),
            buf(2, TILE, D, dtype=F32),
            buf(2, TILE, D, dtype=F32),
            buf(2, rows, D),
            buf(rows, 384),
            buf(rows, 384, dtype=F32),
            buf(rows, 384),
            buf(rows, 384),
            buf(rows, 384),
            buf(2, rows, D),
            buf(2, rows, D),
            buf(rows, D),
            buf(TILE, D, dtype=F32),
            buf(TILE, D),
            buf(TILE, D),
            buf(rows, 384),
            buf(2, rows, PAD),
            buf(2, rows, PAD),
            buf(length + 8, PAD, dtype=F32),
            buf(2, rows, PAD),
            buf(rows, D),
            buf(TILE, 384),
            buf(TILE, 384),
            buf(TILE, 384),
            buf(rows, 384, dtype=F32),
            buf(TILE, D),
            buf(rows, 192),
            buf(rows, 192),
            buf(rows, 256),
            buf(rows, 256),
            buf(2, 384, 192),
            buf(8, D, dtype=F32),
            buf(128, PAD, dtype=F32),
            buf(128, PAD),
            buf(16, 384, dtype=F32),
            buf(144, 128, dtype=F32),
            buf(8, D, dtype=F32),
            pltpu.SemaphoreType.DMA((16,)),
            pltpu.SemaphoreType.DMA((16,)),
            pltpu.SemaphoreType.DMA((20,)),
            buf(5, STEP_ROWS[4], 384),
            pltpu.SemaphoreType.DMA((40,)),
            pltpu.SemaphoreType.DMA((40,)),
            pltpu.SemaphoreType.REGULAR((20,)),
            buf(PART, 384),
            buf(PART // 2, 384),
            buf(7, CHUNK, 384),
            pltpu.SemaphoreType.DMA((42,)),
            pltpu.SemaphoreType.DMA((42,)),
        ],
        compiler_params=pltpu.CompilerParams(
            collective_id=0, has_side_effects=True, vmem_limit_bytes=63 * 1024 * 1024
        ),
    )(
        hidden_in,
        grad_out,
        table_cos,
        table_sin,
        *place_table(length),
        gainfirst,
        shiftfirst,
        gainsecond,
        shiftsecond,
        convtaps,
        posweight,
        posbias,
        midbias,
        sinefreq,
        midweight,
        filterout,
        valueright,
        valueleft,
        shaperight,
        shapeleft,
        outright,
        outleft,
        gateright,
        gateleft,
        liftright,
        liftleft,
        lowerright,
        lowerleft,
    )
    count = D // (lax.axis_size("wide") * lax.axis_size("narrow"))
    square = out((192, D), F32)
    grads = pl.pallas_call(
        finish_kernel,
        out_shape=(
            out((rows, 384)),
            out((rows, 384)),
            out((D,), F32),
            out((D,), F32),
            square,
            square,
            square,
            square,
            out((3, D), F32),
            out((5, 128), F32),
            out((128,), F32),
            out((128,), F32),
            out((128, 128), F32),
            out((128,), F32),
            out((count, 128), F32),
            square,
            square,
            out((D,), F32),
            out((D,), F32),
            out(gateright.shape, F32),
            out(gateleft.shape, F32),
            out(liftright.shape, F32),
            out(liftleft.shape, F32),
            out(lowerright.shape, F32),
            out(lowerleft.shape, F32),
        ),
        in_specs=[hbm] * 4,
        out_specs=[hbm] * 2 + [vmem] * 2 + [hbm] * 4 + [vmem] * 7 + [hbm] * 2 + [vmem] * 2 + [hbm] * 6,
        scratch_shapes=[
            buf(CHANNEL_ROWS, 384),
            buf(2, 2 * PART, 384),
            buf(rows, 384),
            buf(rows, 384),
            *[buf(192, D, dtype=F32)] * 6,
            buf(*gateright.shape, dtype=F32),
            buf(*gateleft.shape, dtype=F32),
            buf(*liftright.shape, dtype=F32),
            buf(*liftleft.shape, dtype=F32),
            buf(*lowerright.shape, dtype=F32),
            buf(*lowerleft.shape, dtype=F32),
            buf(144, 128, dtype=F32),
            pltpu.SemaphoreType.DMA((7,)),
            pltpu.SemaphoreType.DMA((14,)),
        ],
        compiler_params=pltpu.CompilerParams(vmem_limit_bytes=60 * 1024 * 1024),
    )(*results)
    return (*grads[:14], grads[14].T, *grads[15:])


def solution(mesh):
    pairs = mesh.shape["wide"] == 2 * SEQS and mesh.shape["narrow"] == 2
    return jax.shard_map(
        pair_body if pairs else body,
        mesh=mesh,
        in_specs=(
            P("wide", None),
            P(),
            P(),
            P(),
            P(),
            P(),
            P(),
            P(),
            P(),
            P(),
            P(),
            P(),
            P(),
            P(),
            P(),
            P(),
            P(),
            P(),
            P(None, "narrow"),
            P(None, "narrow"),
            P(None, "narrow"),
            P(None, "narrow"),
            P(None, "narrow"),
            P("narrow", None),
            P("wide", "narrow"),
        ),
        out_specs=(
            P("wide", "narrow"),
            P("wide", "narrow"),
            P(),
            P(),
            P(),
            P(),
            P(),
            P(),
            P(),
            P(),
            P(),
            P(),
            P(),
            P(),
            P(None, ("wide", "narrow")),
            P(),
            P(),
            P(),
            P(),
            P(None, "narrow"),
            P(None, "narrow"),
            P(None, "narrow"),
            P(None, "narrow"),
            P(None, "narrow"),
            P("narrow", None),
        ),
        check_vma=False,
    )
```
